32 devices in a mesh: dp: 8 (over y, x, core), head: 4 (over z).
Axes of the slice: x: 2, y: 2, z: 4, core: 2. Of those that a mesh axis runs over, the one named last changes fastest.
Arguments:
- tokens: bfloat16 [8, 4, 512, 768], P('dp'), may hold values from -6 to 6
- doc_ids: int32 [8, 4, 512], P('dp'), may hold values from 0 to 7, never falling along the last dimension, each value on 1 to 192 neighbouring positions
- reset: int32 [8, 4], P('dp'), may hold values 0 or 1
- mem_init: bfloat16 [10, 768], replicated, may hold values from -6 to 6
- w_query: bfloat16 [768, 768], P(None, 'head'), may hold values from -0.21875 to 0.21875
- w_key: bfloat16 [768, 768], P(None, 'head'), may hold values from -0.21875 to 0.21875
- w_value: bfloat16 [768, 768], P(None, 'head'), may hold values from -0.21875 to 0.21875
- b_query: bfloat16 [12, 64], P('head'), may hold values from -2 to 2
- b_value: bfloat16 [12, 64], P('head'), may hold values from -2 to 2
- w_out: bfloat16 [768, 768], P('head'), may hold values from -1.25 to 1.25
- b_out: bfloat16 [768], replicated, may hold values from -2 to 2
- gain_attn: bfloat16 [768], replicated, may hold values from 0.5 to 1.5
- shift_attn: bfloat16 [768], replicated, may hold values from -2 to 2
- w_in: bfloat16 [768, 3072], P(None, ('dp', 'head')), may hold values from -0.21875 to 0.21875
- b_in: bfloat16 [3072], P(('dp', 'head')), may hold values from -3 to 3
- w_down: bfloat16 [3072, 768], P(('dp', 'head')), may hold values from -0.109375 to 0.109375
- b_down: bfloat16 [768], replicated, may hold values from -2 to 2
- gain_ffn: bfloat16 [768], replicated, may hold values from 0.5 to 1.5
- shift_ffn: bfloat16 [768], replicated, may hold values from -2 to 2
- cotangent: bfloat16 [8, 4, 512, 768], P('dp', None, 'head'), may hold values from -6 to 6
Outputs:
- output: bfloat16 [8, 4, 512, 768], P('dp', None, 'head')
- memory_norm: float32 [8, 4], P('dp')
- grad_tokens: float32 [8, 4, 512, 768], P('dp', None, 'head')
- grad_w_query: float32 [768, 768], P('dp', 'head')
- grad_w_key: float32 [768, 768], P('dp', 'head')
- grad_w_value: float32 [768, 768], P('dp', 'head')
- grad_b_query: float32 [12, 64], P('head', 'dp')
- grad_b_value: float32 [12, 64], P('head', 'dp')
- grad_w_out: float32 [768, 768], P('head', 'dp')
- grad_b_out: float32 [768], P(('dp', 'head'))
- grad_gain_attn: float32 [768], P(('dp', 'head'))
- grad_shift_attn: float32 [768], P(('dp', 'head'))
- grad_w_in: float32 [768, 3072], P(None, ('dp', 'head'))
- grad_b_in: float32 [3072], P(('dp', 'head'))
- grad_w_down: float32 [3072, 768], P(('dp', 'head'))
- grad_b_down: float32 [768], P(('dp', 'head'))
- grad_gain_ffn: float32 [768], P(('dp', 'head'))
- grad_shift_ffn: float32 [768], P(('dp', 'head'))
- grad_mem_init: float32 [10, 768], P(None, ('dp', 'head'))
The draws below stay inside these ranges and needn't reach their ends.
Inputs may be any that keep to these rules, and one draw needn't show every extreme that they name: `doc_ids`: within a segment the document numbers never fall, and each document has at most 192 tokens.
All inputs are finite; a program needn't handle non-finite values. No bound on the sum of `reset` on one device may be relied on, other than what follows from the above.
Results may differ from the reference program's by a relative error of at most 0.017.
Values may be sent and summed in bfloat16 or wider, within the bound.
No kernel may reach another device: no remote copies, remote signals or barrier semaphores. Data moves between devices by JAX's collectives and lax.ppermute only.
A program may use at most 192 MiB of HBM per device.

```python
import math
import jax
import jax.numpy as jnp
import numpy as np
from jax import lax

D = 768
HEADS = 12
HEAD_DIM = 64
FF = 3072
MEM = 10
SEG_LEN = 512
SEGS = 4
DOCS = 8
DOC_MOST = 192
CHAINS = 8


def set_ends(array, rng, smallest, top_value):
    dims = array.shape
    index_at = [jax.random.randint(jax.random.fold_in(rng, axis), (), 0, dims[axis]) for axis in range(len(dims))]
    array = array.at[tuple(index_at)].set(smallest)
    longest = dims.index(max(dims))
    index_at[longest] = (index_at[longest] + 1) % dims[longest]
    return array.at[tuple(index_at)].set(top_value)


def with_spikes(entries, own_key, source, target, parts, factor):
    owner, partner = [(jnp.arange(entries.shape[axis_at]) // (entries.shape[axis_at] // parts)).reshape([-1 if axis == axis_at else 1 for axis in range(entries.ndim)]) for axis_at in (source, target)]
    chosen = jax.random.permutation(own_key, parts)[partner]
    strong = (owner == chosen) | (owner == (partner + parts // 2) % parts)
    return jnp.where(strong, factor * entries, entries)


def level_of(stream_key, dims, cuts, low, top_value):
    factor_of = 1.0
    for position, blocks in cuts:
        draws = jax.random.uniform(jax.random.fold_in(jax.random.fold_in(stream_key, 6), position), (blocks,), jnp.float32, low / len(cuts), top_value / len(cuts))
        factor_of = factor_of * jnp.repeat(jnp.exp(draws), dims[position] // blocks).reshape((-1,) + (1,) * (len(dims) - 1 - position))
    return factor_of


def profile(amount, total, bound, lean):
    loads = [(1 << 20) // math.isqrt(grade ** lean) + 1 for grade in range(2, amount + 1)]
    spare, counts = total - bound - (amount - 1), [1] * (amount - 1)
    while spare > 0:
        candidates = [i for i in range(amount - 1) if counts[i] < bound]
        mass, left = sum([loads[i] for i in candidates]), spare
        for i in candidates:
            more = min(bound - counts[i], max(1, left * loads[i] // mass), spare)
            counts[i] = counts[i] + more
            spare = spare - more
    return np.array([bound] + counts)


def uneven(key, number_of, total, limit, lean):
    if number_of == 2:
        one = jax.random.randint(key, (), max(1, total - limit), min(limit, total - 1) + 1)
        return jnp.stack([one, total - one])
    sizes = jnp.asarray(profile(number_of, total, limit, lean), jnp.int32)
    twos = (number_of - 1) // 2
    giver, receiver = sizes[1:1 + 2 * twos:2], sizes[2:2 + 2 * twos:2]
    slack = jnp.minimum(giver - 1, limit - receiver)
    moved = jax.random.randint(jax.random.fold_in(key, 1), (twos,), 0, 1 << 20) % (slack + 1)
    sizes = sizes.at[1:1 + 2 * twos:2].set(giver - moved).at[2:2 + 2 * twos:2].set(receiver + moved)
    return sizes[jax.random.permutation(jax.random.fold_in(key, 2), number_of)]


def noise(stream_key, extent, deviation, reach, cuts=(), kind=jnp.bfloat16):
    values = deviation * jax.random.normal(stream_key, extent, jnp.float32)
    if cuts:
        values = values * level_of(stream_key, extent, cuts, -0.22, 0.18)
    return jnp.clip(values, -reach, reach).astype(kind)


def heavy_noise(key, shape, width, bound, cuts, heavy, kind=jnp.bfloat16):
    drawn = width * jax.random.normal(key, shape, jnp.float32)
    if cuts:
        drawn = drawn * level_of(key, shape, cuts, -0.22, 0.18)
    return jnp.clip(with_spikes(drawn, jax.random.fold_in(key, 3), *heavy), -bound, bound).astype(kind)


def setup_inputs(seed: int = 0) -> dict:
    key_list = jax.random.split(jax.random.key(seed), 21)
    tokens = noise(key_list[0], (CHAINS, SEGS, SEG_LEN, D), 1.0, 6.0, ((0, 8),))
    doc_ids = jax.vmap(lambda own: jnp.searchsorted(jnp.cumsum(uneven(own, DOCS, SEG_LEN, DOC_MOST, 2)), jnp.arange(SEG_LEN), side="right"))(jax.random.split(key_list[1], CHAINS * SEGS)).reshape((CHAINS, SEGS, SEG_LEN)).astype(jnp.int32)
    reset = set_ends((jax.random.randint(key_list[2], (CHAINS, SEGS), 0, 2) < 1).astype(jnp.int32), jax.random.fold_in(key_list[2], 1), 0, 1)
    mem_init = noise(key_list[3], (MEM, D), 1.0, 6.0)
    w_query = noise(key_list[4], (D, D), D ** -0.5, 0.21875, ((1, 4),))
    w_key = noise(key_list[5], (D, D), D ** -0.5, 0.21875, ((1, 4),))
    w_value = noise(key_list[6], (D, D), D ** -0.5, 0.21875, ((1, 4),))
    b_query = noise(key_list[7], (HEADS, HEAD_DIM), 0.3, 2.0, ((0, 4),))
    b_value = noise(key_list[8], (HEADS, HEAD_DIM), 0.3, 2.0, ((0, 4),))
    w_out = noise(key_list[9], (D, D), (D // 32) ** -0.5, 1.25, ((0, 4),))
    b_out = noise(key_list[10], (D,), 0.3, 2.0)
    gain_attn = jnp.clip(1.0 + 0.1 * jax.random.normal(key_list[11], (D,), jnp.float32), 0.5, 1.5).astype(jnp.bfloat16)
    shift_attn = noise(key_list[12], (D,), 0.3, 2.0)
    w_in = noise(key_list[13], (D, FF), D ** -0.5, 0.21875, ((1, 32),))
    b_in = noise(key_list[14], (FF,), 0.5, 3.0, ((0, 32),))
    w_down = noise(key_list[15], (FF, D), FF ** -0.5, 0.109375, ((0, 32),))
    b_down = noise(key_list[16], (D,), 0.3, 2.0)
    gain_ffn = jnp.clip(1.0 + 0.1 * jax.random.normal(key_list[17], (D,), jnp.float32), 0.5, 1.5).astype(jnp.bfloat16)
    shift_ffn = noise(key_list[18], (D,), 0.3, 2.0)
    cotangent = heavy_noise(key_list[19], (CHAINS, SEGS, SEG_LEN, D), 1.0, 6.0, ((0, 8), (2, 4)), (0, 3, 8, 2.0))
    return dict(tokens=tokens, doc_ids=doc_ids, reset=reset, mem_init=mem_init, w_query=w_query, w_key=w_key, w_value=w_value, b_query=b_query, b_value=b_value, w_out=w_out, b_out=b_out, gain_attn=gain_attn, shift_attn=shift_attn, w_in=w_in, b_in=b_in, w_down=w_down, b_down=b_down, gain_ffn=gain_ffn, shift_ffn=shift_ffn, cotangent=cotangent)


EPSILON = 1e-06
SCALE = 0.125
NEGATIVE = -1e+30
ROOT_HALF = 0.7071067811865476
HIGHEST = lax.Precision.HIGHEST

@jax.custom_vjp
def low(v):
    return lax.optimization_barrier(v.astype(jnp.bfloat16)).astype(jnp.float32)

@jax.custom_vjp
def low_back(v):
    return v

def low_keep(v):
    return (low(v), None)

def low_pass(kept, grad):
    return (grad,)

def back_keep(v):
    return (v, None)

def back_low(kept, grad):
    return (low(grad),)
low.defvjp(low_keep, low_pass)
low_back.defvjp(back_keep, back_low)

def dense_product(left, right):
    return jnp.dot(left, right, precision=HIGHEST)

def plain_norm(inputs):
    mean = lax.optimization_barrier(jnp.mean(inputs, -1, keepdims=True))
    centred = inputs - mean
    variance = lax.optimization_barrier(jnp.mean(centred * centred, -1, keepdims=True))
    return centred * lax.rsqrt(variance + EPSILON)

def gelu_exact(inputs):
    return 0.5 * inputs * (1.0 + jax.scipy.special.erf(inputs * ROOT_HALF))

def attend(queries, keys_in, values, allowed):
    scores = jnp.einsum('qhd,khd->hqk', queries, keys_in, precision=HIGHEST) * SCALE
    scores = jnp.where(allowed[None], low_back(scores), NEGATIVE)
    row_max = lax.optimization_barrier(jnp.max(scores, -1, keepdims=True))
    raised = jnp.exp(scores - row_max)
    soft_weights = raised / lax.optimization_barrier(jnp.sum(raised, -1, keepdims=True))
    return jnp.einsum('hqk,khd->qhd', low(soft_weights), values, precision=HIGHEST)

def chain_forward(params, chain_tokens, documents, resets):
    w_query, w_key, w_value, b_query, b_value, w_out, b_out, gain_attn, shift_attn, w_in, b_in, w_down, b_down, gain_ffn, shift_ffn, mem_init = params
    carried = mem_init
    marker = jnp.full((MEM,), -1, jnp.int32)
    outputs = []
    norm_list = []
    for segment in range(SEGS):
        read_memory = jnp.where(resets[segment] > 0, mem_init, carried)
        all_rows = jnp.concatenate([read_memory, chain_tokens[segment], read_memory], 0)
        rows_low = low(all_rows)
        queries = low(low_back(dense_product(rows_low, w_query) + b_query.reshape(-1)))
        key_low = low(low_back(dense_product(rows_low, w_key)))
        values = low(low_back(dense_product(rows_low, w_value) + b_value.reshape(-1)))
        row_marks = jnp.concatenate([marker, documents[segment].astype(jnp.int32), marker])
        allowed = (row_marks[:, None] == row_marks[None, :]) | (row_marks[:, None] < 0) | (row_marks[None, :] < 0)
        attended = jax.checkpoint(attend)(queries.reshape(-1, HEADS, HEAD_DIM), key_low.reshape(-1, HEADS, HEAD_DIM), values.reshape(-1, HEADS, HEAD_DIM), allowed)
        attended = low(low_back(attended.reshape(-1, D)))
        mixed_sum = low_back(dense_product(attended[MEM:], w_out))
        z_attn = all_rows[MEM:] + mixed_sum + b_out
        hidden = plain_norm(z_attn) * gain_attn + shift_attn
        pre_act = low_back(dense_product(low(hidden), w_in) + b_in)
        ffn_out = low_back(dense_product(low(gelu_exact(pre_act)), w_down) + b_down)
        result = plain_norm(hidden + ffn_out) * gain_ffn + shift_ffn
        outputs.append(result[:SEG_LEN])
        carried = result[SEG_LEN:]
        norm_list.append(jnp.sqrt(jnp.mean(carried * carried)))
    return (jnp.stack(outputs), jnp.stack(norm_list))

def reference(tokens, doc_ids, reset, mem_init, w_query, w_key, w_value, b_query, b_value, w_out, b_out, gain_attn, shift_attn, w_in, b_in, w_down, b_down, gain_ffn, shift_ffn, cotangent):
    params = (w_query.astype(jnp.float32), w_key.astype(jnp.float32), w_value.astype(jnp.float32), b_query.astype(jnp.float32), b_value.astype(jnp.float32), w_out.astype(jnp.float32), b_out.astype(jnp.float32), gain_attn.astype(jnp.float32), shift_attn.astype(jnp.float32), w_in.astype(jnp.float32), b_in.astype(jnp.float32), w_down.astype(jnp.float32), b_down.astype(jnp.float32), gain_ffn.astype(jnp.float32), shift_ffn.astype(jnp.float32), mem_init.astype(jnp.float32))

    def whole(token_values, weights):

        def chain_step(carry, items):
            result, norms = chain_forward(weights, items[0], items[1], items[2])
            return (carry, (result, norms))
        carry, (result, norms) = lax.scan(chain_step, jnp.zeros((), jnp.float32), (token_values, doc_ids, reset))
        return (result, norms)
    (result, norms), pull = jax.vjp(whole, tokens.astype(jnp.float32), params)
    grad_tokens, grads = pull((cotangent.astype(jnp.float32), jnp.zeros_like(norms)))
    return (result.astype(jnp.bfloat16), norms, grad_tokens, grads[0], grads[1], grads[2], grads[3], grads[4], grads[5], grads[6], grads[7], grads[8], grads[9], grads[10], grads[11], grads[12], grads[13], grads[14], grads[15])
```

```python
import functools

import jax
import jax.numpy as jnp
from jax import lax
from jax.experimental import pallas as pl
from jax.experimental.pallas import tpu as pltpu
from jax.sharding import PartitionSpec as P

EPSILON = 1e-06
SCALE = 0.125
NEGATIVE = -1e30
ROOT_HALF = 0.7071067811865476
DENSITY = 0.3989422804014327
LOW = jnp.bfloat16
FULL = jnp.float32
PAD = 16
VECTORS = ("b_query", "b_value", "b_out", "gain_attn", "shift_attn", "b_down", "gain_ffn", "shift_ffn")
VMEM_LIMIT = 60 * 1024 * 1024


def nn(left, right):
    return lax.dot_general(left, right, (((1,), (0,)), ((), ())), preferred_element_type=FULL)


def nt(left, right):
    return lax.dot_general(left, right, (((1,), (1,)), ((), ())), preferred_element_type=FULL)


def tn(left, right):
    return lax.dot_general(left, right, (((0,), (0,)), ((), ())), preferred_element_type=FULL)


def norm_parts(rows):
    centred = rows - jnp.mean(rows, -1, keepdims=True)
    inverse = lax.rsqrt(jnp.mean(centred * centred, -1, keepdims=True) + EPSILON)
    return centred * inverse, inverse


def norm_pull(normed, inverse, grad):
    along = jnp.mean(grad * normed, -1, keepdims=True)
    return inverse * (grad - jnp.mean(grad, -1, keepdims=True) - normed * along)


def gelu(v):
    return 0.5 * v * (1.0 + lax.erf(v * ROOT_HALF))


def gelu_slope(v):
    return 0.5 * (1.0 + lax.erf(v * ROOT_HALF)) + v * (DENSITY * jnp.exp(-0.5 * v * v))


def swap(array, axis, bit):
    return lax.ppermute(array, axis, [(i, i ^ bit) for i in range(lax.axis_size(axis))])


def bits_of(count):
    return [1 << i for i in range(count.bit_length() - 1)]


def gather_blocks(array, order, dim):
    rounds = [array] + [swap(array, "head", j) for j in range(1, lax.axis_size("head"))]
    array = jnp.concatenate(rounds, dim)
    for bit in order:
        array = jnp.concatenate([array, swap(array, "dp", bit)], dim)
    return array


def scatter_blocks(array, order):
    for bit in reversed(order):
        half = array.shape[1] // 2
        other = swap(array[:, half:], "dp", bit)
        array = (array[:, :half].astype(FULL) + other.astype(FULL)).astype(array.dtype)
    heads = lax.axis_size("head")
    block = array.shape[1] // heads
    total = array[:, :block].astype(FULL)
    for j in range(1, heads):
        total = total + swap(array[:, j * block : (j + 1) * block], "head", j).astype(FULL)
    return total


def scatter_rows(array, order, keep_full=False):
    count = lax.axis_size("dp")
    levels = len(bits_of(count))
    me = lax.axis_index("dp")
    array = array.reshape(array.shape[0], *([2] * levels), -1, array.shape[-1])
    left = bits_of(count)[::-1]
    for step, bit in enumerate(order):
        axis = 1 + left.index(bit)
        left.remove(bit)
        mine = (me // bit) % 2
        other = swap(lax.dynamic_index_in_dim(array, 1 - mine, axis, False), "dp", bit)
        own = lax.dynamic_index_in_dim(array, mine, axis, False)
        array = own.astype(FULL) + other.astype(FULL)
        if not (keep_full and step == levels - 1):
            array = array.astype(LOW)
    return array


def natural_to_relative(array, axes):
    me = 0
    for axis in axes:
        me = me * lax.axis_size(axis) + lax.axis_index(axis)
    index = jnp.arange(array.shape[0])
    pick = ((me ^ index)[:, None] == index[None, :]).astype(FULL)
    return jnp.einsum("jn,n...->j...", pick, array, precision=lax.Precision.HIGHEST)


def head_mask(rows, width, heads):
    group = lax.broadcasted_iota(jnp.int32, (rows, width), 0) // PAD
    column = lax.broadcasted_iota(jnp.int32, (rows, width), 1) // (width // heads)
    return group == column


def by_head(rows, mask, heads):
    return jnp.where(mask, jnp.concatenate([rows] * heads, 0), jnp.zeros((), rows.dtype))


def own_head(rows, mask, heads):
    kept = jnp.where(mask, rows, 0.0)
    total = kept[:PAD]
    for i in range(1, heads):
        total = total + kept[i * PAD : (i + 1) * PAD]
    return total


def vector(vec_ref, name):
    i = VECTORS.index(name)
    return vec_ref[i : i + 1, :]


def chain_forward(
    heads,
    memory_rows,
    reset_ref,
    init_ref,
    attn_ref,
    first_ref,
    second_ref,
    bias_ref,
    vec_ref,
    key_ref,
    value_ref,
    read_ref,
    qkv_ref,
    soft_ref,
    soft_mem_ref,
    attended_ref,
    z_attn_ref,
    hidden_ref,
    pre_ref,
    z_ffn_ref,
    norm_ref,
):
    segments, _, width = key_ref.shape
    rows = heads * PAD
    mask = head_mask(rows, width, heads)
    real_key = lax.broadcasted_iota(jnp.int32, (rows, PAD), 1) < memory_rows
    real_row = lax.broadcasted_iota(jnp.int32, (PAD, width), 0) < memory_rows
    half = first_ref.shape[1]

    def step(s, carried):
        fresh = (reset_ref[0, s] > 0) | (s == 0)
        read = jnp.where(fresh, init_ref[...], carried)
        read_ref[s] = read
        low = read.astype(LOW)
        queries = (nt(low, attn_ref[0]) + vector(vec_ref, "b_query")).astype(LOW)
        keys = nt(low, attn_ref[1]).astype(LOW)
        values = (nt(low, attn_ref[2]) + vector(vec_ref, "b_value")).astype(LOW)
        qkv_ref[s, 0] = queries
        qkv_ref[s, 1] = keys
        qkv_ref[s, 2] = values
        spread = by_head(queries, mask, heads)
        scores = nt(spread, key_ref[s]) * SCALE
        scores_mem = jnp.where(real_key, nt(spread, keys) * SCALE, NEGATIVE)
        top = jnp.maximum(
            jnp.max(scores, -1, keepdims=True), jnp.max(scores_mem, -1, keepdims=True)
        )
        raised = jnp.exp(scores - top)
        raised_mem = jnp.exp(scores_mem - top)
        total = jnp.sum(raised, -1, keepdims=True) + 2.0 * jnp.sum(raised_mem, -1, keepdims=True)
        soft = raised / total
        soft_mem = raised_mem / total
        soft_ref[s] = soft
        soft_mem_ref[s] = soft_mem
        mixed = nn(soft.astype(LOW), value_ref[s]) + 2.0 * nn(soft_mem.astype(LOW), values)
        attended = own_head(mixed, mask, heads).astype(LOW)
        attended_ref[s] = attended
        z_attn = read + nn(attended, attn_ref[3]) + vector(vec_ref, "b_out")
        z_attn_ref[s] = z_attn
        normed, _ = norm_parts(z_attn)
        hidden = normed * vector(vec_ref, "gain_attn") + vector(vec_ref, "shift_attn")
        hidden_low = hidden.astype(LOW)
        hidden_ref[s] = hidden_low
        z_ffn = hidden + vector(vec_ref, "b_down")
        for i, pair_ref in enumerate((first_ref, second_ref)):
            pre = nt(hidden_low, pair_ref[0]) + bias_ref[:, i * half : (i + 1) * half]
            pre_ref[s, :, i * half : (i + 1) * half] = pre
            z_ffn = z_ffn + nn(gelu(pre).astype(LOW), pair_ref[1])
        z_ffn_ref[s] = z_ffn
        normed, _ = norm_parts(z_ffn)
        result = normed * vector(vec_ref, "gain_ffn") + vector(vec_ref, "shift_ffn")
        square = jnp.sum(jnp.where(real_row, result * result, 0.0), axis=(0, 1), keepdims=True)
        norm_ref[s] = jnp.broadcast_to(
            jnp.sqrt(square / (memory_rows * width)), norm_ref.shape[1:]
        )
        return result

    lax.fori_loop(0, segments, step, init_ref[...])


def chain_backward(
    heads,
    memory_rows,
    reset_ref,
    attn_ref,
    first_ref,
    second_ref,
    vec_ref,
    key_ref,
    value_ref,
    qkv_ref,
    soft_ref,
    soft_mem_ref,
    z_attn_ref,
    pre_ref,
    z_ffn_ref,
    token_part_ref,
    score_ref,
    attended_ref,
    mixed_ref,
    small_ref,
    ffn_ref,
    pre_grad_ref,
    bias_grad_ref,
    vec_grad_ref,
    init_grad_ref,
):
    segments, _, width = key_ref.shape
    rows = heads * PAD
    mask = head_mask(rows, width, heads)
    half = first_ref.shape[1]
    vec_grad_ref[...] = jnp.zeros_like(vec_grad_ref)
    bias_grad_ref[...] = jnp.zeros_like(bias_grad_ref)

    def add_vector(name, grad):
        i = VECTORS.index(name)
        vec_grad_ref[i : i + 1, :] += jnp.sum(grad, 0, keepdims=True)

    last = segments - 1
    grad_key = token_part_ref[last, :PAD].astype(LOW)
    grad_value = token_part_ref[last, PAD:].astype(LOW)
    small_ref[last, 0] = jnp.zeros((PAD, width), LOW)
    small_ref[last, 1] = grad_key
    small_ref[last, 2] = grad_value
    add_vector("b_value", 2.0 * grad_value.astype(FULL))
    grad_read = 2.0 * (nn(grad_key, attn_ref[1]) + nn(grad_value, attn_ref[2]))
    stop = reset_ref[0, last] > 0
    init_grad_ref[...] = jnp.where(stop, grad_read, 0.0)
    grad_write = jnp.where(stop, 0.0, grad_read)

    def step(back, grad_write):
        s = segments - 2 - back
        normed, inverse = norm_parts(z_ffn_ref[s])
        add_vector("gain_ffn", grad_write * normed)
        add_vector("shift_ffn", grad_write)
        grad_sum = norm_pull(normed, inverse, grad_write * vector(vec_ref, "gain_ffn"))
        grad_low = grad_sum.astype(LOW)
        ffn_ref[s] = grad_low
        add_vector("b_down", grad_low.astype(FULL))
        grad_hidden = grad_sum
        for i, pair_ref in enumerate((first_ref, second_ref)):
            part = slice(i * half, (i + 1) * half)
            grad_act = nt(grad_low, pair_ref[1])
            grad_pre = (grad_act * gelu_slope(pre_ref[s, :, part])).astype(LOW)
            pre_grad_ref[s, :, part] = grad_pre
            bias_grad_ref[:, part] += jnp.sum(grad_pre.astype(FULL), 0, keepdims=True)
            grad_hidden = grad_hidden + nn(grad_pre, pair_ref[0])
        normed, inverse = norm_parts(z_attn_ref[s])
        add_vector("gain_attn", grad_hidden * normed)
        add_vector("shift_attn", grad_hidden)
        grad_attn = norm_pull(normed, inverse, grad_hidden * vector(vec_ref, "gain_attn"))
        add_vector("b_out", grad_attn)
        grad_mixed = grad_attn.astype(LOW)
        mixed_ref[s] = grad_mixed
        grad_attended = nt(grad_mixed, attn_ref[3]).astype(LOW)
        attended_ref[s] = grad_attended
        queries, keys, values = qkv_ref[s, 0], qkv_ref[s, 1], qkv_ref[s, 2]
        spread = by_head(grad_attended, mask, heads)
        soft, soft_mem = soft_ref[s], soft_mem_ref[s]
        pull = nt(spread, value_ref[s])
        pull_mem = nt(spread, values)
        inner = jnp.sum(soft * pull, -1, keepdims=True) + 2.0 * jnp.sum(
            soft_mem * pull_mem, -1, keepdims=True
        )
        grad_score = (soft * (pull - inner)).astype(LOW)
        grad_score_mem = (soft_mem * (pull_mem - inner)).astype(LOW)
        score_ref[s] = grad_score
        grad_query = nn(grad_score, key_ref[s]) + 2.0 * nn(grad_score_mem, keys)
        grad_query = (SCALE * own_head(grad_query, mask, heads)).astype(LOW)
        grad_key = SCALE * tn(grad_score_mem, by_head(queries, mask, heads))
        grad_key = (token_part_ref[s, :PAD] + grad_key).astype(LOW)
        grad_value = tn(soft_mem.astype(LOW), spread)
        grad_value = (token_part_ref[s, PAD:] + grad_value).astype(LOW)
        small_ref[s, 0] = grad_query
        small_ref[s, 1] = grad_key
        small_ref[s, 2] = grad_value
        add_vector("b_query", grad_query.astype(FULL))
        add_vector("b_value", 2.0 * grad_value.astype(FULL))
        grad_read = 2.0 * (nn(grad_key, attn_ref[1]) + nn(grad_value, attn_ref[2]))
        grad_read = grad_read + nn(grad_query, attn_ref[0]) + grad_attn
        stop = (reset_ref[0, s] > 0) | (s == 0)
        init_grad_ref[...] += jnp.where(stop, grad_read, 0.0)
        return jnp.where(stop, 0.0, grad_read)

    lax.fori_loop(0, segments - 1, step, grad_write)


def whole_call(body, operands, shapes, flops):
    in_vmem = pl.BlockSpec(memory_space=pltpu.VMEM)
    in_smem = pl.BlockSpec(memory_space=pltpu.SMEM)
    size = sum(a.size * a.dtype.itemsize for a in operands)
    return pl.pallas_call(
        body,
        out_shape=shapes,
        in_specs=[in_smem] + [in_vmem] * (len(operands) - 1),
        out_specs=[in_vmem] * len(shapes),
        compiler_params=pltpu.CompilerParams(vmem_limit_bytes=VMEM_LIMIT),
        cost_estimate=pl.CostEstimate(flops=flops, bytes_accessed=size, transcendentals=0),
    )(*operands)


def token_soft(q, k, km, allowed, real_key):
    scores = jnp.where(allowed, nt(q, k) * SCALE, NEGATIVE)
    scores_mem = jnp.where(real_key, nt(q, km) * SCALE, NEGATIVE)
    top = jnp.maximum(jnp.max(scores, -1, keepdims=True), jnp.max(scores_mem, -1, keepdims=True))
    raised = jnp.exp(scores - top)
    raised_mem = jnp.exp(scores_mem - top)
    total = jnp.sum(raised, -1, keepdims=True) + 2.0 * jnp.sum(raised_mem, -1, keepdims=True)
    inverse = 1.0 / total
    return raised * inverse, raised_mem * inverse


def token_attention(
    memory_rows, head_dim, row_ref, column_ref, q_ref, k_ref, v_ref, km_ref, vm_ref, out_ref
):
    q, k, v, km, vm = q_ref[...], k_ref[...], v_ref[...], km_ref[...], vm_ref[...]
    allowed = column_ref[...] == row_ref[...]
    real_key = lax.broadcasted_iota(jnp.int32, (q.shape[0], PAD), 1) < memory_rows
    lane = lax.broadcasted_iota(jnp.int32, q.shape, 1) // head_dim
    total = jnp.zeros(q.shape, FULL)
    for head in range(q.shape[1] // head_dim):
        mine = jnp.where(lane == head, q, jnp.zeros((), LOW))
        soft, soft_mem = token_soft(mine, k, km, allowed, real_key)
        mixed = nn(soft.astype(LOW), v) + 2.0 * nn(soft_mem.astype(LOW), vm)
        total = jnp.where(lane == head, mixed, total)
    out_ref[...] = total.astype(LOW)


def token_attention_back(
    memory_rows,
    head_dim,
    row_ref,
    column_ref,
    q_ref,
    k_ref,
    v_ref,
    km_ref,
    vm_ref,
    grad_ref,
    dq_ref,
    dk_ref,
    dv_ref,
    dmem_ref,
):
    q, k, v, km, vm, grad = (r[...] for r in (q_ref, k_ref, v_ref, km_ref, vm_ref, grad_ref))
    allowed = column_ref[...] == row_ref[...]
    real_key = lax.broadcasted_iota(jnp.int32, (q.shape[0], PAD), 1) < memory_rows
    lane = lax.broadcasted_iota(jnp.int32, q.shape, 1) // head_dim
    zero = jnp.zeros((), LOW)
    dq, dk, dv = (jnp.zeros(q.shape, FULL) for _ in range(3))
    dkm, dvm = (jnp.zeros(km.shape, FULL) for _ in range(2))
    for head in range(q.shape[1] // head_dim):
        mine = jnp.where(lane == head, q, zero)
        mine_grad = jnp.where(lane == head, grad, zero)
        soft, soft_mem = token_soft(mine, k, km, allowed, real_key)
        pull, pull_mem = nt(mine_grad, v), nt(mine_grad, vm)
        inner = jnp.sum(soft * pull, -1, keepdims=True) + 2.0 * jnp.sum(
            soft_mem * pull_mem, -1, keepdims=True
        )
        score = (soft * (pull - inner)).astype(LOW)
        score_mem = (soft_mem * (pull_mem - inner)).astype(LOW)
        dq = jnp.where(lane == head, nn(score, k) + 2.0 * nn(score_mem, km), dq)
        dk = dk + tn(score, mine)
        dv = dv + tn(soft.astype(LOW), mine_grad)
        dkm = dkm + tn(score_mem, mine)
        dvm = dvm + tn(soft_mem.astype(LOW), mine_grad)
    dq_ref[...] = (SCALE * dq).astype(LOW)
    dk_ref[...] = (SCALE * dk).astype(LOW)
    dv_ref[...] = dv.astype(LOW)
    dmem_ref[:PAD] = SCALE * dkm
    dmem_ref[PAD:] = dvm


def head_pairs(body, doc, operands, shapes, width, flops):
    seg_len = doc.shape[0]
    columns = lambda array: pl.BlockSpec((array.shape[0], width), lambda i: (0, i))
    return pl.pallas_call(
        body,
        grid=(operands[0].shape[1] // width,),
        out_shape=shapes,
        in_specs=[
            pl.BlockSpec((1, seg_len), lambda i: (0, 0)),
            pl.BlockSpec((seg_len, 1), lambda i: (0, 0)),
        ]
        + [columns(a) for a in operands],
        out_specs=[columns(s) for s in shapes],
        compiler_params=pltpu.CompilerParams(vmem_limit_bytes=VMEM_LIMIT),
        cost_estimate=pl.CostEstimate(
            flops=flops, bytes_accessed=8 * seg_len * operands[0].shape[1], transcendentals=0
        ),
    )(doc[None, :], doc[:, None], *operands)


def on_device(
    tokens,
    doc_ids,
    reset,
    mem_init,
    w_query,
    w_key,
    w_value,
    b_query,
    b_value,
    w_out,
    b_out,
    gain_attn,
    shift_attn,
    w_in,
    b_in,
    w_down,
    b_down,
    gain_ffn,
    shift_ffn,
    cotangent,
):
    chains, segments, seg_len, width = tokens.shape
    dps, groups = lax.axis_size("dp"), lax.axis_size("head")
    assert chains == 1 and segments == groups
    memory_rows = mem_init.shape[0]
    heads_here, head_dim = b_query.shape
    heads = heads_here * groups
    here = heads_here * head_dim
    units = w_in.shape[1]
    half_units = units // 2
    quarter = seg_len // groups
    dp, head = lax.axis_index("dp"), lax.axis_index("head")
    leader = (head == 0).astype(FULL)
    bits = bits_of(dps)
    order_a = bits[1:] + bits[:1]
    order_b = bits[1:][::-1] + bits[:1]
    levels = len(bits)
    tokens, doc_ids, cotangent = tokens[0], doc_ids[0], cotangent[0]

    shard = jnp.concatenate([w_query.T, w_key.T, w_value.T, w_out], 0)
    share = shard.shape[0] // dps
    chunk = lax.dynamic_slice_in_dim(shard, dp * share, share, 0)
    chunk = jnp.stack([swap(chunk, "head", j) for j in range(1, groups)])
    parts = []
    for rows, order in ((slice(0, share // 2), order_a), (slice(share // 2, share), order_b)):
        part = chunk[:, rows]
        have = []
        for bit in order:
            place = sum(1 for b in have if b > bit)
            have.append(bit)
            mine = (dp // bit) % 2
            other = swap(part, "dp", bit)
            part = jnp.where(
                mine == 1, jnp.stack([other, part], place), jnp.stack([part, other], place)
            )
        parts.append(part.reshape(dps, groups - 1, share // 2, width))
    others = jnp.concatenate(parts, 2).transpose(1, 0, 2, 3).reshape(groups - 1, 4, here, width)
    w_attn = jnp.concatenate([shard.reshape(4, 1, here, width), others.transpose(1, 0, 2, 3)], 1)
    w_attn = w_attn.reshape(4, groups * here, width)
    up = w_in.T
    first = gather_blocks(jnp.stack([up[:half_units], w_down[:half_units]]), order_a, 1)
    second = gather_blocks(jnp.stack([up[half_units:], w_down[half_units:]]), order_b, 1)

    head_bias = jnp.concatenate([b_query.reshape(1, -1), b_value.reshape(1, -1)], 0)
    bias_rows = jnp.concatenate([head_bias.reshape(1, -1), b_in.reshape(1, -1)], 1)
    bias_rows = jnp.concatenate(
        [bias_rows] + [swap(bias_rows, "head", j) for j in range(1, groups)], 0
    )
    head_bias = bias_rows[:, : 2 * here].reshape(groups, 2, here).transpose(1, 0, 2)
    head_bias = head_bias.reshape(2, width).astype(FULL)
    bias_in = bias_rows[:, 2 * here :]
    for bit in order_a:
        bias_in = jnp.concatenate([bias_in, swap(bias_in, "dp", bit)], 0)
    grid_a = [2] * levels + [groups]
    place_a = order_a[::-1]
    a_to_b = [place_a.index(b) for b in order_b[::-1]] + [levels]
    bias_in = bias_in.reshape(*grid_a, 2, half_units).astype(FULL)
    bias_in = jnp.concatenate(
        [
            bias_in[..., 0, :].reshape(1, -1),
            bias_in[..., 1, :].transpose(*a_to_b, levels + 1).reshape(1, -1),
        ],
        1,
    )
    vectors = jnp.concatenate(
        [head_bias]
        + [v[None].astype(FULL) for v in (b_out, gain_attn, shift_attn, b_down, gain_ffn, shift_ffn)],
        0,
    )
    (bias_query, bias_value, bias_out, gain_first, shift_first, bias_down, gain_second, shift_second) = (
        vectors[i : i + 1] for i in range(len(VECTORS))
    )

    keys = nt(tokens.reshape(-1, width), w_attn[1]).astype(LOW).reshape(tokens.shape)
    values = nt(tokens.reshape(-1, width), w_attn[2]) + bias_value
    values = values.astype(LOW).reshape(tokens.shape)
    x = lax.dynamic_index_in_dim(tokens, head, 0, False)
    doc = lax.dynamic_index_in_dim(doc_ids, head, 0, False)
    q = (nt(x, w_attn[0]) + bias_query).astype(LOW)
    k = lax.dynamic_index_in_dim(keys, head, 0, False)
    v = lax.dynamic_index_in_dim(values, head, 0, False)

    init = jnp.pad(mem_init.astype(FULL), ((0, PAD - memory_rows), (0, 0)))
    shape = jax.ShapeDtypeStruct
    ff = first.shape[1] + second.shape[1]
    rows_shape = lambda kind: shape((segments, PAD, width), kind)
    read, qkv, soft, soft_mem, attended_w, z_attn_w, hidden_w, pre_w, z_ffn_w, norms = whole_call(
        functools.partial(chain_forward, heads, memory_rows),
        (reset, init, w_attn, first, second, bias_in, vectors, keys, values),
        (
            rows_shape(FULL),
            shape((segments, 3, PAD, width), LOW),
            shape((segments, heads * PAD, seg_len), FULL),
            shape((segments, heads * PAD, PAD), FULL),
            rows_shape(LOW),
            rows_shape(FULL),
            rows_shape(LOW),
            shape((segments, PAD, ff), FULL),
            rows_shape(FULL),
            shape((segments, 8, 128), FULL),
        ),
        20_000_000_000,
    )
    own_mem = lax.dynamic_index_in_dim(qkv, head, 0, False)
    km, vm = own_mem[1], own_mem[2]

    pair = 2 * head_dim
    (attended,) = head_pairs(
        functools.partial(token_attention, memory_rows, head_dim),
        doc,
        (q, k, v, km, vm),
        (shape((seg_len, width), LOW),),
        pair,
        8_000_000_000,
    )
    z_attn = x.astype(FULL) + nn(attended, w_attn[3]) + bias_out
    normed_attn, inverse_attn = norm_parts(z_attn)
    hidden = normed_attn * gain_first + shift_first
    hidden_low = hidden.astype(LOW)
    z_ffn = hidden + bias_down
    saved = []
    for i, pair_w in enumerate((first, second)):
        size = pair_w.shape[1]
        pre = nt(hidden_low, pair_w[0]) + bias_in[:, i * size : (i + 1) * size]
        act = gelu(pre).astype(LOW)
        z_ffn = z_ffn + nn(act, pair_w[1])
        saved.append((pre, act))
    normed_ffn, inverse_ffn = norm_parts(z_ffn)
    result = (normed_ffn * gain_second + shift_second).astype(LOW)
    output = lax.all_to_all(result.reshape(groups, quarter, width), "head", 0, 0, tiled=True)

    grad_result = lax.all_to_all(cotangent, "head", 0, 0, tiled=True).reshape(seg_len, width)
    grad_result = grad_result.astype(FULL)
    sums = {}
    sums["gain_ffn"] = jnp.sum(grad_result * normed_ffn, 0)
    sums["shift_ffn"] = jnp.sum(grad_result, 0)
    grad_sum = norm_pull(normed_ffn, inverse_ffn, grad_result * gain_second)
    grad_low = grad_sum.astype(LOW)
    sums["b_down"] = jnp.sum(grad_low.astype(FULL), 0)
    grad_hidden = grad_sum
    bias_in_sums = []
    ffn_grads = []
    for (pre, act), pair_w, order in zip(saved, (first, second), (order_a, order_b)):
        grad_pre = (nt(grad_low, pair_w[1]) * gelu_slope(pre)).astype(LOW)
        grad_hidden = grad_hidden + nn(grad_pre, pair_w[0])
        bias_in_sums.append(jnp.sum(grad_pre.astype(FULL), 0))
        both = jnp.stack([tn(grad_pre, hidden_low).astype(LOW), tn(act, grad_low).astype(LOW)])
        ffn_grads.append(scatter_blocks(both, order))
    sums["gain_attn"] = jnp.sum(grad_hidden * normed_attn, 0)
    sums["shift_attn"] = jnp.sum(grad_hidden, 0)
    grad_attn = norm_pull(normed_attn, inverse_attn, grad_hidden * gain_first)
    sums["b_out"] = jnp.sum(grad_attn, 0)
    grad_mixed = grad_attn.astype(LOW)
    grad_attended = nt(grad_mixed, w_attn[3]).astype(LOW)
    dq, dk, dv, token_part = head_pairs(
        functools.partial(token_attention_back, memory_rows, head_dim),
        doc,
        (q, k, v, km, vm, grad_attended),
        (shape((seg_len, width), LOW),) * 3 + (shape((2 * PAD, width), FULL),),
        pair,
        20_000_000_000,
    )
    sums["b_query"] = jnp.sum(dq.astype(FULL), 0)
    sums["b_value"] = jnp.sum(dv.astype(FULL), 0)
    token_parts = [token_part]
    for j in range(1, groups):
        other = swap(token_part, "head", j).reshape(2 * PAD, groups, here)
        other = jnp.stack([other[:, g ^ j] for g in range(groups)], 1)
        token_parts.append(other.reshape(2 * PAD, width))
    token_parts = jnp.stack(token_parts)
    token_parts = natural_to_relative(token_parts, ("head",))
    grad_x = nn(dq, w_attn[0]) + nn(dk, w_attn[1]) + nn(dv, w_attn[2]) + grad_attn
    grad_x = grad_x.astype(LOW).reshape(groups, quarter, width)
    grad_tokens = lax.all_to_all(grad_x, "head", 0, 0, tiled=True).astype(FULL)
    attn_grads = []
    for (one, other), order in (
        (((x, dq), (x, dk)), order_a),
        (((x, dv), (grad_mixed, attended)), order_b),
    ):
        both = jnp.stack([tn(*one).astype(LOW), tn(*other).astype(LOW)])
        both = scatter_rows(both, [bits[0]] + [b for b in order[::-1] if b != bits[0]])
        total = both[..., :here].astype(FULL)
        for j in range(1, groups):
            total = total + swap(both[..., j * here : (j + 1) * here], "head", j).astype(FULL)
        attn_grads.append(total)

    score_w, grad_attended_w, grad_mixed_w, small_w, grad_ffn_w, grad_pre_w, bias_w, vec_w, init_w = (
        whole_call(
            functools.partial(chain_backward, heads, memory_rows),
            (
                reset,
                w_attn,
                first,
                second,
                vectors,
                keys,
                values,
                qkv,
                soft,
                soft_mem,
                z_attn_w,
                pre_w,
                z_ffn_w,
                token_parts,
            ),
            (
                shape((segments - 1, heads * PAD, seg_len), LOW),
                shape((segments - 1, PAD, width), LOW),
                shape((segments - 1, PAD, width), LOW),
                shape((segments, 3, PAD, width), LOW),
                shape((segments - 1, PAD, width), LOW),
                shape((segments - 1, PAD, ff), LOW),
                shape((1, ff), FULL),
                shape((len(VECTORS), width), FULL),
                shape((PAD, width), FULL),
            ),
            20_000_000_000,
        )
    )

    mask = head_mask(heads * PAD, width, heads)
    writes = segments - 1
    query_w = [by_head(qkv[s, 0], mask, heads) for s in range(writes)]
    pulled_w = [by_head(grad_attended_w[s], mask, heads) for s in range(writes)]
    soft_low = soft[:writes].astype(LOW)
    at = head * quarter
    score_here = lax.dynamic_slice_in_dim(score_w, at, quarter, 2)
    soft_here = lax.dynamic_slice_in_dim(soft_low, at, quarter, 2)
    dk_here = jnp.concatenate(
        [(SCALE * tn(score_here[s], query_w[s])).astype(LOW) for s in range(writes)]
    )
    dv_here = jnp.concatenate([tn(soft_here[s], pulled_w[s]).astype(LOW) for s in range(writes)])
    extra = nn(dk_here, w_attn[1]) + nn(dv_here, w_attn[2])
    extra = jnp.pad(extra.reshape(writes, quarter, width), ((0, 1), (0, 0), (0, 0)))
    grad_tokens = grad_tokens + extra

    mine = heads_here * PAD
    dk_own = jnp.concatenate(
        [(SCALE * tn(score_w[s, :mine], query_w[s][:mine, :here])).astype(LOW) for s in range(writes)]
    )
    dv_own = jnp.concatenate(
        [tn(soft_low[s, :mine], pulled_w[s][:mine, :here]).astype(LOW) for s in range(writes)]
    )
    token_rows = tokens[:writes].reshape(-1, width)
    mem_rows = read.astype(LOW).reshape(-1, width)
    small_own = small_w[..., :here]
    own_grads = jnp.stack(
        [
            tn(mem_rows, small_own[:, 0].reshape(-1, here)),
            tn(token_rows, dk_own) + 2.0 * tn(mem_rows, small_own[:, 1].reshape(-1, here)),
            tn(token_rows, dv_own) + 2.0 * tn(mem_rows, small_own[:, 2].reshape(-1, here)),
            tn(grad_mixed_w.reshape(-1, width), attended_w[:writes, :, :here].reshape(-1, here)),
        ]
    ).astype(LOW)
    own_grads = jnp.concatenate(
        [scatter_rows(own_grads[:2], order_a, True), scatter_rows(own_grads[2:], order_b, True)]
    )
    attn_total = jnp.concatenate(attn_grads) + own_grads
    sums_value_w = jnp.sum(dv_own.astype(FULL), 0)

    def own_units(array):
        parts = []
        for i, place in enumerate((place_a, order_b[::-1])):
            size = array.shape[-1] // 2
            part = array[:, :, i * size : (i + 1) * size]
            part = part.reshape(*array.shape[:2], *([2] * levels), groups, half_units)
            part = part[..., 0, :]
            natural = [2 + place.index(b) for b in bits[::-1]]
            parts.append(part.transpose(0, 1, *natural, 2 + levels))
        return jnp.concatenate(parts, -1).reshape(-1, dps * units)

    def packed(array):
        return array[:, :memory_rows].reshape(-1, array.shape[-1])

    act_w = gelu(pre_w[:writes]).astype(LOW)
    factors = jnp.stack(
        [
            packed(hidden_w[:writes]),
            packed(grad_ffn_w),
            own_units(act_w[:, :memory_rows]),
            own_units(grad_pre_w[:, :memory_rows]),
        ]
    )
    spare = -factors.shape[1] % PAD
    factors = jnp.pad(factors, ((0, 0), (0, spare), (0, 0)))[None]
    for bit in bits:
        factors = jnp.concatenate([factors, swap(factors, "dp", bit)], 0)
    pick = [
        jnp.concatenate([factors[j, i, :, j * units : (j + 1) * units] for j in range(dps)], 0)
        for i in (2, 3)
    ]
    grad_up = tn(pick[1], factors[:, 0].reshape(-1, width))
    grad_down = tn(pick[0], factors[:, 1].reshape(-1, width))
    ffn_total = jnp.concatenate(ffn_grads, 1) + jnp.stack([grad_up, grad_down])

    bias_sum = jnp.concatenate(bias_in_sums) + bias_w[0] * leader
    bias_parts = []
    for i, place in enumerate((place_a, order_b[::-1])):
        size = ff // 2
        part = bias_sum[i * size : (i + 1) * size].reshape(*grid_a, half_units)
        natural = [place.index(b) for b in bits[::-1]]
        bias_parts.append(part.transpose(*natural, levels, levels + 1))
    bias_sum = jnp.concatenate(bias_parts, -1).reshape(dps * groups, units)
    names = ("b_down", "gain_ffn", "shift_ffn", "gain_attn", "shift_attn", "b_out")
    rows = [sums[n] + vec_w[VECTORS.index(n)] * leader for n in names]
    rows = jnp.concatenate([jnp.stack(rows), init_w[:memory_rows] * leader])
    rows = rows.reshape(rows.shape[0], dps * groups, -1).transpose(1, 0, 2)
    row_count, row_part = rows.shape[1:]
    rows = natural_to_relative(rows.reshape(dps * groups, -1), ("dp", "head"))
    value_w = jnp.concatenate([sums_value_w, jnp.zeros((width - here,), FULL)])
    head_rows = jnp.stack(
        [
            sums["b_query"] + vec_w[VECTORS.index("b_query")] * leader,
            sums["b_value"] + vec_w[VECTORS.index("b_value")] * leader + value_w,
        ]
    )
    head_part = head_dim // dps
    head_rows = head_rows.reshape(2, groups, heads_here, dps, head_part).transpose(3, 1, 0, 2, 4)
    head_rows = natural_to_relative(head_rows.reshape(dps, -1), ("dp",))
    head_rows = head_rows.reshape(dps * groups, -1)
    small = jnp.concatenate([bias_sum, rows, head_rows], 1)
    for bit in bits[::-1]:
        size = small.shape[0] // 2
        small = small[:size] + swap(small[size:], "dp", bit)
    small = small[0] + sum(swap(small[j], "head", j) for j in range(1, groups))
    grad_b_in = small[:units]
    at = units + row_count * row_part
    rows = small[units:at].reshape(row_count, row_part)
    head_rows = small[at:].reshape(2, heads_here, head_part)
    vec_out = dict(zip(names, rows))
    return (
        output[None],
        norms[:, 0, 0][None],
        grad_tokens[None],
        attn_total[0],
        attn_total[1],
        attn_total[2],
        head_rows[0],
        head_rows[1],
        attn_total[3].T,
        vec_out["b_out"],
        vec_out["gain_attn"],
        vec_out["shift_attn"],
        ffn_total[0].T,
        grad_b_in,
        ffn_total[1],
        vec_out["b_down"],
        vec_out["gain_ffn"],
        vec_out["shift_ffn"],
        rows[len(names) :],
    )


def solution(mesh):
    in_specs = (
        P("dp", None, None, None),
        P("dp", None, None),
        P("dp", None),
        P(),
        P(None, "head"),
        P(None, "head"),
        P(None, "head"),
        P("head", None),
        P("head", None),
        P("head", None),
        P(),
        P(),
        P(),
        P(None, ("dp", "head")),
        P(("dp", "head")),
        P(("dp", "head"), None),
        P(),
        P(),
        P(),
        P("dp", None, "head", None),
    )
    out_specs = (
        P("dp", None, "head", None),
        P("dp", None),
        P("dp", None, "head", None),
        P("dp", "head"),
        P("dp", "head"),
        P("dp", "head"),
        P("head", "dp"),
        P("head", "dp"),
        P("head", "dp"),
        P(("dp", "head")),
        P(("dp", "head")),
        P(("dp", "head")),
        P(None, ("dp", "head")),
        P(("dp", "head")),
        P(("dp", "head"), None),
        P(("dp", "head")),
        P(("dp", "head")),
        P(("dp", "head")),
        P(None, ("dp", "head")),
    )
    return jax.shard_map(
        on_device, mesh=mesh, in_specs=in_specs, out_specs=out_specs, check_vma=False
    )
```

```python
import functools

import jax
import jax.numpy as jnp
from jax import lax
from jax.experimental import pallas as pl
from jax.experimental.pallas import tpu as pltpu
from jax.sharding import PartitionSpec as P

EPSILON = 1e-06
SCALE = 0.125
NEGATIVE = -1e30
ROOT_HALF = 0.7071067811865476
DENSITY = 0.3989422804014327
LOW = jnp.bfloat16
FULL = jnp.float32
PAD = 16
VECTORS = ("b_query", "b_value", "b_out", "gain_attn", "shift_attn", "b_down", "gain_ffn", "shift_ffn")
VMEM_LIMIT = 60 * 1024 * 1024


def nn(left, right):
    return lax.dot_general(left, right, (((1,), (0,)), ((), ())), preferred_element_type=FULL)


def nt(left, right):
    return lax.dot_general(left, right, (((1,), (1,)), ((), ())), preferred_element_type=FULL)


def tn(left, right):
    return lax.dot_general(left, right, (((0,), (0,)), ((), ())), preferred_element_type=FULL)


def norm_parts(rows):
    centred = rows - jnp.mean(rows, -1, keepdims=True)
    inverse = lax.rsqrt(jnp.mean(centred * centred, -1, keepdims=True) + EPSILON)
    return centred * inverse, inverse


def norm_pull(normed, inverse, grad):
    along = jnp.mean(grad * normed, -1, keepdims=True)
    return inverse * (grad - jnp.mean(grad, -1, keepdims=True) - normed * along)


def gelu(v):
    return 0.5 * v * (1.0 + lax.erf(v * ROOT_HALF))


def gelu_slope(v):
    return 0.5 * (1.0 + lax.erf(v * ROOT_HALF)) + v * (DENSITY * jnp.exp(-0.5 * v * v))


def swap(array, axis, bit):
    return lax.ppermute(array, axis, [(i, i ^ bit) for i in range(lax.axis_size(axis))])


def bits_of(count):
    return [1 << i for i in range(count.bit_length() - 1)]


def gather(array, stages):
    for axis, bit in stages:
        array = jnp.concatenate([array, swap(array, axis, bit)], 0)
    return array


def halve(array, stage):
    half = array.shape[0] // 2
    return array[:half], swap(array[half:], *stage)


def plus(pair, kind=LOW):
    keep, other = pair
    return (keep.astype(FULL) + other.astype(FULL)).astype(kind)


def partner(index, stages, axis):
    place = 0
    for k, (name, bit) in enumerate(stages):
        if name == axis:
            place = place + ((index >> k) & 1) * bit
    return place


def position(partner_bits, order):
    place = 0
    for k, bit in enumerate(order):
        place = place + ((partner_bits // bit) % 2) * (1 << k)
    return place


def order_in(order, index_order):
    return [1 << index_order.index(bit) for bit in order]


def head_mask(rows, width, heads):
    group = lax.broadcasted_iota(jnp.int32, (rows, width), 0) // PAD
    column = lax.broadcasted_iota(jnp.int32, (rows, width), 1) // (width // heads)
    return group == column


def by_head(rows, mask, heads):
    return jnp.where(mask, jnp.concatenate([rows] * heads, 0), jnp.zeros((), rows.dtype))


def own_head(rows, mask, heads):
    kept = jnp.where(mask, rows, 0.0)
    total = kept[:PAD]
    for i in range(1, heads):
        total = total + kept[i * PAD : (i + 1) * PAD]
    return total


def vector(vec_ref, name):
    i = VECTORS.index(name)
    return vec_ref[i : i + 1, :]


class Units:
    def __init__(self, dps, heads, rows, width):
        self.dps, self.heads, self.rows, self.width = dps, heads, rows, width
        self.blocks = dps * heads
        self.chunks = max(2 * self.blocks * rows // width, 4)
        self.size = 2 * self.blocks * rows // self.chunks
        self.whole = rows % 16 != 0

    def at(self, index):
        return (index % self.heads) * self.dps + index // self.heads

    def pieces(self):
        if self.whole:
            return [(0, self.chunks)]
        part = self.blocks // 4
        return [(half * self.blocks + p * part, part) for half in range(2) for p in range(4)]

    def copies(self):
        for number, (first, count) in enumerate(self.pieces()):
            for entry in range(count):
                if self.whole:
                    yield number, entry, entry, 0, self.size
                    continue
                half, index = divmod(first + entry, self.blocks)
                row = (half * self.blocks + self.at(index)) * self.rows
                yield number, entry, row // self.size, row % self.size, self.rows

    def scratch(self):
        buffer = pltpu.VMEM((self.chunks, self.size, self.width), LOW)
        count = sum(2 for _ in self.copies())
        return (buffer, buffer, pltpu.SemaphoreType.DMA((count,)))

    def loads(self, pieces, up_ref, down_ref, arrived):
        made = []
        for number, entry, chunk, row, rows in self.copies():
            for side, to_ref in enumerate((up_ref, down_ref)):
                made.append(
                    pltpu.make_async_copy(
                        pieces[number].at[entry, side],
                        to_ref.at[chunk, pl.ds(row, rows)],
                        arrived.at[len(made)],
                    )
                )
        return made

    def assembled(self, halves):
        rows = []
        for array in halves:
            array = array.reshape(self.dps, self.heads, 2, self.rows, self.width)
            rows.append(array.transpose(1, 0, 3, 2, 4).reshape(-1, 2, self.width))
        rows = jnp.concatenate(rows, 0).reshape(self.chunks, self.size, 2, self.width)
        return [rows.transpose(0, 2, 1, 3)]

    def taken_apart(self, piece):
        rows = piece.transpose(0, 2, 1, 3).reshape(2, self.heads, self.dps, self.rows, 2, -1)
        rows = rows.transpose(0, 2, 1, 4, 3, 5)
        return [half.reshape(self.blocks, 2, self.rows, self.width) for half in rows]


def head_groups(ref, flip):
    value = ref[...]
    half = value.shape[1] // 2
    low, high = value[:, :half], value[:, half:]
    if flip & 2:
        low, high = high, low
    if flip & 1:
        low, high = pltpu.roll(low, half // 2, 1), pltpu.roll(high, half // 2, 1)
    return jnp.concatenate([low, high], 1)


def chain_forward(
    layout,
    heads,
    memory_rows,
    reset_ref,
    init_ref,
    attn_ref,
    bias_ref,
    vec_ref,
    key_ref,
    value_ref,
    *refs,
):
    count = len(layout.pieces())
    pieces, refs = refs[:count], refs[count:]
    (
        read_ref,
        qkv_ref,
        soft_ref,
        soft_mem_ref,
        attended_ref,
        z_attn_ref,
        hidden_ref,
        pre_ref,
        z_ffn_ref,
        norm_ref,
        up_ref,
        down_ref,
        arrived,
    ) = refs
    segments, _, width = key_ref.shape
    loads = layout.loads(pieces, up_ref, down_ref, arrived)
    for load in loads:
        load.start()
    rows = heads * PAD
    mask = head_mask(rows, width, heads)
    real_key = lax.broadcasted_iota(jnp.int32, (rows, PAD), 1) < memory_rows
    real_row = lax.broadcasted_iota(jnp.int32, (PAD, width), 0) < memory_rows
    chunks, size, _ = up_ref.shape

    def step(s, carried):
        fresh = (reset_ref[0, s] > 0) | (s == 0)
        read = jnp.where(fresh, init_ref[...], carried)
        read_ref[s] = read
        low = read.astype(LOW)
        queries = (nt(low, attn_ref[0]) + vector(vec_ref, "b_query")).astype(LOW)
        keys = nt(low, attn_ref[1]).astype(LOW)
        values = (nt(low, attn_ref[2]) + vector(vec_ref, "b_value")).astype(LOW)
        qkv_ref[s, 0] = queries
        qkv_ref[s, 1] = keys
        qkv_ref[s, 2] = values
        spread = by_head(queries, mask, heads)
        scores = nt(spread, key_ref[s]) * SCALE
        scores_mem = jnp.where(real_key, nt(spread, keys) * SCALE, NEGATIVE)
        top = jnp.maximum(
            jnp.max(scores, -1, keepdims=True), jnp.max(scores_mem, -1, keepdims=True)
        )
        raised = jnp.exp(scores - top)
        raised_mem = jnp.exp(scores_mem - top)
        total = jnp.sum(raised, -1, keepdims=True) + 2.0 * jnp.sum(raised_mem, -1, keepdims=True)
        soft = raised / total
        soft_mem = raised_mem / total
        soft_ref[s] = soft
        soft_mem_ref[s] = soft_mem
        mixed = nn(soft.astype(LOW), value_ref[s]) + 2.0 * nn(soft_mem.astype(LOW), values)
        attended = own_head(mixed, mask, heads).astype(LOW)
        attended_ref[s] = attended
        z_attn = read + nn(attended, attn_ref[3]) + vector(vec_ref, "b_out")
        z_attn_ref[s] = z_attn
        normed, _ = norm_parts(z_attn)
        hidden = normed * vector(vec_ref, "gain_attn") + vector(vec_ref, "shift_attn")
        hidden_low = hidden.astype(LOW)
        hidden_ref[s] = hidden_low
        z_ffn = hidden + vector(vec_ref, "b_down")

        @pl.when(s == 0)
        def _():
            for load in loads:
                load.wait()

        for i in range(chunks):
            pre = nt(hidden_low, up_ref[i]) + bias_ref[i]
            pre_ref[s, :, i * size : (i + 1) * size] = pre
            z_ffn = z_ffn + nn(gelu(pre).astype(LOW), down_ref[i])
        z_ffn_ref[s] = z_ffn
        normed, _ = norm_parts(z_ffn)
        result = normed * vector(vec_ref, "gain_ffn") + vector(vec_ref, "shift_ffn")
        square = jnp.sum(jnp.where(real_row, result * result, 0.0), axis=(0, 1), keepdims=True)
        lane = lax.broadcasted_iota(jnp.int32, norm_ref.shape, 1)
        norm = jnp.sqrt(square / (memory_rows * width))
        norm_ref[...] = jnp.where(lane == s, norm, norm_ref[...])
        return result

    norm_ref[...] = jnp.zeros_like(norm_ref)
    lax.fori_loop(0, segments, step, init_ref[...])


def chain_backward(
    layout,
    heads,
    memory_rows,
    reset_ref,
    place_ref,
    attn_ref,
    vec_ref,
    key_ref,
    value_ref,
    qkv_ref,
    soft_ref,
    soft_mem_ref,
    z_attn_ref,
    pre_ref,
    z_ffn_ref,
    hidden_ref,
    *refs,
):
    segments, _, width = key_ref.shape
    part_refs, refs = refs[:segments], refs[segments:]
    count = len(layout.pieces())
    pieces, refs = refs[:count], refs[count:]
    (
        score_ref,
        attended_ref,
        mixed_ref,
        small_ref,
        factor_ref,
        bias_grad_ref,
        vec_grad_ref,
        init_grad_ref,
        ffn_ref,
        pre_grad_ref,
        token_part_ref,
        up_ref,
        down_ref,
        arrived,
    ) = refs
    loads = layout.loads(pieces, up_ref, down_ref, arrived)
    for load in loads:
        load.start()
    for j in range(segments):
        token_part_ref[j] = head_groups(part_refs[j], j)
    me = place_ref[1]
    rows = heads * PAD
    mask = head_mask(rows, width, heads)
    chunks, size, _ = up_ref.shape
    half = chunks * size // 2
    vec_grad_ref[...] = jnp.zeros_like(vec_grad_ref)
    bias_grad_ref[...] = jnp.zeros_like(bias_grad_ref)

    def add_vector(name, grad):
        i = VECTORS.index(name)
        vec_grad_ref[i : i + 1, :] += jnp.sum(grad, 0, keepdims=True)

    last = segments - 1
    grad_key = token_part_ref[last ^ me, :PAD].astype(LOW)
    grad_value = token_part_ref[last ^ me, PAD:].astype(LOW)
    small_ref[last, 0] = jnp.zeros((PAD, width), LOW)
    small_ref[last, 1] = grad_key
    small_ref[last, 2] = grad_value
    add_vector("b_value", 2.0 * grad_value.astype(FULL))
    grad_read = 2.0 * (nn(grad_key, attn_ref[1]) + nn(grad_value, attn_ref[2]))
    stop = reset_ref[0, last] > 0
    init_grad_ref[...] = jnp.where(stop, grad_read, 0.0)
    grad_write = jnp.where(stop, 0.0, grad_read)

    def step(back, grad_write):
        s = segments - 2 - back
        normed, inverse = norm_parts(z_ffn_ref[s])
        add_vector("gain_ffn", grad_write * normed)
        add_vector("shift_ffn", grad_write)
        grad_sum = norm_pull(normed, inverse, grad_write * vector(vec_ref, "gain_ffn"))
        grad_low = grad_sum.astype(LOW)
        ffn_ref[s] = grad_low
        add_vector("b_down", grad_low.astype(FULL))
        grad_hidden = grad_sum

        @pl.when(back == 0)
        def _():
            for load in loads:
                load.wait()

        for i in range(chunks):
            part = slice(i * size, (i + 1) * size)
            grad_act = nt(grad_low, down_ref[i])
            grad_pre = (grad_act * gelu_slope(pre_ref[s, :, part])).astype(LOW)
            pre_grad_ref[s, :, part] = grad_pre
            bias_grad_ref[i] += jnp.sum(grad_pre.astype(FULL), 0, keepdims=True)
            grad_hidden = grad_hidden + nn(grad_pre, up_ref[i])
        normed, inverse = norm_parts(z_attn_ref[s])
        add_vector("gain_attn", grad_hidden * normed)
        add_vector("shift_attn", grad_hidden)
        grad_attn = norm_pull(normed, inverse, grad_hidden * vector(vec_ref, "gain_attn"))
        add_vector("b_out", grad_attn)
        grad_mixed = grad_attn.astype(LOW)
        mixed_ref[s] = grad_mixed
        grad_attended = nt(grad_mixed, attn_ref[3]).astype(LOW)
        attended_ref[s] = grad_attended
        queries, keys, values = qkv_ref[s, 0], qkv_ref[s, 1], qkv_ref[s, 2]
        spread = by_head(grad_attended, mask, heads)
        soft, soft_mem = soft_ref[s], soft_mem_ref[s]
        pull = nt(spread, value_ref[s])
        pull_mem = nt(spread, values)
        inner = jnp.sum(soft * pull, -1, keepdims=True) + 2.0 * jnp.sum(
            soft_mem * pull_mem, -1, keepdims=True
        )
        grad_score = (soft * (pull - inner)).astype(LOW)
        grad_score_mem = (soft_mem * (pull_mem - inner)).astype(LOW)
        score_ref[s] = grad_score
        grad_query = nn(grad_score, key_ref[s]) + 2.0 * nn(grad_score_mem, keys)
        grad_query = (SCALE * own_head(grad_query, mask, heads)).astype(LOW)
        grad_key = SCALE * tn(grad_score_mem, by_head(queries, mask, heads))
        grad_key = (token_part_ref[s ^ me, :PAD] + grad_key).astype(LOW)
        grad_value = tn(soft_mem.astype(LOW), spread)
        grad_value = (token_part_ref[s ^ me, PAD:] + grad_value).astype(LOW)
        small_ref[s, 0] = grad_query
        small_ref[s, 1] = grad_key
        small_ref[s, 2] = grad_value
        add_vector("b_query", grad_query.astype(FULL))
        add_vector("b_value", 2.0 * grad_value.astype(FULL))
        grad_read = 2.0 * (nn(grad_key, attn_ref[1]) + nn(grad_value, attn_ref[2]))
        grad_read = grad_read + nn(grad_query, attn_ref[0]) + grad_attn
        stop = (reset_ref[0, s] > 0) | (s == 0)
        init_grad_ref[...] += jnp.where(stop, grad_read, 0.0)
        return jnp.where(stop, 0.0, grad_read)

    lax.fori_loop(0, segments - 1, step, grad_write)

    packed, wide = factor_ref.shape[1], (segments - 1) * PAD
    row = lax.broadcasted_iota(jnp.int32, (packed, wide), 0)
    source = lax.broadcasted_iota(jnp.int32, (packed, wide), 1)
    take = (source // PAD == row // memory_rows) & (source % PAD == row % memory_rows)
    take = jnp.where(take, 1.0, 0.0).astype(LOW)
    mine = width // 2

    def own_units(ref):
        first = ref[: segments - 1, :, :mine].reshape(wide, mine)
        second = ref[: segments - 1, :, half : half + mine].reshape(wide, mine)
        return jnp.concatenate([first, second], 1)

    acts = gelu(own_units(pre_ref)).astype(LOW)
    factor_ref[0] = nn(take, hidden_ref[: segments - 1].reshape(wide, width)).astype(LOW)
    factor_ref[1] = nn(take, ffn_ref[...].reshape(wide, width)).astype(LOW)
    factor_ref[2] = nn(take, acts).astype(LOW)
    factor_ref[3] = nn(take, own_units(pre_grad_ref)).astype(LOW)


def whole_call(body, scalars, operands, outside, shapes, flops, scratch=(), outside_shapes=()):
    in_vmem = pl.BlockSpec(memory_space=pltpu.VMEM)
    in_smem = pl.BlockSpec(memory_space=pltpu.SMEM)
    anywhere = pl.BlockSpec(memory_space=pl.ANY)
    size = sum(a.size * a.dtype.itemsize for a in (*operands, *outside, *shapes))
    return pl.pallas_call(
        body,
        out_shape=(*shapes, *outside_shapes),
        in_specs=[in_smem] * len(scalars) + [in_vmem] * len(operands) + [anywhere] * len(outside),
        out_specs=[in_vmem] * len(shapes) + [anywhere] * len(outside_shapes),
        scratch_shapes=scratch,
        compiler_params=pltpu.CompilerParams(vmem_limit_bytes=VMEM_LIMIT),
        cost_estimate=pl.CostEstimate(flops=flops, bytes_accessed=size, transcendentals=0),
    )(*scalars, *operands, *outside)


def unit_owner(column, half, stages, order_b, layout, index):
    if half:
        dp = position(partner(index, stages, "dp"), order_b)
        at = (index % layout.heads) * layout.dps + dp
    else:
        at = layout.at(index)
    return column // layout.rows == at


def project(
    layout,
    stages,
    order_b,
    place_ref,
    token_ref,
    attn_ref,
    bias_ref,
    other_ref,
    key_ref,
    value_ref,
    x_ref,
    q_ref,
    k_ref,
    v_ref,
    vec_ref,
    bias_in_ref,
):
    devices, entries = bias_ref.shape
    width, rows = layout.width, layout.rows
    here = width // layout.heads
    packets = bias_ref[...].astype(FULL)

    def laid_out(first, count, period, owner):
        entry = lax.broadcasted_iota(jnp.int32, (entries, count), 0)
        column = lax.broadcasted_iota(jnp.int32, (entries, count), 1)
        pick = jnp.where(entry == first + column % period, 1.0, 0.0).astype(LOW)
        index = lax.broadcasted_iota(jnp.int32, (devices, count), 0)
        column = lax.broadcasted_iota(jnp.int32, (devices, count), 1)
        chosen = jnp.where(owner(column, index), nn(packets.astype(LOW), pick), 0.0)
        return jnp.sum(chosen, 0, keepdims=True)

    def of_head(column, index):
        head = partner(index, stages, "head")
        return (partner(index, stages, "dp") == 0) & (head == column // here)

    vec_ref[0:1, :] = laid_out(0, width, here, of_head)
    vec_ref[1:2, :] = laid_out(here, width, here, of_head)
    vec_ref[2:, :] = other_ref[...].astype(FULL)
    for half in range(2):
        owner = functools.partial(
            unit_owner, half=half, stages=stages, order_b=order_b, layout=layout
        )
        row = laid_out(
            2 * here + half * rows,
            layout.blocks * rows,
            rows,
            lambda column, index: owner(column, index=index),
        )
        per = layout.chunks // 2
        for i in range(per):
            bias_in_ref[half * per + i] = row[:, i * layout.size : (i + 1) * layout.size]

    for s in range(token_ref.shape[0]):
        x = token_ref[s]
        key_ref[s] = nt(x, attn_ref[1]).astype(LOW)
        value_ref[s] = (nt(x, attn_ref[2]) + vector(vec_ref, "b_value")).astype(LOW)
    own = place_ref[1]
    x = token_ref[own]
    x_ref[...] = x
    q_ref[...] = (nt(x, attn_ref[0]) + vector(vec_ref, "b_query")).astype(LOW)
    k_ref[...] = key_ref[own]
    v_ref[...] = value_ref[own]


SUMS = ("b_out", "gain_attn", "shift_attn", "b_down", "gain_ffn", "shift_ffn")


def token_layer(layout, x_ref, attended_ref, cot_ref, bias_ref, vec_ref, attn_ref, *refs):
    count = len(layout.pieces())
    pieces, refs = refs[:count], refs[count:]
    (
        result_ref,
        skip_ref,
        mixed_ref,
        grad_attended_ref,
        bias_sum_ref,
        sum_ref,
        *grad_refs,
        out_w_ref,
        out_arrived,
        up_ref,
        down_ref,
        arrived,
        z_attn_ref,
        hidden_ref,
        low_ref,
        total_ref,
        pre_ref,
        act_ref,
        stage_ref,
        sent,
    ) = refs
    out_load = pltpu.make_async_copy(attn_ref.at[3], out_w_ref, out_arrived)
    out_load.start()
    loads = layout.loads(pieces, up_ref, down_ref, arrived)
    for load in loads:
        load.start()
    chunks = layout.chunks
    out_load.wait()
    sum_ref[...] = jnp.zeros_like(sum_ref)

    def add_vector(name, grad):
        i = SUMS.index(name)
        sum_ref[i : i + 1, :] += jnp.sum(grad, 0, keepdims=True)

    z_attn = x_ref[...].astype(FULL) + nn(attended_ref[...], out_w_ref[...])
    z_attn = z_attn + vector(vec_ref, "b_out")
    z_attn_ref[...] = z_attn
    normed, _ = norm_parts(z_attn)
    hidden = normed * vector(vec_ref, "gain_attn") + vector(vec_ref, "shift_attn")
    hidden_ref[...] = hidden.astype(LOW)
    total_ref[...] = hidden + vector(vec_ref, "b_down")
    for load in loads:
        load.wait()

    def forward(i, nothing):
        pre = nt(hidden_ref[...], up_ref[i]) + bias_ref[i]
        pre_ref[i] = pre
        act = gelu(pre).astype(LOW)
        act_ref[i] = act
        total_ref[...] += nn(act, down_ref[i])
        return nothing

    lax.fori_loop(0, chunks, forward, 0)
    normed, inverse = norm_parts(total_ref[...])
    result = normed * vector(vec_ref, "gain_ffn") + vector(vec_ref, "shift_ffn")
    result_ref[...] = result.astype(LOW)
    grad = cot_ref[...].astype(FULL)
    add_vector("gain_ffn", grad * normed)
    add_vector("shift_ffn", grad)
    grad = norm_pull(normed, inverse, grad * vector(vec_ref, "gain_ffn"))
    total_ref[...] = grad
    low_ref[...] = grad.astype(LOW)
    add_vector("b_down", low_ref[...].astype(FULL))

    copies = list(layout.copies())
    spans = [first for first, _ in layout.pieces()]
    stores = []
    for i in range(chunks):
        grad_pre = (nt(low_ref[...], down_ref[i]) * gelu_slope(pre_ref[i])).astype(LOW)
        bias_sum_ref[i] = jnp.sum(grad_pre.astype(FULL), 0, keepdims=True)
        total_ref[...] += nn(grad_pre, up_ref[i])
        slot = i % 2
        if i > 1:
            for store in stores[i - 2]:
                store.wait()
        stage_ref[slot, 0] = tn(grad_pre, hidden_ref[...]).astype(LOW)
        stage_ref[slot, 1] = tn(act_ref[i], low_ref[...]).astype(LOW)
        stores.append([])
        for number, entry, chunk, row, rows in copies:
            if chunk != i:
                continue
            for side in range(2):
                to_ref = grad_refs[number // (len(spans) // len(grad_refs))]
                entry_at = spans[number] - spans[number - number % (len(spans) // len(grad_refs))]
                store = pltpu.make_async_copy(
                    stage_ref.at[slot, side, pl.ds(row, rows)],
                    to_ref.at[entry_at + entry, side],
                    sent.at[i, len(stores[i])],
                )
                store.start()
                stores[i].append(store)

    grad_hidden = total_ref[...]
    normed, inverse = norm_parts(z_attn_ref[...])
    add_vector("gain_attn", grad_hidden * normed)
    add_vector("shift_attn", grad_hidden)
    grad = norm_pull(normed, inverse, grad_hidden * vector(vec_ref, "gain_attn"))
    add_vector("b_out", grad)
    skip_ref[...] = grad
    mixed_ref[...] = grad.astype(LOW)
    grad_attended_ref[...] = nt(mixed_ref[...], out_w_ref[...]).astype(LOW)
    for i in range(max(chunks - 2, 0), chunks):
        for store in stores[i]:
            store.wait()


def spread_rows(out_ref, index, grad, place_ref, order, count):
    rows = grad.shape[0] // count
    for c in range(count):
        at = position(place_ref[0] ^ c, order)
        out_ref[(at, *index)] = grad[c * rows : (c + 1) * rows].astype(out_ref.dtype)


def attention_grads(
    order_a,
    order_b,
    count,
    place_ref,
    x_ref,
    mixed_ref,
    attended_ref,
    dq0_ref,
    dq1_ref,
    dk0_ref,
    dk1_ref,
    dv0_ref,
    dv1_ref,
    attn_ref,
    skip_ref,
    a_ref,
    b_ref,
    grad_x_ref,
    sums_ref,
):
    x = x_ref[...]
    total = skip_ref[...]
    half = dq0_ref.shape[1]
    pairs = ((dq0_ref, dq1_ref), (dk0_ref, dk1_ref), (dv0_ref, dv1_ref))
    for m, (low, high) in enumerate(pairs):
        low, high = low[...], high[...]
        both = jnp.concatenate([tn(x, low), tn(x, high)], 1)
        if m < 2:
            spread_rows(a_ref, (m,), both, place_ref, order_a, count)
        else:
            spread_rows(b_ref, (0,), both, place_ref, order_b, count)
        total = total + nn(low, attn_ref[m, :half]) + nn(high, attn_ref[m, half:])
        if m != 1:
            i = m // 2
            sums_ref[i : i + 1, :half] = jnp.sum(low.astype(FULL), 0, keepdims=True)
            sums_ref[i : i + 1, half:] = jnp.sum(high.astype(FULL), 0, keepdims=True)
    spread_rows(b_ref, (1,), tn(mixed_ref[...], attended_ref[...]), place_ref, order_b, count)
    grad_x_ref[...] = total.astype(LOW)


def exact(left, right):
    return lax.dot_general(
        left,
        right,
        (((1,), (0,)), ((), ())),
        precision=lax.Precision.HIGHEST,
        preferred_element_type=FULL,
    )


def pack_sums(
    layout, stages, order_b, heads_here, memory_rows, place_ref, rows_ref, bias_ref, out_ref
):
    devices, _, _ = out_ref.shape
    count, width = rows_ref.shape
    groups, dps = layout.heads, layout.dps
    here, part = width // groups, width // devices
    head_dim = here // heads_here
    head_part = head_dim // dps
    shape = (devices, count, width)
    index, row, column = (lax.broadcasted_iota(jnp.int32, shape, i) for i in range(3))
    dp = place_ref[0] ^ partner(index, stages, "dp")
    head = place_ref[1] ^ partner(index, stages, "head")
    plain = len(SUMS) + memory_rows
    of_device = column // part == dp * groups + head
    of_head = (column // here == partner(index, stages, "head")) & (
        column % head_dim // head_part == dp
    )
    chosen = ((row < plain) & of_device) | ((row >= plain) & of_head)
    chosen = jnp.where(chosen, jnp.broadcast_to(rows_ref[...][None], shape), 0.0)
    chosen = chosen.reshape(devices * count, width)
    source = lax.broadcasted_iota(jnp.int32, (width, part), 0)
    target = lax.broadcasted_iota(jnp.int32, (width, part), 1)
    plain_fold = jnp.where(source % part == target, 1.0, 0.0)
    head_column = source // head_dim % heads_here * head_part + source % head_part
    head_fold = jnp.where(head_column == target, 1.0, 0.0)
    row = lax.broadcasted_iota(jnp.int32, (devices, count, part), 1)
    folded = jnp.where(
        row < plain,
        exact(chosen, plain_fold).reshape(devices, count, part),
        exact(chosen, head_fold).reshape(devices, count, part),
    )
    out_ref[...] = jnp.zeros_like(out_ref)
    out_ref[:, :, :part] = folded
    per = layout.chunks // 2
    span = per * layout.size
    index, column = (lax.broadcasted_iota(jnp.int32, (devices, span), i) for i in range(2))
    source = lax.broadcasted_iota(jnp.int32, (span, layout.rows), 0)
    target = lax.broadcasted_iota(jnp.int32, (span, layout.rows), 1)
    fold = jnp.where(source % layout.rows == target, 1.0, 0.0)
    for half in range(2):
        row = jnp.concatenate([bias_ref[half * per + i] for i in range(per)], 1)
        mine = unit_owner(column, half, stages, order_b, layout, index)
        out_ref[:, plain + 2 + half, : layout.rows] = exact(jnp.where(mine, row, 0.0), fold)


def write_grads(
    layout,
    stages,
    order_a,
    order_b,
    count,
    heads,
    heads_here,
    quarter,
    memory_rows,
    place_ref,
    score_ref,
    soft_ref,
    qkv_ref,
    attended_grad_ref,
    mixed_ref,
    attended_ref,
    small_ref,
    read_ref,
    token_ref,
    attn_ref,
    moved_ref,
    layer_sum_ref,
    head_sum_ref,
    bias_sum_ref,
    bias_grad_ref,
    vec_grad_ref,
    init_grad_ref,
    a_ref,
    b_ref,
    grad_token_ref,
    pack_ref,
    rows_ref,
    bias_ref,
):
    writes, rows, _ = score_ref.shape
    width = qkv_ref.shape[-1]
    here = width // heads * heads_here
    mine = heads_here * PAD
    mask = head_mask(rows, width, heads)
    at = pl.multiple_of(place_ref[1] * quarter, quarter)
    grads = [jnp.zeros((width, here), FULL) for _ in range(4)]
    total = jnp.zeros((1, here), FULL)
    for s in range(writes + 1):
        low = read_ref[s].astype(LOW)
        grads[1] = grads[1] + 2.0 * tn(low, small_ref[s, 1, :, :here])
        grads[2] = grads[2] + 2.0 * tn(low, small_ref[s, 2, :, :here])
        if s == writes:
            break
        grads[0] = grads[0] + tn(low, small_ref[s, 0, :, :here])
        grads[3] = grads[3] + tn(mixed_ref[s], attended_ref[s, :, :here])
        spread = by_head(qkv_ref[s, 0], mask, heads)
        pulled = by_head(attended_grad_ref[s], mask, heads)
        soft = soft_ref[s].astype(LOW)
        dk_own = (SCALE * tn(score_ref[s, :mine], spread[:mine, :here])).astype(LOW)
        dv_own = tn(soft[:mine], pulled[:mine, :here]).astype(LOW)
        total = total + jnp.sum(dv_own.astype(FULL), 0, keepdims=True)
        grads[1] = grads[1] + tn(token_ref[s], dk_own)
        grads[2] = grads[2] + tn(token_ref[s], dv_own)
        score_here = score_ref[s, :, pl.ds(at, quarter)]
        soft_here = soft_ref[s, :, pl.ds(at, quarter)].astype(LOW)
        dk = (SCALE * tn(score_here, spread)).astype(LOW)
        dv = tn(soft_here, pulled).astype(LOW)
        extra = nn(dk, attn_ref[1]) + nn(dv, attn_ref[2])
        grad_token_ref[s] = moved_ref[s].astype(FULL) + extra
    grad_token_ref[writes] = moved_ref[writes].astype(FULL)
    spread_rows(a_ref, (), jnp.concatenate(grads[:2], 1), place_ref, order_a, count)
    spread_rows(b_ref, (), jnp.concatenate(grads[2:], 1), place_ref, order_b, count)

    lead = jnp.where(place_ref[1] == 0, 1.0, 0.0)
    rows_ref[...] = jnp.zeros_like(rows_ref)
    for i, name in enumerate(SUMS):
        at = VECTORS.index(name)
        rows_ref[i : i + 1, :] = (
            layer_sum_ref[i : i + 1, :] + lead * vec_grad_ref[at : at + 1, :]
        )
    for i in range(memory_rows):
        at = len(SUMS) + i
        rows_ref[at : at + 1, :] = lead * init_grad_ref[i : i + 1, :]
    at = len(SUMS) + memory_rows
    rows_ref[at : at + 1, :] = head_sum_ref[0:1, :] + lead * vec_grad_ref[0:1, :]
    rows_ref[at + 1 : at + 2, :] = head_sum_ref[1:2, :] + lead * vec_grad_ref[1:2, :]
    rows_ref[at + 1 : at + 2, :here] += total
    bias_ref[...] = bias_sum_ref[...] + lead * bias_grad_ref[...]
    pack_sums(
        layout, stages, order_b, heads_here, memory_rows, place_ref, rows_ref, bias_ref, pack_ref
    )


def finish(
    order_a,
    order_b,
    memory_rows,
    factor_ref,
    ffn_keep_ref,
    ffn_other_ref,
    attn_keep_ref,
    attn_other_ref,
    a_keep_ref,
    a_other_ref,
    b_keep_ref,
    b_other_ref,
    pack_keep_ref,
    pack_other_ref,
    query_ref,
    key_ref,
    value_ref,
    b_query_ref,
    b_value_ref,
    out_ref,
    b_out_ref,
    gain_attn_ref,
    shift_attn_ref,
    up_ref,
    b_in_ref,
    down_ref,
    b_down_ref,
    gain_ffn_ref,
    shift_ffn_ref,
    init_ref,
):
    count, _, rows, width = factor_ref.shape
    block = width // 2 // count
    column = lax.broadcasted_iota(jnp.int32, (rows, width), 1)

    def own(j, i):
        first, second = position(j, order_a), position(j, order_b) + count
        keep = (column // block == first) | (column // block == second)
        return jnp.where(keep, factor_ref[j, i], jnp.zeros((), LOW))

    units = []
    for side, left, right in ((0, 3, 0), (1, 2, 1)):
        chosen = jnp.concatenate([own(j, left) for j in range(count)], 0)
        others = jnp.concatenate([factor_ref[j, right] for j in range(count)], 0)
        product = tn(chosen, others)
        halves = []
        for i in range(2):
            total = plus((ffn_keep_ref[0, i, side], ffn_other_ref[0, i, side]), FULL)
            for j in range(count):
                at = (i * count + j) * block
                total = total + product[at : at + block]
            halves.append(total)
        units.append(jnp.concatenate(halves, 0))
    up_ref[...] = units[0].T
    down_ref[...] = units[1]
    here = attn_keep_ref.shape[-1]
    own_parts = []
    for keep_ref, other_ref in ((a_keep_ref, a_other_ref), (b_keep_ref, b_other_ref)):
        total = plus((keep_ref[0], other_ref[0]), FULL)
        own_parts += [total[:, :here], total[:, here:]]
    totals = [
        plus((attn_keep_ref[0, m], attn_other_ref[0, m]), FULL) + own_parts[m] for m in range(4)
    ]
    query_ref[...] = totals[0]
    key_ref[...] = totals[1]
    value_ref[...] = totals[2]
    out_ref[...] = totals[3].T
    pack = pack_keep_ref[0] + pack_other_ref[0]
    refs = {
        "b_out": b_out_ref,
        "gain_attn": gain_attn_ref,
        "shift_attn": shift_attn_ref,
        "b_down": b_down_ref,
        "gain_ffn": gain_ffn_ref,
        "shift_ffn": shift_ffn_ref,
    }
    part = init_ref.shape[1]
    for i, name in enumerate(SUMS):
        refs[name][...] = pack[i : i + 1, :part]
    at = len(SUMS) + memory_rows
    init_ref[...] = pack[len(SUMS) : at, :part]
    heads_here, head_part = b_query_ref.shape
    for i in range(heads_here):
        columns = slice(i * head_part, (i + 1) * head_part)
        b_query_ref[i : i + 1, :] = pack[at : at + 1, columns]
        b_value_ref[i : i + 1, :] = pack[at + 1 : at + 2, columns]
    b_in_ref[:, :block] = pack[at + 2 : at + 3, :block]
    b_in_ref[:, block:] = pack[at + 3 : at + 4, :block]


def token_soft(q, k, km, allowed, real_key):
    scores = jnp.where(allowed, nt(q, k) * SCALE, NEGATIVE)
    scores_mem = jnp.where(real_key, nt(q, km) * SCALE, NEGATIVE)
    top = jnp.maximum(jnp.max(scores, -1, keepdims=True), jnp.max(scores_mem, -1, keepdims=True))
    raised = jnp.exp(scores - top)
    raised_mem = jnp.exp(scores_mem - top)
    total = jnp.sum(raised, -1, keepdims=True) + 2.0 * jnp.sum(raised_mem, -1, keepdims=True)
    inverse = 1.0 / total
    return raised * inverse, raised_mem * inverse


def token_attention(
    memory_rows, head_dim, row_ref, column_ref, q_ref, k_ref, v_ref, km_ref, vm_ref, out_ref
):
    q, k, v, km, vm = q_ref[...], k_ref[...], v_ref[...], km_ref[...], vm_ref[...]
    allowed = column_ref[...] == row_ref[...]
    real_key = lax.broadcasted_iota(jnp.int32, (q.shape[0], PAD), 1) < memory_rows
    lane = lax.broadcasted_iota(jnp.int32, q.shape, 1) // head_dim
    total = jnp.zeros(q.shape, FULL)
    for head in range(q.shape[1] // head_dim):
        mine = jnp.where(lane == head, q, jnp.zeros((), LOW))
        soft, soft_mem = token_soft(mine, k, km, allowed, real_key)
        mixed = nn(soft.astype(LOW), v) + 2.0 * nn(soft_mem.astype(LOW), vm)
        total = jnp.where(lane == head, mixed, total)
    out_ref[...] = total.astype(LOW)


def token_attention_back(
    memory_rows,
    head_dim,
    row_ref,
    column_ref,
    q_ref,
    k_ref,
    v_ref,
    km_ref,
    vm_ref,
    grad_ref,
    dq_ref,
    dk_ref,
    dv_ref,
    dmem_ref,
):
    q, k, v, km, vm, grad = (r[...] for r in (q_ref, k_ref, v_ref, km_ref, vm_ref, grad_ref))
    allowed = column_ref[...] == row_ref[...]
    real_key = lax.broadcasted_iota(jnp.int32, (q.shape[0], PAD), 1) < memory_rows
    lane = lax.broadcasted_iota(jnp.int32, q.shape, 1) // head_dim
    zero = jnp.zeros((), LOW)
    dq, dk, dv = (jnp.zeros(q.shape, FULL) for _ in range(3))
    dkm, dvm = (jnp.zeros(km.shape, FULL) for _ in range(2))
    for head in range(q.shape[1] // head_dim):
        mine = jnp.where(lane == head, q, zero)
        mine_grad = jnp.where(lane == head, grad, zero)
        soft, soft_mem = token_soft(mine, k, km, allowed, real_key)
        pull, pull_mem = nt(mine_grad, v), nt(mine_grad, vm)
        inner = jnp.sum(soft * pull, -1, keepdims=True) + 2.0 * jnp.sum(
            soft_mem * pull_mem, -1, keepdims=True
        )
        score = (soft * (pull - inner)).astype(LOW)
        score_mem = (soft_mem * (pull_mem - inner)).astype(LOW)
        dq = jnp.where(lane == head, nn(score, k) + 2.0 * nn(score_mem, km), dq)
        dk = dk + tn(score, mine)
        dv = dv + tn(soft.astype(LOW), mine_grad)
        dkm = dkm + tn(score_mem, mine)
        dvm = dvm + tn(soft_mem.astype(LOW), mine_grad)
    dq_ref[...] = (SCALE * dq).astype(LOW)
    dk_ref[...] = (SCALE * dk).astype(LOW)
    dv_ref[...] = dv.astype(LOW)
    dmem_ref[:PAD] = SCALE * dkm
    dmem_ref[PAD:] = dvm


def head_pairs(body, doc, operands, shapes, width, flops, first=0):
    seg_len = doc.shape[0]
    columns = lambda array: pl.BlockSpec((array.shape[0], width), lambda i: (0, i + first))
    results = lambda array: pl.BlockSpec((array.shape[0], width), lambda i: (0, i))
    return pl.pallas_call(
        body,
        grid=(shapes[0].shape[1] // width,),
        out_shape=shapes,
        in_specs=[
            pl.BlockSpec((1, seg_len), lambda i: (0, 0)),
            pl.BlockSpec((seg_len, 1), lambda i: (0, 0)),
        ]
        + [columns(a) for a in operands],
        out_specs=[results(s) for s in shapes],
        compiler_params=pltpu.CompilerParams(vmem_limit_bytes=VMEM_LIMIT),
        cost_estimate=pl.CostEstimate(
            flops=flops, bytes_accessed=8 * seg_len * operands[0].shape[1], transcendentals=0
        ),
    )(doc[None, :], doc[:, None], *operands)


def on_device(
    tokens,
    doc_ids,
    reset,
    mem_init,
    w_query,
    w_key,
    w_value,
    b_query,
    b_value,
    w_out,
    b_out,
    gain_attn,
    shift_attn,
    w_in,
    b_in,
    w_down,
    b_down,
    gain_ffn,
    shift_ffn,
    cotangent,
):
    chains, segments, seg_len, width = tokens.shape
    dps, groups = lax.axis_size("dp"), lax.axis_size("head")
    assert chains == 1 and segments == groups
    memory_rows = mem_init.shape[0]
    heads_here, head_dim = b_query.shape
    heads = heads_here * groups
    here = heads_here * head_dim
    units = w_in.shape[1]
    half_units = units // 2
    quarter = seg_len // groups
    dp, head = lax.axis_index("dp"), lax.axis_index("head")
    place = jnp.stack([dp, head])
    bits = bits_of(dps)
    levels = len(bits)
    order_a = bits[1:] + bits[:1]
    order_b = bits[1:][::-1] + bits[:1]
    head_order = bits_of(groups)[::-1]
    head_stages = [("head", bit) for bit in head_order]
    stages_a = head_stages + [("dp", bit) for bit in order_a]
    stages_b = head_stages + [("dp", bit) for bit in order_b]
    layout = Units(dps, groups, half_units, width)
    landing = layout.scratch()
    shape = jax.ShapeDtypeStruct
    tokens, doc_ids, cotangent = tokens[0], doc_ids[0], cotangent[0]

    shard = jnp.concatenate([w_query.T, w_key.T, w_value.T, w_out], 0)
    share = shard.shape[0] // dps
    chunk = gather(lax.dynamic_slice_in_dim(shard, dp * share, share, 0)[None], head_stages)
    biases = jnp.concatenate([b_query.reshape(-1), b_value.reshape(-1), b_in])[None]
    biases = gather(biases, head_stages)
    up = w_in.T.reshape(2, half_units, width)
    down = w_down.reshape(2, half_units, width)
    halves = [jnp.stack([up[i], down[i]])[None] for i in range(2)]
    chunk, biases, halves = lax.optimization_barrier((chunk, biases, halves))
    halves = [gather(half, head_stages) for half in halves]
    biases = gather(biases, stages_a[len(head_stages) :])
    chunk = jnp.stack([chunk[position(j, head_order)] for j in range(1, groups)])
    parts = []
    for rows, order in ((slice(0, share // 2), order_a), (slice(share // 2, share), order_b)):
        part = chunk[:, rows]
        have = []
        for bit in order:
            at = sum(1 for b in have if b > bit)
            have.append(bit)
            mine = (dp // bit) % 2
            other = swap(part, "dp", bit)
            part = jnp.where(mine == 1, jnp.stack([other, part], at), jnp.stack([part, other], at))
        parts.append(part.reshape(dps, groups - 1, share // 2, width))
    others = jnp.concatenate(parts, 2).transpose(1, 0, 2, 3).reshape(groups - 1, 4, here, width)
    w_attn = jnp.concatenate([shard.reshape(4, 1, here, width), others.transpose(1, 0, 2, 3)], 1)
    w_attn = w_attn.reshape(4, groups * here, width)
    halves, w_attn, biases, cotangent = lax.optimization_barrier(
        (halves, w_attn, biases, cotangent)
    )
    pieces = []
    for half, stages in zip(halves, (stages_a, stages_b)):
        half = gather(half, stages[len(head_stages) : -2])
        other = swap(half, *stages[-2])
        pieces += [half, other, swap(half, *stages[-1]), swap(other, *stages[-1])]
    if layout.whole:
        pieces = layout.assembled([jnp.concatenate(pieces[i : i + 4], 0) for i in (0, 4)])

    doc = lax.dynamic_index_in_dim(doc_ids, head, 0, False)
    vectors = jnp.concatenate([b_out, gain_attn, shift_attn, b_down, gain_ffn, shift_ffn])
    keys, values, x, q, k, v, vectors, bias_in = whole_call(
        functools.partial(project, layout, stages_a, order_b),
        (place,),
        (tokens, w_attn, biases, vectors.reshape(-1, width)),
        (),
        (shape(tokens.shape, LOW),) * 2
        + (shape((seg_len, width), LOW),) * 4
        + (shape((len(VECTORS), width), FULL), shape((layout.chunks, 1, layout.size), FULL)),
        6_000_000_000,
    )

    init = jnp.pad(mem_init.astype(FULL), ((0, PAD - memory_rows), (0, 0)))
    ff = layout.chunks * layout.size
    rows_shape = lambda kind: shape((segments, PAD, width), kind)
    read, qkv, soft, soft_mem, attended_w, z_attn_w, hidden_w, pre_w, z_ffn_w, norms = whole_call(
        functools.partial(chain_forward, layout, heads, memory_rows),
        (reset,),
        (init, w_attn, bias_in, vectors, keys, values),
        pieces,
        (
            rows_shape(FULL),
            shape((segments, 3, PAD, width), LOW),
            shape((segments, heads * PAD, seg_len), FULL),
            shape((segments, heads * PAD, PAD), FULL),
            rows_shape(LOW),
            rows_shape(FULL),
            rows_shape(LOW),
            shape((segments, PAD, ff), FULL),
            rows_shape(FULL),
            shape((1, 128), FULL),
        ),
        20_000_000_000,
        landing,
    )
    own_mem = lax.dynamic_index_in_dim(qkv, head, 0, False)
    km, vm = own_mem[1], own_mem[2]

    pair = 2 * head_dim
    (attended,) = head_pairs(
        functools.partial(token_attention, memory_rows, head_dim),
        doc,
        (q, k, v, km, vm),
        (shape((seg_len, width), LOW),),
        pair,
        8_000_000_000,
    )
    cotangent = lax.all_to_all(cotangent, "head", 0, 0, tiled=True).reshape(seg_len, width)
    if layout.whole:
        grad_shapes = (shape((layout.chunks, 2, layout.size, width), LOW),)
    else:
        grad_shapes = (shape((layout.blocks // 2, 2, half_units, width), LOW),) * 4
    sides = 2 * max(layout.size // (layout.size if layout.whole else half_units), 1)
    result, grad_attn, grad_mixed, grad_attended, bias_sum, layer_sums, *ffn_grads = whole_call(
        functools.partial(token_layer, layout),
        (),
        (x, attended, cotangent, bias_in, vectors),
        (w_attn, *pieces),
        (
            shape((seg_len, width), LOW),
            shape((seg_len, width), FULL),
            shape((seg_len, width), LOW),
            shape((seg_len, width), LOW),
            shape((layout.chunks, 1, layout.size), FULL),
            shape((8, width), FULL),
        ),
        25_000_000_000,
        (pltpu.VMEM((width, width), LOW), pltpu.SemaphoreType.DMA(()))
        + landing
        + (
            pltpu.VMEM((seg_len, width), FULL),
            pltpu.VMEM((seg_len, width), LOW),
            pltpu.VMEM((seg_len, width), LOW),
            pltpu.VMEM((seg_len, width), FULL),
            pltpu.VMEM((layout.chunks, seg_len, layout.size), FULL),
            pltpu.VMEM((layout.chunks, seg_len, layout.size), LOW),
            pltpu.VMEM((2, 2, layout.size, width), LOW),
            pltpu.SemaphoreType.DMA((layout.chunks, sides)),
        ),
        grad_shapes,
    )
    output = lax.all_to_all(result.reshape(groups, quarter, width), "head", 0, 0, tiled=True)
    if layout.whole:
        half_blocks = layout.blocks // 2
        ffn_grads = [
            part
            for half in layout.taken_apart(ffn_grads[0])
            for part in (half[:half_blocks], half[half_blocks:])
        ]

    back_a, back_b = stages_a[::-1], stages_b[::-1]

    def advance(moving, level):
        return [
            halve(plus(pair), back[level]) for pair, back in zip(moving, (back_a, back_b))
        ]

    def attention_back(block, count):
        cut = width // 2
        return head_pairs(
            functools.partial(token_attention_back, memory_rows, head_dim),
            doc,
            (q, k, v, km, vm, grad_attended),
            (shape((seg_len, cut), LOW),) * 3 + (shape((2 * PAD, cut), FULL),),
            pair,
            10_000_000_000,
            block * count,
        )

    blocks = width // pair // 2
    moving = [
        (keep, swap(send, *back[0]))
        for keep, send, back in zip(ffn_grads[::2], ffn_grads[1::2], (back_a, back_b))
    ]
    back_low = attention_back(0, blocks)
    back_low, moving, grad_attended = lax.optimization_barrier((back_low, moving, grad_attended))
    moving = advance(moving, 1)
    back_high = attention_back(1, blocks)
    token_part = jnp.concatenate([back_low[3], back_high[3]], 1)
    token_parts = [token_part] + [swap(token_part, "head", j) for j in range(1, groups)]
    part_rows = width // dps
    attn_a, attn_b, grad_x, head_sums = whole_call(
        functools.partial(attention_grads, order_a, order_b, dps),
        (place,),
        (
            x,
            grad_mixed,
            attended,
            back_low[0],
            back_high[0],
            back_low[1],
            back_high[1],
            back_low[2],
            back_high[2],
            w_attn,
            grad_attn,
        ),
        (),
        (
            shape((dps, 2, part_rows, width), LOW),
            shape((dps, 2, part_rows, width), LOW),
            shape((seg_len, width), LOW),
            shape((2, width), FULL),
        ),
        10_000_000_000,
    )
    token_parts, attn_a, attn_b, grad_x, moving = lax.optimization_barrier(
        (token_parts, attn_a, attn_b, grad_x, moving)
    )
    for level in range(2, levels):
        moving = advance(moving, level)
    down_a, down_b = ([("dp", bit) for bit in order[::-1]] for order in (order_a, order_b))

    def advance_both(pairs, level):
        return [halve(plus(pair), down[level]) for pair, down in zip(pairs, (down_a, down_b))]

    attn_moving = [halve(attn_a, down_a[0]), halve(attn_b, down_b[0])]
    moved = lax.all_to_all(grad_x.reshape(groups, quarter, width), "head", 0, 0, tiled=True)

    writes = segments - 1
    packed_rows = writes * memory_rows + (-writes * memory_rows) % PAD
    score_w, grad_attended_w, grad_mixed_w, small_w, factors, bias_w, vec_w, init_w = whole_call(
        functools.partial(chain_backward, layout, heads, memory_rows),
        (reset, place),
        (
            w_attn,
            vectors,
            keys,
            values,
            qkv,
            soft,
            soft_mem,
            z_attn_w,
            pre_w,
            z_ffn_w,
            hidden_w,
            *token_parts,
        ),
        pieces,
        (
            shape((writes, heads * PAD, seg_len), LOW),
            shape((writes, PAD, width), LOW),
            shape((writes, PAD, width), LOW),
            shape((segments, 3, PAD, width), LOW),
            shape((4, packed_rows, width), LOW),
            shape((layout.chunks, 1, layout.size), FULL),
            shape((len(VECTORS), width), FULL),
            shape((PAD, width), FULL),
        ),
        20_000_000_000,
        (
            pltpu.VMEM((writes, PAD, width), LOW),
            pltpu.VMEM((writes, PAD, ff), LOW),
            pltpu.VMEM((segments, 2 * PAD, width), FULL),
        )
        + landing,
    )
    score_w, factors, moving, attn_moving, moved = lax.optimization_barrier(
        (score_w, factors, moving, attn_moving, moved)
    )

    ffn_moving = halve(jnp.stack([plus(pair) for pair in moving], 1), ("head", head_order[-1]))
    attn_moving = advance_both(attn_moving, 1)
    factors = gather(factors[None], [("dp", order_a[0])])
    sum_rows = len(SUMS) + memory_rows + 4
    sum_rows = sum_rows + (-sum_rows) % 8
    own_a, own_b, grad_tokens, pack = whole_call(
        functools.partial(
            write_grads,
            layout,
            stages_a,
            order_a,
            order_b,
            dps,
            heads,
            heads_here,
            quarter,
            memory_rows,
        ),
        (place,),
        (
            score_w,
            soft,
            qkv,
            grad_attended_w,
            grad_mixed_w,
            attended_w,
            small_w,
            read,
            tokens,
            w_attn,
            moved,
            layer_sums,
            head_sums,
            bias_sum,
            bias_w,
            vec_w,
            init_w,
        ),
        (),
        (
            shape((dps, part_rows, 2 * here), LOW),
            shape((dps, part_rows, 2 * here), LOW),
            shape((segments, quarter, width), FULL),
            shape((dps * groups, sum_rows, max(width // dps // groups, half_units)), FULL),
        ),
        5_000_000_000,
        (
            pltpu.VMEM((sum_rows, width), FULL),
            pltpu.VMEM((layout.chunks, 1, layout.size), FULL),
        ),
    )
    own_a, own_b, pack, ffn_moving, attn_moving, factors = lax.optimization_barrier(
        (own_a, own_b, pack, ffn_moving, attn_moving, factors)
    )
    own = [halve(own_a, down_a[0]), halve(own_b, down_b[0])]
    pack = halve(pack, back_a[0])
    for level in range(2, levels):
        attn_moving = advance_both(attn_moving, level)
    for bit in head_order[:-1][::-1]:
        ffn_moving = halve(plus(ffn_moving), ("head", bit))
    factors = gather(factors, stages_a[len(head_stages) + 1 :])
    for level in range(1, levels):
        own = advance_both(own, level)
    for stage in back_a[1:]:
        pack = halve(plus(pack, FULL), stage)
    both = jnp.concatenate([plus(pair)[0] for pair in attn_moving], 0)
    both = [both[..., g * here : (g + 1) * here] for g in range(groups)]
    attn_moving = jnp.stack([both[partner(i, head_stages, "head")] for i in range(groups)])
    attn_moving = halve(attn_moving, ("head", head_order[-1]))
    for bit in head_order[:-1][::-1]:
        attn_moving = halve(plus(attn_moving), ("head", bit))
    part = width // dps // groups
    row = shape((1, part), FULL)
    outs = whole_call(
        functools.partial(
            finish, order_in(order_a, order_a), order_in(order_b, order_a), memory_rows
        ),
        (),
        (factors, *ffn_moving, *attn_moving, *own[0], *own[1], *pack),
        (),
        (
            *(shape((part_rows, here), FULL),) * 3,
            *(shape((heads_here, head_dim // dps), FULL),) * 2,
            shape((here, part_rows), FULL),
            *(row,) * 3,
            shape((width, units), FULL),
            shape((1, units), FULL),
            shape((units, width), FULL),
            *(row,) * 3,
            shape((memory_rows, part), FULL),
        ),
        1_000_000_000,
    )
    flat = (6, 7, 8, 10, 12, 13, 14)
    outs = [out.reshape(-1) if i in flat else out for i, out in enumerate(outs)]
    return (output[None], norms[:, :segments], grad_tokens[None], *outs)


def solution(mesh):
    in_specs = (
        P("dp", None, None, None),
        P("dp", None, None),
        P("dp", None),
        P(),
        P(None, "head"),
        P(None, "head"),
        P(None, "head"),
        P("head", None),
        P("head", None),
        P("head", None),
        P(),
        P(),
        P(),
        P(None, ("dp", "head")),
        P(("dp", "head")),
        P(("dp", "head"), None),
        P(),
        P(),
        P(),
        P("dp", None, "head", None),
    )
    out_specs = (
        P("dp", None, "head", None),
        P("dp", None),
        P("dp", None, "head", None),
        P("dp", "head"),
        P("dp", "head"),
        P("dp", "head"),
        P("head", "dp"),
        P("head", "dp"),
        P("head", "dp"),
        P(("dp", "head")),
        P(("dp", "head")),
        P(("dp", "head")),
        P(None, ("dp", "head")),
        P(("dp", "head")),
        P(("dp", "head"), None),
        P(("dp", "head")),
        P(("dp", "head")),
        P(("dp", "head")),
        P(None, ("dp", "head")),
    )
    return jax.shard_map(
        on_device, mesh=mesh, in_specs=in_specs, out_specs=out_specs, check_vma=False
    )
```

```python
import functools

import jax
import jax.numpy as jnp
from jax import lax
from jax.experimental import pallas as pl
from jax.experimental.pallas import tpu as pltpu
from jax.sharding import PartitionSpec as P

EPSILON = 1e-06
SCALE = 0.125
NEGATIVE = -1e30
ROOT_HALF = 0.7071067811865476
DENSITY = 0.3989422804014327
LOW = jnp.bfloat16
FULL = jnp.float32
PAD = 16
VECTORS = ("b_query", "b_value", "b_out", "gain_attn", "shift_attn", "b_down", "gain_ffn", "shift_ffn")
VMEM_LIMIT = 60 * 1024 * 1024


def nn(left, right):
    return lax.dot_general(left, right, (((1,), (0,)), ((), ())), preferred_element_type=FULL)


def nt(left, right):
    return lax.dot_general(left, right, (((1,), (1,)), ((), ())), preferred_element_type=FULL)


def tn(left, right):
    return lax.dot_general(left, right, (((0,), (0,)), ((), ())), preferred_element_type=FULL)


def norm_parts(rows):
    centred = rows - jnp.mean(rows, -1, keepdims=True)
    inverse = lax.rsqrt(jnp.mean(centred * centred, -1, keepdims=True) + EPSILON)
    return centred * inverse, inverse


def norm_pull(normed, inverse, grad):
    along = jnp.mean(grad * normed, -1, keepdims=True)
    return inverse * (grad - jnp.mean(grad, -1, keepdims=True) - normed * along)


def gelu(v):
    return 0.5 * v * (1.0 + lax.erf(v * ROOT_HALF))


def gelu_slope(v):
    return 0.5 * (1.0 + lax.erf(v * ROOT_HALF)) + v * (DENSITY * jnp.exp(-0.5 * v * v))


def swap(array, axis, bit):
    return lax.ppermute(array, axis, [(i, i ^ bit) for i in range(lax.axis_size(axis))])


def bits_of(count):
    return [1 << i for i in range(count.bit_length() - 1)]


def gather(array, stages):
    for axis, bit in stages:
        array = jnp.concatenate([array, swap(array, axis, bit)], 0)
    return array


def summed(terms, kind=LOW, first=0):
    size = terms[-1].shape[0] - first
    total = terms[0][first : first + size].astype(FULL)
    for term in terms[1:]:
        total = total + term[first : first + size].astype(FULL)
    return total.astype(kind)


def add_up(count, *refs):
    out_refs = refs[sum(count) :]
    at = 0
    for number, out_ref in zip(count, out_refs):
        total = refs[at][...].astype(FULL)
        for ref in refs[at + 1 : at + number]:
            total = total + ref[...].astype(FULL)
        out_ref[...] = total.astype(out_ref.dtype)
        at += number


def parcels(groups):
    halves = [terms[-1].shape[0] // 2 for terms in groups]
    steps = min(min(halves), 4)
    in_specs, operands, out_specs, shapes = [], [], [], []

    def spec(half, rest, first):
        index = lambda i: (first + i,) + (0,) * len(rest)
        return pl.BlockSpec((half // steps, *rest), index)

    for half, terms in zip(halves, groups):
        rest = terms[0].shape[1:]
        in_specs += [spec(half, rest, steps)] * len(terms)
        operands += terms
        out_specs.append(spec(half, rest, 0))
        shapes.append(jax.ShapeDtypeStruct((half, *rest), terms[0].dtype))
    return pl.pallas_call(
        functools.partial(add_up, [len(terms) for terms in groups]),
        grid=(steps,),
        out_shape=shapes,
        in_specs=in_specs,
        out_specs=out_specs,
        compiler_params=pltpu.CompilerParams(vmem_limit_bytes=VMEM_LIMIT),
        cost_estimate=pl.CostEstimate(flops=1000, bytes_accessed=1000, transcendentals=0),
    )(*operands)


def posted(groups, sends, stages):
    return [
        terms + [swap(send, *stage)] for terms, send, stage in zip(groups, sends, stages)
    ]


def reduce_step(terms, stage):
    half = terms[-1].shape[0] // 2
    return terms + [swap(summed(terms, terms[0].dtype, half), *stage)]


def partner(index, stages, axis):
    place = 0
    for k, (name, bit) in enumerate(stages):
        if name == axis:
            place = place + ((index >> k) & 1) * bit
    return place


def position(partner_bits, order):
    place = 0
    for k, bit in enumerate(order):
        place = place + ((partner_bits // bit) % 2) * (1 << k)
    return place


def order_in(order, index_order):
    return [1 << index_order.index(bit) for bit in order]


def head_mask(rows, width, heads):
    group = lax.broadcasted_iota(jnp.int32, (rows, width), 0) // PAD
    column = lax.broadcasted_iota(jnp.int32, (rows, width), 1) // (width // heads)
    return group == column


def by_head(rows, mask, heads):
    return jnp.where(mask, jnp.concatenate([rows] * heads, 0), jnp.zeros((), rows.dtype))


def own_head(rows, mask, heads):
    kept = jnp.where(mask, rows, 0.0)
    total = kept[:PAD]
    for i in range(1, heads):
        total = total + kept[i * PAD : (i + 1) * PAD]
    return total


def vector(vec_ref, name):
    i = VECTORS.index(name)
    return vec_ref[i : i + 1, :]


class Units:
    def __init__(self, dps, heads, rows, width):
        self.dps, self.heads, self.rows, self.width = dps, heads, rows, width
        self.blocks = dps * heads
        self.chunks = max(2 * self.blocks * rows // width, 4)
        self.size = 2 * self.blocks * rows // self.chunks
        self.whole = rows % 16 != 0

    def at(self, index):
        return (index % self.heads) * self.dps + index // self.heads

    def pieces(self):
        if self.whole:
            return [(0, self.chunks)]
        part = self.blocks // 4
        return [(half * self.blocks + p * part, part) for half in range(2) for p in range(4)]

    def copies(self):
        for number, (first, count) in enumerate(self.pieces()):
            for entry in range(count):
                if self.whole:
                    yield number, entry, entry, 0, self.size
                    continue
                half, index = divmod(first + entry, self.blocks)
                row = (half * self.blocks + self.at(index)) * self.rows
                yield number, entry, row // self.size, row % self.size, self.rows

    def scratch(self):
        buffer = pltpu.VMEM((self.chunks, self.size, self.width), LOW)
        count = sum(2 for _ in self.copies())
        return (buffer, buffer, pltpu.SemaphoreType.DMA((count,)))

    def loads(self, pieces, up_ref, down_ref, arrived):
        made = []
        for number, entry, chunk, row, rows in self.copies():
            for side, to_ref in enumerate((up_ref, down_ref)):
                made.append(
                    pltpu.make_async_copy(
                        pieces[number].at[entry, side],
                        to_ref.at[chunk, pl.ds(row, rows)],
                        arrived.at[len(made)],
                    )
                )
        return made

    def assembled(self, halves):
        rows = []
        for array in halves:
            array = array.reshape(self.dps, self.heads, 2, self.rows, self.width)
            rows.append(array.transpose(1, 0, 3, 2, 4).reshape(-1, 2, self.width))
        rows = jnp.concatenate(rows, 0).reshape(self.chunks, self.size, 2, self.width)
        return [rows.transpose(0, 2, 1, 3)]

    def taken_apart(self, piece):
        rows = piece.transpose(0, 2, 1, 3).reshape(2, self.heads, self.dps, self.rows, 2, -1)
        rows = rows.transpose(0, 2, 1, 4, 3, 5)
        return [half.reshape(self.blocks, 2, self.rows, self.width) for half in rows]


def head_groups(ref, flip):
    value = ref[...]
    half = value.shape[1] // 2
    low, high = value[:, :half], value[:, half:]
    if flip & 2:
        low, high = high, low
    if flip & 1:
        low, high = pltpu.roll(low, half // 2, 1), pltpu.roll(high, half // 2, 1)
    return jnp.concatenate([low, high], 1)


def memory_queries(read, attn_ref, vec_ref):
    low = read.astype(LOW)
    queries = (nt(low, attn_ref[0]) + vector(vec_ref, "b_query")).astype(LOW)
    keys = nt(low, attn_ref[1]).astype(LOW)
    values = (nt(low, attn_ref[2]) + vector(vec_ref, "b_value")).astype(LOW)
    return queries, keys, values


def memory_attention(heads, memory_rows, queries, keys, values, key_low, value_low):
    rows, width = heads * PAD, queries.shape[1]
    mask = head_mask(rows, width, heads)
    real_key = lax.broadcasted_iota(jnp.int32, (rows, PAD), 1) < memory_rows
    spread = by_head(queries, mask, heads)
    scores = nt(spread, key_low) * SCALE
    scores_mem = jnp.where(real_key, nt(spread, keys) * SCALE, NEGATIVE)
    top = jnp.maximum(jnp.max(scores, -1, keepdims=True), jnp.max(scores_mem, -1, keepdims=True))
    raised = jnp.exp(scores - top)
    raised_mem = jnp.exp(scores_mem - top)
    total = jnp.sum(raised, -1, keepdims=True) + 2.0 * jnp.sum(raised_mem, -1, keepdims=True)
    soft = raised / total
    soft_mem = raised_mem / total
    mixed = nn(soft.astype(LOW), value_low) + 2.0 * nn(soft_mem.astype(LOW), values)
    return own_head(mixed, mask, heads).astype(LOW), soft, soft_mem


def memory_norm(result, memory_rows):
    real_row = lax.broadcasted_iota(jnp.int32, result.shape, 0) < memory_rows
    square = jnp.sum(jnp.where(real_row, result * result, 0.0), axis=(0, 1), keepdims=True)
    return jnp.sqrt(square / (memory_rows * result.shape[1]))


def chain_forward(
    layout,
    heads,
    memory_rows,
    reset_ref,
    init_ref,
    bias_ref,
    vec_ref,
    attn_from,
    key_from,
    value_from,
    *refs,
):
    count = len(layout.pieces())
    pieces, refs = refs[:count], refs[count:]
    (
        read_ref,
        qkv_ref,
        soft_ref,
        soft_mem_ref,
        attended_ref,
        z_attn_ref,
        hidden_ref,
        pre_ref,
        z_ffn_ref,
        norm_ref,
        attn_ref,
        key_ref,
        value_ref,
        attn_arrived,
        key_arrived,
        value_arrived,
        up_ref,
        down_ref,
        arrived,
    ) = refs
    last = key_ref.shape[0]
    attn_loads = [
        pltpu.make_async_copy(attn_from.at[i], attn_ref.at[i], attn_arrived.at[i])
        for i in range(4)
    ]

    def token_loads(s):
        return [
            pltpu.make_async_copy(key_from.at[s], key_ref.at[s], key_arrived.at[s]),
            pltpu.make_async_copy(value_from.at[s], value_ref.at[s], value_arrived.at[s]),
        ]

    loads = layout.loads(pieces, up_ref, down_ref, arrived)
    for load in attn_loads[:3] + token_loads(0) + attn_loads[3:] + loads:
        load.start()
    for s in range(1, last):
        for load in token_loads(s):
            load.start()
    chunks, size, _ = up_ref.shape
    norm_ref[...] = jnp.zeros_like(norm_ref)
    for load in attn_loads[:3]:
        load.wait()

    def enter(s, carried):
        fresh = (reset_ref[0, s] > 0) | (s == 0)
        read = jnp.where(fresh, init_ref[...], carried)
        read_ref[s] = read
        queries, keys, values = memory_queries(read, attn_ref, vec_ref)
        qkv_ref[s, 0] = queries
        qkv_ref[s, 1] = keys
        qkv_ref[s, 2] = values
        return read, queries, keys, values

    def step(s, carried):
        read, queries, keys, values = enter(s, carried)
        for load in token_loads(s):
            load.wait()
        attended, soft, soft_mem = memory_attention(
            heads, memory_rows, queries, keys, values, key_ref[s], value_ref[s]
        )
        soft_ref[s] = soft
        soft_mem_ref[s] = soft_mem
        attended_ref[s] = attended

        @pl.when(s == 0)
        def _():
            attn_loads[3].wait()

        z_attn = read + nn(attended, attn_ref[3]) + vector(vec_ref, "b_out")
        z_attn_ref[s] = z_attn
        normed, _ = norm_parts(z_attn)
        hidden = normed * vector(vec_ref, "gain_attn") + vector(vec_ref, "shift_attn")
        hidden_low = hidden.astype(LOW)
        hidden_ref[s] = hidden_low
        z_ffn = hidden + vector(vec_ref, "b_down")

        @pl.when(s == 0)
        def _():
            for load in loads:
                load.wait()

        for i in range(chunks):
            pre = nt(hidden_low, up_ref[i]) + bias_ref[i]
            pre_ref[s, :, i * size : (i + 1) * size] = pre
            z_ffn = z_ffn + nn(gelu(pre).astype(LOW), down_ref[i])
        z_ffn_ref[s] = z_ffn
        normed, _ = norm_parts(z_ffn)
        result = normed * vector(vec_ref, "gain_ffn") + vector(vec_ref, "shift_ffn")
        lane = lax.broadcasted_iota(jnp.int32, norm_ref.shape, 1)
        norm_ref[...] = jnp.where(lane == s, memory_norm(result, memory_rows), norm_ref[...])
        return result

    carried = lax.fori_loop(0, last, step, init_ref[...])
    enter(last, carried)


def last_norm(layout, heads, memory_rows, bias_ref, vec_ref, read_ref, qkv_ref, *refs):
    attn_from, key_from, value_from = refs[:3]
    count = len(layout.pieces())
    pieces, refs = refs[3 : 3 + count], refs[3 + count :]
    norm_ref, out_ref, key_ref, value_ref, arrived_here, up_ref, down_ref, arrived = refs
    last = read_ref.shape[0] - 1
    own_loads = [
        pltpu.make_async_copy(key_from.at[last], key_ref, arrived_here.at[0]),
        pltpu.make_async_copy(value_from.at[last], value_ref, arrived_here.at[1]),
        pltpu.make_async_copy(attn_from.at[3], out_ref, arrived_here.at[2]),
    ]
    loads = layout.loads(pieces, up_ref, down_ref, arrived)
    for load in own_loads + loads:
        load.start()
    for load in own_loads:
        load.wait()
    attended, _, _ = memory_attention(
        heads,
        memory_rows,
        qkv_ref[last, 0],
        qkv_ref[last, 1],
        qkv_ref[last, 2],
        key_ref[...],
        value_ref[...],
    )
    z_attn = read_ref[last] + nn(attended, out_ref[...]) + vector(vec_ref, "b_out")
    normed, _ = norm_parts(z_attn)
    hidden = normed * vector(vec_ref, "gain_attn") + vector(vec_ref, "shift_attn")
    hidden_low = hidden.astype(LOW)
    z_ffn = hidden + vector(vec_ref, "b_down")
    for load in loads:
        load.wait()
    for i in range(layout.chunks):
        pre = nt(hidden_low, up_ref[i]) + bias_ref[i]
        z_ffn = z_ffn + nn(gelu(pre).astype(LOW), down_ref[i])
    normed, _ = norm_parts(z_ffn)
    result = normed * vector(vec_ref, "gain_ffn") + vector(vec_ref, "shift_ffn")
    norm_ref[...] = jnp.broadcast_to(memory_norm(result, memory_rows), norm_ref.shape)


def chain_backward(
    layout,
    heads,
    memory_rows,
    reset_ref,
    place_ref,
    vec_ref,
    qkv_ref,
    soft_ref,
    soft_mem_ref,
    z_attn_ref,
    pre_ref,
    z_ffn_ref,
    hidden_ref,
    *refs,
):
    segments, _, _, width = qkv_ref.shape
    part_refs, refs = refs[:segments], refs[segments:]
    attn_from, key_from, value_from, *refs = refs
    count = len(layout.pieces())
    pieces, refs = refs[:count], refs[count:]
    (
        score_ref,
        attended_ref,
        mixed_ref,
        small_ref,
        factor_ref,
        bias_grad_ref,
        vec_grad_ref,
        init_grad_ref,
        ffn_ref,
        pre_grad_ref,
        token_part_ref,
        attn_ref,
        key_ref,
        value_ref,
        attn_arrived,
        key_arrived,
        value_arrived,
        up_ref,
        down_ref,
        arrived,
    ) = refs
    attn_loads = [
        pltpu.make_async_copy(attn_from.at[i], attn_ref.at[i], attn_arrived.at[i])
        for i in range(4)
    ]

    def token_loads(s):
        return [
            pltpu.make_async_copy(key_from.at[s], key_ref.at[s], key_arrived.at[s]),
            pltpu.make_async_copy(value_from.at[s], value_ref.at[s], value_arrived.at[s]),
        ]

    loads = layout.loads(pieces, up_ref, down_ref, arrived)
    for load in attn_loads[1:3] + loads + attn_loads[3:] + attn_loads[:1]:
        load.start()
    for s in range(segments - 2, -1, -1):
        for load in token_loads(s):
            load.start()
    for j in range(segments):
        token_part_ref[j] = head_groups(part_refs[j], j)
    me = place_ref[1]
    rows = heads * PAD
    mask = head_mask(rows, width, heads)
    chunks, size, _ = up_ref.shape
    half = chunks * size // 2
    vec_grad_ref[...] = jnp.zeros_like(vec_grad_ref)
    bias_grad_ref[...] = jnp.zeros_like(bias_grad_ref)

    def add_vector(name, grad):
        i = VECTORS.index(name)
        vec_grad_ref[i : i + 1, :] += jnp.sum(grad, 0, keepdims=True)

    last = segments - 1
    for load in attn_loads[1:3]:
        load.wait()
    grad_key = token_part_ref[last ^ me, :PAD].astype(LOW)
    grad_value = token_part_ref[last ^ me, PAD:].astype(LOW)
    small_ref[last, 0] = jnp.zeros((PAD, width), LOW)
    small_ref[last, 1] = grad_key
    small_ref[last, 2] = grad_value
    add_vector("b_value", 2.0 * grad_value.astype(FULL))
    grad_read = 2.0 * (nn(grad_key, attn_ref[1]) + nn(grad_value, attn_ref[2]))
    stop = reset_ref[0, last] > 0
    init_grad_ref[...] = jnp.where(stop, grad_read, 0.0)
    grad_write = jnp.where(stop, 0.0, grad_read)

    def step(back, grad_write):
        s = segments - 2 - back
        normed, inverse = norm_parts(z_ffn_ref[s])
        add_vector("gain_ffn", grad_write * normed)
        add_vector("shift_ffn", grad_write)
        grad_sum = norm_pull(normed, inverse, grad_write * vector(vec_ref, "gain_ffn"))
        grad_low = grad_sum.astype(LOW)
        ffn_ref[s] = grad_low
        add_vector("b_down", grad_low.astype(FULL))
        grad_hidden = grad_sum

        @pl.when(back == 0)
        def _():
            for load in loads:
                load.wait()

        for i in range(chunks):
            part = slice(i * size, (i + 1) * size)
            grad_act = nt(grad_low, down_ref[i])
            grad_pre = (grad_act * gelu_slope(pre_ref[s, :, part])).astype(LOW)
            pre_grad_ref[s, :, part] = grad_pre
            bias_grad_ref[i] += jnp.sum(grad_pre.astype(FULL), 0, keepdims=True)
            grad_hidden = grad_hidden + nn(grad_pre, up_ref[i])
        normed, inverse = norm_parts(z_attn_ref[s])
        add_vector("gain_attn", grad_hidden * normed)
        add_vector("shift_attn", grad_hidden)
        grad_attn = norm_pull(normed, inverse, grad_hidden * vector(vec_ref, "gain_attn"))
        add_vector("b_out", grad_attn)
        grad_mixed = grad_attn.astype(LOW)
        mixed_ref[s] = grad_mixed

        @pl.when(back == 0)
        def _():
            attn_loads[0].wait()
            attn_loads[3].wait()

        for load in token_loads(s):
            load.wait()
        grad_attended = nt(grad_mixed, attn_ref[3]).astype(LOW)
        attended_ref[s] = grad_attended
        queries, keys, values = qkv_ref[s, 0], qkv_ref[s, 1], qkv_ref[s, 2]
        spread = by_head(grad_attended, mask, heads)
        soft, soft_mem = soft_ref[s], soft_mem_ref[s]
        pull = nt(spread, value_ref[s])
        pull_mem = nt(spread, values)
        inner = jnp.sum(soft * pull, -1, keepdims=True) + 2.0 * jnp.sum(
            soft_mem * pull_mem, -1, keepdims=True
        )
        grad_score = (soft * (pull - inner)).astype(LOW)
        grad_score_mem = (soft_mem * (pull_mem - inner)).astype(LOW)
        score_ref[s] = grad_score
        grad_query = nn(grad_score, key_ref[s]) + 2.0 * nn(grad_score_mem, keys)
        grad_query = (SCALE * own_head(grad_query, mask, heads)).astype(LOW)
        grad_key = SCALE * tn(grad_score_mem, by_head(queries, mask, heads))
        grad_key = (token_part_ref[s ^ me, :PAD] + grad_key).astype(LOW)
        grad_value = tn(soft_mem.astype(LOW), spread)
        grad_value = (token_part_ref[s ^ me, PAD:] + grad_value).astype(LOW)
        small_ref[s, 0] = grad_query
        small_ref[s, 1] = grad_key
        small_ref[s, 2] = grad_value
        add_vector("b_query", grad_query.astype(FULL))
        add_vector("b_value", 2.0 * grad_value.astype(FULL))
        grad_read = 2.0 * (nn(grad_key, attn_ref[1]) + nn(grad_value, attn_ref[2]))
        grad_read = grad_read + nn(grad_query, attn_ref[0]) + grad_attn
        stop = (reset_ref[0, s] > 0) | (s == 0)
        init_grad_ref[...] += jnp.where(stop, grad_read, 0.0)
        return jnp.where(stop, 0.0, grad_read)

    lax.fori_loop(0, segments - 1, step, grad_write)

    packed, wide = factor_ref.shape[1], (segments - 1) * PAD
    row = lax.broadcasted_iota(jnp.int32, (packed, wide), 0)
    source = lax.broadcasted_iota(jnp.int32, (packed, wide), 1)
    take = (source // PAD == row // memory_rows) & (source % PAD == row % memory_rows)
    take = jnp.where(take, 1.0, 0.0).astype(LOW)
    mine = width // 2

    def own_units(ref):
        first = ref[: segments - 1, :, :mine].reshape(wide, mine)
        second = ref[: segments - 1, :, half : half + mine].reshape(wide, mine)
        return jnp.concatenate([first, second], 1)

    acts = gelu(own_units(pre_ref)).astype(LOW)
    factor_ref[0] = nn(take, hidden_ref[: segments - 1].reshape(wide, width)).astype(LOW)
    factor_ref[1] = nn(take, ffn_ref[...].reshape(wide, width)).astype(LOW)
    factor_ref[2] = nn(take, acts).astype(LOW)
    factor_ref[3] = nn(take, own_units(pre_grad_ref)).astype(LOW)


def whole_call(body, scalars, operands, outside, shapes, flops, scratch=(), outside_shapes=()):
    in_vmem = pl.BlockSpec(memory_space=pltpu.VMEM)
    in_smem = pl.BlockSpec(memory_space=pltpu.SMEM)
    anywhere = pl.BlockSpec(memory_space=pl.ANY)
    size = sum(a.size * a.dtype.itemsize for a in (*operands, *outside, *shapes))
    return pl.pallas_call(
        body,
        out_shape=(*shapes, *outside_shapes),
        in_specs=[in_smem] * len(scalars) + [in_vmem] * len(operands) + [anywhere] * len(outside),
        out_specs=[in_vmem] * len(shapes) + [anywhere] * len(outside_shapes),
        scratch_shapes=scratch,
        compiler_params=pltpu.CompilerParams(vmem_limit_bytes=VMEM_LIMIT),
        cost_estimate=pl.CostEstimate(flops=flops // 1000, bytes_accessed=size // 1000, transcendentals=0),
    )(*scalars, *operands, *outside)


def unit_owner(column, half, stages, order_b, layout, index):
    if half:
        dp = position(partner(index, stages, "dp"), order_b)
        at = (index % layout.heads) * layout.dps + dp
    else:
        at = layout.at(index)
    return column // layout.rows == at


def project(
    layout,
    stages,
    order_b,
    place_ref,
    token_ref,
    attn_ref,
    bias_ref,
    other_ref,
    key_ref,
    value_ref,
    x_ref,
    q_ref,
    k_ref,
    v_ref,
    vec_ref,
    bias_in_ref,
):
    devices, entries = bias_ref.shape
    width, rows = layout.width, layout.rows
    here = width // layout.heads
    packets = bias_ref[...].astype(FULL)

    def laid_out(first, count, period, owner):
        entry = lax.broadcasted_iota(jnp.int32, (entries, count), 0)
        column = lax.broadcasted_iota(jnp.int32, (entries, count), 1)
        pick = jnp.where(entry == first + column % period, 1.0, 0.0).astype(LOW)
        index = lax.broadcasted_iota(jnp.int32, (devices, count), 0)
        column = lax.broadcasted_iota(jnp.int32, (devices, count), 1)
        chosen = jnp.where(owner(column, index), nn(packets.astype(LOW), pick), 0.0)
        return jnp.sum(chosen, 0, keepdims=True)

    def of_head(column, index):
        head = partner(index, stages, "head")
        return (partner(index, stages, "dp") == 0) & (head == column // here)

    vec_ref[0:1, :] = laid_out(0, width, here, of_head)
    vec_ref[1:2, :] = laid_out(here, width, here, of_head)
    vec_ref[2:, :] = other_ref[...].astype(FULL)
    for half in range(2):
        owner = functools.partial(
            unit_owner, half=half, stages=stages, order_b=order_b, layout=layout
        )
        row = laid_out(
            2 * here + half * rows,
            layout.blocks * rows,
            rows,
            lambda column, index: owner(column, index=index),
        )
        per = layout.chunks // 2
        for i in range(per):
            bias_in_ref[half * per + i] = row[:, i * layout.size : (i + 1) * layout.size]

    for s in range(token_ref.shape[0]):
        x = token_ref[s]
        key_ref[s] = nt(x, attn_ref[1]).astype(LOW)
        value_ref[s] = (nt(x, attn_ref[2]) + vector(vec_ref, "b_value")).astype(LOW)
    own = place_ref[1]
    x = token_ref[own]
    x_ref[...] = x
    q_ref[...] = (nt(x, attn_ref[0]) + vector(vec_ref, "b_query")).astype(LOW)
    k_ref[...] = key_ref[own]
    v_ref[...] = value_ref[own]


SUMS = ("b_out", "gain_attn", "shift_attn", "b_down", "gain_ffn", "shift_ffn")


def token_layer(layout, x_ref, attended_ref, cot_ref, bias_ref, vec_ref, attn_ref, *refs):
    count = len(layout.pieces())
    pieces, refs = refs[:count], refs[count:]
    (
        result_ref,
        skip_ref,
        mixed_ref,
        grad_attended_ref,
        bias_sum_ref,
        sum_ref,
        *grad_refs,
        out_w_ref,
        out_arrived,
        up_ref,
        down_ref,
        arrived,
        z_attn_ref,
        hidden_ref,
        low_ref,
        total_ref,
        pre_ref,
        act_ref,
        stage_ref,
        sent,
    ) = refs
    out_load = pltpu.make_async_copy(attn_ref.at[3], out_w_ref, out_arrived)
    out_load.start()
    loads = layout.loads(pieces, up_ref, down_ref, arrived)
    for load in loads:
        load.start()
    chunks = layout.chunks
    out_load.wait()
    sum_ref[...] = jnp.zeros_like(sum_ref)

    def add_vector(name, grad):
        i = SUMS.index(name)
        sum_ref[i : i + 1, :] += jnp.sum(grad, 0, keepdims=True)

    z_attn = x_ref[...].astype(FULL) + nn(attended_ref[...], out_w_ref[...])
    z_attn = z_attn + vector(vec_ref, "b_out")
    z_attn_ref[...] = z_attn
    normed, _ = norm_parts(z_attn)
    hidden = normed * vector(vec_ref, "gain_attn") + vector(vec_ref, "shift_attn")
    hidden_ref[...] = hidden.astype(LOW)
    total_ref[...] = hidden + vector(vec_ref, "b_down")
    for load in loads:
        load.wait()

    def forward(i, nothing):
        pre = nt(hidden_ref[...], up_ref[i]) + bias_ref[i]
        pre_ref[i] = pre
        act = gelu(pre).astype(LOW)
        act_ref[i] = act
        total_ref[...] += nn(act, down_ref[i])
        return nothing

    lax.fori_loop(0, chunks, forward, 0)
    normed, inverse = norm_parts(total_ref[...])
    result = normed * vector(vec_ref, "gain_ffn") + vector(vec_ref, "shift_ffn")
    result_ref[...] = result.astype(LOW)
    grad = cot_ref[...].astype(FULL)
    add_vector("gain_ffn", grad * normed)
    add_vector("shift_ffn", grad)
    grad = norm_pull(normed, inverse, grad * vector(vec_ref, "gain_ffn"))
    total_ref[...] = grad
    low_ref[...] = grad.astype(LOW)
    add_vector("b_down", low_ref[...].astype(FULL))

    copies = list(layout.copies())
    spans = [first for first, _ in layout.pieces()]
    stores = []
    for i in range(chunks):
        grad_pre = (nt(low_ref[...], down_ref[i]) * gelu_slope(pre_ref[i])).astype(LOW)
        bias_sum_ref[i] = jnp.sum(grad_pre.astype(FULL), 0, keepdims=True)
        total_ref[...] += nn(grad_pre, up_ref[i])
        slot = i % 2
        if i > 1:
            for store in stores[i - 2]:
                store.wait()
        stage_ref[slot, 0] = tn(grad_pre, hidden_ref[...]).astype(LOW)
        stage_ref[slot, 1] = tn(act_ref[i], low_ref[...]).astype(LOW)
        stores.append([])
        for number, entry, chunk, row, rows in copies:
            if chunk != i:
                continue
            for side in range(2):
                to_ref = grad_refs[number // (len(spans) // len(grad_refs))]
                entry_at = spans[number] - spans[number - number % (len(spans) // len(grad_refs))]
                store = pltpu.make_async_copy(
                    stage_ref.at[slot, side, pl.ds(row, rows)],
                    to_ref.at[entry_at + entry, side],
                    sent.at[i, len(stores[i])],
                )
                store.start()
                stores[i].append(store)

    grad_hidden = total_ref[...]
    normed, inverse = norm_parts(z_attn_ref[...])
    add_vector("gain_attn", grad_hidden * normed)
    add_vector("shift_attn", grad_hidden)
    grad = norm_pull(normed, inverse, grad_hidden * vector(vec_ref, "gain_attn"))
    add_vector("b_out", grad)
    skip_ref[...] = grad
    mixed_ref[...] = grad.astype(LOW)
    grad_attended_ref[...] = nt(mixed_ref[...], out_w_ref[...]).astype(LOW)
    for i in range(max(chunks - 2, 0), chunks):
        for store in stores[i]:
            store.wait()


def spread_rows(out_ref, index, grad, place_ref, order, count):
    rows = grad.shape[0] // count
    for c in range(count):
        at = position(place_ref[0] ^ c, order)
        out_ref[(at, *index)] = grad[c * rows : (c + 1) * rows].astype(out_ref.dtype)


def part_rows(keep_ref, send_ref, index, grad, place_ref, order, count):
    rows = grad.shape[0] // count
    for c in range(count):
        block = grad[c * rows : (c + 1) * rows].astype(keep_ref.dtype)
        at = position(place_ref[0] ^ c, order)

        @pl.when(at < count // 2)
        def _():
            keep_ref[(at, *index)] = block

        @pl.when(at >= count // 2)
        def _():
            send_ref[(at - count // 2, *index)] = block


def attention_grads(
    order_a,
    order_b,
    count,
    place_ref,
    x_ref,
    mixed_ref,
    attended_ref,
    dq0_ref,
    dq1_ref,
    dk0_ref,
    dk1_ref,
    dv0_ref,
    dv1_ref,
    attn_ref,
    skip_ref,
    keep_a_ref,
    send_a_ref,
    keep_b_ref,
    send_b_ref,
    grad_x_ref,
    sums_ref,
):
    x = x_ref[...]
    total = skip_ref[...]
    half = dq0_ref.shape[1]
    pairs = ((dq0_ref, dq1_ref), (dk0_ref, dk1_ref), (dv0_ref, dv1_ref))
    for m, (low, high) in enumerate(pairs):
        low, high = low[...], high[...]
        both = jnp.concatenate([tn(x, low), tn(x, high)], 1)
        if m < 2:
            part_rows(keep_a_ref, send_a_ref, (m,), both, place_ref, order_a, count)
        else:
            part_rows(keep_b_ref, send_b_ref, (0,), both, place_ref, order_b, count)
        total = total + nn(low, attn_ref[m, :half]) + nn(high, attn_ref[m, half:])
        if m != 1:
            i = m // 2
            sums_ref[i : i + 1, :half] = jnp.sum(low.astype(FULL), 0, keepdims=True)
            sums_ref[i : i + 1, half:] = jnp.sum(high.astype(FULL), 0, keepdims=True)
    both = tn(mixed_ref[...], attended_ref[...])
    part_rows(keep_b_ref, send_b_ref, (1,), both, place_ref, order_b, count)
    grad_x_ref[...] = total.astype(LOW)


def exact(left, right):
    return lax.dot_general(
        left,
        right,
        (((1,), (0,)), ((), ())),
        precision=lax.Precision.HIGHEST,
        preferred_element_type=FULL,
    )


def pack_sums(
    layout, stages, order_b, heads_here, memory_rows, place_ref, rows_ref, bias_ref, out_ref
):
    devices, _, _ = out_ref.shape
    count, width = rows_ref.shape
    groups, dps = layout.heads, layout.dps
    here, part = width // groups, width // devices
    head_dim = here // heads_here
    head_part = head_dim // dps
    shape = (devices, count, width)
    index, row, column = (lax.broadcasted_iota(jnp.int32, shape, i) for i in range(3))
    dp = place_ref[0] ^ partner(index, stages, "dp")
    head = place_ref[1] ^ partner(index, stages, "head")
    plain = len(SUMS) + memory_rows
    of_device = column // part == dp * groups + head
    of_head = (column // here == partner(index, stages, "head")) & (
        column % head_dim // head_part == dp
    )
    chosen = ((row < plain) & of_device) | ((row >= plain) & of_head)
    chosen = jnp.where(chosen, jnp.broadcast_to(rows_ref[...][None], shape), 0.0)
    chosen = chosen.reshape(devices * count, width)
    source = lax.broadcasted_iota(jnp.int32, (width, part), 0)
    target = lax.broadcasted_iota(jnp.int32, (width, part), 1)
    plain_fold = jnp.where(source % part == target, 1.0, 0.0)
    head_column = source // head_dim % heads_here * head_part + source % head_part
    head_fold = jnp.where(head_column == target, 1.0, 0.0)
    row = lax.broadcasted_iota(jnp.int32, (devices, count, part), 1)
    folded = jnp.where(
        row < plain,
        exact(chosen, plain_fold).reshape(devices, count, part),
        exact(chosen, head_fold).reshape(devices, count, part),
    )
    out_ref[...] = jnp.zeros_like(out_ref)
    out_ref[:, :, :part] = folded
    per = layout.chunks // 2
    span = per * layout.size
    index, column = (lax.broadcasted_iota(jnp.int32, (devices, span), i) for i in range(2))
    source = lax.broadcasted_iota(jnp.int32, (span, layout.rows), 0)
    target = lax.broadcasted_iota(jnp.int32, (span, layout.rows), 1)
    fold = jnp.where(source % layout.rows == target, 1.0, 0.0)
    for half in range(2):
        row = jnp.concatenate([bias_ref[half * per + i] for i in range(per)], 1)
        mine = unit_owner(column, half, stages, order_b, layout, index)
        out_ref[:, plain + 2 + half, : layout.rows] = exact(jnp.where(mine, row, 0.0), fold)


def own_grads(
    order_a,
    order_b,
    count,
    heads,
    heads_here,
    place_ref,
    score_ref,
    soft_ref,
    qkv_ref,
    attended_grad_ref,
    mixed_ref,
    attended_ref,
    small_ref,
    read_ref,
    token_ref,
    keep_ref,
    send_ref,
):
    writes, rows, _ = score_ref.shape
    width = qkv_ref.shape[-1]
    here = width // heads * heads_here
    mine = heads_here * PAD
    mask = head_mask(rows, width, heads)[:mine]
    grads = [jnp.zeros((width, here), FULL) for _ in range(4)]
    for s in range(writes + 1):
        low = read_ref[s].astype(LOW)
        grads[1] = grads[1] + 2.0 * tn(low, small_ref[s, 1, :, :here])
        grads[2] = grads[2] + 2.0 * tn(low, small_ref[s, 2, :, :here])
        if s == writes:
            break
        grads[0] = grads[0] + tn(low, small_ref[s, 0, :, :here])
        grads[3] = grads[3] + tn(mixed_ref[s], attended_ref[s, :, :here])
        spread = by_head(qkv_ref[s, 0], mask, heads_here)[:, :here]
        pulled = by_head(attended_grad_ref[s], mask, heads_here)[:, :here]
        dk = (SCALE * tn(score_ref[s, :mine], spread)).astype(LOW)
        dv = tn(soft_ref[s, :mine].astype(LOW), pulled).astype(LOW)
        grads[1] = grads[1] + tn(token_ref[s], dk)
        grads[2] = grads[2] + tn(token_ref[s], dv)
    first, second = jnp.concatenate(grads[:2], 1), jnp.concatenate(grads[2:], 1)
    part_rows(keep_ref, send_ref, (0,), first, place_ref, order_a, count)
    part_rows(keep_ref, send_ref, (1,), second, place_ref, order_b, count)


def write_rows(
    layout,
    stages,
    order_b,
    heads,
    heads_here,
    quarter,
    memory_rows,
    place_ref,
    score_ref,
    soft_ref,
    qkv_ref,
    attended_grad_ref,
    moved_ref,
    layer_sum_ref,
    head_sum_ref,
    bias_sum_ref,
    bias_grad_ref,
    vec_grad_ref,
    init_grad_ref,
    attn_from,
    grad_token_ref,
    pack_ref,
    rows_ref,
    bias_ref,
    attn_ref,
    arrived,
):
    writes, rows, _ = score_ref.shape
    width = qkv_ref.shape[-1]
    here = width // heads * heads_here
    mine = heads_here * PAD
    loads = [
        pltpu.make_async_copy(attn_from.at[i + 1], attn_ref.at[i], arrived.at[i])
        for i in range(2)
    ]
    for load in loads:
        load.start()
    mask = head_mask(rows, width, heads)
    at = pl.multiple_of(place_ref[1] * quarter, quarter)
    total = jnp.zeros((1, here), FULL)
    for load in loads:
        load.wait()
    for s in range(writes):
        spread = by_head(qkv_ref[s, 0], mask, heads)
        pulled = by_head(attended_grad_ref[s], mask, heads)
        dv_own = tn(soft_ref[s, :mine].astype(LOW), pulled[:mine, :here]).astype(LOW)
        total = total + jnp.sum(dv_own.astype(FULL), 0, keepdims=True)
        score_here = score_ref[s, :, pl.ds(at, quarter)]
        soft_here = soft_ref[s, :, pl.ds(at, quarter)].astype(LOW)
        dk = (SCALE * tn(score_here, spread)).astype(LOW)
        dv = tn(soft_here, pulled).astype(LOW)
        extra = nn(dk, attn_ref[0]) + nn(dv, attn_ref[1])
        grad_token_ref[s] = moved_ref[s].astype(FULL) + extra
    grad_token_ref[writes] = moved_ref[writes].astype(FULL)

    lead = jnp.where(place_ref[1] == 0, 1.0, 0.0)
    rows_ref[...] = jnp.zeros_like(rows_ref)
    for i, name in enumerate(SUMS):
        at = VECTORS.index(name)
        rows_ref[i : i + 1, :] = (
            layer_sum_ref[i : i + 1, :] + lead * vec_grad_ref[at : at + 1, :]
        )
    for i in range(memory_rows):
        at = len(SUMS) + i
        rows_ref[at : at + 1, :] = lead * init_grad_ref[i : i + 1, :]
    at = len(SUMS) + memory_rows
    rows_ref[at : at + 1, :] = head_sum_ref[0:1, :] + lead * vec_grad_ref[0:1, :]
    rows_ref[at + 1 : at + 2, :] = head_sum_ref[1:2, :] + lead * vec_grad_ref[1:2, :]
    rows_ref[at + 1 : at + 2, :here] += total
    bias_ref[...] = bias_sum_ref[...] + lead * bias_grad_ref[...]
    pack_sums(
        layout, stages, order_b, heads_here, memory_rows, place_ref, rows_ref, bias_ref, pack_ref
    )


def finish(
    order_a,
    order_b,
    memory_rows,
    factor_ref,
    ffn_a_ref,
    ffn_b_ref,
    attn_ref,
    own_ref,
    sum_ref,
    query_ref,
    key_ref,
    value_ref,
    b_query_ref,
    b_value_ref,
    out_ref,
    b_out_ref,
    gain_attn_ref,
    shift_attn_ref,
    up_ref,
    b_in_ref,
    down_ref,
    b_down_ref,
    gain_ffn_ref,
    shift_ffn_ref,
    init_ref,
):
    count, _, rows, width = factor_ref.shape
    block = width // 2 // count
    column = lax.broadcasted_iota(jnp.int32, (rows, width), 1)

    def own(j, i):
        first, second = position(j, order_a), position(j, order_b) + count
        keep = (column // block == first) | (column // block == second)
        return jnp.where(keep, factor_ref[j, i], jnp.zeros((), LOW))

    units = []
    for side, left, right in ((0, 3, 0), (1, 2, 1)):
        chosen = jnp.concatenate([own(j, left) for j in range(count)], 0)
        others = jnp.concatenate([factor_ref[j, right] for j in range(count)], 0)
        product = tn(chosen, others)
        halves = []
        for i in range(2):
            total = (ffn_a_ref, ffn_b_ref)[i][0, side]
            for j in range(count):
                at = (i * count + j) * block
                total = total + product[at : at + block]
            halves.append(total)
        units.append(jnp.concatenate(halves, 0))
    up_ref[...] = units[0].T
    down_ref[...] = units[1]
    here = attn_ref.shape[-1]
    own_parts = []
    for i in range(2):
        total = own_ref[0, i]
        own_parts += [total[:, :here], total[:, here:]]
    totals = [attn_ref[0, m] + own_parts[m] for m in range(4)]
    query_ref[...] = totals[0]
    key_ref[...] = totals[1]
    value_ref[...] = totals[2]
    out_ref[...] = totals[3].T
    pack = sum_ref[0]
    refs = {
        "b_out": b_out_ref,
        "gain_attn": gain_attn_ref,
        "shift_attn": shift_attn_ref,
        "b_down": b_down_ref,
        "gain_ffn": gain_ffn_ref,
        "shift_ffn": shift_ffn_ref,
    }
    part = init_ref.shape[1]
    for i, name in enumerate(SUMS):
        refs[name][...] = pack[i : i + 1, :part]
    at = len(SUMS) + memory_rows
    init_ref[...] = pack[len(SUMS) : at, :part]
    heads_here, head_part = b_query_ref.shape
    for i in range(heads_here):
        columns = slice(i * head_part, (i + 1) * head_part)
        b_query_ref[i : i + 1, :] = pack[at : at + 1, columns]
        b_value_ref[i : i + 1, :] = pack[at + 1 : at + 2, columns]
    b_in_ref[:, :block] = pack[at + 2 : at + 3, :block]
    b_in_ref[:, block:] = pack[at + 3 : at + 4, :block]


def scores_of(q, k, km, allowed, real_key):
    scores = jnp.where(allowed, nt(q, k) * SCALE, NEGATIVE)
    return scores, jnp.where(real_key, nt(q, km) * SCALE, NEGATIVE)


def token_attention(head_dim, row_ref, column_ref, q_ref, k_ref, v_ref, sum_ref, top_ref, total_ref):
    q, k, v = q_ref[...], k_ref[...], v_ref[...]
    allowed = column_ref[...] == row_ref[...]
    lane = lax.broadcasted_iota(jnp.int32, q.shape, 1) // head_dim
    sums, tops, totals = (jnp.zeros(q.shape, FULL) for _ in range(3))
    for head in range(q.shape[1] // head_dim):
        mine = jnp.where(lane == head, q, jnp.zeros((), LOW))
        scores = jnp.where(allowed, nt(mine, k) * SCALE, NEGATIVE)
        top = jnp.max(scores, -1, keepdims=True)
        raised = jnp.exp(scores - top)
        totals = jnp.where(lane == head, jnp.sum(raised, -1, keepdims=True), totals)
        tops = jnp.where(lane == head, top, tops)
        sums = jnp.where(lane == head, nn(raised.astype(LOW), v), sums)
    sum_ref[...] = sums
    top_ref[...] = tops
    total_ref[...] = totals


def with_memory(
    memory_rows, head_dim, q_ref, km_ref, vm_ref, sum_ref, top_ref, total_ref, out_ref, log_ref
):
    q, km, vm = q_ref[...], km_ref[...], vm_ref[...]
    real_key = lax.broadcasted_iota(jnp.int32, (q.shape[0], PAD), 1) < memory_rows
    lane = lax.broadcasted_iota(jnp.int32, q.shape, 1) // head_dim
    tops, totals, mixes = (jnp.zeros(q.shape, FULL) for _ in range(3))
    for head in range(q.shape[1] // head_dim):
        mine = jnp.where(lane == head, q, jnp.zeros((), LOW))
        scores = jnp.where(real_key, nt(mine, km) * SCALE, NEGATIVE)
        at = head * head_dim
        top = jnp.maximum(jnp.max(scores, -1, keepdims=True), top_ref[:, at : at + 1])
        raised = jnp.exp(scores - top)
        tops = jnp.where(lane == head, top, tops)
        totals = jnp.where(lane == head, 2.0 * jnp.sum(raised, -1, keepdims=True), totals)
        mixes = jnp.where(lane == head, 2.0 * nn(raised.astype(LOW), vm), mixes)
    shrink = jnp.exp(top_ref[...] - tops)
    totals = totals + total_ref[...] * shrink
    out_ref[...] = ((mixes + sum_ref[...] * shrink) / totals).astype(LOW)
    log_ref[...] = tops + jnp.log(totals)


def token_attention_back(
    memory_rows,
    head_dim,
    row_ref,
    column_ref,
    q_ref,
    k_ref,
    v_ref,
    km_ref,
    vm_ref,
    log_ref,
    grad_ref,
    dq_ref,
    dk_ref,
    dv_ref,
    dmem_ref,
):
    q, k, v, km, vm, grad = (r[...] for r in (q_ref, k_ref, v_ref, km_ref, vm_ref, grad_ref))
    allowed = column_ref[...] == row_ref[...]
    real_key = lax.broadcasted_iota(jnp.int32, (q.shape[0], PAD), 1) < memory_rows
    lane = lax.broadcasted_iota(jnp.int32, q.shape, 1) // head_dim
    zero = jnp.zeros((), LOW)
    dq, dk, dv = (jnp.zeros(q.shape, FULL) for _ in range(3))
    dkm, dvm = (jnp.zeros(km.shape, FULL) for _ in range(2))
    for head in range(q.shape[1] // head_dim):
        mine = jnp.where(lane == head, q, zero)
        mine_grad = jnp.where(lane == head, grad, zero)
        scores, scores_mem = scores_of(mine, k, km, allowed, real_key)
        log_total = log_ref[:, head * head_dim : head * head_dim + 1]
        soft, soft_mem = jnp.exp(scores - log_total), jnp.exp(scores_mem - log_total)
        pull, pull_mem = nt(mine_grad, v), nt(mine_grad, vm)
        inner = jnp.sum(soft * pull, -1, keepdims=True) + 2.0 * jnp.sum(
            soft_mem * pull_mem, -1, keepdims=True
        )
        score = (soft * (pull - inner)).astype(LOW)
        score_mem = (soft_mem * (pull_mem - inner)).astype(LOW)
        dq = jnp.where(lane == head, nn(score, k) + 2.0 * nn(score_mem, km), dq)
        dk = dk + tn(score, mine)
        dv = dv + tn(soft.astype(LOW), mine_grad)
        dkm = dkm + tn(score_mem, mine)
        dvm = dvm + tn(soft_mem.astype(LOW), mine_grad)
    dq_ref[...] = (SCALE * dq).astype(LOW)
    dk_ref[...] = (SCALE * dk).astype(LOW)
    dv_ref[...] = dv.astype(LOW)
    dmem_ref[:PAD] = SCALE * dkm
    dmem_ref[PAD:] = dvm


def head_pairs(body, doc, operands, shapes, width, flops, first=0):
    seg_len = operands[0].shape[0]
    columns = lambda array: pl.BlockSpec((array.shape[0], width), lambda i: (0, i + first))
    results = lambda array: pl.BlockSpec((array.shape[0], width), lambda i: (0, i))
    return pl.pallas_call(
        body,
        grid=(shapes[0].shape[1] // width,),
        out_shape=shapes,
        in_specs=[pl.BlockSpec(a.shape, lambda i: (0, 0)) for a in doc]
        + [columns(a) for a in operands],
        out_specs=[results(s) for s in shapes],
        compiler_params=pltpu.CompilerParams(vmem_limit_bytes=VMEM_LIMIT),
        cost_estimate=pl.CostEstimate(
            flops=flops // 1000, bytes_accessed=seg_len, transcendentals=0
        ),
    )(*doc, *operands)


def on_device(
    tokens,
    doc_ids,
    reset,
    mem_init,
    w_query,
    w_key,
    w_value,
    b_query,
    b_value,
    w_out,
    b_out,
    gain_attn,
    shift_attn,
    w_in,
    b_in,
    w_down,
    b_down,
    gain_ffn,
    shift_ffn,
    cotangent,
):
    chains, segments, seg_len, width = tokens.shape
    dps, groups = lax.axis_size("dp"), lax.axis_size("head")
    assert chains == 1 and segments == groups
    memory_rows = mem_init.shape[0]
    heads_here, head_dim = b_query.shape
    heads = heads_here * groups
    here = heads_here * head_dim
    units = w_in.shape[1]
    half_units = units // 2
    quarter = seg_len // groups
    dp, head = lax.axis_index("dp"), lax.axis_index("head")
    place = jnp.stack([dp, head])
    bits = bits_of(dps)
    levels = len(bits)
    order_a = bits[1:] + bits[:1]
    order_b = bits[1:][::-1] + bits[:1]
    head_order = bits_of(groups)[::-1]
    head_stages = [("head", bit) for bit in head_order]
    stages_a = head_stages + [("dp", bit) for bit in order_a]
    stages_b = head_stages + [("dp", bit) for bit in order_b]
    layout = Units(dps, groups, half_units, width)
    landing = layout.scratch()
    shape = jax.ShapeDtypeStruct
    tokens, doc_ids, cotangent = tokens[0], doc_ids[0], cotangent[0]

    shard = jnp.concatenate([w_query.T, w_key.T, w_value.T, w_out], 0)
    share = shard.shape[0] // dps
    chunk = lax.dynamic_slice_in_dim(shard, dp * share, share, 0)[None]
    biases = jnp.concatenate([b_query.reshape(-1), b_value.reshape(-1), b_in])[None]
    up = w_in.T.reshape(2, half_units, width)
    down = w_down.reshape(2, half_units, width)
    halves = [jnp.stack([up[i], down[i]])[None] for i in range(2)]
    for i, stage in enumerate(head_stages):
        chunk, biases = gather(chunk, [stage]), gather(biases, [stage])
        if i:
            halves = [gather(half, [head_stages[i - 1]]) for half in halves]
        chunk, biases, halves = lax.optimization_barrier((chunk, biases, halves))
    halves = [gather(half, head_stages[-1:]) for half in halves]
    biases = gather(biases, stages_a[len(head_stages) : -1])
    chunk = jnp.stack([chunk[position(j, head_order)] for j in range(1, groups)])
    parts = []
    for rows, order in ((slice(0, share // 2), order_a), (slice(share // 2, share), order_b)):
        part = chunk[:, rows]
        have = []
        for bit in order:
            at = sum(1 for b in have if b > bit)
            have.append(bit)
            mine = (dp // bit) % 2
            other = swap(part, "dp", bit)
            part = jnp.where(mine == 1, jnp.stack([other, part], at), jnp.stack([part, other], at))
        parts.append(part.reshape(dps, groups - 1, share // 2, width))
    others = jnp.concatenate(parts, 2).transpose(1, 0, 2, 3).reshape(groups - 1, 4, here, width)
    doc = lax.dynamic_index_in_dim(doc_ids, head, 0, False)
    doc_row, doc_column = doc[None, :], doc[:, None]
    init = jnp.pad(mem_init.astype(FULL), ((0, PAD - memory_rows), (0, 0)))
    vectors = jnp.concatenate([b_out, gain_attn, shift_attn, b_down, gain_ffn, shift_ffn])
    vectors = vectors.reshape(-1, width)
    halves, others, biases, cotangent, doc_row, doc_column, init, vectors = (
        lax.optimization_barrier(
            (halves, others, biases, cotangent, doc_row, doc_column, init, vectors)
        )
    )
    biases = gather(biases, stages_a[-1:])
    cotangent = lax.all_to_all(cotangent, "head", 0, 0, tiled=True).reshape(seg_len, width)
    w_attn = jnp.concatenate([shard.reshape(4, 1, here, width), others.transpose(1, 0, 2, 3)], 1)
    w_attn = w_attn.reshape(4, groups * here, width)
    halves = [
        gather(half, stages[len(head_stages) : -2])
        for half, stages in zip(halves, (stages_a, stages_b))
    ]
    keys, values, x, q, k, v, vectors, bias_in = whole_call(
        functools.partial(project, layout, stages_a, order_b),
        (place,),
        (tokens, w_attn, biases, vectors),
        (),
        (shape(tokens.shape, LOW),) * 2
        + (shape((seg_len, width), LOW),) * 4
        + (shape((len(VECTORS), width), FULL), shape((layout.chunks, 1, layout.size), FULL)),
        6_000_000_000,
    )

    pair = 2 * head_dim
    partial = head_pairs(
        functools.partial(token_attention, head_dim),
        (doc_row, doc_column),
        (q, k, v),
        (shape((seg_len, width), FULL),) * 3,
        pair,
        8_000_000_000,
    )
    halves = lax.optimization_barrier(halves)
    other_halves = [
        swap(half, *stages[-2]) for half, stages in zip(halves, (stages_a, stages_b))
    ]
    other_halves, partial, keys, cotangent = lax.optimization_barrier(
        (other_halves, partial, keys, cotangent)
    )
    pieces = []
    for half, other, stages in zip(halves, other_halves, (stages_a, stages_b)):
        pieces += [half, other, swap(half, *stages[-1]), swap(other, *stages[-1])]
    if layout.whole:
        pieces = layout.assembled([jnp.concatenate(pieces[i : i + 4], 0) for i in (0, 4)])

    ff = layout.chunks * layout.size
    writes = segments - 1
    rows_shape = lambda kind: shape((writes, PAD, width), kind)
    tokens_scratch = (
        pltpu.VMEM((4, width, width), LOW),
        pltpu.VMEM((writes, seg_len, width), LOW),
        pltpu.VMEM((writes, seg_len, width), LOW),
        pltpu.SemaphoreType.DMA((4,)),
        pltpu.SemaphoreType.DMA((writes,)),
        pltpu.SemaphoreType.DMA((writes,)),
    )
    read, qkv, soft, soft_mem, attended_w, z_attn_w, hidden_w, pre_w, z_ffn_w, norms = whole_call(
        functools.partial(chain_forward, layout, heads, memory_rows),
        (reset,),
        (init, bias_in, vectors),
        (w_attn, keys, values, *pieces),
        (
            shape((segments, PAD, width), FULL),
            shape((segments, 3, PAD, width), LOW),
            shape((writes, heads * PAD, seg_len), FULL),
            shape((writes, heads * PAD, PAD), FULL),
            rows_shape(LOW),
            rows_shape(FULL),
            rows_shape(LOW),
            shape((writes, PAD, ff), FULL),
            rows_shape(FULL),
            shape((1, 128), FULL),
        ),
        20_000_000_000,
        tokens_scratch + landing,
    )
    own_mem = lax.dynamic_index_in_dim(qkv, head, 0, False)
    km, vm = own_mem[1], own_mem[2]

    attended, log_total = head_pairs(
        functools.partial(with_memory, memory_rows, head_dim),
        (),
        (q, km, vm, *partial),
        (shape((seg_len, width), LOW), shape((seg_len, width), FULL)),
        pair,
        8_000_000_000,
    )
    if layout.whole:
        grad_shapes = (shape((layout.chunks, 2, layout.size, width), LOW),)
    else:
        grad_shapes = (shape((layout.blocks // 2, 2, half_units, width), LOW),) * 4
    sides = 2 * max(layout.size // (layout.size if layout.whole else half_units), 1)
    result, grad_attn, grad_mixed, grad_attended, bias_sum, layer_sums, *ffn_grads = whole_call(
        functools.partial(token_layer, layout),
        (),
        (x, attended, cotangent, bias_in, vectors),
        (w_attn, *pieces),
        (
            shape((seg_len, width), LOW),
            shape((seg_len, width), FULL),
            shape((seg_len, width), LOW),
            shape((seg_len, width), LOW),
            shape((layout.chunks, 1, layout.size), FULL),
            shape((8, width), FULL),
        ),
        25_000_000_000,
        (pltpu.VMEM((width, width), LOW), pltpu.SemaphoreType.DMA(()))
        + landing
        + (
            pltpu.VMEM((seg_len, width), FULL),
            pltpu.VMEM((seg_len, width), LOW),
            pltpu.VMEM((seg_len, width), LOW),
            pltpu.VMEM((seg_len, width), FULL),
            pltpu.VMEM((layout.chunks, seg_len, layout.size), FULL),
            pltpu.VMEM((layout.chunks, seg_len, layout.size), LOW),
            pltpu.VMEM((2, 2, layout.size, width), LOW),
            pltpu.SemaphoreType.DMA((layout.chunks, sides)),
        ),
        grad_shapes,
    )
    if layout.whole:
        half_blocks = layout.blocks // 2
        ffn_grads = [
            part
            for half in layout.taken_apart(ffn_grads[0])
            for part in (half[:half_blocks], half[half_blocks:])
        ]

    back_a, back_b = stages_a[::-1], stages_b[::-1]

    def stages_of(level):
        return back_a[level], back_b[level]

    def attention_back(block, count):
        cut = width // 2
        return head_pairs(
            functools.partial(token_attention_back, memory_rows, head_dim),
            (doc_row, doc_column),
            (q, k, v, km, vm, log_total, grad_attended),
            (shape((seg_len, cut), LOW),) * 3 + (shape((2 * PAD, cut), FULL),),
            pair,
            10_000_000_000,
            block * count,
        )

    blocks = width // pair // 2
    moving = [
        [keep, swap(send, *back[0])]
        for keep, send, back in zip(ffn_grads[::2], ffn_grads[1::2], (back_a, back_b))
    ]
    back_low = attention_back(0, blocks)
    back_low, moving, grad_attended, result = lax.optimization_barrier(
        (back_low, moving, grad_attended, result)
    )
    sends = parcels(moving)
    sends, grad_attended = lax.optimization_barrier((sends, grad_attended))
    moving = posted(moving, sends, stages_of(1))
    output = lax.all_to_all(result.reshape(groups, quarter, width), "head", 0, 0, tiled=True)
    back_high = attention_back(1, blocks)
    token_part = jnp.concatenate([back_low[3], back_high[3]], 1)
    token_part, back_high = lax.optimization_barrier((token_part, back_high))
    token_parts = [token_part] + [swap(token_part, "head", j) for j in range(1, groups)]
    share = width // dps
    keep_a, send_a, keep_b, send_b, grad_x, head_sums = whole_call(
        functools.partial(attention_grads, order_a, order_b, dps),
        (place,),
        (
            x,
            grad_mixed,
            attended,
            back_low[0],
            back_high[0],
            back_low[1],
            back_high[1],
            back_low[2],
            back_high[2],
            w_attn,
            grad_attn,
        ),
        (),
        (
            *(shape((dps // 2, 2, share, width), LOW),) * 4,
            shape((seg_len, width), LOW),
            shape((2, width), FULL),
        ),
        10_000_000_000,
    )
    down_a, down_b = ([("dp", bit) for bit in order[::-1]] for order in (order_a, order_b))

    def advance_both(parts, level):
        return [reduce_step(p, down[level]) for p, down in zip(parts, (down_a, down_b))]

    token_parts, send_a, send_b, grad_x, moving, output = lax.optimization_barrier(
        (token_parts, send_a, send_b, grad_x, moving, output)
    )
    attn_moving = [[keep_a, swap(send_a, *down_a[0])], [keep_b, swap(send_b, *down_b[0])]]
    sends = parcels(moving)
    attn_moving, sends = lax.optimization_barrier((attn_moving, sends))
    moving = posted(moving, sends, stages_of(2))
    for level in range(3, levels):
        moving = posted(moving, parcels(moving), stages_of(level))
    sends = parcels(attn_moving)
    sends, grad_x, token_parts = lax.optimization_barrier((sends, grad_x, token_parts))
    attn_moving = posted(attn_moving, sends, (down_a[1], down_b[1]))
    moved = lax.all_to_all(grad_x.reshape(groups, quarter, width), "head", 0, 0, tiled=True)

    packed_rows = writes * memory_rows + (-writes * memory_rows) % PAD
    score_w, grad_attended_w, grad_mixed_w, small_w, factors, bias_w, vec_w, init_w = whole_call(
        functools.partial(chain_backward, layout, heads, memory_rows),
        (reset, place),
        (
            vectors,
            qkv,
            soft,
            soft_mem,
            z_attn_w,
            pre_w,
            z_ffn_w,
            hidden_w,
            *token_parts,
        ),
        (w_attn, keys, values, *pieces),
        (
            shape((writes, heads * PAD, seg_len), LOW),
            shape((writes, PAD, width), LOW),
            shape((writes, PAD, width), LOW),
            shape((segments, 3, PAD, width), LOW),
            shape((4, packed_rows, width), LOW),
            shape((layout.chunks, 1, layout.size), FULL),
            shape((len(VECTORS), width), FULL),
            shape((PAD, width), FULL),
        ),
        20_000_000_000,
        (
            pltpu.VMEM((writes, PAD, width), LOW),
            pltpu.VMEM((writes, PAD, ff), LOW),
            pltpu.VMEM((segments, 2 * PAD, width), FULL),
        )
        + tokens_scratch
        + landing,
    )
    score_w, factors, moving, attn_moving, moved = lax.optimization_barrier(
        (score_w, factors, moving, attn_moving, moved)
    )

    if levels > 2:
        sends = parcels(moving + attn_moving)
        sends, score_w = lax.optimization_barrier((sends, score_w))
        moving = posted(moving, sends[:2], stages_of(levels))
        attn_moving = posted(attn_moving, sends[2:], (down_a[2], down_b[2]))
    for level in range(3, levels):
        attn_moving = advance_both(attn_moving, level)
    factors = gather(factors[None], [("dp", order_a[0])])
    sum_rows = len(SUMS) + memory_rows + 4
    sum_rows = sum_rows + (-sum_rows) % 8
    grad_tokens, pack = whole_call(
        functools.partial(
            write_rows, layout, stages_a, order_b, heads, heads_here, quarter, memory_rows
        ),
        (place,),
        (
            score_w,
            soft,
            qkv,
            grad_attended_w,
            moved,
            layer_sums,
            head_sums,
            bias_sum,
            bias_w,
            vec_w,
            init_w,
        ),
        (w_attn,),
        (
            shape((segments, quarter, width), FULL),
            shape((dps * groups, sum_rows, max(width // dps // groups, half_units)), FULL),
        ),
        5_000_000_000,
        (
            pltpu.VMEM((sum_rows, width), FULL),
            pltpu.VMEM((layout.chunks, 1, layout.size), FULL),
            pltpu.VMEM((2, width, width), LOW),
            pltpu.SemaphoreType.DMA((2,)),
        ),
    )
    pack, attn_moving, factors, score_w = lax.optimization_barrier(
        (pack, attn_moving, factors, score_w)
    )
    pack = reduce_step([pack], back_a[0])
    factors = gather(factors, [("dp", order_a[1])])
    both = jnp.concatenate([summed(terms)[0] for terms in attn_moving], 0)
    both = [both[..., g * here : (g + 1) * here] for g in range(groups)]
    attn_moving = [jnp.stack([both[partner(i, head_stages, "head")] for i in range(groups)])]
    attn_moving = reduce_step(attn_moving, ("head", head_order[-1]))
    keep_own, send_own = whole_call(
        functools.partial(own_grads, order_a, order_b, dps, heads, heads_here),
        (place,),
        (
            score_w,
            soft,
            qkv,
            grad_attended_w,
            grad_mixed_w,
            attended_w,
            small_w,
            read,
            tokens,
        ),
        (),
        (shape((dps // 2, 2, share, 2 * here), LOW),) * 2,
        5_000_000_000,
    )
    keep_own, send_own, pack, moving, read = lax.optimization_barrier(
        (keep_own, send_own, pack, moving, read)
    )
    own = [keep_own, swap(send_own, *down_a[0])]
    pack = reduce_step(pack, back_a[1])
    for level in range(levels + 1, len(back_a)):
        moving = [reduce_step(p, stage) for p, stage in zip(moving, stages_of(level))]
    (last_value,) = whole_call(
        functools.partial(last_norm, layout, heads, memory_rows),
        (),
        (bias_in, vectors, read, qkv),
        (w_attn, keys, values, *pieces),
        (shape((1, 128), FULL),),
        5_000_000_000,
        (
            pltpu.VMEM((width, width), LOW),
            pltpu.VMEM((seg_len, width), LOW),
            pltpu.VMEM((seg_len, width), LOW),
            pltpu.SemaphoreType.DMA((3,)),
        )
        + landing,
    )
    own, pack, factors, attn_moving, last_value = lax.optimization_barrier(
        (own, pack, factors, attn_moving, last_value)
    )
    norms = jnp.concatenate([norms[:, :writes], last_value[:, :1]], 1)
    factors = gather(factors, stages_a[len(head_stages) + 2 :])
    for stage in back_a[2:]:
        pack = reduce_step(pack, stage)
    own = [[term[:, i] for term in own] for i in range(2)]
    for level in range(1, levels):
        own = advance_both(own, level)
    own = jnp.stack([summed(terms, FULL) for terms in own], 1)
    for bit in head_order[:-1][::-1]:
        attn_moving = reduce_step(attn_moving, ("head", bit))
    part = width // dps // groups
    row = shape((1, part), FULL)
    outs = whole_call(
        functools.partial(
            finish, order_in(order_a, order_a), order_in(order_b, order_a), memory_rows
        ),
        (),
        (
            factors,
            *(summed(terms, FULL) for terms in (*moving, attn_moving)),
            own,
            summed(pack, FULL),
        ),
        (),
        (
            *(shape((share, here), FULL),) * 3,
            *(shape((heads_here, head_dim // dps), FULL),) * 2,
            shape((here, share), FULL),
            *(row,) * 3,
            shape((width, units), FULL),
            shape((1, units), FULL),
            shape((units, width), FULL),
            *(row,) * 3,
            shape((memory_rows, part), FULL),
        ),
        1_000_000_000,
    )
    flat = (6, 7, 8, 10, 12, 13, 14)
    outs = [out.reshape(-1) if i in flat else out for i, out in enumerate(outs)]
    return (output[None], norms, grad_tokens[None], *outs)


def solution(mesh):
    in_specs = (
        P("dp", None, None, None),
        P("dp", None, None),
        P("dp", None),
        P(),
        P(None, "head"),
        P(None, "head"),
        P(None, "head"),
        P("head", None),
        P("head", None),
        P("head", None),
        P(),
        P(),
        P(),
        P(None, ("dp", "head")),
        P(("dp", "head")),
        P(("dp", "head"), None),
        P(),
        P(),
        P(),
        P("dp", None, "head", None),
    )
    out_specs = (
        P("dp", None, "head", None),
        P("dp", None),
        P("dp", None, "head", None),
        P("dp", "head"),
        P("dp", "head"),
        P("dp", "head"),
        P("head", "dp"),
        P("head", "dp"),
        P("head", "dp"),
        P(("dp", "head")),
        P(("dp", "head")),
        P(("dp", "head")),
        P(None, ("dp", "head")),
        P(("dp", "head")),
        P(("dp", "head"), None),
        P(("dp", "head")),
        P(("dp", "head")),
        P(("dp", "head")),
        P(None, ("dp", "head")),
    )
    return jax.shard_map(
        on_device, mesh=mesh, in_specs=in_specs, out_specs=out_specs, check_vma=False
    )
```

```python
import functools

import jax
import jax.numpy as jnp
from jax import lax
from jax.experimental import pallas as pl
from jax.experimental.pallas import tpu as pltpu
from jax.sharding import PartitionSpec as P

EPSILON = 1e-06
SCALE = 0.125
NEGATIVE = -1e30
ROOT_HALF = 0.7071067811865476
DENSITY = 0.3989422804014327
LOW = jnp.bfloat16
FULL = jnp.float32
PAD = 16
VECTORS = ("b_query", "b_value", "b_out", "gain_attn", "shift_attn", "b_down", "gain_ffn", "shift_ffn")
VMEM_LIMIT = 60 * 1024 * 1024


def nn(left, right):
    return lax.dot_general(left, right, (((1,), (0,)), ((), ())), preferred_element_type=FULL)


def nt(left, right):
    return lax.dot_general(left, right, (((1,), (1,)), ((), ())), preferred_element_type=FULL)


def tn(left, right):
    return lax.dot_general(left, right, (((0,), (0,)), ((), ())), preferred_element_type=FULL)


def norm_parts(rows):
    centred = rows - jnp.mean(rows, -1, keepdims=True)
    inverse = lax.rsqrt(jnp.mean(centred * centred, -1, keepdims=True) + EPSILON)
    return centred * inverse, inverse


def norm_pull(normed, inverse, grad):
    along = jnp.mean(grad * normed, -1, keepdims=True)
    return inverse * (grad - jnp.mean(grad, -1, keepdims=True) - normed * along)


def gelu(v):
    return 0.5 * v * (1.0 + lax.erf(v * ROOT_HALF))


def gelu_slope(v):
    return 0.5 * (1.0 + lax.erf(v * ROOT_HALF)) + v * (DENSITY * jnp.exp(-0.5 * v * v))


def swap(array, axis, bit):
    return lax.ppermute(array, axis, [(i, i ^ bit) for i in range(lax.axis_size(axis))])


def bits_of(count):
    return [1 << i for i in range(count.bit_length() - 1)]


def gather(array, stages):
    for axis, bit in stages:
        array = jnp.concatenate([array, swap(array, axis, bit)], 0)
    return array


def summed(terms, kind=LOW, first=0):
    size = terms[-1].shape[0] - first
    total = terms[0][first : first + size].astype(FULL)
    for term in terms[1:]:
        total = total + term[first : first + size].astype(FULL)
    return total.astype(kind)


def add_up(count, together, *refs):
    out_refs = list(refs[sum(count) :])
    pair_ref = None
    if together:
        pair_ref = out_refs[0]
        out_refs = [None, None] + out_refs[1:]
    at = 0
    for number_of, (number, out_ref) in enumerate(zip(count, out_refs)):
        total = refs[at][...].astype(FULL)
        for ref in refs[at + 1 : at + number]:
            total = total + ref[...].astype(FULL)
        total = total.astype(refs[at].dtype)
        at += number
        if pair_ref is not None and number_of < 2:
            pair_ref[:, number_of] = total
        else:
            out_ref[...] = total


def parcels(groups, together=False):
    halves = [terms[-1].shape[0] // 2 for terms in groups]
    steps = min(min(halves), 4)
    in_specs, operands, out_specs, shapes = [], [], [], []

    def spec(half, rest, first):
        index = lambda i: (first + i,) + (0,) * len(rest)
        return pl.BlockSpec((half // steps, *rest), index)

    for half, terms in zip(halves, groups):
        rest = terms[0].shape[1:]
        in_specs += [spec(half, rest, steps)] * len(terms)
        operands += terms
        if together and len(operands) < len(groups[0]) + len(groups[1]) + 1:
            if len(shapes):
                continue
            rest = (2, *rest)
        out_specs.append(spec(half, rest, 0))
        shapes.append(jax.ShapeDtypeStruct((half, *rest), terms[0].dtype))
    return pl.pallas_call(
        functools.partial(add_up, [len(terms) for terms in groups], together),
        grid=(steps,),
        out_shape=shapes,
        in_specs=in_specs,
        out_specs=out_specs,
        compiler_params=pltpu.CompilerParams(vmem_limit_bytes=VMEM_LIMIT),
        cost_estimate=pl.CostEstimate(flops=1000, bytes_accessed=1000, transcendentals=0),
    )(*operands)


def posted(groups, sends, stages):
    return [
        terms + [swap(send, *stage)] for terms, send, stage in zip(groups, sends, stages)
    ]


def reduce_step(terms, stage):
    half = terms[-1].shape[0] // 2
    return terms + [swap(summed(terms, terms[0].dtype, half), *stage)]


def partner(index, stages, axis):
    place = 0
    for k, (name, bit) in enumerate(stages):
        if name == axis:
            place = place + ((index >> k) & 1) * bit
    return place


def position(partner_bits, order):
    place = 0
    for k, bit in enumerate(order):
        place = place + ((partner_bits // bit) % 2) * (1 << k)
    return place


def order_in(order, index_order):
    return [1 << index_order.index(bit) for bit in order]


def head_mask(rows, width, heads):
    group = lax.broadcasted_iota(jnp.int32, (rows, width), 0) // PAD
    column = lax.broadcasted_iota(jnp.int32, (rows, width), 1) // (width // heads)
    return group == column


def by_head(rows, mask, heads):
    return jnp.where(mask, jnp.concatenate([rows] * heads, 0), jnp.zeros((), rows.dtype))


def own_head(rows, mask, heads):
    kept = jnp.where(mask, rows, 0.0)
    total = kept[:PAD]
    for i in range(1, heads):
        total = total + kept[i * PAD : (i + 1) * PAD]
    return total


def vector(vec_ref, name):
    i = VECTORS.index(name)
    return vec_ref[i : i + 1, :]


class Units:
    def __init__(self, dps, heads, rows, width):
        self.dps, self.heads, self.rows, self.width = dps, heads, rows, width
        self.blocks = dps * heads
        self.chunks = max(2 * self.blocks * rows // width, 4)
        self.size = 2 * self.blocks * rows // self.chunks
        self.whole = rows % 16 != 0

    def at(self, index):
        return (index % self.heads) * self.dps + index // self.heads

    def pieces(self):
        if self.whole:
            return [(0, self.chunks)]
        part = self.blocks // 4
        return [(half * self.blocks + p * part, part) for half in range(2) for p in range(4)]

    def copies(self):
        for number, (first, count) in enumerate(self.pieces()):
            for entry in range(count):
                if self.whole:
                    yield number, entry, entry, 0, self.size
                    continue
                half, index = divmod(first + entry, self.blocks)
                row = (half * self.blocks + self.at(index)) * self.rows
                yield number, entry, row // self.size, row % self.size, self.rows

    def scratch(self):
        buffer = pltpu.VMEM((self.chunks, self.size, self.width), LOW)
        count = sum(2 for _ in self.copies())
        return (buffer, buffer, pltpu.SemaphoreType.DMA((count,)))

    def loads(self, pieces, up_ref, down_ref, arrived):
        made = []
        for number, entry, chunk, row, rows in self.copies():
            for side, to_ref in enumerate((up_ref, down_ref)):
                made.append(
                    pltpu.make_async_copy(
                        pieces[number].at[entry, side],
                        to_ref.at[chunk, pl.ds(row, rows)],
                        arrived.at[len(made)],
                    )
                )
        return made

    def assembled(self, halves):
        rows = []
        for array in halves:
            array = array.reshape(self.dps, self.heads, 2, self.rows, self.width)
            rows.append(array.transpose(1, 0, 3, 2, 4).reshape(-1, 2, self.width))
        rows = jnp.concatenate(rows, 0).reshape(self.chunks, self.size, 2, self.width)
        return [rows.transpose(0, 2, 1, 3)]

    def taken_apart(self, piece):
        rows = piece.transpose(0, 2, 1, 3).reshape(2, self.heads, self.dps, self.rows, 2, -1)
        rows = rows.transpose(0, 2, 1, 4, 3, 5)
        return [half.reshape(self.blocks, 2, self.rows, self.width) for half in rows]


def head_groups(ref, flip):
    value = ref[...]
    half = value.shape[1] // 2
    low, high = value[:, :half], value[:, half:]
    if flip & 2:
        low, high = high, low
    if flip & 1:
        low, high = pltpu.roll(low, half // 2, 1), pltpu.roll(high, half // 2, 1)
    return jnp.concatenate([low, high], 1)


def memory_queries(read, attn_ref, vec_ref):
    low = read.astype(LOW)
    queries = (nt(low, attn_ref[0]) + vector(vec_ref, "b_query")).astype(LOW)
    keys = nt(low, attn_ref[1]).astype(LOW)
    values = (nt(low, attn_ref[2]) + vector(vec_ref, "b_value")).astype(LOW)
    return queries, keys, values


def memory_attention(heads, memory_rows, queries, keys, values, key_low, value_low):
    rows, width = heads * PAD, queries.shape[1]
    mask = head_mask(rows, width, heads)
    real_key = lax.broadcasted_iota(jnp.int32, (rows, PAD), 1) < memory_rows
    spread = by_head(queries, mask, heads)
    scores = nt(spread, key_low) * SCALE
    scores_mem = jnp.where(real_key, nt(spread, keys) * SCALE, NEGATIVE)
    top = jnp.maximum(jnp.max(scores, -1, keepdims=True), jnp.max(scores_mem, -1, keepdims=True))
    raised = jnp.exp(scores - top)
    raised_mem = jnp.exp(scores_mem - top)
    total = jnp.sum(raised, -1, keepdims=True) + 2.0 * jnp.sum(raised_mem, -1, keepdims=True)
    soft = raised / total
    soft_mem = raised_mem / total
    mixed = nn(soft.astype(LOW), value_low) + 2.0 * nn(soft_mem.astype(LOW), values)
    return own_head(mixed, mask, heads).astype(LOW), soft, soft_mem


def memory_norm(result, memory_rows):
    real_row = lax.broadcasted_iota(jnp.int32, result.shape, 0) < memory_rows
    square = jnp.sum(jnp.where(real_row, result * result, 0.0), axis=(0, 1), keepdims=True)
    return jnp.sqrt(square / (memory_rows * result.shape[1]))


def chain_forward(
    layout,
    heads,
    memory_rows,
    reset_ref,
    init_ref,
    bias_ref,
    vec_ref,
    attn_from,
    key_from,
    value_from,
    *refs,
):
    count = len(layout.pieces())
    pieces, refs = refs[:count], refs[count:]
    (
        read_ref,
        qkv_ref,
        soft_ref,
        soft_mem_ref,
        attended_ref,
        z_attn_ref,
        hidden_ref,
        pre_ref,
        z_ffn_ref,
        norm_ref,
        attn_ref,
        key_ref,
        value_ref,
        attn_arrived,
        key_arrived,
        value_arrived,
        up_ref,
        down_ref,
        arrived,
    ) = refs
    last = key_ref.shape[0]
    attn_loads = [
        pltpu.make_async_copy(attn_from.at[i], attn_ref.at[i], attn_arrived.at[i])
        for i in range(4)
    ]

    def token_loads(s):
        return [
            pltpu.make_async_copy(key_from.at[s], key_ref.at[s], key_arrived.at[s]),
            pltpu.make_async_copy(value_from.at[s], value_ref.at[s], value_arrived.at[s]),
        ]

    loads = layout.loads(pieces, up_ref, down_ref, arrived)
    for load in attn_loads[:3] + token_loads(0) + attn_loads[3:] + loads:
        load.start()
    for s in range(1, last):
        for load in token_loads(s):
            load.start()
    chunks, size, _ = up_ref.shape
    norm_ref[...] = jnp.zeros_like(norm_ref)
    for load in attn_loads[:3]:
        load.wait()

    def enter(s, carried):
        fresh = (reset_ref[0, s] > 0) | (s == 0)
        read = jnp.where(fresh, init_ref[...], carried)
        read_ref[s] = read
        queries, keys, values = memory_queries(read, attn_ref, vec_ref)
        qkv_ref[s, 0] = queries
        qkv_ref[s, 1] = keys
        qkv_ref[s, 2] = values
        return read, queries, keys, values

    def step(s, carried):
        read, queries, keys, values = enter(s, carried)
        for load in token_loads(s):
            load.wait()
        attended, soft, soft_mem = memory_attention(
            heads, memory_rows, queries, keys, values, key_ref[s], value_ref[s]
        )
        soft_ref[s] = soft
        soft_mem_ref[s] = soft_mem
        attended_ref[s] = attended

        @pl.when(s == 0)
        def _():
            attn_loads[3].wait()

        z_attn = read + nn(attended, attn_ref[3]) + vector(vec_ref, "b_out")
        z_attn_ref[s] = z_attn
        normed, _ = norm_parts(z_attn)
        hidden = normed * vector(vec_ref, "gain_attn") + vector(vec_ref, "shift_attn")
        hidden_low = hidden.astype(LOW)
        hidden_ref[s] = hidden_low
        z_ffn = hidden + vector(vec_ref, "b_down")

        @pl.when(s == 0)
        def _():
            for load in loads:
                load.wait()

        for i in range(chunks):
            pre = nt(hidden_low, up_ref[i]) + bias_ref[i]
            pre_ref[s, :, i * size : (i + 1) * size] = pre
            z_ffn = z_ffn + nn(gelu(pre).astype(LOW), down_ref[i])
        z_ffn_ref[s] = z_ffn
        normed, _ = norm_parts(z_ffn)
        result = normed * vector(vec_ref, "gain_ffn") + vector(vec_ref, "shift_ffn")
        lane = lax.broadcasted_iota(jnp.int32, norm_ref.shape, 1)
        norm_ref[...] = jnp.where(lane == s, memory_norm(result, memory_rows), norm_ref[...])
        return result

    carried = lax.fori_loop(0, last, step, init_ref[...])
    enter(last, carried)


def last_norm(heads, memory_rows, bias_ref, vec_ref, read, qkv, key, value, weights):
    out_w, up_ref, down_ref = weights
    attended, _, _ = memory_attention(heads, memory_rows, *qkv, key, value)
    z_attn = read + nn(attended, out_w) + vector(vec_ref, "b_out")
    normed, _ = norm_parts(z_attn)
    hidden = normed * vector(vec_ref, "gain_attn") + vector(vec_ref, "shift_attn")
    hidden_low = hidden.astype(LOW)
    z_ffn = hidden + vector(vec_ref, "b_down")
    for i in range(up_ref.shape[0]):
        pre = nt(hidden_low, up_ref[i]) + bias_ref[i]
        z_ffn = z_ffn + nn(gelu(pre).astype(LOW), down_ref[i])
    normed, _ = norm_parts(z_ffn)
    result = normed * vector(vec_ref, "gain_ffn") + vector(vec_ref, "shift_ffn")
    return memory_norm(result, memory_rows)


def chain_backward(
    layout,
    head_order,
    heads,
    memory_rows,
    reset_ref,
    place_ref,
    bias_ref,
    read_ref,
    norms_ref,
    vec_ref,
    qkv_ref,
    soft_ref,
    soft_mem_ref,
    z_attn_ref,
    pre_ref,
    z_ffn_ref,
    hidden_ref,
    *refs,
):
    segments, _, _, width = qkv_ref.shape
    part_ref, *refs = refs
    attn_from, key_from, value_from, *refs = refs
    count = len(layout.pieces())
    pieces, refs = refs[:count], refs[count:]
    (
        score_ref,
        attended_ref,
        mixed_ref,
        small_ref,
        factor_ref,
        bias_grad_ref,
        vec_grad_ref,
        init_grad_ref,
        norm_ref,
        ffn_ref,
        pre_grad_ref,
        token_part_ref,
        attn_ref,
        key_ref,
        value_ref,
        attn_arrived,
        key_arrived,
        value_arrived,
        up_ref,
        down_ref,
        arrived,
    ) = refs
    attn_loads = [
        pltpu.make_async_copy(attn_from.at[i], attn_ref.at[i], attn_arrived.at[i])
        for i in range(4)
    ]

    def token_loads(s):
        return [
            pltpu.make_async_copy(key_from.at[s], key_ref.at[s], key_arrived.at[s]),
            pltpu.make_async_copy(value_from.at[s], value_ref.at[s], value_arrived.at[s]),
        ]

    loads = layout.loads(pieces, up_ref, down_ref, arrived)
    for load in attn_loads[1:3] + loads + attn_loads[3:] + attn_loads[:1]:
        load.start()
    for s in range(segments - 1, -1, -1):
        for load in token_loads(s):
            load.start()
    for j in range(segments):
        token_part_ref[j] = head_groups(part_ref.at[position(j, head_order)], j)
    me = place_ref[1]
    rows = heads * PAD
    mask = head_mask(rows, width, heads)
    chunks, size, _ = up_ref.shape
    half = chunks * size // 2
    vec_grad_ref[...] = jnp.zeros_like(vec_grad_ref)
    bias_grad_ref[...] = jnp.zeros_like(bias_grad_ref)

    def add_vector(name, grad):
        i = VECTORS.index(name)
        vec_grad_ref[i : i + 1, :] += jnp.sum(grad, 0, keepdims=True)

    last = segments - 1
    for load in attn_loads[1:3]:
        load.wait()
    grad_key = token_part_ref[last ^ me, :PAD].astype(LOW)
    grad_value = token_part_ref[last ^ me, PAD:].astype(LOW)
    small_ref[last, 0] = jnp.zeros((PAD, width), LOW)
    small_ref[last, 1] = grad_key
    small_ref[last, 2] = grad_value
    add_vector("b_value", 2.0 * grad_value.astype(FULL))
    grad_read = 2.0 * (nn(grad_key, attn_ref[1]) + nn(grad_value, attn_ref[2]))
    stop = reset_ref[0, last] > 0
    init_grad_ref[...] = jnp.where(stop, grad_read, 0.0)
    grad_write = jnp.where(stop, 0.0, grad_read)

    for load in [attn_loads[0], attn_loads[3], *loads, *token_loads(last)]:
        load.wait()
    norm = last_norm(
        heads,
        memory_rows,
        bias_ref,
        vec_ref,
        read_ref[last],
        [qkv_ref[last, i] for i in range(3)],
        key_ref[last],
        value_ref[last],
        (attn_ref[3], up_ref, down_ref),
    )
    lane = lax.broadcasted_iota(jnp.int32, norm_ref.shape, 1)
    norm_ref[...] = jnp.where(lane == last, norm, norms_ref[...])

    def step(back, grad_write):
        s = segments - 2 - back
        normed, inverse = norm_parts(z_ffn_ref[s])
        add_vector("gain_ffn", grad_write * normed)
        add_vector("shift_ffn", grad_write)
        grad_sum = norm_pull(normed, inverse, grad_write * vector(vec_ref, "gain_ffn"))
        grad_low = grad_sum.astype(LOW)
        ffn_ref[s] = grad_low
        add_vector("b_down", grad_low.astype(FULL))
        grad_hidden = grad_sum

        for i in range(chunks):
            part = slice(i * size, (i + 1) * size)
            grad_act = nt(grad_low, down_ref[i])
            grad_pre = (grad_act * gelu_slope(pre_ref[s, :, part])).astype(LOW)
            pre_grad_ref[s, :, part] = grad_pre
            bias_grad_ref[i] += jnp.sum(grad_pre.astype(FULL), 0, keepdims=True)
            grad_hidden = grad_hidden + nn(grad_pre, up_ref[i])
        normed, inverse = norm_parts(z_attn_ref[s])
        add_vector("gain_attn", grad_hidden * normed)
        add_vector("shift_attn", grad_hidden)
        grad_attn = norm_pull(normed, inverse, grad_hidden * vector(vec_ref, "gain_attn"))
        add_vector("b_out", grad_attn)
        grad_mixed = grad_attn.astype(LOW)
        mixed_ref[s] = grad_mixed

        for load in token_loads(s):
            load.wait()
        grad_attended = nt(grad_mixed, attn_ref[3]).astype(LOW)
        attended_ref[s] = grad_attended
        queries, keys, values = qkv_ref[s, 0], qkv_ref[s, 1], qkv_ref[s, 2]
        spread = by_head(grad_attended, mask, heads)
        soft, soft_mem = soft_ref[s], soft_mem_ref[s]
        pull = nt(spread, value_ref[s])
        pull_mem = nt(spread, values)
        inner = jnp.sum(soft * pull, -1, keepdims=True) + 2.0 * jnp.sum(
            soft_mem * pull_mem, -1, keepdims=True
        )
        grad_score = (soft * (pull - inner)).astype(LOW)
        grad_score_mem = (soft_mem * (pull_mem - inner)).astype(LOW)
        score_ref[s] = grad_score
        grad_query = nn(grad_score, key_ref[s]) + 2.0 * nn(grad_score_mem, keys)
        grad_query = (SCALE * own_head(grad_query, mask, heads)).astype(LOW)
        grad_key = SCALE * tn(grad_score_mem, by_head(queries, mask, heads))
        grad_key = (token_part_ref[s ^ me, :PAD] + grad_key).astype(LOW)
        grad_value = tn(soft_mem.astype(LOW), spread)
        grad_value = (token_part_ref[s ^ me, PAD:] + grad_value).astype(LOW)
        small_ref[s, 0] = grad_query
        small_ref[s, 1] = grad_key
        small_ref[s, 2] = grad_value
        add_vector("b_query", grad_query.astype(FULL))
        add_vector("b_value", 2.0 * grad_value.astype(FULL))
        grad_read = 2.0 * (nn(grad_key, attn_ref[1]) + nn(grad_value, attn_ref[2]))
        grad_read = grad_read + nn(grad_query, attn_ref[0]) + grad_attn
        stop = (reset_ref[0, s] > 0) | (s == 0)
        init_grad_ref[...] += jnp.where(stop, grad_read, 0.0)
        return jnp.where(stop, 0.0, grad_read)

    lax.fori_loop(0, segments - 1, step, grad_write)

    packed, wide = factor_ref.shape[1], (segments - 1) * PAD
    row = lax.broadcasted_iota(jnp.int32, (packed, wide), 0)
    source = lax.broadcasted_iota(jnp.int32, (packed, wide), 1)
    take = (source // PAD == row // memory_rows) & (source % PAD == row % memory_rows)
    take = jnp.where(take, 1.0, 0.0).astype(LOW)
    mine = width // 2

    def own_units(ref):
        first = ref[: segments - 1, :, :mine].reshape(wide, mine)
        second = ref[: segments - 1, :, half : half + mine].reshape(wide, mine)
        return jnp.concatenate([first, second], 1)

    acts = gelu(own_units(pre_ref)).astype(LOW)
    factor_ref[0] = nn(take, hidden_ref[: segments - 1].reshape(wide, width)).astype(LOW)
    factor_ref[1] = nn(take, ffn_ref[...].reshape(wide, width)).astype(LOW)
    factor_ref[2] = nn(take, acts).astype(LOW)
    factor_ref[3] = nn(take, own_units(pre_grad_ref)).astype(LOW)


def whole_call(body, scalars, operands, outside, shapes, flops, scratch=(), outside_shapes=()):
    in_vmem = pl.BlockSpec(memory_space=pltpu.VMEM)
    in_smem = pl.BlockSpec(memory_space=pltpu.SMEM)
    anywhere = pl.BlockSpec(memory_space=pl.ANY)
    size = sum(a.size * a.dtype.itemsize for a in (*operands, *outside, *shapes))
    return pl.pallas_call(
        body,
        out_shape=(*shapes, *outside_shapes),
        in_specs=[in_smem] * len(scalars) + [in_vmem] * len(operands) + [anywhere] * len(outside),
        out_specs=[in_vmem] * len(shapes) + [anywhere] * len(outside_shapes),
        scratch_shapes=scratch,
        compiler_params=pltpu.CompilerParams(vmem_limit_bytes=VMEM_LIMIT),
        cost_estimate=pl.CostEstimate(flops=flops // 1000, bytes_accessed=size // 1000, transcendentals=0),
    )(*scalars, *operands, *outside)


def unit_owner(column, order, stages, head_order, layout, index):
    head = position(partner(index, stages, "head"), head_order)
    at = head * layout.dps + position(partner(index, stages, "dp"), order)
    return column // layout.rows == at


def project(
    layout,
    stages,
    order_a,
    order_b,
    head_order,
    place_ref,
    token_ref,
    attn_ref,
    bias_ref,
    other_ref,
    key_ref,
    value_ref,
    x_ref,
    q_ref,
    k_ref,
    v_ref,
    vec_ref,
    bias_in_ref,
):
    devices, entries = bias_ref.shape
    width, rows = layout.width, layout.rows
    here = width // layout.heads
    packets = bias_ref[...].astype(FULL)

    def laid_out(first, count, period, owner):
        entry = lax.broadcasted_iota(jnp.int32, (entries, count), 0)
        column = lax.broadcasted_iota(jnp.int32, (entries, count), 1)
        pick = jnp.where(entry == first + column % period, 1.0, 0.0).astype(LOW)
        index = lax.broadcasted_iota(jnp.int32, (devices, count), 0)
        column = lax.broadcasted_iota(jnp.int32, (devices, count), 1)
        chosen = jnp.where(owner(column, index), nn(packets.astype(LOW), pick), 0.0)
        return jnp.sum(chosen, 0, keepdims=True)

    def of_head(column, index):
        head = partner(index, stages, "head")
        return (partner(index, stages, "dp") == 0) & (head == column // here)

    vec_ref[0:1, :] = laid_out(0, width, here, of_head)
    vec_ref[1:2, :] = laid_out(here, width, here, of_head)
    vec_ref[2:, :] = other_ref[...].astype(FULL)
    for half, order in enumerate((order_a, order_b)):
        owner = functools.partial(
            unit_owner, order=order, stages=stages, head_order=head_order, layout=layout
        )
        row = laid_out(
            2 * here + half * rows,
            layout.blocks * rows,
            rows,
            lambda column, index: owner(column, index=index),
        )
        per = layout.chunks // 2
        for i in range(per):
            bias_in_ref[half * per + i] = row[:, i * layout.size : (i + 1) * layout.size]

    for s in range(token_ref.shape[0]):
        x = token_ref[s]
        key_ref[s] = nt(x, attn_ref[1]).astype(LOW)
        value_ref[s] = (nt(x, attn_ref[2]) + vector(vec_ref, "b_value")).astype(LOW)
    own = place_ref[1]
    x = token_ref[own]
    x_ref[...] = x
    q_ref[...] = (nt(x, attn_ref[0]) + vector(vec_ref, "b_query")).astype(LOW)
    k_ref[...] = key_ref[own]
    v_ref[...] = value_ref[own]


SUMS = ("b_out", "gain_attn", "shift_attn", "b_down", "gain_ffn", "shift_ffn")


def token_layer(layout, x_ref, attended_ref, cot_ref, bias_ref, vec_ref, attn_ref, *refs):
    count = len(layout.pieces())
    pieces, refs = refs[:count], refs[count:]
    (
        result_ref,
        skip_ref,
        mixed_ref,
        grad_attended_ref,
        bias_sum_ref,
        sum_ref,
        *grad_refs,
        out_w_ref,
        out_arrived,
        up_ref,
        down_ref,
        arrived,
        z_attn_ref,
        hidden_ref,
        low_ref,
        total_ref,
        pre_ref,
        act_ref,
        stage_ref,
        sent,
    ) = refs
    out_load = pltpu.make_async_copy(attn_ref.at[3], out_w_ref, out_arrived)
    out_load.start()
    loads = layout.loads(pieces, up_ref, down_ref, arrived)
    for load in loads:
        load.start()
    chunks = layout.chunks
    out_load.wait()
    sum_ref[...] = jnp.zeros_like(sum_ref)

    def add_vector(name, grad):
        i = SUMS.index(name)
        sum_ref[i : i + 1, :] += jnp.sum(grad, 0, keepdims=True)

    z_attn = x_ref[...].astype(FULL) + nn(attended_ref[...], out_w_ref[...])
    z_attn = z_attn + vector(vec_ref, "b_out")
    z_attn_ref[...] = z_attn
    normed, _ = norm_parts(z_attn)
    hidden = normed * vector(vec_ref, "gain_attn") + vector(vec_ref, "shift_attn")
    hidden_ref[...] = hidden.astype(LOW)
    total_ref[...] = hidden + vector(vec_ref, "b_down")
    for load in loads:
        load.wait()

    def forward(i, nothing):
        pre = nt(hidden_ref[...], up_ref[i]) + bias_ref[i]
        pre_ref[i] = pre
        act = gelu(pre).astype(LOW)
        act_ref[i] = act
        total_ref[...] += nn(act, down_ref[i])
        return nothing

    lax.fori_loop(0, chunks, forward, 0)
    normed, inverse = norm_parts(total_ref[...])
    result = normed * vector(vec_ref, "gain_ffn") + vector(vec_ref, "shift_ffn")
    result_ref[...] = result.astype(LOW)
    grad = cot_ref[...].astype(FULL)
    add_vector("gain_ffn", grad * normed)
    add_vector("shift_ffn", grad)
    grad = norm_pull(normed, inverse, grad * vector(vec_ref, "gain_ffn"))
    total_ref[...] = grad
    low_ref[...] = grad.astype(LOW)
    add_vector("b_down", low_ref[...].astype(FULL))

    copies = list(layout.copies())
    spans = [first for first, _ in layout.pieces()]
    stores = []
    for i in range(chunks):
        grad_pre = (nt(low_ref[...], down_ref[i]) * gelu_slope(pre_ref[i])).astype(LOW)
        bias_sum_ref[i] = jnp.sum(grad_pre.astype(FULL), 0, keepdims=True)
        total_ref[...] += nn(grad_pre, up_ref[i])
        slot = i % 2
        if i > 1:
            for store in stores[i - 2]:
                store.wait()
        stage_ref[slot, 0] = tn(grad_pre, hidden_ref[...]).astype(LOW)
        stage_ref[slot, 1] = tn(act_ref[i], low_ref[...]).astype(LOW)
        stores.append([])
        for number, entry, chunk, row, rows in copies:
            if chunk != i:
                continue
            for side in range(2):
                to_ref = grad_refs[number // (len(spans) // len(grad_refs))]
                entry_at = spans[number] - spans[number - number % (len(spans) // len(grad_refs))]
                store = pltpu.make_async_copy(
                    stage_ref.at[slot, side, pl.ds(row, rows)],
                    to_ref.at[entry_at + entry, side],
                    sent.at[i, len(stores[i])],
                )
                store.start()
                stores[i].append(store)

    grad_hidden = total_ref[...]
    normed, inverse = norm_parts(z_attn_ref[...])
    add_vector("gain_attn", grad_hidden * normed)
    add_vector("shift_attn", grad_hidden)
    grad = norm_pull(normed, inverse, grad_hidden * vector(vec_ref, "gain_attn"))
    add_vector("b_out", grad)
    skip_ref[...] = grad
    mixed_ref[...] = grad.astype(LOW)
    grad_attended_ref[...] = nt(mixed_ref[...], out_w_ref[...]).astype(LOW)
    for i in range(max(chunks - 2, 0), chunks):
        for store in stores[i]:
            store.wait()


def part_rows(keep_ref, send_ref, first, columns, grad, place_ref, order, count):
    rows = grad.shape[0] // count
    for c in range(count):
        block = grad[c * rows : (c + 1) * rows].astype(keep_ref.dtype)
        at = position(place_ref[0] ^ c, order)

        @pl.when(at < count // 2)
        def _():
            keep_ref[at, first : first + rows, columns] = block

        @pl.when(at >= count // 2)
        def _():
            send_ref[at - count // 2, first : first + rows, columns] = block


SUM_ROWS = 32


def pack_sums(
    layout, order_a, order_b, head_order, heads_here, memory_rows, place_ref, groups, rows, halves
):
    count, width = rows.shape
    dps = layout.dps
    devices = dps * groups
    here, part = width // layout.heads, width // (dps * layout.heads)
    head_dim = here // heads_here
    head_part = head_dim // dps

    def partners(index):
        head = index % groups
        dp = 0
        for k, bit in enumerate(order_a):
            dp = dp + ((index // groups >> k) & 1) * bit
        return dp, head

    shape = (devices, count, width)
    index, row, column = (lax.broadcasted_iota(jnp.int32, shape, i) for i in range(3))
    dp_flip, head_flip = partners(index)
    dp, head = place_ref[0] ^ dp_flip, place_ref[1] ^ head_flip
    plain = len(SUMS) + memory_rows
    of_device = column // part == dp * layout.heads + head
    of_head = (column // here == head_flip) & (column % head_dim // head_part == dp)
    chosen = ((row < plain) & of_device) | ((row >= plain) & of_head)
    chosen = jnp.where(chosen, jnp.broadcast_to(rows[None], shape), 0.0)
    chosen = chosen.reshape(devices * count, width).astype(LOW)
    source = lax.broadcasted_iota(jnp.int32, (width, part), 0)
    target = lax.broadcasted_iota(jnp.int32, (width, part), 1)
    plain_fold = jnp.where(source % part == target, 1.0, 0.0).astype(LOW)
    head_column = source // head_dim % heads_here * head_part + source % head_part
    head_fold = jnp.where(head_column == target, 1.0, 0.0).astype(LOW)
    row = lax.broadcasted_iota(jnp.int32, (devices, count, part), 1)
    folded = jnp.where(
        row < plain,
        nn(chosen, plain_fold).reshape(devices, count, part),
        nn(chosen, head_fold).reshape(devices, count, part),
    )
    unit_rows = []
    span = halves[0].shape[1]
    index, column = (lax.broadcasted_iota(jnp.int32, (devices, span), i) for i in range(2))
    source = lax.broadcasted_iota(jnp.int32, (span, layout.rows), 0)
    target = lax.broadcasted_iota(jnp.int32, (span, layout.rows), 1)
    fold = jnp.where(source % layout.rows == target, 1.0, 0.0).astype(LOW)
    for order, half in zip((order_a, order_b), halves):
        dp_flip, head_flip = partners(index)
        at = position(head_flip, head_order) * dps + position(dp_flip, order)
        chosen = jnp.where(column // layout.rows == at, half, 0.0)
        unit_rows.append(nn(chosen.astype(LOW), fold))
    return folded, unit_rows


def put_sums(ref, entry, first_row, first_column, packed, index, memory_rows):
    folded, unit_rows = packed
    plain = len(SUMS) + memory_rows
    part, block = folded.shape[2], unit_rows[0].shape[1]
    columns = slice(first_column, first_column + part)
    ref[entry, first_row : first_row + plain + 2, columns] = folded[index, : plain + 2].astype(LOW)
    columns = slice(first_column, first_column + block)
    for half, rows in enumerate(unit_rows):
        row = first_row + plain + 2 + half
        ref[entry, row : row + 1, columns] = rows[index : index + 1].astype(LOW)


def half_rows(ref, layout):
    per = layout.chunks // 2
    return [
        jnp.concatenate([ref[half * per + i] for i in range(per)], 1) for half in range(2)
    ]


def value_grads(
    order,
    count,
    place_ref,
    x_ref,
    mixed_ref,
    attended_ref,
    dv0_ref,
    dv1_ref,
    skip_ref,
    attn_from,
    keep_ref,
    send_ref,
    grad_x_ref,
    sum_ref,
    attn_ref,
    arrived,
):
    load = pltpu.make_async_copy(attn_from.at[2], attn_ref, arrived)
    load.start()
    x, low, high = x_ref[...], dv0_ref[...], dv1_ref[...]
    half = low.shape[1]
    share = x.shape[1] // count
    every = slice(None)
    both = jnp.concatenate([tn(x, low), tn(x, high)], 1)
    part_rows(keep_ref, send_ref, 0, every, both, place_ref, order, count)
    both = tn(mixed_ref[...], attended_ref[...])
    part_rows(keep_ref, send_ref, share, every, both, place_ref, order, count)
    sum_ref[:, :half] = jnp.sum(low.astype(FULL), 0, keepdims=True)
    sum_ref[:, half:] = jnp.sum(high.astype(FULL), 0, keepdims=True)
    load.wait()
    grad_x_ref[...] = skip_ref[...] + nn(low, attn_ref[:half]) + nn(high, attn_ref[half:])


def query_key_grads(
    layout,
    order_a,
    order_b,
    head_order,
    heads_here,
    memory_rows,
    place_ref,
    x_ref,
    dq0_ref,
    dq1_ref,
    dk0_ref,
    dk1_ref,
    part_ref,
    value_sum_ref,
    layer_sum_ref,
    bias_sum_ref,
    attn_from,
    keep_ref,
    send_ref,
    grad_x_ref,
    rows_ref,
    attn_ref,
    arrived,
):
    loads = [
        pltpu.make_async_copy(attn_from.at[i], attn_ref.at[i], arrived.at[i]) for i in range(2)
    ]
    for load in loads:
        load.start()
    count = layout.dps
    x = x_ref[...]
    half = dq0_ref.shape[1]
    share = x.shape[1] // count
    pairs = [(dq0_ref[...], dq1_ref[...]), (dk0_ref[...], dk1_ref[...])]
    for m, (low, high) in enumerate(pairs):
        both = jnp.concatenate([tn(x, low), tn(x, high)], 1)
        part_rows(keep_ref, send_ref, m * share, slice(None), both, place_ref, order_a, count)
    plain = len(SUMS) + memory_rows
    rows_ref[...] = jnp.zeros_like(rows_ref)
    rows_ref[: len(SUMS), :] = layer_sum_ref[: len(SUMS), :]
    for at, array in zip((0, half), pairs[0]):
        rows_ref[plain : plain + 1, at : at + half] = jnp.sum(array.astype(FULL), 0, keepdims=True)
    rows_ref[plain + 1 : plain + 2, :] = value_sum_ref[...]
    packed = pack_sums(
        layout,
        order_a,
        order_b,
        head_order,
        heads_here,
        memory_rows,
        place_ref,
        layout.heads,
        rows_ref[...],
        half_rows(bias_sum_ref, layout),
    )
    here = x.shape[1] // layout.heads
    for at in range(count):
        ref = keep_ref if at < count // 2 else send_ref
        entry = at % (count // 2)
        ref[entry, 2 * share :, :] = jnp.zeros((SUM_ROWS, x.shape[1]), LOW)
        for g in range(layout.heads):
            index = at * layout.heads + g
            put_sums(ref, entry, 2 * share, g * here, packed, index, memory_rows)
    total = part_ref[...]
    for m, (low, high) in enumerate(pairs):
        loads[m].wait()
        total = total + nn(low, attn_ref[m, :half]) + nn(high, attn_ref[m, half:])
    grad_x_ref[...] = total.astype(LOW)


def own_grads(
    layout,
    order_a,
    order_b,
    head_order,
    heads,
    heads_here,
    memory_rows,
    place_ref,
    score_ref,
    soft_ref,
    qkv_ref,
    attended_grad_ref,
    mixed_ref,
    attended_ref,
    small_ref,
    read_ref,
    token_ref,
    bias_grad_ref,
    vec_grad_ref,
    init_grad_ref,
    keep_ref,
    send_ref,
    rows_ref,
):
    count = layout.dps
    writes, rows, _ = score_ref.shape
    width = qkv_ref.shape[-1]
    here = width // heads * heads_here
    mine = heads_here * PAD
    mask = head_mask(rows, width, heads)[:mine]
    total = jnp.zeros((1, here), FULL)
    grads = [jnp.zeros((width, here), FULL) for _ in range(4)]
    for s in range(writes + 1):
        low = read_ref[s].astype(LOW)
        grads[1] = grads[1] + 2.0 * tn(low, small_ref[s, 1, :, :here])
        grads[2] = grads[2] + 2.0 * tn(low, small_ref[s, 2, :, :here])
        if s == writes:
            break
        grads[0] = grads[0] + tn(low, small_ref[s, 0, :, :here])
        grads[3] = grads[3] + tn(mixed_ref[s], attended_ref[s, :, :here])
        spread = by_head(qkv_ref[s, 0], mask, heads_here)[:, :here]
        pulled = by_head(attended_grad_ref[s], mask, heads_here)[:, :here]
        dk = (SCALE * tn(score_ref[s, :mine], spread)).astype(LOW)
        dv = tn(soft_ref[s, :mine].astype(LOW), pulled).astype(LOW)
        grads[1] = grads[1] + tn(token_ref[s], dk)
        grads[2] = grads[2] + tn(token_ref[s], dv)
        total = total + jnp.sum(dv.astype(FULL), 0, keepdims=True)
    both = jnp.concatenate(grads, 1)
    part_rows(keep_ref, send_ref, 0, slice(None), both, place_ref, order_a, count)
    rows_ref[...] = jnp.zeros_like(rows_ref)
    for i, name in enumerate(SUMS):
        at = VECTORS.index(name)
        rows_ref[i : i + 1, :] = vec_grad_ref[at : at + 1, :]
    for i in range(memory_rows):
        at = len(SUMS) + i
        rows_ref[at : at + 1, :] = init_grad_ref[i : i + 1, :]
    at = len(SUMS) + memory_rows
    rows_ref[at : at + 2, :] = vec_grad_ref[0:2, :]
    rows_ref[at + 1 : at + 2, :here] += total
    packed = pack_sums(
        layout,
        order_a,
        order_b,
        head_order,
        heads_here,
        memory_rows,
        place_ref,
        1,
        rows_ref[...],
        half_rows(bias_grad_ref, layout),
    )
    share = width // count
    for at in range(count):
        ref = keep_ref if at < count // 2 else send_ref
        entry = at % (count // 2)
        ref[entry, share:, :] = jnp.zeros((SUM_ROWS, width), LOW)
        put_sums(ref, entry, share, 0, packed, at, memory_rows)


def write_rows(
    heads,
    quarter,
    place_ref,
    score_ref,
    soft_ref,
    qkv_ref,
    attended_grad_ref,
    moved_ref,
    attn_from,
    grad_token_ref,
    attn_ref,
    arrived,
):
    writes, rows, _ = score_ref.shape
    loads = [
        pltpu.make_async_copy(attn_from.at[i + 1], attn_ref.at[i], arrived.at[i])
        for i in range(2)
    ]
    for load in loads:
        load.start()
    mask = head_mask(rows, qkv_ref.shape[-1], heads)
    at = pl.multiple_of(place_ref[1] * quarter, quarter)
    for load in loads:
        load.wait()
    for s in range(writes):
        spread = by_head(qkv_ref[s, 0], mask, heads)
        pulled = by_head(attended_grad_ref[s], mask, heads)
        score_here = score_ref[s, :, pl.ds(at, quarter)]
        soft_here = soft_ref[s, :, pl.ds(at, quarter)].astype(LOW)
        dk = (SCALE * tn(score_here, spread)).astype(LOW)
        dv = tn(soft_here, pulled).astype(LOW)
        extra = nn(dk, attn_ref[0]) + nn(dv, attn_ref[1])
        grad_token_ref[s] = moved_ref[s].astype(FULL) + extra
    grad_token_ref[writes] = moved_ref[writes].astype(FULL)


def finish(
    order_a,
    order_b,
    memory_rows,
    numbers,
    *refs,
):
    groups = []
    for number in numbers:
        groups.append(refs[:number])
        refs = refs[number:]
    factor_refs, *groups = groups

    def total_of(group, *at):
        total = group[0][(0, *at)].astype(FULL)
        for ref in group[1:]:
            total = total + ref[(0, *at)].astype(FULL)
        return total

    ffn_a, ffn_b, attn_terms, own_terms = groups
    (
    query_ref,
    key_ref,
    value_ref,
    b_query_ref,
    b_value_ref,
    out_ref,
    b_out_ref,
    gain_attn_ref,
    shift_attn_ref,
    up_ref,
    b_in_ref,
    down_ref,
    b_down_ref,
    gain_ffn_ref,
    shift_ffn_ref,
    init_ref,
    ) = refs
    factor = jnp.concatenate([ref[...] for ref in factor_refs], 0)
    count, _, rows, width = factor.shape
    block = width // 2 // count
    column = lax.broadcasted_iota(jnp.int32, (rows, width), 1)

    def own(j, i):
        first, second = position(j, order_a), position(j, order_b) + count
        keep = (column // block == first) | (column // block == second)
        return jnp.where(keep, factor[j, i], jnp.zeros((), LOW))

    units = []
    for side, left, right in ((0, 3, 0), (1, 2, 1)):
        chosen = jnp.concatenate([own(j, left) for j in range(count)], 0)
        others = jnp.concatenate([factor[j, right] for j in range(count)], 0)
        product = tn(chosen, others)
        halves = []
        for i in range(2):
            total = total_of((ffn_a, ffn_b)[i], side)
            for j in range(count):
                at = (i * count + j) * block
                total = total + product[at : at + block]
            halves.append(total)
        units.append(jnp.concatenate(halves, 0))
    up_ref[...] = units[0]
    down_ref[...] = units[1]
    attn, own_total = total_of(attn_terms), total_of(own_terms)
    here = attn.shape[-1] // 2
    share = own_total.shape[0] - SUM_ROWS
    totals = []
    for m in range(4):
        row, column = m % 2 * share, m // 2 * here
        from_tokens = attn[row : row + share, column : column + here]
        totals.append(from_tokens + own_total[:share, m * here : (m + 1) * here])
    query_ref[...] = totals[0]
    key_ref[...] = totals[1]
    value_ref[...] = totals[2]
    out_ref[...] = totals[3].T
    pack = attn[2 * share : 2 * share + SUM_ROWS, :here] + own_total[share:, :here]
    refs = {
        "b_out": b_out_ref,
        "gain_attn": gain_attn_ref,
        "shift_attn": shift_attn_ref,
        "b_down": b_down_ref,
        "gain_ffn": gain_ffn_ref,
        "shift_ffn": shift_ffn_ref,
    }
    part = init_ref.shape[1]
    for i, name in enumerate(SUMS):
        refs[name][...] = pack[i : i + 1, :part]
    at = len(SUMS) + memory_rows
    init_ref[...] = pack[len(SUMS) : at, :part]
    heads_here, head_part = b_query_ref.shape
    for i in range(heads_here):
        columns = slice(i * head_part, (i + 1) * head_part)
        b_query_ref[i : i + 1, :] = pack[at : at + 1, columns]
        b_value_ref[i : i + 1, :] = pack[at + 1 : at + 2, columns]
    b_in_ref[:, :block] = pack[at + 2 : at + 3, :block]
    b_in_ref[:, block:] = pack[at + 3 : at + 4, :block]


def columns_of(head, head_dim, array, factor=None):
    lane = lax.broadcasted_iota(jnp.int32, array.shape, 1) // head_dim
    if factor is not None:
        array = array * jnp.asarray(factor, array.dtype)
    return jnp.where(lane == head, array, jnp.zeros((), array.dtype))


def memory_scores(memory_rows, km, mine):
    scores = nt(km, mine)
    real_key = lax.broadcasted_iota(jnp.int32, scores.shape, 0) < memory_rows
    return jnp.where(real_key, scores, NEGATIVE)


def token_attention(head_dim, place_ref, row_ref, column_ref, q_ref, k_ref, v_ref, sum_ref, stat_ref):
    q, k, v = q_ref[...], k_ref[...], v_ref[...]
    allowed = column_ref[...] == row_ref[...]
    stat_ref[...] = jnp.zeros_like(stat_ref)
    for head in range(q.shape[1] // head_dim):
        scores = nt(k, columns_of(head, head_dim, q, SCALE))
        scores = jnp.where(allowed, scores, NEGATIVE)
        top = jnp.max(scores, 0, keepdims=True)
        raised = jnp.exp(scores - top)
        stat_ref[0, 2 * head : 2 * head + 1] = top
        stat_ref[0, 2 * head + 1 : 2 * head + 2] = jnp.sum(raised, 0, keepdims=True)
        rows = slice(head * head_dim, (head + 1) * head_dim)
        sum_ref[0, rows] = tn(v, raised.astype(LOW))[rows]


def with_memory(
    memory_rows, head_dim, place_ref, q_ref, qkv_ref, sum_ref, stat_ref, out_ref, log_ref
):
    q, km, vm = q_ref[...], qkv_ref[place_ref[1], 1], qkv_ref[place_ref[1], 2]
    log_ref[...] = jnp.zeros_like(log_ref)
    mixed = []
    for head in range(q.shape[1] // head_dim):
        scores = memory_scores(memory_rows, km, columns_of(head, head_dim, q, SCALE))
        top_before = stat_ref[0, 2 * head : 2 * head + 1]
        top = jnp.maximum(jnp.max(scores, 0, keepdims=True), top_before)
        raised = jnp.exp(scores - top)
        shrink = jnp.exp(top_before - top)
        total = stat_ref[0, 2 * head + 1 : 2 * head + 2] * shrink
        total = total + 2.0 * jnp.sum(raised, 0, keepdims=True)
        rows = slice(head * head_dim, (head + 1) * head_dim)
        both = sum_ref[0, rows] * shrink + 2.0 * tn(vm, raised.astype(LOW))[rows]
        mixed.append(both * (1.0 / total))
        log_ref[0, head : head + 1] = top + jnp.log(total)
    out_ref[...] = jnp.concatenate(mixed, 0).T.astype(LOW)


def token_attention_back(
    memory_rows,
    head_dim,
    place_ref,
    row_ref,
    column_ref,
    q_ref,
    k_ref,
    v_ref,
    qkv_ref,
    log_ref,
    grad_ref,
    dq_ref,
    dk_ref,
    dv_ref,
    dmem_ref,
):
    q, k, v, grad = (ref[...] for ref in (q_ref, k_ref, v_ref, grad_ref))
    km, vm = qkv_ref[place_ref[1], 1], qkv_ref[place_ref[1], 2]
    allowed = column_ref[...] == row_ref[...]
    lane = lax.broadcasted_iota(jnp.int32, q.shape, 1) // head_dim
    dq, dk, dv = (jnp.zeros(q.shape, FULL) for _ in range(3))
    dkm, dvm = (jnp.zeros(km.shape, FULL) for _ in range(2))
    for head in range(q.shape[1] // head_dim):
        mine = columns_of(head, head_dim, q, SCALE)
        mine_grad = columns_of(head, head_dim, grad)
        log_total = log_ref[0, head : head + 1]
        scores = jnp.where(allowed, nt(k, mine), NEGATIVE)
        soft = jnp.exp(scores - log_total)
        soft_mem = jnp.exp(memory_scores(memory_rows, km, mine) - log_total)
        pull, pull_mem = nt(v, mine_grad), nt(vm, mine_grad)
        inner = jnp.sum(soft * pull, 0, keepdims=True) + 2.0 * jnp.sum(
            soft_mem * pull_mem, 0, keepdims=True
        )
        score = (soft * (pull - inner)).astype(LOW)
        score_mem = (soft_mem * (pull_mem - inner)).astype(LOW)
        dq = jnp.where(lane == head, tn(score, k) + 2.0 * tn(score_mem, km), dq)
        dk = dk + nn(score, mine)
        dv = dv + nn(soft.astype(LOW), mine_grad)
        dkm = dkm + nn(score_mem, mine)
        dvm = dvm + nn(soft_mem.astype(LOW), mine_grad)
    dq_ref[...] = (SCALE * dq).astype(LOW)
    dk_ref[...] = dk.astype(LOW)
    dv_ref[...] = dv.astype(LOW)
    dmem_ref[:PAD] = dkm
    dmem_ref[PAD:] = dvm


def head_pairs(body, place, doc, operands, shapes, width, flops, steps, first=0):
    seg_len = operands[0].shape[0]

    def spec(array, first):
        if len(array.shape) == 4:
            return pl.BlockSpec((*array.shape[:3], width), lambda i: (0, 0, 0, i + first))
        if len(array.shape) == 3:
            return pl.BlockSpec((1, *array.shape[1:]), lambda i: (i + first, 0, 0))
        return pl.BlockSpec((array.shape[0], width), lambda i: (0, i + first))

    return pl.pallas_call(
        body,
        grid=(steps,),
        out_shape=shapes,
        in_specs=[pl.BlockSpec(memory_space=pltpu.SMEM)]
        + [pl.BlockSpec(a.shape, lambda i: (0, 0)) for a in doc]
        + [spec(a, first) for a in operands],
        out_specs=[spec(s, 0) for s in shapes],
        compiler_params=pltpu.CompilerParams(vmem_limit_bytes=VMEM_LIMIT),
        cost_estimate=pl.CostEstimate(
            flops=flops // 1000, bytes_accessed=seg_len, transcendentals=0
        ),
    )(place, *doc, *operands)


def on_device(
    tokens,
    doc_ids,
    reset,
    mem_init,
    w_query,
    w_key,
    w_value,
    b_query,
    b_value,
    w_out,
    b_out,
    gain_attn,
    shift_attn,
    w_in,
    b_in,
    w_down,
    b_down,
    gain_ffn,
    shift_ffn,
    cotangent,
):
    chains, segments, seg_len, width = tokens.shape
    dps, groups = lax.axis_size("dp"), lax.axis_size("head")
    assert chains == 1 and segments == groups
    memory_rows = mem_init.shape[0]
    heads_here, head_dim = b_query.shape
    heads = heads_here * groups
    here = heads_here * head_dim
    units = w_in.shape[1]
    half_units = units // 2
    quarter = seg_len // groups
    dp, head = lax.axis_index("dp"), lax.axis_index("head")
    place = jnp.stack([dp, head])
    bits = bits_of(dps)
    levels = len(bits)
    order_a = bits[1:] + bits[:1]
    order_b = bits[1:][::-1] + bits[:1]
    head_order = bits_of(groups)[::-1]
    head_stages = [("head", bit) for bit in head_order]
    stages_a = head_stages + [("dp", bit) for bit in order_a]
    stages_b = head_stages + [("dp", bit) for bit in order_b]
    layout = Units(dps, groups, half_units, width)
    landing = layout.scratch()
    shape = jax.ShapeDtypeStruct
    dp_stages = [("dp", bit) for bit in bits]
    bias_groups = (head_stages[:1], dp_stages[1:], head_stages[1:] + dp_stages[:1])
    bias_stages = [stage for group in bias_groups for stage in group]
    tokens, doc_ids, cotangent = tokens[0], doc_ids[0], cotangent[0]

    shard = jnp.concatenate([w_query.T, w_key.T, w_value.T, w_out], 0)
    share = shard.shape[0] // dps
    chunk = lax.dynamic_slice_in_dim(shard, dp * share, share, 0)[None]
    biases = jnp.concatenate([b_query.reshape(-1), b_value.reshape(-1), b_in])[None]
    up = w_in.T.reshape(2, half_units, width)
    down = w_down.reshape(2, half_units, width)
    halves = [jnp.stack([up[i], down[i]])[None] for i in range(2)]
    for i, stage in enumerate(head_stages):
        chunk = gather(chunk, [stage])
        if i:
            halves = [gather(half, [head_stages[i - 1]]) for half in halves]
        biases = gather(biases, bias_groups[i])
        chunk, biases, halves = lax.optimization_barrier((chunk, biases, halves))
    halves = [gather(half, head_stages[-1:]) for half in halves]
    biases = gather(biases, bias_groups[2])
    chunk = jnp.stack([chunk[position(j, head_order)] for j in range(1, groups)])
    parts = []

    def joined(part, have, bit):
        at = sum(1 for b in have if b > bit)
        mine = (dp // bit) % 2
        other = swap(part, "dp", bit)
        return jnp.where(mine == 1, jnp.stack([other, part], at), jnp.stack([part, other], at))

    for rows, order in ((slice(0, share // 2), order_a), (slice(share // 2, share), order_b)):
        part = chunk[:, rows]
        for i, bit in enumerate(order[:-1]):
            part = joined(part, order[:i], bit)
        parts.append(part)
    doc = lax.dynamic_index_in_dim(doc_ids, head, 0, False)
    doc_row, doc_column = doc[None, :], doc[:, None]
    init = jnp.pad(mem_init.astype(FULL), ((0, PAD - memory_rows), (0, 0)))
    vectors = jnp.concatenate([b_out, gain_attn, shift_attn, b_down, gain_ffn, shift_ffn])
    vectors = vectors.reshape(-1, width)
    halves, parts, biases, cotangent, doc_row, doc_column, init, vectors = (
        lax.optimization_barrier(
            (halves, parts, biases, cotangent, doc_row, doc_column, init, vectors)
        )
    )
    parts = [
        joined(part, order[:-1], order[-1]).reshape(dps, groups - 1, share // 2, width)
        for part, order in zip(parts, (order_a, order_b))
    ]
    others = jnp.concatenate(parts, 2).transpose(1, 0, 2, 3).reshape(groups - 1, 4, here, width)
    cotangent = lax.all_to_all(cotangent, "head", 0, 0, tiled=True).reshape(seg_len, width)
    w_attn = jnp.concatenate([shard.reshape(4, 1, here, width), others.transpose(1, 0, 2, 3)], 1)
    w_attn = w_attn.reshape(4, groups * here, width)
    halves = [
        gather(half, stages[len(head_stages) : -2])
        for half, stages in zip(halves, (stages_a, stages_b))
    ]
    keys, values, x, q, k, v, vectors, bias_in = whole_call(
        functools.partial(project, layout, bias_stages, order_a, order_b, head_order),
        (place,),
        (tokens, w_attn, biases, vectors),
        (),
        (shape(tokens.shape, LOW),) * 2
        + (shape((seg_len, width), LOW),) * 4
        + (shape((len(VECTORS), width), FULL), shape((layout.chunks, 1, layout.size), FULL)),
        6_000_000_000,
    )

    pair = 2 * head_dim
    partial = head_pairs(
        functools.partial(token_attention, head_dim),
        place,
        (doc_row, doc_column),
        (q, k, v),
        (shape((width // pair, pair, seg_len), FULL), shape((width // pair, 8, seg_len), FULL)),
        pair,
        8_000_000_000,
        width // pair,
    )
    halves = lax.optimization_barrier(halves)
    other_halves = [
        swap(half, *stages[-2]) for half, stages in zip(halves, (stages_a, stages_b))
    ]
    other_halves, partial, keys, cotangent = lax.optimization_barrier(
        (other_halves, partial, keys, cotangent)
    )
    pieces = []
    for half, other, stages in zip(halves, other_halves, (stages_a, stages_b)):
        pieces += [half, other, swap(half, *stages[-1]), swap(other, *stages[-1])]
    if layout.whole:
        pieces = layout.assembled([jnp.concatenate(pieces[i : i + 4], 0) for i in (0, 4)])

    ff = layout.chunks * layout.size
    writes = segments - 1
    rows_shape = lambda kind: shape((writes, PAD, width), kind)
    tokens_scratch = lambda count: (
        pltpu.VMEM((4, width, width), LOW),
        pltpu.VMEM((count, seg_len, width), LOW),
        pltpu.VMEM((count, seg_len, width), LOW),
        pltpu.SemaphoreType.DMA((4,)),
        pltpu.SemaphoreType.DMA((count,)),
        pltpu.SemaphoreType.DMA((count,)),
    )
    read, qkv, soft, soft_mem, attended_w, z_attn_w, hidden_w, pre_w, z_ffn_w, norms = whole_call(
        functools.partial(chain_forward, layout, heads, memory_rows),
        (reset,),
        (init, bias_in, vectors),
        (w_attn, keys, values, *pieces),
        (
            shape((segments, PAD, width), FULL),
            shape((segments, 3, PAD, width), LOW),
            shape((writes, heads * PAD, seg_len), FULL),
            shape((writes, heads * PAD, PAD), FULL),
            rows_shape(LOW),
            rows_shape(FULL),
            rows_shape(LOW),
            shape((writes, PAD, ff), FULL),
            rows_shape(FULL),
            shape((1, 128), FULL),
        ),
        20_000_000_000,
        tokens_scratch(writes) + landing,
    )

    attended, log_total = head_pairs(
        functools.partial(with_memory, memory_rows, head_dim),
        place,
        (),
        (q, qkv, *partial),
        (shape((seg_len, width), LOW), shape((width // pair, 8, seg_len), FULL)),
        pair,
        8_000_000_000,
        width // pair,
    )
    if layout.whole:
        grad_shapes = (shape((layout.chunks, 2, layout.size, width), LOW),)
    else:
        grad_shapes = (shape((layout.blocks // 2, 2, half_units, width), LOW),) * 4
    sides = 2 * max(layout.size // (layout.size if layout.whole else half_units), 1)
    result, grad_attn, grad_mixed, grad_attended, bias_sum, layer_sums, *ffn_grads = whole_call(
        functools.partial(token_layer, layout),
        (),
        (x, attended, cotangent, bias_in, vectors),
        (w_attn, *pieces),
        (
            shape((seg_len, width), LOW),
            shape((seg_len, width), FULL),
            shape((seg_len, width), LOW),
            shape((seg_len, width), LOW),
            shape((layout.chunks, 1, layout.size), FULL),
            shape((8, width), FULL),
        ),
        25_000_000_000,
        (pltpu.VMEM((width, width), LOW), pltpu.SemaphoreType.DMA(()))
        + landing
        + (
            pltpu.VMEM((seg_len, width), FULL),
            pltpu.VMEM((seg_len, width), LOW),
            pltpu.VMEM((seg_len, width), LOW),
            pltpu.VMEM((seg_len, width), FULL),
            pltpu.VMEM((layout.chunks, seg_len, layout.size), FULL),
            pltpu.VMEM((layout.chunks, seg_len, layout.size), LOW),
            pltpu.VMEM((2, 2, layout.size, width), LOW),
            pltpu.SemaphoreType.DMA((layout.chunks, sides)),
        ),
        grad_shapes,
    )
    if layout.whole:
        half_blocks = layout.blocks // 2
        ffn_grads = [
            part
            for half in layout.taken_apart(ffn_grads[0])
            for part in (half[:half_blocks], half[half_blocks:])
        ]

    back_a, back_b = stages_a[::-1], stages_b[::-1]

    def stages_of(level):
        return back_a[level], back_b[level]

    def attention_back(block, count):
        cut = width // 2
        return head_pairs(
            functools.partial(token_attention_back, memory_rows, head_dim),
            place,
            (doc_row, doc_column),
            (q, k, v, qkv, log_total, grad_attended),
            (shape((seg_len, cut), LOW),) * 3 + (shape((2 * PAD, cut), FULL),),
            pair,
            10_000_000_000,
            count,
            block * count,
        )

    blocks = width // pair // 2
    moving = [
        [keep, swap(send, *back[0])]
        for keep, send, back in zip(ffn_grads[::2], ffn_grads[1::2], (back_a, back_b))
    ]
    back_low = attention_back(0, blocks)
    back_low, moving, grad_attended, result = lax.optimization_barrier(
        (back_low, moving, grad_attended, result)
    )
    sends = parcels(moving)
    sends, grad_attended, result = lax.optimization_barrier((sends, grad_attended, result))
    moving = posted(moving, sends, stages_of(1))
    output = lax.all_to_all(result.reshape(groups, quarter, width), "head", 0, 0, tiled=True)
    back_high = attention_back(1, blocks)
    token_part = jnp.concatenate([back_low[3], back_high[3]], 1)
    token_part, back_high = lax.optimization_barrier((token_part, back_high))
    token_parts = gather(token_part[None], head_stages[:1])
    share = width // dps
    rows_a, rows_b, rows_own = 2 * share + SUM_ROWS, 2 * share, share + SUM_ROWS
    keep_b, send_b, grad_x, value_sum = whole_call(
        functools.partial(value_grads, order_b, dps),
        (place,),
        (x, grad_mixed, attended, back_low[2], back_high[2], grad_attn),
        (w_attn,),
        (
            *(shape((dps // 2, rows_b, width), LOW),) * 2,
            shape((seg_len, width), FULL),
            shape((1, width), FULL),
        ),
        5_000_000_000,
        (pltpu.VMEM((width, width), LOW), pltpu.SemaphoreType.DMA(())),
    )
    down_a, down_b = ([("dp", bit) for bit in order[::-1]] for order in (order_a, order_b))
    grad_x, send_b, moving, output, token_parts = lax.optimization_barrier(
        (grad_x, send_b, moving, output, token_parts)
    )
    token_parts = gather(token_parts, head_stages[1:])
    other_b = swap(send_b, *down_b[0])
    sends = parcels(moving)
    sends, grad_x = lax.optimization_barrier((sends, grad_x))
    moving = posted(moving, sends, stages_of(2))
    for level in range(3, levels):
        moving = posted(moving, parcels(moving), stages_of(level))
    sum_scratch = (pltpu.VMEM((SUM_ROWS, width), FULL),)
    keep_a, send_a, grad_x = whole_call(
        functools.partial(
            query_key_grads, layout, order_a, order_b, head_order, heads_here, memory_rows
        ),
        (place,),
        (
            x,
            back_low[0],
            back_high[0],
            back_low[1],
            back_high[1],
            grad_x,
            value_sum,
            layer_sums,
            bias_sum,
        ),
        (w_attn,),
        (
            *(shape((dps // 2, rows_a, width), LOW),) * 2,
            shape((seg_len, width), LOW),
        ),
        10_000_000_000,
        sum_scratch + (pltpu.VMEM((2, width, width), LOW), pltpu.SemaphoreType.DMA((2,))),
    )

    def advance_both(parts, level):
        return [reduce_step(p, down[level]) for p, down in zip(parts, (down_a, down_b))]

    token_parts, send_a, other_b, grad_x, moving = lax.optimization_barrier(
        (token_parts, send_a, other_b, grad_x, moving)
    )
    attn_moving = [[keep_a, swap(send_a, *down_a[0])], [keep_b, other_b]]
    sends = parcels(moving, True)
    attn_moving, sends = lax.optimization_barrier((attn_moving, sends))
    others = swap(sends[0], *back_a[levels])
    sends = parcels(attn_moving)
    sends, grad_x, token_parts = lax.optimization_barrier((sends, grad_x, token_parts))
    attn_moving = posted(attn_moving, sends, (down_a[1], down_b[1]))
    moved = lax.all_to_all(grad_x.reshape(groups, quarter, width), "head", 0, 0, tiled=True)

    packed_rows = writes * memory_rows + (-writes * memory_rows) % PAD
    score_w, grad_attended_w, grad_mixed_w, small_w, factors, bias_w, vec_w, init_w, norms = whole_call(
        functools.partial(chain_backward, layout, head_order, heads, memory_rows),
        (reset, place),
        (
            bias_in,
            read,
            norms,
            vectors,
            qkv,
            soft,
            soft_mem,
            z_attn_w,
            pre_w,
            z_ffn_w,
            hidden_w,
            token_parts,
        ),
        (w_attn, keys, values, *pieces),
        (
            shape((writes, heads * PAD, seg_len), LOW),
            shape((writes, PAD, width), LOW),
            shape((writes, PAD, width), LOW),
            shape((segments, 3, PAD, width), LOW),
            shape((4, packed_rows, width), LOW),
            shape((layout.chunks, 1, layout.size), FULL),
            shape((len(VECTORS), width), FULL),
            shape((PAD, width), FULL),
            shape((1, 128), FULL),
        ),
        20_000_000_000,
        (
            pltpu.VMEM((writes, PAD, width), LOW),
            pltpu.VMEM((writes, PAD, ff), LOW),
            pltpu.VMEM((segments, 2 * PAD, width), FULL),
        )
        + tokens_scratch(segments)
        + landing,
    )
    score_w, factors, moving, others, attn_moving, moved = lax.optimization_barrier(
        (score_w, factors, moving, others, attn_moving, moved)
    )

    moving = [terms + [others[:, i]] for i, terms in enumerate(moving)]
    sends = parcels(moving + attn_moving, True)
    sends, score_w = lax.optimization_barrier((sends, score_w))
    others = swap(sends[0], *back_a[levels + 1])
    moving = [terms + [others[:, i]] for i, terms in enumerate(moving)]
    attn_moving = posted(attn_moving, sends[1:], (down_a[2], down_b[2]))
    for level in range(3, levels):
        attn_moving = advance_both(attn_moving, level)
    factors = gather(factors[None], [("dp", order_a[0])])
    keep_own, send_own = whole_call(
        functools.partial(
            own_grads, layout, order_a, order_b, head_order, heads, heads_here, memory_rows
        ),
        (place,),
        (
            score_w,
            soft,
            qkv,
            grad_attended_w,
            grad_mixed_w,
            attended_w,
            small_w,
            read,
            tokens,
            bias_w,
            vec_w,
            init_w,
        ),
        (),
        (shape((dps // 2, rows_own, width), LOW),) * 2,
        5_000_000_000,
        sum_scratch,
    )
    keep_own, send_own, attn_moving, factors, score_w, moving = lax.optimization_barrier(
        (keep_own, send_own, attn_moving, factors, score_w, moving)
    )
    own = [keep_own, swap(send_own, *down_a[0])]
    left, right = (summed(terms)[0] for terms in attn_moving)
    right = jnp.pad(right, ((0, SUM_ROWS), (0, 0)))
    both = [
        jnp.concatenate([part[:, g * here : (g + 1) * here] for part in (left, right)], 1)
        for g in range(groups)
    ]
    attn_moving = [jnp.stack([both[partner(i, head_stages, "head")] for i in range(groups)])]
    attn_send = summed(attn_moving, LOW, groups // 2)
    own_send = summed(own, LOW, own[-1].shape[0] // 2)
    attn_send, own_send, score_w = lax.optimization_barrier((attn_send, own_send, score_w))
    attn_moving = attn_moving + [swap(attn_send, "head", head_order[-1])]
    own = own + [swap(own_send, *down_a[1])]
    factors = gather(factors, [("dp", order_a[1])])
    (grad_tokens,) = whole_call(
        functools.partial(write_rows, heads, quarter),
        (place,),
        (score_w, soft, qkv, grad_attended_w, moved),
        (w_attn,),
        (shape((segments, quarter, width), FULL),),
        5_000_000_000,
        (pltpu.VMEM((2, width, width), LOW), pltpu.SemaphoreType.DMA((2,))),
    )
    grad_tokens, own, factors, attn_moving = lax.optimization_barrier(
        (grad_tokens, own, factors, attn_moving)
    )
    for bit in head_order[:-1][::-1]:
        attn_moving = reduce_step(attn_moving, ("head", bit))
    factors = gather(factors, stages_a[len(head_stages) + 2 : -1])
    factors = [factors, swap(factors, *stages_a[-1])]
    for level in range(2, levels):
        own = reduce_step(own, down_a[level])
    own, factors, attn_moving, moving = lax.optimization_barrier(
        (own, factors, attn_moving, moving)
    )
    part = width // dps // groups
    row = shape((1, part), FULL)
    groups_in = [factors, *moving, attn_moving, own]
    first_entry = lambda array: pl.BlockSpec(
        (1, *array.shape[1:]), lambda i: (0,) * len(array.shape)
    )
    whole = lambda array: pl.BlockSpec(array.shape, lambda i: (0,) * len(array.shape))
    shapes = (
        *(shape((share, here), FULL),) * 3,
        *(shape((heads_here, head_dim // dps), FULL),) * 2,
        shape((here, share), FULL),
        *(row,) * 3,
        shape((units, width), FULL),
        shape((1, units), FULL),
        shape((units, width), FULL),
        *(row,) * 3,
        shape((memory_rows, part), FULL),
    )
    outs = pl.pallas_call(
        functools.partial(
            finish,
            order_in(order_a, order_a),
            order_in(order_b, order_a),
            memory_rows,
            [len(group) for group in groups_in],
        ),
        grid=(1,),
        out_shape=shapes,
        in_specs=[whole(a) for a in factors]
        + [first_entry(a) for group in groups_in[1:] for a in group],
        out_specs=[whole(a) for a in shapes],
        compiler_params=pltpu.CompilerParams(vmem_limit_bytes=VMEM_LIMIT),
        cost_estimate=pl.CostEstimate(flops=1000, bytes_accessed=1000, transcendentals=0),
    )(*(a for group in groups_in for a in group))
    flat = (6, 7, 8, 10, 12, 13, 14)
    outs = [out.reshape(-1) if i in flat else out for i, out in enumerate(outs)]
    outs[9] = outs[9].T
    return (output[None], norms[:, :segments], grad_tokens[None], *outs)


def solution(mesh):
    in_specs = (
        P("dp", None, None, None),
        P("dp", None, None),
        P("dp", None),
        P(),
        P(None, "head"),
        P(None, "head"),
        P(None, "head"),
        P("head", None),
        P("head", None),
        P("head", None),
        P(),
        P(),
        P(),
        P(None, ("dp", "head")),
        P(("dp", "head")),
        P(("dp", "head"), None),
        P(),
        P(),
        P(),
        P("dp", None, "head", None),
    )
    out_specs = (
        P("dp", None, "head", None),
        P("dp", None),
        P("dp", None, "head", None),
        P("dp", "head"),
        P("dp", "head"),
        P("dp", "head"),
        P("head", "dp"),
        P("head", "dp"),
        P("head", "dp"),
        P(("dp", "head")),
        P(("dp", "head")),
        P(("dp", "head")),
        P(None, ("dp", "head")),
        P(("dp", "head")),
        P(("dp", "head"), None),
        P(("dp", "head")),
        P(("dp", "head")),
        P(("dp", "head")),
        P(None, ("dp", "head")),
    )
    return jax.shard_map(
        on_device, mesh=mesh, in_specs=in_specs, out_specs=out_specs, check_vma=False
    )
```

```python
import functools

import jax
import jax.numpy as jnp
from jax import lax
from jax.experimental import pallas as pl
from jax.experimental.pallas import tpu as pltpu
from jax.sharding import PartitionSpec as P

EPSILON = 1e-06
SCALE = 0.125
NEGATIVE = -1e30
ROOT_HALF = 0.7071067811865476
DENSITY = 0.3989422804014327
LOW = jnp.bfloat16
FULL = jnp.float32
PAD = 16
VECTORS = ("b_query", "b_value", "b_out", "gain_attn", "shift_attn", "b_down", "gain_ffn", "shift_ffn")
VMEM_LIMIT = 60 * 1024 * 1024


def nn(left, right):
    return lax.dot_general(left, right, (((1,), (0,)), ((), ())), preferred_element_type=FULL)


def nt(left, right):
    return lax.dot_general(left, right, (((1,), (1,)), ((), ())), preferred_element_type=FULL)


def tn(left, right):
    return lax.dot_general(left, right, (((0,), (0,)), ((), ())), preferred_element_type=FULL)


def norm_parts(rows):
    centred = rows - jnp.mean(rows, -1, keepdims=True)
    inverse = lax.rsqrt(jnp.mean(centred * centred, -1, keepdims=True) + EPSILON)
    return centred * inverse, inverse


def norm_pull(normed, inverse, grad):
    along = jnp.mean(grad * normed, -1, keepdims=True)
    return inverse * (grad - jnp.mean(grad, -1, keepdims=True) - normed * along)


def gelu(v):
    return 0.5 * v * (1.0 + lax.erf(v * ROOT_HALF))


def gelu_slope(v):
    return 0.5 * (1.0 + lax.erf(v * ROOT_HALF)) + v * (DENSITY * jnp.exp(-0.5 * v * v))


def swap(array, axis, bit):
    return lax.ppermute(array, axis, [(i, i ^ bit) for i in range(lax.axis_size(axis))])


def bits_of(count):
    return [1 << i for i in range(count.bit_length() - 1)]


def gather(array, stages):
    for axis, bit in stages:
        array = jnp.concatenate([array, swap(array, axis, bit)], 0)
    return array


def summed(terms, kind=LOW, first=0):
    size = terms[-1].shape[0] - first
    total = terms[0][first : first + size].astype(FULL)
    for term in terms[1:]:
        total = total + term[first : first + size].astype(FULL)
    return total.astype(kind)


def add_up(count, together, *refs):
    out_refs = list(refs[sum(count) :])
    pair_ref = None
    if together:
        pair_ref = out_refs[0]
        out_refs = [None, None] + out_refs[1:]
    at = 0
    for number_of, (number, out_ref) in enumerate(zip(count, out_refs)):
        total = refs[at][...].astype(FULL)
        for ref in refs[at + 1 : at + number]:
            total = total + ref[...].astype(FULL)
        total = total.astype(refs[at].dtype)
        at += number
        if pair_ref is not None and number_of < 2:
            pair_ref[:, number_of] = total
        else:
            out_ref[...] = total


def parcels(groups, together=False):
    halves = [terms[-1].shape[0] // 2 for terms in groups]
    steps = min(min(halves), 4)
    in_specs, operands, out_specs, shapes = [], [], [], []

    def spec(half, rest, first):
        index = lambda i: (first + i,) + (0,) * len(rest)
        return pl.BlockSpec((half // steps, *rest), index)

    for half, terms in zip(halves, groups):
        rest = terms[0].shape[1:]
        in_specs += [spec(half, rest, steps)] * len(terms)
        operands += terms
        if together and len(operands) < len(groups[0]) + len(groups[1]) + 1:
            if len(shapes):
                continue
            rest = (2, *rest)
        out_specs.append(spec(half, rest, 0))
        shapes.append(jax.ShapeDtypeStruct((half, *rest), terms[0].dtype))
    return pl.pallas_call(
        functools.partial(add_up, [len(terms) for terms in groups], together),
        grid=(steps,),
        out_shape=shapes,
        in_specs=in_specs,
        out_specs=out_specs,
        compiler_params=pltpu.CompilerParams(vmem_limit_bytes=VMEM_LIMIT),
        cost_estimate=pl.CostEstimate(flops=1000, bytes_accessed=1000, transcendentals=0),
    )(*operands)


def posted(groups, sends, stages):
    return [
        terms + [swap(send, *stage)] for terms, send, stage in zip(groups, sends, stages)
    ]


def reduce_step(terms, stage):
    half = terms[-1].shape[0] // 2
    return terms + [swap(summed(terms, terms[0].dtype, half), *stage)]


def partner(index, stages, axis):
    place = 0
    for k, (name, bit) in enumerate(stages):
        if name == axis:
            place = place + ((index >> k) & 1) * bit
    return place


def position(partner_bits, order):
    place = 0
    for k, bit in enumerate(order):
        place = place + ((partner_bits // bit) % 2) * (1 << k)
    return place


def order_in(order, index_order):
    return [1 << index_order.index(bit) for bit in order]


def head_mask(rows, width, heads):
    group = lax.broadcasted_iota(jnp.int32, (rows, width), 0) // PAD
    column = lax.broadcasted_iota(jnp.int32, (rows, width), 1) // (width // heads)
    return group == column


def by_head(rows, mask, heads):
    return jnp.where(mask, jnp.concatenate([rows] * heads, 0), jnp.zeros((), rows.dtype))


def own_head(rows, mask, heads):
    kept = jnp.where(mask, rows, 0.0)
    total = kept[:PAD]
    for i in range(1, heads):
        total = total + kept[i * PAD : (i + 1) * PAD]
    return total


def vector(vec_ref, name):
    i = VECTORS.index(name)
    return vec_ref[i : i + 1, :]


class Units:
    def __init__(self, dps, heads, rows, width):
        self.dps, self.heads, self.rows, self.width = dps, heads, rows, width
        self.blocks = dps * heads
        self.chunks = max(2 * self.blocks * rows // width, 4)
        self.size = 2 * self.blocks * rows // self.chunks
        self.whole = rows % 16 != 0

    def at(self, index):
        return (index % self.heads) * self.dps + index // self.heads

    def pieces(self):
        if self.whole:
            return [(0, self.chunks)]
        part = self.blocks // 4
        return [(half * self.blocks + p * part, part) for half in range(2) for p in range(4)]

    def copies(self):
        for number, (first, count) in enumerate(self.pieces()):
            for entry in range(count):
                if self.whole:
                    yield number, entry, entry, 0, self.size
                    continue
                half, index = divmod(first + entry, self.blocks)
                row = (half * self.blocks + self.at(index)) * self.rows
                yield number, entry, row // self.size, row % self.size, self.rows

    def scratch(self):
        buffer = pltpu.VMEM((self.chunks, self.size, self.width), LOW)
        count = sum(2 for _ in self.copies())
        return (buffer, buffer, pltpu.SemaphoreType.DMA((count,)))

    def loads(self, pieces, up_ref, down_ref, arrived):
        made = []
        for number, entry, chunk, row, rows in self.copies():
            for side, to_ref in enumerate((up_ref, down_ref)):
                made.append(
                    pltpu.make_async_copy(
                        pieces[number].at[entry, side],
                        to_ref.at[chunk, pl.ds(row, rows)],
                        arrived.at[len(made)],
                    )
                )
        return made

    def assembled(self, halves):
        rows = []
        for array in halves:
            array = array.reshape(self.dps, self.heads, 2, self.rows, self.width)
            rows.append(array.transpose(1, 0, 3, 2, 4).reshape(-1, 2, self.width))
        rows = jnp.concatenate(rows, 0).reshape(self.chunks, self.size, 2, self.width)
        return [rows.transpose(0, 2, 1, 3)]

    def taken_apart(self, piece):
        rows = piece.transpose(0, 2, 1, 3).reshape(2, self.heads, self.dps, self.rows, 2, -1)
        rows = rows.transpose(0, 2, 1, 4, 3, 5)
        return [half.reshape(self.blocks, 2, self.rows, self.width) for half in rows]


def head_groups(ref, flip):
    value = ref[...]
    half = value.shape[1] // 2
    low, high = value[:, :half], value[:, half:]
    if flip & 2:
        low, high = high, low
    if flip & 1:
        low, high = pltpu.roll(low, half // 2, 1), pltpu.roll(high, half // 2, 1)
    return jnp.concatenate([low, high], 1)


def memory_queries(read, attn_ref, vec_ref):
    low = read.astype(LOW)
    queries = (nt(low, attn_ref[0]) + vector(vec_ref, "b_query")).astype(LOW)
    keys = nt(low, attn_ref[1]).astype(LOW)
    values = (nt(low, attn_ref[2]) + vector(vec_ref, "b_value")).astype(LOW)
    return queries, keys, values


def memory_attention(heads, memory_rows, queries, keys, values, key_low, value_low):
    rows, width = heads * PAD, queries.shape[1]
    mask = head_mask(rows, width, heads)
    real_key = lax.broadcasted_iota(jnp.int32, (rows, PAD), 1) < memory_rows
    spread = by_head(queries, mask, heads)
    scores = nt(spread, key_low) * SCALE
    scores_mem = jnp.where(real_key, nt(spread, keys) * SCALE, NEGATIVE)
    top = jnp.maximum(jnp.max(scores, -1, keepdims=True), jnp.max(scores_mem, -1, keepdims=True))
    raised = jnp.exp(scores - top)
    raised_mem = jnp.exp(scores_mem - top)
    total = jnp.sum(raised, -1, keepdims=True) + 2.0 * jnp.sum(raised_mem, -1, keepdims=True)
    soft = raised / total
    soft_mem = raised_mem / total
    mixed = nn(soft.astype(LOW), value_low) + 2.0 * nn(soft_mem.astype(LOW), values)
    return own_head(mixed, mask, heads).astype(LOW), soft, soft_mem


def memory_norm(result, memory_rows):
    real_row = lax.broadcasted_iota(jnp.int32, result.shape, 0) < memory_rows
    square = jnp.sum(jnp.where(real_row, result * result, 0.0), axis=(0, 1), keepdims=True)
    return jnp.sqrt(square / (memory_rows * result.shape[1]))


def chain_forward(
    layout,
    heads,
    memory_rows,
    reset_ref,
    init_ref,
    bias_ref,
    vec_ref,
    attn_from,
    key_from,
    value_from,
    *refs,
):
    count = len(layout.pieces())
    pieces, refs = refs[:count], refs[count:]
    (
        read_ref,
        qkv_ref,
        soft_ref,
        soft_mem_ref,
        attended_ref,
        z_attn_ref,
        hidden_ref,
        pre_ref,
        z_ffn_ref,
        norm_ref,
        attn_ref,
        key_ref,
        value_ref,
        attn_arrived,
        key_arrived,
        value_arrived,
        up_ref,
        down_ref,
        arrived,
    ) = refs
    last = key_ref.shape[0]
    attn_loads = [
        pltpu.make_async_copy(attn_from.at[i], attn_ref.at[i], attn_arrived.at[i])
        for i in range(4)
    ]

    def token_loads(s):
        return [
            pltpu.make_async_copy(key_from.at[s], key_ref.at[s], key_arrived.at[s]),
            pltpu.make_async_copy(value_from.at[s], value_ref.at[s], value_arrived.at[s]),
        ]

    loads = layout.loads(pieces, up_ref, down_ref, arrived)
    for load in attn_loads[:3] + token_loads(0) + attn_loads[3:] + loads:
        load.start()
    for s in range(1, last):
        for load in token_loads(s):
            load.start()
    chunks, size, _ = up_ref.shape
    norm_ref[...] = jnp.zeros_like(norm_ref)
    for load in attn_loads[:3]:
        load.wait()

    def enter(s, carried):
        fresh = (reset_ref[0, s] > 0) | (s == 0)
        read = jnp.where(fresh, init_ref[...], carried)
        read_ref[s] = read
        queries, keys, values = memory_queries(read, attn_ref, vec_ref)
        qkv_ref[s, 0] = queries
        qkv_ref[s, 1] = keys
        qkv_ref[s, 2] = values
        return read, queries, keys, values

    def step(s, carried):
        read, queries, keys, values = enter(s, carried)
        for load in token_loads(s):
            load.wait()
        attended, soft, soft_mem = memory_attention(
            heads, memory_rows, queries, keys, values, key_ref[s], value_ref[s]
        )
        soft_ref[s] = soft
        soft_mem_ref[s] = soft_mem
        attended_ref[s] = attended

        @pl.when(s == 0)
        def _():
            attn_loads[3].wait()

        z_attn = read + nn(attended, attn_ref[3]) + vector(vec_ref, "b_out")
        z_attn_ref[s] = z_attn
        normed, _ = norm_parts(z_attn)
        hidden = normed * vector(vec_ref, "gain_attn") + vector(vec_ref, "shift_attn")
        hidden_low = hidden.astype(LOW)
        hidden_ref[s] = hidden_low
        z_ffn = hidden + vector(vec_ref, "b_down")

        @pl.when(s == 0)
        def _():
            for load in loads:
                load.wait()

        for i in range(chunks):
            pre = nt(hidden_low, up_ref[i]) + bias_ref[i]
            pre_ref[s, :, i * size : (i + 1) * size] = pre
            z_ffn = z_ffn + nn(gelu(pre).astype(LOW), down_ref[i])
        z_ffn_ref[s] = z_ffn
        normed, _ = norm_parts(z_ffn)
        result = normed * vector(vec_ref, "gain_ffn") + vector(vec_ref, "shift_ffn")
        lane = lax.broadcasted_iota(jnp.int32, norm_ref.shape, 1)
        norm_ref[...] = jnp.where(lane == s, memory_norm(result, memory_rows), norm_ref[...])
        return result

    carried = lax.fori_loop(0, last, step, init_ref[...])
    enter(last, carried)


def last_norm(heads, memory_rows, bias_ref, vec_ref, read, qkv, key, value, weights):
    out_w, up_ref, down_ref = weights
    attended, _, _ = memory_attention(heads, memory_rows, *qkv, key, value)
    z_attn = read + nn(attended, out_w) + vector(vec_ref, "b_out")
    normed, _ = norm_parts(z_attn)
    hidden = normed * vector(vec_ref, "gain_attn") + vector(vec_ref, "shift_attn")
    hidden_low = hidden.astype(LOW)
    z_ffn = hidden + vector(vec_ref, "b_down")
    for i in range(up_ref.shape[0]):
        pre = nt(hidden_low, up_ref[i]) + bias_ref[i]
        z_ffn = z_ffn + nn(gelu(pre).astype(LOW), down_ref[i])
    normed, _ = norm_parts(z_ffn)
    result = normed * vector(vec_ref, "gain_ffn") + vector(vec_ref, "shift_ffn")
    return memory_norm(result, memory_rows)


def chain_backward(
    layout,
    head_order,
    heads,
    memory_rows,
    reset_ref,
    place_ref,
    bias_ref,
    read_ref,
    norms_ref,
    vec_ref,
    qkv_ref,
    soft_ref,
    soft_mem_ref,
    z_attn_ref,
    pre_ref,
    z_ffn_ref,
    hidden_ref,
    *refs,
):
    segments, _, _, width = qkv_ref.shape
    part_ref, *refs = refs
    attn_from, key_from, value_from, *refs = refs
    count = len(layout.pieces())
    pieces, refs = refs[:count], refs[count:]
    (
        score_ref,
        attended_ref,
        mixed_ref,
        small_ref,
        factor_ref,
        bias_grad_ref,
        vec_grad_ref,
        init_grad_ref,
        norm_ref,
        ffn_ref,
        pre_grad_ref,
        token_part_ref,
        attn_ref,
        key_ref,
        value_ref,
        attn_arrived,
        key_arrived,
        value_arrived,
        up_ref,
        down_ref,
        arrived,
    ) = refs
    attn_loads = [
        pltpu.make_async_copy(attn_from.at[i], attn_ref.at[i], attn_arrived.at[i])
        for i in range(4)
    ]

    def token_loads(s):
        return [
            pltpu.make_async_copy(key_from.at[s], key_ref.at[s], key_arrived.at[s]),
            pltpu.make_async_copy(value_from.at[s], value_ref.at[s], value_arrived.at[s]),
        ]

    loads = layout.loads(pieces, up_ref, down_ref, arrived)
    for load in attn_loads[1:3] + loads + attn_loads[3:] + attn_loads[:1]:
        load.start()
    for s in range(segments - 1, -1, -1):
        for load in token_loads(s):
            load.start()
    for j in range(segments):
        token_part_ref[j] = head_groups(part_ref.at[position(j, head_order)], j)
    me = place_ref[1]
    rows = heads * PAD
    mask = head_mask(rows, width, heads)
    chunks, size, _ = up_ref.shape
    half = chunks * size // 2
    vec_grad_ref[...] = jnp.zeros_like(vec_grad_ref)
    bias_grad_ref[...] = jnp.zeros_like(bias_grad_ref)

    def add_vector(name, grad):
        i = VECTORS.index(name)
        vec_grad_ref[i : i + 1, :] += jnp.sum(grad, 0, keepdims=True)

    last = segments - 1
    for load in attn_loads[1:3]:
        load.wait()
    grad_key = token_part_ref[last ^ me, :PAD].astype(LOW)
    grad_value = token_part_ref[last ^ me, PAD:].astype(LOW)
    small_ref[last, 0] = jnp.zeros((PAD, width), LOW)
    small_ref[last, 1] = grad_key
    small_ref[last, 2] = grad_value
    add_vector("b_value", 2.0 * grad_value.astype(FULL))
    grad_read = 2.0 * (nn(grad_key, attn_ref[1]) + nn(grad_value, attn_ref[2]))
    stop = reset_ref[0, last] > 0
    init_grad_ref[...] = jnp.where(stop, grad_read, 0.0)
    grad_write = jnp.where(stop, 0.0, grad_read)

    for load in [attn_loads[0], attn_loads[3], *loads, *token_loads(last)]:
        load.wait()
    norm = last_norm(
        heads,
        memory_rows,
        bias_ref,
        vec_ref,
        read_ref[last],
        [qkv_ref[last, i] for i in range(3)],
        key_ref[last],
        value_ref[last],
        (attn_ref[3], up_ref, down_ref),
    )
    lane = lax.broadcasted_iota(jnp.int32, norm_ref.shape, 1)
    norm_ref[...] = jnp.where(lane == last, norm, norms_ref[...])

    def step(back, grad_write):
        s = segments - 2 - back
        normed, inverse = norm_parts(z_ffn_ref[s])
        add_vector("gain_ffn", grad_write * normed)
        add_vector("shift_ffn", grad_write)
        grad_sum = norm_pull(normed, inverse, grad_write * vector(vec_ref, "gain_ffn"))
        grad_low = grad_sum.astype(LOW)
        ffn_ref[s] = grad_low
        add_vector("b_down", grad_low.astype(FULL))
        grad_hidden = grad_sum

        for i in range(chunks):
            part = slice(i * size, (i + 1) * size)
            grad_act = nt(grad_low, down_ref[i])
            grad_pre = (grad_act * gelu_slope(pre_ref[s, :, part])).astype(LOW)
            pre_grad_ref[s, :, part] = grad_pre
            bias_grad_ref[i] += jnp.sum(grad_pre.astype(FULL), 0, keepdims=True)
            grad_hidden = grad_hidden + nn(grad_pre, up_ref[i])
        normed, inverse = norm_parts(z_attn_ref[s])
        add_vector("gain_attn", grad_hidden * normed)
        add_vector("shift_attn", grad_hidden)
        grad_attn = norm_pull(normed, inverse, grad_hidden * vector(vec_ref, "gain_attn"))
        add_vector("b_out", grad_attn)
        grad_mixed = grad_attn.astype(LOW)
        mixed_ref[s] = grad_mixed

        for load in token_loads(s):
            load.wait()
        grad_attended = nt(grad_mixed, attn_ref[3]).astype(LOW)
        attended_ref[s] = grad_attended
        queries, keys, values = qkv_ref[s, 0], qkv_ref[s, 1], qkv_ref[s, 2]
        spread = by_head(grad_attended, mask, heads)
        soft, soft_mem = soft_ref[s], soft_mem_ref[s]
        pull = nt(spread, value_ref[s])
        pull_mem = nt(spread, values)
        inner = jnp.sum(soft * pull, -1, keepdims=True) + 2.0 * jnp.sum(
            soft_mem * pull_mem, -1, keepdims=True
        )
        grad_score = (soft * (pull - inner)).astype(LOW)
        grad_score_mem = (soft_mem * (pull_mem - inner)).astype(LOW)
        score_ref[s] = grad_score
        grad_query = nn(grad_score, key_ref[s]) + 2.0 * nn(grad_score_mem, keys)
        grad_query = (SCALE * own_head(grad_query, mask, heads)).astype(LOW)
        grad_key = SCALE * tn(grad_score_mem, by_head(queries, mask, heads))
        grad_key = (token_part_ref[s ^ me, :PAD] + grad_key).astype(LOW)
        grad_value = tn(soft_mem.astype(LOW), spread)
        grad_value = (token_part_ref[s ^ me, PAD:] + grad_value).astype(LOW)
        small_ref[s, 0] = grad_query
        small_ref[s, 1] = grad_key
        small_ref[s, 2] = grad_value
        add_vector("b_query", grad_query.astype(FULL))
        add_vector("b_value", 2.0 * grad_value.astype(FULL))
        grad_read = 2.0 * (nn(grad_key, attn_ref[1]) + nn(grad_value, attn_ref[2]))
        grad_read = grad_read + nn(grad_query, attn_ref[0]) + grad_attn
        stop = (reset_ref[0, s] > 0) | (s == 0)
        init_grad_ref[...] += jnp.where(stop, grad_read, 0.0)
        return jnp.where(stop, 0.0, grad_read)

    lax.fori_loop(0, segments - 1, step, grad_write)

    packed, wide = factor_ref.shape[1], (segments - 1) * PAD
    row = lax.broadcasted_iota(jnp.int32, (packed, wide), 0)
    source = lax.broadcasted_iota(jnp.int32, (packed, wide), 1)
    take = (source // PAD == row // memory_rows) & (source % PAD == row % memory_rows)
    take = jnp.where(take, 1.0, 0.0).astype(LOW)
    mine = width // 2

    def own_units(ref):
        first = ref[: segments - 1, :, :mine].reshape(wide, mine)
        second = ref[: segments - 1, :, half : half + mine].reshape(wide, mine)
        return jnp.concatenate([first, second], 1)

    acts = gelu(own_units(pre_ref)).astype(LOW)
    factor_ref[0] = nn(take, hidden_ref[: segments - 1].reshape(wide, width)).astype(LOW)
    factor_ref[1] = nn(take, ffn_ref[...].reshape(wide, width)).astype(LOW)
    factor_ref[2] = nn(take, acts).astype(LOW)
    factor_ref[3] = nn(take, own_units(pre_grad_ref)).astype(LOW)


def whole_call(
    body,
    scalars,
    operands,
    outside,
    shapes,
    flops,
    scratch=(),
    outside_shapes=(),
    limit=VMEM_LIMIT,
):
    in_vmem = pl.BlockSpec(memory_space=pltpu.VMEM)
    in_smem = pl.BlockSpec(memory_space=pltpu.SMEM)
    anywhere = pl.BlockSpec(memory_space=pl.ANY)
    size = sum(a.size * a.dtype.itemsize for a in (*operands, *outside, *shapes))
    return pl.pallas_call(
        body,
        out_shape=(*shapes, *outside_shapes),
        in_specs=[in_smem] * len(scalars) + [in_vmem] * len(operands) + [anywhere] * len(outside),
        out_specs=[in_vmem] * len(shapes) + [anywhere] * len(outside_shapes),
        scratch_shapes=scratch,
        compiler_params=pltpu.CompilerParams(vmem_limit_bytes=limit),
        cost_estimate=pl.CostEstimate(flops=flops // 1000, bytes_accessed=size // 1000, transcendentals=0),
    )(*scalars, *operands, *outside)


def unit_owner(column, order, stages, head_order, layout, index):
    head = position(partner(index, stages, "head"), head_order)
    at = head * layout.dps + position(partner(index, stages, "dp"), order)
    return column // layout.rows == at


def attention_loads(layout, place_ref, order_a, order_b, pieces, attn_ref, arrived):
    loads = []

    def copy(source, target):
        loads.append(pltpu.make_async_copy(source, target, arrived.at[len(loads)]))

    if layout.whole:
        copy(pieces[0], attn_ref)
        return loads
    here = layout.width // layout.heads
    for m in range(4):
        copy(pieces[0].at[m], attn_ref.at[m, pl.ds(0, here)])
    per = layout.dps // 4
    rows = here // per // 2
    for side, order in enumerate((order_a, order_b)):
        for index in range(layout.dps):
            flip = sum(((index >> k) & 1) * bit for k, bit in enumerate(order))
            owner = place_ref[0] ^ flip
            piece = pieces[1 + 4 * side + index // (layout.dps // 4)]
            for group in range(1, layout.heads):
                row = group * here + (owner % per) * 2 * rows + side * rows
                copy(
                    piece.at[index % (layout.dps // 4), group - 1],
                    attn_ref.at[owner // per, pl.ds(pl.multiple_of(row, 16), rows)],
                )
    return loads


def project(
    layout,
    stages,
    order_a,
    order_b,
    head_order,
    place_ref,
    token_ref,
    bias_ref,
    other_ref,
    *refs,
):
    count = 1 if layout.whole else 9
    pieces, refs = refs[:count], refs[count:]
    (
        key_ref,
        value_ref,
        x_ref,
        q_ref,
        k_ref,
        v_ref,
        vec_ref,
        bias_in_ref,
        attn_to,
        attn_ref,
        arrived,
        stored,
    ) = refs
    loads = attention_loads(layout, place_ref, order_a, order_b, pieces, attn_ref, arrived)
    for load in loads:
        load.start()
    devices, entries = bias_ref.shape
    width, rows = layout.width, layout.rows
    here = width // layout.heads
    packets = bias_ref[...].astype(FULL)

    def laid_out(first, count, period, owner):
        entry = lax.broadcasted_iota(jnp.int32, (entries, count), 0)
        column = lax.broadcasted_iota(jnp.int32, (entries, count), 1)
        pick = jnp.where(entry == first + column % period, 1.0, 0.0).astype(LOW)
        index = lax.broadcasted_iota(jnp.int32, (devices, count), 0)
        column = lax.broadcasted_iota(jnp.int32, (devices, count), 1)
        chosen = jnp.where(owner(column, index), nn(packets.astype(LOW), pick), 0.0)
        return jnp.sum(chosen, 0, keepdims=True)

    def of_head(column, index):
        head = partner(index, stages, "head")
        return (partner(index, stages, "dp") == 0) & (head == column // here)

    vec_ref[0:1, :] = laid_out(0, width, here, of_head)
    vec_ref[1:2, :] = laid_out(here, width, here, of_head)
    vec_ref[2:, :] = other_ref[...].astype(FULL)
    for half, order in enumerate((order_a, order_b)):
        owner = functools.partial(
            unit_owner, order=order, stages=stages, head_order=head_order, layout=layout
        )
        row = laid_out(
            2 * here + half * rows,
            layout.blocks * rows,
            rows,
            lambda column, index: owner(column, index=index),
        )
        per = layout.chunks // 2
        for i in range(per):
            bias_in_ref[half * per + i] = row[:, i * layout.size : (i + 1) * layout.size]

    for load in loads:
        load.wait()
    store = pltpu.make_async_copy(attn_ref, attn_to, stored)
    store.start()
    for s in range(token_ref.shape[0]):
        x = token_ref[s]
        key_ref[s] = nt(x, attn_ref[1]).astype(LOW)
        value_ref[s] = (nt(x, attn_ref[2]) + vector(vec_ref, "b_value")).astype(LOW)
    own = place_ref[1]
    x = token_ref[own]
    x_ref[...] = x
    q_ref[...] = (nt(x, attn_ref[0]) + vector(vec_ref, "b_query")).astype(LOW)
    k_ref[...] = key_ref[own]
    v_ref[...] = value_ref[own]
    store.wait()


SUMS = ("b_out", "gain_attn", "shift_attn", "b_down", "gain_ffn", "shift_ffn")


def token_layer(
    layout,
    memory_rows,
    head_dim,
    place_ref,
    x_ref,
    q_ref,
    qkv_ref,
    part_ref,
    stat_ref,
    cot_ref,
    bias_ref,
    vec_ref,
    attn_ref,
    *refs,
):
    count = len(layout.pieces())
    pieces, refs = refs[:count], refs[count:]
    (
        attended_ref,
        log_ref,
        result_ref,
        skip_ref,
        mixed_ref,
        grad_attended_ref,
        bias_sum_ref,
        sum_ref,
        *grad_refs,
        out_w_ref,
        out_arrived,
        up_ref,
        down_ref,
        arrived,
        z_attn_ref,
        hidden_ref,
        low_ref,
        total_ref,
        pre_ref,
        act_ref,
        stage_ref,
        sent,
    ) = refs
    out_load = pltpu.make_async_copy(attn_ref.at[3], out_w_ref, out_arrived)
    out_load.start()
    loads = layout.loads(pieces, up_ref, down_ref, arrived)
    for load in loads:
        load.start()
    chunks = layout.chunks
    pair = part_ref.shape[1]
    log_ref[...] = jnp.zeros_like(log_ref)
    for i in range(part_ref.shape[0]):
        columns = slice(i * pair, (i + 1) * pair)
        mixed, logs = with_memory(
            memory_rows,
            head_dim,
            q_ref[:, columns],
            qkv_ref[place_ref[1], 1, :, columns],
            qkv_ref[place_ref[1], 2, :, columns],
            part_ref[i],
            stat_ref[i],
        )
        attended_ref[:, columns] = mixed
        for head, log in enumerate(logs):
            log_ref[i, head : head + 1] = log
    out_load.wait()
    sum_ref[...] = jnp.zeros_like(sum_ref)

    def add_vector(name, grad):
        i = SUMS.index(name)
        sum_ref[i : i + 1, :] += jnp.sum(grad, 0, keepdims=True)

    z_attn = x_ref[...].astype(FULL) + nn(attended_ref[...], out_w_ref[...])
    z_attn = z_attn + vector(vec_ref, "b_out")
    z_attn_ref[...] = z_attn
    normed, _ = norm_parts(z_attn)
    hidden = normed * vector(vec_ref, "gain_attn") + vector(vec_ref, "shift_attn")
    hidden_ref[...] = hidden.astype(LOW)
    total_ref[...] = hidden + vector(vec_ref, "b_down")
    for load in loads:
        load.wait()

    for i in range(chunks):
        pre = nt(hidden_ref[...], up_ref[i]) + bias_ref[i]
        pre_ref[i] = pre
        act = gelu(pre).astype(LOW)
        act_ref[i] = act
        total_ref[...] += nn(act, down_ref[i])
    normed, inverse = norm_parts(total_ref[...])
    result = normed * vector(vec_ref, "gain_ffn") + vector(vec_ref, "shift_ffn")
    result_ref[...] = result.astype(LOW)
    grad = cot_ref[...].astype(FULL)
    add_vector("gain_ffn", grad * normed)
    add_vector("shift_ffn", grad)
    grad = norm_pull(normed, inverse, grad * vector(vec_ref, "gain_ffn"))
    total_ref[...] = grad
    low_ref[...] = grad.astype(LOW)
    add_vector("b_down", low_ref[...].astype(FULL))

    copies = list(layout.copies())
    spans = [first for first, _ in layout.pieces()]
    stores = []
    for i in range(chunks):
        grad_pre = (nt(low_ref[...], down_ref[i]) * gelu_slope(pre_ref[i])).astype(LOW)
        bias_sum_ref[i] = jnp.sum(grad_pre.astype(FULL), 0, keepdims=True)
        total_ref[...] += nn(grad_pre, up_ref[i])
        slot = i % 2
        if i > 1:
            for store in stores[i - 2]:
                store.wait()
        stage_ref[slot, 0] = tn(grad_pre, hidden_ref[...]).astype(LOW)
        stage_ref[slot, 1] = tn(act_ref[i], low_ref[...]).astype(LOW)
        stores.append([])
        for number, entry, chunk, row, rows in copies:
            if chunk != i:
                continue
            for side in range(2):
                to_ref = grad_refs[number // (len(spans) // len(grad_refs))]
                entry_at = spans[number] - spans[number - number % (len(spans) // len(grad_refs))]
                store = pltpu.make_async_copy(
                    stage_ref.at[slot, side, pl.ds(row, rows)],
                    to_ref.at[entry_at + entry, side],
                    sent.at[i, len(stores[i])],
                )
                store.start()
                stores[i].append(store)

    grad_hidden = total_ref[...]
    normed, inverse = norm_parts(z_attn_ref[...])
    add_vector("gain_attn", grad_hidden * normed)
    add_vector("shift_attn", grad_hidden)
    grad = norm_pull(normed, inverse, grad_hidden * vector(vec_ref, "gain_attn"))
    add_vector("b_out", grad)
    skip_ref[...] = grad
    mixed_ref[...] = grad.astype(LOW)
    grad_attended_ref[...] = nt(mixed_ref[...], out_w_ref[...]).astype(LOW)
    for i in range(max(chunks - 2, 0), chunks):
        for store in stores[i]:
            store.wait()


def part_rows(keep_ref, send_ref, first, columns, grad, place_ref, order, count):
    rows = grad.shape[0] // count
    for c in range(count):
        block = grad[c * rows : (c + 1) * rows].astype(keep_ref.dtype)
        at = position(place_ref[0] ^ c, order)

        @pl.when(at < count // 2)
        def _():
            keep_ref[at, first : first + rows, columns] = block

        @pl.when(at >= count // 2)
        def _():
            send_ref[at - count // 2, first : first + rows, columns] = block


SUM_ROWS = 32


def pack_sums(
    layout, order_a, order_b, head_order, heads_here, memory_rows, place_ref, groups, rows, halves
):
    count, width = rows.shape
    dps = layout.dps
    devices = dps * groups
    here, part = width // layout.heads, width // (dps * layout.heads)
    head_dim = here // heads_here
    head_part = head_dim // dps

    def partners(index):
        head = index % groups
        dp = 0
        for k, bit in enumerate(order_a):
            dp = dp + ((index // groups >> k) & 1) * bit
        return dp, head

    shape = (devices, count, width)
    index, row, column = (lax.broadcasted_iota(jnp.int32, shape, i) for i in range(3))
    dp_flip, head_flip = partners(index)
    dp, head = place_ref[0] ^ dp_flip, place_ref[1] ^ head_flip
    plain = len(SUMS) + memory_rows
    of_device = column // part == dp * layout.heads + head
    of_head = (column // here == head_flip) & (column % head_dim // head_part == dp)
    chosen = ((row < plain) & of_device) | ((row >= plain) & of_head)
    chosen = jnp.where(chosen, jnp.broadcast_to(rows[None], shape), 0.0)
    chosen = chosen.reshape(devices * count, width).astype(LOW)
    source = lax.broadcasted_iota(jnp.int32, (width, part), 0)
    target = lax.broadcasted_iota(jnp.int32, (width, part), 1)
    plain_fold = jnp.where(source % part == target, 1.0, 0.0).astype(LOW)
    head_column = source // head_dim % heads_here * head_part + source % head_part
    head_fold = jnp.where(head_column == target, 1.0, 0.0).astype(LOW)
    row = lax.broadcasted_iota(jnp.int32, (devices, count, part), 1)
    folded = jnp.where(
        row < plain,
        nn(chosen, plain_fold).reshape(devices, count, part),
        nn(chosen, head_fold).reshape(devices, count, part),
    )
    unit_rows = []
    span = halves[0].shape[1]
    index, column = (lax.broadcasted_iota(jnp.int32, (devices, span), i) for i in range(2))
    source = lax.broadcasted_iota(jnp.int32, (span, layout.rows), 0)
    target = lax.broadcasted_iota(jnp.int32, (span, layout.rows), 1)
    fold = jnp.where(source % layout.rows == target, 1.0, 0.0).astype(LOW)
    for order, half in zip((order_a, order_b), halves):
        dp_flip, head_flip = partners(index)
        at = position(head_flip, head_order) * dps + position(dp_flip, order)
        chosen = jnp.where(column // layout.rows == at, half, 0.0)
        unit_rows.append(nn(chosen.astype(LOW), fold))
    return folded, unit_rows


def put_sums(ref, entry, first_row, first_column, packed, index, memory_rows):
    folded, unit_rows = packed
    plain = len(SUMS) + memory_rows
    part, block = folded.shape[2], unit_rows[0].shape[1]
    columns = slice(first_column, first_column + part)
    ref[entry, first_row : first_row + plain + 2, columns] = folded[index, : plain + 2].astype(LOW)
    columns = slice(first_column, first_column + block)
    for half, rows in enumerate(unit_rows):
        row = first_row + plain + 2 + half
        ref[entry, row : row + 1, columns] = rows[index : index + 1].astype(LOW)


def half_rows(ref, layout):
    per = layout.chunks // 2
    return [
        jnp.concatenate([ref[half * per + i] for i in range(per)], 1) for half in range(2)
    ]


def value_grads(
    order,
    count,
    place_ref,
    x_ref,
    mixed_ref,
    attended_ref,
    dv0_ref,
    dv1_ref,
    skip_ref,
    attn_from,
    keep_ref,
    send_ref,
    grad_x_ref,
    sum_ref,
    attn_ref,
    arrived,
):
    load = pltpu.make_async_copy(attn_from.at[2], attn_ref, arrived)
    load.start()
    x, low, high = x_ref[...], dv0_ref[...], dv1_ref[...]
    half = low.shape[1]
    share = x.shape[1] // count
    every = slice(None)
    both = jnp.concatenate([tn(x, low), tn(x, high)], 1)
    part_rows(keep_ref, send_ref, 0, every, both, place_ref, order, count)
    both = tn(mixed_ref[...], attended_ref[...])
    part_rows(keep_ref, send_ref, share, every, both, place_ref, order, count)
    sum_ref[:, :half] = jnp.sum(low.astype(FULL), 0, keepdims=True)
    sum_ref[:, half:] = jnp.sum(high.astype(FULL), 0, keepdims=True)
    load.wait()
    grad_x_ref[...] = skip_ref[...] + nn(low, attn_ref[:half]) + nn(high, attn_ref[half:])


def query_key_grads(
    layout,
    order_a,
    order_b,
    head_order,
    heads_here,
    memory_rows,
    place_ref,
    x_ref,
    dq0_ref,
    dq1_ref,
    dk0_ref,
    dk1_ref,
    part_ref,
    value_sum_ref,
    layer_sum_ref,
    bias_sum_ref,
    attn_from,
    keep_ref,
    send_ref,
    grad_x_ref,
    rows_ref,
    attn_ref,
    arrived,
):
    loads = [
        pltpu.make_async_copy(attn_from.at[i], attn_ref.at[i], arrived.at[i]) for i in range(2)
    ]
    for load in loads:
        load.start()
    count = layout.dps
    x = x_ref[...]
    half = dq0_ref.shape[1]
    share = x.shape[1] // count
    pairs = [(dq0_ref[...], dq1_ref[...]), (dk0_ref[...], dk1_ref[...])]
    for m, (low, high) in enumerate(pairs):
        both = jnp.concatenate([tn(x, low), tn(x, high)], 1)
        part_rows(keep_ref, send_ref, m * share, slice(None), both, place_ref, order_a, count)
    plain = len(SUMS) + memory_rows
    rows_ref[...] = jnp.zeros_like(rows_ref)
    rows_ref[: len(SUMS), :] = layer_sum_ref[: len(SUMS), :]
    for at, array in zip((0, half), pairs[0]):
        rows_ref[plain : plain + 1, at : at + half] = jnp.sum(array.astype(FULL), 0, keepdims=True)
    rows_ref[plain + 1 : plain + 2, :] = value_sum_ref[...]
    packed = pack_sums(
        layout,
        order_a,
        order_b,
        head_order,
        heads_here,
        memory_rows,
        place_ref,
        layout.heads,
        rows_ref[...],
        half_rows(bias_sum_ref, layout),
    )
    here = x.shape[1] // layout.heads
    for at in range(count):
        ref = keep_ref if at < count // 2 else send_ref
        entry = at % (count // 2)
        ref[entry, 2 * share :, :] = jnp.zeros((SUM_ROWS, x.shape[1]), LOW)
        for g in range(layout.heads):
            index = at * layout.heads + g
            put_sums(ref, entry, 2 * share, g * here, packed, index, memory_rows)
    total = part_ref[...]
    for m, (low, high) in enumerate(pairs):
        loads[m].wait()
        total = total + nn(low, attn_ref[m, :half]) + nn(high, attn_ref[m, half:])
    grad_x_ref[...] = total.astype(LOW)


def own_grads(
    layout,
    order_a,
    order_b,
    head_order,
    heads,
    heads_here,
    memory_rows,
    place_ref,
    score_ref,
    soft_ref,
    qkv_ref,
    attended_grad_ref,
    mixed_ref,
    attended_ref,
    small_ref,
    read_ref,
    token_ref,
    bias_grad_ref,
    vec_grad_ref,
    init_grad_ref,
    keep_ref,
    send_ref,
    rows_ref,
):
    count = layout.dps
    writes, rows, _ = score_ref.shape
    width = qkv_ref.shape[-1]
    here = width // heads * heads_here
    mine = heads_here * PAD
    mask = head_mask(rows, width, heads)[:mine]
    total = jnp.zeros((1, here), FULL)
    grads = [jnp.zeros((width, here), FULL) for _ in range(4)]
    for s in range(writes + 1):
        low = read_ref[s].astype(LOW)
        grads[1] = grads[1] + 2.0 * tn(low, small_ref[s, 1, :, :here])
        grads[2] = grads[2] + 2.0 * tn(low, small_ref[s, 2, :, :here])
        if s == writes:
            break
        grads[0] = grads[0] + tn(low, small_ref[s, 0, :, :here])
        grads[3] = grads[3] + tn(mixed_ref[s], attended_ref[s, :, :here])
        spread = by_head(qkv_ref[s, 0], mask, heads_here)[:, :here]
        pulled = by_head(attended_grad_ref[s], mask, heads_here)[:, :here]
        dk = (SCALE * tn(score_ref[s, :mine], spread)).astype(LOW)
        dv = tn(soft_ref[s, :mine].astype(LOW), pulled).astype(LOW)
        grads[1] = grads[1] + tn(token_ref[s], dk)
        grads[2] = grads[2] + tn(token_ref[s], dv)
        total = total + jnp.sum(dv.astype(FULL), 0, keepdims=True)
    both = jnp.concatenate(grads, 1)
    part_rows(keep_ref, send_ref, 0, slice(None), both, place_ref, order_a, count)
    rows_ref[...] = jnp.zeros_like(rows_ref)
    for i, name in enumerate(SUMS):
        at = VECTORS.index(name)
        rows_ref[i : i + 1, :] = vec_grad_ref[at : at + 1, :]
    for i in range(memory_rows):
        at = len(SUMS) + i
        rows_ref[at : at + 1, :] = init_grad_ref[i : i + 1, :]
    at = len(SUMS) + memory_rows
    rows_ref[at : at + 2, :] = vec_grad_ref[0:2, :]
    rows_ref[at + 1 : at + 2, :here] += total
    packed = pack_sums(
        layout,
        order_a,
        order_b,
        head_order,
        heads_here,
        memory_rows,
        place_ref,
        1,
        rows_ref[...],
        half_rows(bias_grad_ref, layout),
    )
    share = width // count
    for at in range(count):
        ref = keep_ref if at < count // 2 else send_ref
        entry = at % (count // 2)
        ref[entry, share:, :] = jnp.zeros((SUM_ROWS, width), LOW)
        put_sums(ref, entry, share, 0, packed, at, memory_rows)


def write_rows(
    heads,
    quarter,
    place_ref,
    score_ref,
    soft_ref,
    qkv_ref,
    attended_grad_ref,
    moved_ref,
    attn_from,
    grad_token_ref,
    attn_ref,
    arrived,
):
    writes, rows, _ = score_ref.shape
    loads = [
        pltpu.make_async_copy(attn_from.at[i + 1], attn_ref.at[i], arrived.at[i])
        for i in range(2)
    ]
    for load in loads:
        load.start()
    mask = head_mask(rows, qkv_ref.shape[-1], heads)
    at = pl.multiple_of(place_ref[1] * quarter, quarter)
    for load in loads:
        load.wait()
    for s in range(writes):
        spread = by_head(qkv_ref[s, 0], mask, heads)
        pulled = by_head(attended_grad_ref[s], mask, heads)
        score_here = score_ref[s, :, pl.ds(at, quarter)]
        soft_here = soft_ref[s, :, pl.ds(at, quarter)].astype(LOW)
        dk = (SCALE * tn(score_here, spread)).astype(LOW)
        dv = tn(soft_here, pulled).astype(LOW)
        extra = nn(dk, attn_ref[0]) + nn(dv, attn_ref[1])
        grad_token_ref[s] = moved_ref[s].astype(FULL) + extra
    grad_token_ref[writes] = moved_ref[writes].astype(FULL)


def finish(
    order_a,
    order_b,
    memory_rows,
    numbers,
    *refs,
):
    groups = []
    for number in numbers:
        groups.append(refs[:number])
        refs = refs[number:]
    factor_refs, *groups = groups

    def total_of(group, *at):
        total = group[0][(0, *at)].astype(FULL)
        for ref in group[1:]:
            total = total + ref[(0, *at)].astype(FULL)
        return total

    ffn_a, ffn_b, attn_terms, own_terms = groups
    (
    query_ref,
    key_ref,
    value_ref,
    b_query_ref,
    b_value_ref,
    out_ref,
    b_out_ref,
    gain_attn_ref,
    shift_attn_ref,
    up_ref,
    b_in_ref,
    down_ref,
    b_down_ref,
    gain_ffn_ref,
    shift_ffn_ref,
    init_ref,
    ) = refs
    factor = jnp.concatenate([ref[...] for ref in factor_refs], 0)
    count, _, rows, width = factor.shape
    block = width // 2 // count
    column = lax.broadcasted_iota(jnp.int32, (rows, width), 1)

    def own(j, i):
        first, second = position(j, order_a), position(j, order_b) + count
        keep = (column // block == first) | (column // block == second)
        return jnp.where(keep, factor[j, i], jnp.zeros((), LOW))

    units = []
    for side, left, right in ((0, 3, 0), (1, 2, 1)):
        chosen = jnp.concatenate([own(j, left) for j in range(count)], 0)
        others = jnp.concatenate([factor[j, right] for j in range(count)], 0)
        product = tn(chosen, others)
        halves = []
        for i in range(2):
            total = total_of((ffn_a, ffn_b)[i], side)
            for j in range(count):
                at = (i * count + j) * block
                total = total + product[at : at + block]
            halves.append(total)
        units.append(jnp.concatenate(halves, 0))
    up_ref[...] = units[0]
    down_ref[...] = units[1]
    attn, own_total = total_of(attn_terms), total_of(own_terms)
    here = attn.shape[-1] // 2
    share = own_total.shape[0] - SUM_ROWS
    totals = []
    for m in range(4):
        row, column = m % 2 * share, m // 2 * here
        from_tokens = attn[row : row + share, column : column + here]
        totals.append(from_tokens + own_total[:share, m * here : (m + 1) * here])
    query_ref[...] = totals[0]
    key_ref[...] = totals[1]
    value_ref[...] = totals[2]
    out_ref[...] = totals[3].T
    pack = attn[2 * share : 2 * share + SUM_ROWS, :here] + own_total[share:, :here]
    refs = {
        "b_out": b_out_ref,
        "gain_attn": gain_attn_ref,
        "shift_attn": shift_attn_ref,
        "b_down": b_down_ref,
        "gain_ffn": gain_ffn_ref,
        "shift_ffn": shift_ffn_ref,
    }
    part = init_ref.shape[1]
    for i, name in enumerate(SUMS):
        refs[name][...] = pack[i : i + 1, :part]
    at = len(SUMS) + memory_rows
    init_ref[...] = pack[len(SUMS) : at, :part]
    heads_here, head_part = b_query_ref.shape
    for i in range(heads_here):
        columns = slice(i * head_part, (i + 1) * head_part)
        b_query_ref[i : i + 1, :] = pack[at : at + 1, columns]
        b_value_ref[i : i + 1, :] = pack[at + 1 : at + 2, columns]
    b_in_ref[:, :block] = pack[at + 2 : at + 3, :block]
    b_in_ref[:, block:] = pack[at + 3 : at + 4, :block]


def columns_of(head, head_dim, array, factor=None):
    lane = lax.broadcasted_iota(jnp.int32, array.shape, 1) // head_dim
    if factor is not None:
        array = array * jnp.asarray(factor, array.dtype)
    return jnp.where(lane == head, array, jnp.zeros((), array.dtype))


def memory_scores(memory_rows, km, mine):
    scores = nt(km, mine)
    real_key = lax.broadcasted_iota(jnp.int32, scores.shape, 0) < memory_rows
    return jnp.where(real_key, scores, NEGATIVE)


def token_attention(head_dim, place_ref, row_ref, column_ref, q_ref, k_ref, v_ref, sum_ref, stat_ref):
    q, k, v = q_ref[...], k_ref[...], v_ref[...]
    allowed = column_ref[...] == row_ref[...]
    stat_ref[...] = jnp.zeros_like(stat_ref)
    for head in range(q.shape[1] // head_dim):
        scores = nt(k, columns_of(head, head_dim, q, SCALE))
        scores = jnp.where(allowed, scores, NEGATIVE)
        top = jnp.max(scores, 0, keepdims=True)
        raised = jnp.exp(scores - top)
        stat_ref[0, 2 * head : 2 * head + 1] = top
        stat_ref[0, 2 * head + 1 : 2 * head + 2] = jnp.sum(raised, 0, keepdims=True)
        rows = slice(head * head_dim, (head + 1) * head_dim)
        sum_ref[0, rows] = tn(v, raised.astype(LOW))[rows]


def with_memory(memory_rows, head_dim, q, km, vm, sums, stats):
    mixed, logs = [], []
    for head in range(q.shape[1] // head_dim):
        scores = memory_scores(memory_rows, km, columns_of(head, head_dim, q, SCALE))
        top_before = stats[2 * head : 2 * head + 1]
        top = jnp.maximum(jnp.max(scores, 0, keepdims=True), top_before)
        raised = jnp.exp(scores - top)
        shrink = jnp.exp(top_before - top)
        total = stats[2 * head + 1 : 2 * head + 2] * shrink
        total = total + 2.0 * jnp.sum(raised, 0, keepdims=True)
        rows = slice(head * head_dim, (head + 1) * head_dim)
        both = sums[rows] * shrink + 2.0 * tn(vm, raised.astype(LOW))[rows]
        mixed.append(both * (1.0 / total))
        logs.append(top + jnp.log(total))
    return jnp.concatenate(mixed, 0).T.astype(LOW), logs


def token_attention_back(
    memory_rows,
    head_dim,
    place_ref,
    row_ref,
    column_ref,
    q_ref,
    k_ref,
    v_ref,
    qkv_ref,
    log_ref,
    grad_ref,
    dq_ref,
    dk_ref,
    dv_ref,
    dmem_ref,
):
    q, k, v, grad = (ref[...] for ref in (q_ref, k_ref, v_ref, grad_ref))
    km, vm = qkv_ref[place_ref[1], 1], qkv_ref[place_ref[1], 2]
    allowed = column_ref[...] == row_ref[...]
    lane = lax.broadcasted_iota(jnp.int32, q.shape, 1) // head_dim
    dq, dk, dv = (jnp.zeros(q.shape, FULL) for _ in range(3))
    dkm, dvm = (jnp.zeros(km.shape, FULL) for _ in range(2))
    for head in range(q.shape[1] // head_dim):
        mine = columns_of(head, head_dim, q, SCALE)
        mine_grad = columns_of(head, head_dim, grad)
        log_total = log_ref[0, head : head + 1]
        scores = jnp.where(allowed, nt(k, mine), NEGATIVE)
        soft = jnp.exp(scores - log_total)
        soft_mem = jnp.exp(memory_scores(memory_rows, km, mine) - log_total)
        pull, pull_mem = nt(v, mine_grad), nt(vm, mine_grad)
        inner = jnp.sum(soft * pull, 0, keepdims=True) + 2.0 * jnp.sum(
            soft_mem * pull_mem, 0, keepdims=True
        )
        score = (soft * (pull - inner)).astype(LOW)
        score_mem = (soft_mem * (pull_mem - inner)).astype(LOW)
        dq = jnp.where(lane == head, tn(score, k) + 2.0 * tn(score_mem, km), dq)
        dk = dk + nn(score, mine)
        dv = dv + nn(soft.astype(LOW), mine_grad)
        dkm = dkm + nn(score_mem, mine)
        dvm = dvm + nn(soft_mem.astype(LOW), mine_grad)
    dq_ref[...] = (SCALE * dq).astype(LOW)
    dk_ref[...] = dk.astype(LOW)
    dv_ref[...] = dv.astype(LOW)
    dmem_ref[:PAD] = dkm
    dmem_ref[PAD:] = dvm


def head_pairs(body, place, doc, operands, shapes, width, flops, steps, first=0):
    seg_len = operands[0].shape[0]

    def spec(array, first):
        if len(array.shape) == 4:
            return pl.BlockSpec((*array.shape[:3], width), lambda i: (0, 0, 0, i + first))
        if len(array.shape) == 3:
            return pl.BlockSpec((1, *array.shape[1:]), lambda i: (i + first, 0, 0))
        return pl.BlockSpec((array.shape[0], width), lambda i: (0, i + first))

    return pl.pallas_call(
        body,
        grid=(steps,),
        out_shape=shapes,
        in_specs=[pl.BlockSpec(memory_space=pltpu.SMEM)]
        + [pl.BlockSpec(a.shape, lambda i: (0, 0)) for a in doc]
        + [spec(a, first) for a in operands],
        out_specs=[spec(s, 0) for s in shapes],
        compiler_params=pltpu.CompilerParams(vmem_limit_bytes=VMEM_LIMIT),
        cost_estimate=pl.CostEstimate(
            flops=flops // 1000, bytes_accessed=seg_len, transcendentals=0
        ),
    )(place, *doc, *operands)


def on_device(
    tokens,
    doc_ids,
    reset,
    mem_init,
    w_query,
    w_key,
    w_value,
    b_query,
    b_value,
    w_out,
    b_out,
    gain_attn,
    shift_attn,
    w_in,
    b_in,
    w_down,
    b_down,
    gain_ffn,
    shift_ffn,
    cotangent,
):
    chains, segments, seg_len, width = tokens.shape
    dps, groups = lax.axis_size("dp"), lax.axis_size("head")
    assert chains == 1 and segments == groups
    memory_rows = mem_init.shape[0]
    heads_here, head_dim = b_query.shape
    heads = heads_here * groups
    here = heads_here * head_dim
    units = w_in.shape[1]
    half_units = units // 2
    quarter = seg_len // groups
    dp, head = lax.axis_index("dp"), lax.axis_index("head")
    place = jnp.stack([dp, head])
    bits = bits_of(dps)
    levels = len(bits)
    order_a = bits[1:] + bits[:1]
    order_b = bits[1:][::-1] + bits[:1]
    head_order = bits_of(groups)[::-1]
    head_stages = [("head", bit) for bit in head_order]
    stages_a = head_stages + [("dp", bit) for bit in order_a]
    stages_b = head_stages + [("dp", bit) for bit in order_b]
    layout = Units(dps, groups, half_units, width)
    landing = layout.scratch()
    shape = jax.ShapeDtypeStruct
    dp_stages = [("dp", bit) for bit in bits]
    bias_groups = (head_stages[:1], dp_stages[1:], head_stages[1:] + dp_stages[:1])
    bias_stages = [stage for group in bias_groups for stage in group]
    tokens, doc_ids, cotangent = tokens[0], doc_ids[0], cotangent[0]

    shard = jnp.concatenate([w_query.T, w_key.T, w_value.T, w_out], 0)
    share = shard.shape[0] // dps
    chunk = lax.dynamic_slice_in_dim(shard, dp * share, share, 0)[None]
    biases = jnp.concatenate([b_query.reshape(-1), b_value.reshape(-1), b_in])[None]
    up = w_in.T.reshape(2, half_units, width)
    down = w_down.reshape(2, half_units, width)
    halves = [jnp.stack([up[i], down[i]])[None] for i in range(2)]
    for i, stage in enumerate(head_stages):
        chunk = gather(chunk, [stage])
        if i:
            halves = [gather(half, [head_stages[i - 1]]) for half in halves]
        biases = gather(biases, bias_groups[i])
        chunk, biases, halves = lax.optimization_barrier((chunk, biases, halves))
    halves = [gather(half, head_stages[-1:]) for half in halves]
    biases = gather(biases, bias_groups[2])
    chunk = jnp.stack([chunk[position(j, head_order)] for j in range(1, groups)])
    sides = (slice(0, share // 2), slice(share // 2, share))
    parts = []
    for rows, order in zip(sides, (order_a, order_b)):
        part = gather(chunk[None, :, rows], [("dp", bit) for bit in order[:-2]])
        parts += [part, swap(part, "dp", order[-2])]
    doc = lax.dynamic_index_in_dim(doc_ids, head, 0, False)
    doc_row, doc_column = doc[None, :], doc[:, None]
    init = jnp.pad(mem_init.astype(FULL), ((0, PAD - memory_rows), (0, 0)))
    vectors = jnp.concatenate([b_out, gain_attn, shift_attn, b_down, gain_ffn, shift_ffn])
    vectors = vectors.reshape(-1, width)
    halves, parts, biases, cotangent, doc_row, doc_column, init, vectors = (
        lax.optimization_barrier(
            (halves, parts, biases, cotangent, doc_row, doc_column, init, vectors)
        )
    )
    cotangent = lax.all_to_all(cotangent, "head", 0, 0, tiled=True).reshape(seg_len, width)
    crossed = [swap(part, "dp", bits[0]) for part in parts]
    parts = [*parts[:2], *crossed[:2], *parts[2:], *crossed[2:]]
    if layout.whole:
        chunks = []
        for i, order in ((0, order_a), (4, order_b)):
            part = jnp.concatenate(parts[i : i + 4], 0)
            native = [position(dp ^ c, order) for c in range(dps)]
            chunks.append(jnp.stack([lax.dynamic_index_in_dim(part, n, 0, False) for n in native]))
        others = jnp.concatenate(chunks, 2).transpose(1, 0, 2, 3).reshape(groups - 1, 4, here, width)
        own = shard.reshape(4, 1, here, width)
        attn_pieces = [
            jnp.concatenate([own, others.transpose(1, 0, 2, 3)], 1).reshape(4, width, width)
        ]
    else:
        attn_pieces = [shard.reshape(4, here, width), *parts]
    halves = [
        gather(half, stages[len(head_stages) : -2])
        for half, stages in zip(halves, (stages_a, stages_b))
    ]
    keys, values, x, q, k, v, vectors, bias_in, w_attn = whole_call(
        functools.partial(project, layout, bias_stages, order_a, order_b, head_order),
        (place,),
        (tokens, biases, vectors),
        attn_pieces,
        (shape(tokens.shape, LOW),) * 2
        + (shape((seg_len, width), LOW),) * 4
        + (shape((len(VECTORS), width), FULL), shape((layout.chunks, 1, layout.size), FULL)),
        6_000_000_000,
        (
            pltpu.VMEM((4, width, width), LOW),
            pltpu.SemaphoreType.DMA((4 + 2 * dps * groups,)),
            pltpu.SemaphoreType.DMA(()),
        ),
        (shape((4, width, width), LOW),),
    )

    pair = 2 * head_dim
    partial = head_pairs(
        functools.partial(token_attention, head_dim),
        place,
        (doc_row, doc_column),
        (q, k, v),
        (shape((width // pair, pair, seg_len), FULL), shape((width // pair, 8, seg_len), FULL)),
        pair,
        8_000_000_000,
        width // pair,
    )
    halves = lax.optimization_barrier(halves)
    other_halves = [
        swap(half, *stages[-2]) for half, stages in zip(halves, (stages_a, stages_b))
    ]
    other_halves, partial, keys, cotangent = lax.optimization_barrier(
        (other_halves, partial, keys, cotangent)
    )
    pieces = []
    for half, other, stages in zip(halves, other_halves, (stages_a, stages_b)):
        pieces += [half, other, swap(half, *stages[-1]), swap(other, *stages[-1])]
    if layout.whole:
        pieces = layout.assembled([jnp.concatenate(pieces[i : i + 4], 0) for i in (0, 4)])

    ff = layout.chunks * layout.size
    writes = segments - 1
    rows_shape = lambda kind: shape((writes, PAD, width), kind)
    tokens_scratch = lambda count: (
        pltpu.VMEM((4, width, width), LOW),
        pltpu.VMEM((count, seg_len, width), LOW),
        pltpu.VMEM((count, seg_len, width), LOW),
        pltpu.SemaphoreType.DMA((4,)),
        pltpu.SemaphoreType.DMA((count,)),
        pltpu.SemaphoreType.DMA((count,)),
    )
    read, qkv, soft, soft_mem, attended_w, z_attn_w, hidden_w, pre_w, z_ffn_w, norms = whole_call(
        functools.partial(chain_forward, layout, heads, memory_rows),
        (reset,),
        (init, bias_in, vectors),
        (w_attn, keys, values, *pieces),
        (
            shape((segments, PAD, width), FULL),
            shape((segments, 3, PAD, width), LOW),
            shape((writes, heads * PAD, seg_len), FULL),
            shape((writes, heads * PAD, PAD), FULL),
            rows_shape(LOW),
            rows_shape(FULL),
            rows_shape(LOW),
            shape((writes, PAD, ff), FULL),
            rows_shape(FULL),
            shape((1, 128), FULL),
        ),
        20_000_000_000,
        tokens_scratch(writes) + landing,
    )

    if layout.whole:
        grad_shapes = (shape((layout.chunks, 2, layout.size, width), LOW),)
    else:
        grad_shapes = (shape((layout.blocks // 2, 2, half_units, width), LOW),) * 4
    sides = 2 * max(layout.size // (layout.size if layout.whole else half_units), 1)
    (
        attended,
        log_total,
        result,
        grad_attn,
        grad_mixed,
        grad_attended,
        bias_sum,
        layer_sums,
        *ffn_grads,
    ) = whole_call(
        functools.partial(token_layer, layout, memory_rows, head_dim),
        (place,),
        (x, q, qkv, *partial, cotangent, bias_in, vectors),
        (w_attn, *pieces),
        (
            shape((seg_len, width), LOW),
            shape((width // pair, 8, seg_len), FULL),
            shape((seg_len, width), LOW),
            shape((seg_len, width), FULL),
            shape((seg_len, width), LOW),
            shape((seg_len, width), LOW),
            shape((layout.chunks, 1, layout.size), FULL),
            shape((8, width), FULL),
        ),
        25_000_000_000,
        (pltpu.VMEM((width, width), LOW), pltpu.SemaphoreType.DMA(()))
        + landing
        + (
            pltpu.VMEM((seg_len, width), FULL),
            pltpu.VMEM((seg_len, width), LOW),
            pltpu.VMEM((seg_len, width), LOW),
            pltpu.VMEM((seg_len, width), FULL),
            pltpu.VMEM((layout.chunks, seg_len, layout.size), FULL),
            pltpu.VMEM((layout.chunks, seg_len, layout.size), LOW),
            pltpu.VMEM((2, 2, layout.size, width), LOW),
            pltpu.SemaphoreType.DMA((layout.chunks, sides)),
        ),
        grad_shapes,
    )
    if layout.whole:
        half_blocks = layout.blocks // 2
        ffn_grads = [
            part
            for half in layout.taken_apart(ffn_grads[0])
            for part in (half[:half_blocks], half[half_blocks:])
        ]

    back_a, back_b = stages_a[::-1], stages_b[::-1]

    def stages_of(level):
        return back_a[level], back_b[level]

    def attention_back(block, count):
        cut = width // 2
        return head_pairs(
            functools.partial(token_attention_back, memory_rows, head_dim),
            place,
            (doc_row, doc_column),
            (q, k, v, qkv, log_total, grad_attended),
            (shape((seg_len, cut), LOW),) * 3 + (shape((2 * PAD, cut), FULL),),
            pair,
            10_000_000_000,
            count,
            block * count,
        )

    blocks = width // pair // 2
    moving = [
        [keep, swap(send, *back[0])]
        for keep, send, back in zip(ffn_grads[::2], ffn_grads[1::2], (back_a, back_b))
    ]
    back_low = attention_back(0, blocks)
    back_low, moving, grad_attended = lax.optimization_barrier((back_low, moving, grad_attended))
    output = lax.all_to_all(result.reshape(groups, quarter, width), "head", 0, 0, tiled=True)
    sends = parcels(moving)
    sends, grad_attended = lax.optimization_barrier((sends, grad_attended))
    moving = posted(moving, sends, stages_of(1))
    back_high = attention_back(1, blocks)
    token_part = jnp.concatenate([back_low[3], back_high[3]], 1)
    token_part, back_high = lax.optimization_barrier((token_part, back_high))
    token_parts = gather(token_part[None], head_stages[:1])
    share = width // dps
    rows_a, rows_b, rows_own = 2 * share + SUM_ROWS, 2 * share, share + SUM_ROWS
    keep_b, send_b, grad_x, value_sum = whole_call(
        functools.partial(value_grads, order_b, dps),
        (place,),
        (x, grad_mixed, attended, back_low[2], back_high[2], grad_attn),
        (w_attn,),
        (
            *(shape((dps // 2, rows_b, width), LOW),) * 2,
            shape((seg_len, width), FULL),
            shape((1, width), FULL),
        ),
        5_000_000_000,
        (pltpu.VMEM((width, width), LOW), pltpu.SemaphoreType.DMA(())),
    )
    down_a, down_b = ([("dp", bit) for bit in order[::-1]] for order in (order_a, order_b))
    grad_x, send_b, moving, token_parts, output = lax.optimization_barrier(
        (grad_x, send_b, moving, token_parts, output)
    )
    token_parts = gather(token_parts, head_stages[1:])
    other_b = swap(send_b, *down_b[0])
    sends = parcels(moving)
    sends, grad_x = lax.optimization_barrier((sends, grad_x))
    moving = posted(moving, sends, stages_of(2))
    for level in range(3, levels):
        moving = posted(moving, parcels(moving), stages_of(level))
    sum_scratch = (pltpu.VMEM((SUM_ROWS, width), FULL),)
    keep_a, send_a, grad_x = whole_call(
        functools.partial(
            query_key_grads, layout, order_a, order_b, head_order, heads_here, memory_rows
        ),
        (place,),
        (
            x,
            back_low[0],
            back_high[0],
            back_low[1],
            back_high[1],
            grad_x,
            value_sum,
            layer_sums,
            bias_sum,
        ),
        (w_attn,),
        (
            *(shape((dps // 2, rows_a, width), LOW),) * 2,
            shape((seg_len, width), LOW),
        ),
        10_000_000_000,
        sum_scratch + (pltpu.VMEM((2, width, width), LOW), pltpu.SemaphoreType.DMA((2,))),
    )

    def advance_both(parts, level):
        return [reduce_step(p, down[level]) for p, down in zip(parts, (down_a, down_b))]

    token_parts, send_a, other_b, grad_x, moving = lax.optimization_barrier(
        (token_parts, send_a, other_b, grad_x, moving)
    )
    attn_moving = [[keep_a, swap(send_a, *down_a[0])], [keep_b, other_b]]
    sends = parcels(moving, True)
    attn_moving, sends = lax.optimization_barrier((attn_moving, sends))
    others = swap(sends[0], *back_a[levels])
    sends = parcels(attn_moving)
    sends, grad_x, token_parts = lax.optimization_barrier((sends, grad_x, token_parts))
    attn_moving = posted(attn_moving, sends, (down_a[1], down_b[1]))
    moved = lax.all_to_all(grad_x.reshape(groups, quarter, width), "head", 0, 0, tiled=True)

    packed_rows = writes * memory_rows + (-writes * memory_rows) % PAD
    score_w, grad_attended_w, grad_mixed_w, small_w, factors, bias_w, vec_w, init_w, norms = whole_call(
        functools.partial(chain_backward, layout, head_order, heads, memory_rows),
        (reset, place),
        (
            bias_in,
            read,
            norms,
            vectors,
            qkv,
            soft,
            soft_mem,
            z_attn_w,
            pre_w,
            z_ffn_w,
            hidden_w,
            token_parts,
        ),
        (w_attn, keys, values, *pieces),
        (
            shape((writes, heads * PAD, seg_len), LOW),
            shape((writes, PAD, width), LOW),
            shape((writes, PAD, width), LOW),
            shape((segments, 3, PAD, width), LOW),
            shape((4, packed_rows, width), LOW),
            shape((layout.chunks, 1, layout.size), FULL),
            shape((len(VECTORS), width), FULL),
            shape((PAD, width), FULL),
            shape((1, 128), FULL),
        ),
        20_000_000_000,
        (
            pltpu.VMEM((writes, PAD, width), LOW),
            pltpu.VMEM((writes, PAD, ff), LOW),
            pltpu.VMEM((segments, 2 * PAD, width), FULL),
        )
        + tokens_scratch(segments)
        + landing,
    )
    score_w, factors, moving, others, attn_moving, moved = lax.optimization_barrier(
        (score_w, factors, moving, others, attn_moving, moved)
    )

    moving = [terms + [others[:, i]] for i, terms in enumerate(moving)]
    sends = parcels(moving + attn_moving, True)
    sends, score_w = lax.optimization_barrier((sends, score_w))
    others = swap(sends[0], *back_a[levels + 1])
    moving = [terms + [others[:, i]] for i, terms in enumerate(moving)]
    attn_moving = posted(attn_moving, sends[1:], (down_a[2], down_b[2]))
    for level in range(3, levels):
        attn_moving = advance_both(attn_moving, level)
    factors = gather(factors[None], [("dp", order_b[0])])
    keep_own, send_own = whole_call(
        functools.partial(
            own_grads, layout, order_a, order_b, head_order, heads, heads_here, memory_rows
        ),
        (place,),
        (
            score_w,
            soft,
            qkv,
            grad_attended_w,
            grad_mixed_w,
            attended_w,
            small_w,
            read,
            tokens,
            bias_w,
            vec_w,
            init_w,
        ),
        (),
        (shape((dps // 2, rows_own, width), LOW),) * 2,
        5_000_000_000,
        sum_scratch,
    )
    keep_own, send_own, attn_moving, factors, score_w, moving = lax.optimization_barrier(
        (keep_own, send_own, attn_moving, factors, score_w, moving)
    )
    own = [keep_own, swap(send_own, *down_a[0])]
    left, right = (summed(terms)[0] for terms in attn_moving)
    right = jnp.pad(right, ((0, SUM_ROWS), (0, 0)))
    both = [
        jnp.concatenate([part[:, g * here : (g + 1) * here] for part in (left, right)], 1)
        for g in range(groups)
    ]
    attn_moving = [jnp.stack([both[partner(i, head_stages, "head")] for i in range(groups)])]
    attn_send = summed(attn_moving, LOW, groups // 2)
    own_send = summed(own, LOW, own[-1].shape[0] // 2)
    attn_send, own_send, score_w = lax.optimization_barrier((attn_send, own_send, score_w))
    attn_moving = attn_moving + [swap(attn_send, "head", head_order[-1])]
    own = own + [swap(own_send, *down_a[1])]
    factors = gather(factors, [("dp", order_b[1])])
    for level in range(2, levels - 1):
        own = reduce_step(own, down_a[level])
    attn_send = summed(attn_moving, LOW, attn_moving[-1].shape[0] // 2)
    own_send = summed(own, LOW, own[-1].shape[0] // 2)
    attn_send, own_send, score_w = lax.optimization_barrier((attn_send, own_send, score_w))
    attn_moving = attn_moving + [swap(attn_send, "head", head_order[0])]
    own = own + [swap(own_send, *down_a[levels - 1])]
    factors = gather(factors, stages_b[len(head_stages) + 2 : -1])
    factors = [factors, swap(factors, *stages_b[-1])]
    (grad_tokens,) = whole_call(
        functools.partial(write_rows, heads, quarter),
        (place,),
        (score_w, soft, qkv, grad_attended_w, moved),
        (w_attn,),
        (shape((segments, quarter, width), FULL),),
        5_000_000_000,
        (pltpu.VMEM((2, width, width), LOW), pltpu.SemaphoreType.DMA((2,))),
    )
    grad_tokens, own, factors, attn_moving = lax.optimization_barrier(
        (grad_tokens, own, factors, attn_moving)
    )
    own, factors, attn_moving, moving = lax.optimization_barrier(
        (own, factors, attn_moving, moving)
    )
    part = width // dps // groups
    row = shape((1, part), FULL)
    groups_in = [factors, *moving, attn_moving, own]
    first_entry = lambda array: pl.BlockSpec(
        (1, *array.shape[1:]), lambda i: (0,) * len(array.shape)
    )
    whole = lambda array: pl.BlockSpec(array.shape, lambda i: (0,) * len(array.shape))
    shapes = (
        *(shape((share, here), FULL),) * 3,
        *(shape((heads_here, head_dim // dps), FULL),) * 2,
        shape((here, share), FULL),
        *(row,) * 3,
        shape((units, width), FULL),
        shape((1, units), FULL),
        shape((units, width), FULL),
        *(row,) * 3,
        shape((memory_rows, part), FULL),
    )
    outs = pl.pallas_call(
        functools.partial(
            finish,
            order_in(order_a, order_b),
            order_in(order_b, order_b),
            memory_rows,
            [len(group) for group in groups_in],
        ),
        grid=(1,),
        out_shape=shapes,
        in_specs=[whole(a) for a in factors]
        + [first_entry(a) for group in groups_in[1:] for a in group],
        out_specs=[whole(a) for a in shapes],
        compiler_params=pltpu.CompilerParams(vmem_limit_bytes=VMEM_LIMIT),
        cost_estimate=pl.CostEstimate(flops=1000, bytes_accessed=1000, transcendentals=0),
    )(*(a for group in groups_in for a in group))
    flat = (6, 7, 8, 10, 12, 13, 14)
    outs = [out.reshape(-1) if i in flat else out for i, out in enumerate(outs)]
    outs[9] = outs[9].T
    return (output[None], norms[:, :segments], grad_tokens[None], *outs)


def solution(mesh):
    in_specs = (
        P("dp", None, None, None),
        P("dp", None, None),
        P("dp", None),
        P(),
        P(None, "head"),
        P(None, "head"),
        P(None, "head"),
        P("head", None),
        P("head", None),
        P("head", None),
        P(),
        P(),
        P(),
        P(None, ("dp", "head")),
        P(("dp", "head")),
        P(("dp", "head"), None),
        P(),
        P(),
        P(),
        P("dp", None, "head", None),
    )
    out_specs = (
        P("dp", None, "head", None),
        P("dp", None),
        P("dp", None, "head", None),
        P("dp", "head"),
        P("dp", "head"),
        P("dp", "head"),
        P("head", "dp"),
        P("head", "dp"),
        P("head", "dp"),
        P(("dp", "head")),
        P(("dp", "head")),
        P(("dp", "head")),
        P(None, ("dp", "head")),
        P(("dp", "head")),
        P(("dp", "head"), None),
        P(("dp", "head")),
        P(("dp", "head")),
        P(("dp", "head")),
        P(None, ("dp", "head")),
    )
    return jax.shard_map(
        on_device, mesh=mesh, in_specs=in_specs, out_specs=out_specs, check_vma=False
    )
```

```python
import functools

import jax
import jax.numpy as jnp
from jax import lax
from jax.experimental import pallas as pl
from jax.experimental.pallas import tpu as pltpu
from jax.sharding import PartitionSpec as P

EPSILON = 1e-06
SCALE = 0.125
NEGATIVE = -1e30
ROOT_HALF = 0.7071067811865476
DENSITY = 0.3989422804014327
LOW = jnp.bfloat16
FULL = jnp.float32
PAD = 16
VECTORS = ("b_query", "b_value", "b_out", "gain_attn", "shift_attn", "b_down", "gain_ffn", "shift_ffn")
VMEM_LIMIT = 60 * 1024 * 1024


def nn(left, right):
    return lax.dot_general(left, right, (((1,), (0,)), ((), ())), preferred_element_type=FULL)


def nt(left, right):
    return lax.dot_general(left, right, (((1,), (1,)), ((), ())), preferred_element_type=FULL)


def tn(left, right):
    return lax.dot_general(left, right, (((0,), (0,)), ((), ())), preferred_element_type=FULL)


def norm_parts(rows):
    centred = rows - jnp.mean(rows, -1, keepdims=True)
    inverse = lax.rsqrt(jnp.mean(centred * centred, -1, keepdims=True) + EPSILON)
    return centred * inverse, inverse


def norm_pull(normed, inverse, grad):
    along = jnp.mean(grad * normed, -1, keepdims=True)
    return inverse * (grad - jnp.mean(grad, -1, keepdims=True) - normed * along)


def gelu(v):
    return 0.5 * v * (1.0 + lax.erf(v * ROOT_HALF))


def gelu_slope(v):
    return 0.5 * (1.0 + lax.erf(v * ROOT_HALF)) + v * (DENSITY * jnp.exp(-0.5 * v * v))


def swap(array, axis, bit):
    return lax.ppermute(array, axis, [(i, i ^ bit) for i in range(lax.axis_size(axis))])


def bits_of(count):
    return [1 << i for i in range(count.bit_length() - 1)]


def gather(array, stages):
    for axis, bit in stages:
        array = jnp.concatenate([array, swap(array, axis, bit)], 0)
    return array


def summed(terms, kind=LOW, first=0):
    size = terms[-1].shape[0] - first
    total = terms[0][first : first + size].astype(FULL)
    for term in terms[1:]:
        total = total + term[first : first + size].astype(FULL)
    return total.astype(kind)


def add_up(count, together, *refs):
    out_refs = list(refs[sum(count) :])
    pair_ref = None
    if together:
        pair_ref = out_refs[0]
        out_refs = [None, None] + out_refs[1:]
    at = 0
    for number_of, (number, out_ref) in enumerate(zip(count, out_refs)):
        total = refs[at][...].astype(FULL)
        for ref in refs[at + 1 : at + number]:
            total = total + ref[...].astype(FULL)
        total = total.astype(refs[at].dtype)
        at += number
        if pair_ref is not None and number_of < 2:
            pair_ref[:, number_of] = total
        else:
            out_ref[...] = total


def parcels(groups, together=False):
    halves = [terms[-1].shape[0] // 2 for terms in groups]
    steps = min(min(halves), 4)
    in_specs, operands, out_specs, shapes = [], [], [], []

    def spec(half, rest, first):
        index = lambda i: (first + i,) + (0,) * len(rest)
        return pl.BlockSpec((half // steps, *rest), index)

    for half, terms in zip(halves, groups):
        rest = terms[0].shape[1:]
        in_specs += [spec(half, rest, steps)] * len(terms)
        operands += terms
        if together and len(operands) < len(groups[0]) + len(groups[1]) + 1:
            if len(shapes):
                continue
            rest = (2, *rest)
        out_specs.append(spec(half, rest, 0))
        shapes.append(jax.ShapeDtypeStruct((half, *rest), terms[0].dtype))
    return pl.pallas_call(
        functools.partial(add_up, [len(terms) for terms in groups], together),
        grid=(steps,),
        out_shape=shapes,
        in_specs=in_specs,
        out_specs=out_specs,
        compiler_params=pltpu.CompilerParams(vmem_limit_bytes=VMEM_LIMIT),
        cost_estimate=pl.CostEstimate(flops=1000, bytes_accessed=1000, transcendentals=0),
    )(*operands)


def posted(groups, sends, stages):
    return [
        terms + [swap(send, *stage)] for terms, send, stage in zip(groups, sends, stages)
    ]


def reduce_step(terms, stage):
    half = terms[-1].shape[0] // 2
    return terms + [swap(summed(terms, terms[0].dtype, half), *stage)]


def partner(index, stages, axis):
    place = 0
    for k, (name, bit) in enumerate(stages):
        if name == axis:
            place = place + ((index >> k) & 1) * bit
    return place


def position(partner_bits, order):
    place = 0
    for k, bit in enumerate(order):
        place = place + ((partner_bits // bit) % 2) * (1 << k)
    return place


def order_in(order, index_order):
    return [1 << index_order.index(bit) for bit in order]


def head_mask(rows, width, heads):
    group = lax.broadcasted_iota(jnp.int32, (rows, width), 0) // PAD
    column = lax.broadcasted_iota(jnp.int32, (rows, width), 1) // (width // heads)
    return group == column


def by_head(rows, mask, heads):
    return jnp.where(mask, jnp.concatenate([rows] * heads, 0), jnp.zeros((), rows.dtype))


def own_head(rows, mask, heads):
    kept = jnp.where(mask, rows, 0.0)
    total = kept[:PAD]
    for i in range(1, heads):
        total = total + kept[i * PAD : (i + 1) * PAD]
    return total


def vector(vec_ref, name):
    i = VECTORS.index(name)
    return vec_ref[i : i + 1, :]


class Units:
    def __init__(self, dps, heads, rows, width):
        self.dps, self.heads, self.rows, self.width = dps, heads, rows, width
        self.blocks = dps * heads
        self.chunks = max(2 * self.blocks * rows // width, 4)
        self.size = 2 * self.blocks * rows // self.chunks
        self.whole = rows % 16 != 0

    def at(self, index):
        return (index % self.heads) * self.dps + index // self.heads

    def pieces(self):
        if self.whole:
            return [(0, self.chunks)]
        part = self.blocks // 8
        return [(half * self.blocks + p * part, part) for half in range(2) for p in range(8)]

    def copies(self):
        for number, (first, count) in enumerate(self.pieces()):
            for entry in range(count):
                if self.whole:
                    yield number, entry, entry, 0, self.size
                    continue
                half, index = divmod(first + entry, self.blocks)
                row = (half * self.blocks + self.at(index)) * self.rows
                yield number, entry, row // self.size, row % self.size, self.rows

    def scratch(self):
        buffer = pltpu.VMEM((self.chunks, self.size, self.width), LOW)
        count = sum(2 for _ in self.copies())
        return (buffer, buffer, pltpu.SemaphoreType.DMA((count,)))

    def loads(self, pieces, up_ref, down_ref, arrived):
        made = []
        for number, entry, chunk, row, rows in self.copies():
            for side, to_ref in enumerate((up_ref, down_ref)):
                made.append(
                    pltpu.make_async_copy(
                        pieces[number].at[entry, side],
                        to_ref.at[chunk, pl.ds(row, rows)],
                        arrived.at[len(made)],
                    )
                )
        return made[::2], made[1::2]

    def assembled(self, halves):
        rows = []
        for array in halves:
            array = array.reshape(self.dps, self.heads, 2, self.rows, self.width)
            rows.append(array.transpose(1, 0, 3, 2, 4).reshape(-1, 2, self.width))
        rows = jnp.concatenate(rows, 0).reshape(self.chunks, self.size, 2, self.width)
        return [rows.transpose(0, 2, 1, 3)]

    def taken_apart(self, piece):
        rows = piece.transpose(0, 2, 1, 3).reshape(2, self.heads, self.dps, self.rows, 2, -1)
        rows = rows.transpose(0, 2, 1, 4, 3, 5)
        return [half.reshape(self.blocks, 2, self.rows, self.width) for half in rows]


def head_groups(ref, flip):
    value = ref[...]
    half = value.shape[1] // 2
    low, high = value[:, :half], value[:, half:]
    if flip & 2:
        low, high = high, low
    if flip & 1:
        low, high = pltpu.roll(low, half // 2, 1), pltpu.roll(high, half // 2, 1)
    return jnp.concatenate([low, high], 1)


def memory_queries(read, attn_ref, vec_ref):
    low = read.astype(LOW)
    queries = (nt(low, attn_ref[0]) + vector(vec_ref, "b_query")).astype(LOW)
    keys = nt(low, attn_ref[1]).astype(LOW)
    values = (nt(low, attn_ref[2]) + vector(vec_ref, "b_value")).astype(LOW)
    return queries, keys, values


def memory_attention(heads, memory_rows, queries, keys, values, key_low, value_low):
    rows, width = heads * PAD, queries.shape[1]
    mask = head_mask(rows, width, heads)
    real_key = lax.broadcasted_iota(jnp.int32, (rows, PAD), 1) < memory_rows
    spread = by_head(queries, mask, heads)
    scores = nt(spread, key_low) * SCALE
    scores_mem = jnp.where(real_key, nt(spread, keys) * SCALE, NEGATIVE)
    top = jnp.maximum(jnp.max(scores, -1, keepdims=True), jnp.max(scores_mem, -1, keepdims=True))
    raised = jnp.exp(scores - top)
    raised_mem = jnp.exp(scores_mem - top)
    total = jnp.sum(raised, -1, keepdims=True) + 2.0 * jnp.sum(raised_mem, -1, keepdims=True)
    soft = raised / total
    soft_mem = raised_mem / total
    mixed = nn(soft.astype(LOW), value_low) + 2.0 * nn(soft_mem.astype(LOW), values)
    return own_head(mixed, mask, heads).astype(LOW), soft, soft_mem


def memory_norm(result, memory_rows):
    real_row = lax.broadcasted_iota(jnp.int32, result.shape, 0) < memory_rows
    square = jnp.sum(jnp.where(real_row, result * result, 0.0), axis=(0, 1), keepdims=True)
    return jnp.sqrt(square / (memory_rows * result.shape[1]))


def chain_forward(
    layout,
    heads,
    memory_rows,
    reset_ref,
    init_ref,
    bias_ref,
    vec_ref,
    attn_from,
    key_from,
    value_from,
    *refs,
):
    count = len(layout.pieces())
    pieces, refs = refs[:count], refs[count:]
    (
        read_ref,
        qkv_ref,
        soft_ref,
        soft_mem_ref,
        attended_ref,
        z_attn_ref,
        hidden_ref,
        pre_ref,
        z_ffn_ref,
        norm_ref,
        attn_ref,
        key_ref,
        value_ref,
        attn_arrived,
        key_arrived,
        value_arrived,
        up_ref,
        down_ref,
        arrived,
    ) = refs
    last = key_ref.shape[0]
    attn_loads = [
        pltpu.make_async_copy(attn_from.at[i], attn_ref.at[i], attn_arrived.at[i])
        for i in range(4)
    ]

    def token_loads(s):
        return [
            pltpu.make_async_copy(key_from.at[s], key_ref.at[s], key_arrived.at[s]),
            pltpu.make_async_copy(value_from.at[s], value_ref.at[s], value_arrived.at[s]),
        ]

    up_loads, down_loads = layout.loads(pieces, up_ref, down_ref, arrived)
    for load in attn_loads[:3] + token_loads(0) + attn_loads[3:] + up_loads + down_loads:
        load.start()
    for s in range(1, last):
        for load in token_loads(s):
            load.start()
    chunks, size, _ = up_ref.shape
    norm_ref[...] = jnp.zeros_like(norm_ref)
    for load in attn_loads[:3]:
        load.wait()

    def enter(s, carried):
        fresh = (reset_ref[0, s] > 0) | (s == 0)
        read = jnp.where(fresh, init_ref[...], carried)
        read_ref[s] = read
        queries, keys, values = memory_queries(read, attn_ref, vec_ref)
        qkv_ref[s, 0] = queries
        qkv_ref[s, 1] = keys
        qkv_ref[s, 2] = values
        return read, queries, keys, values

    def step(s, carried):
        read, queries, keys, values = enter(s, carried)
        for load in token_loads(s):
            load.wait()
        attended, soft, soft_mem = memory_attention(
            heads, memory_rows, queries, keys, values, key_ref[s], value_ref[s]
        )
        soft_ref[s] = soft
        soft_mem_ref[s] = soft_mem
        attended_ref[s] = attended

        if s == 0:
            attn_loads[3].wait()
        z_attn = read + nn(attended, attn_ref[3]) + vector(vec_ref, "b_out")
        z_attn_ref[s] = z_attn
        normed, _ = norm_parts(z_attn)
        hidden = normed * vector(vec_ref, "gain_attn") + vector(vec_ref, "shift_attn")
        hidden_low = hidden.astype(LOW)
        hidden_ref[s] = hidden_low
        z_ffn = hidden + vector(vec_ref, "b_down")

        if s == 0:
            for load in up_loads:
                load.wait()
        acts = []
        for i in range(chunks):
            pre = nt(hidden_low, up_ref[i]) + bias_ref[i]
            pre_ref[s, :, i * size : (i + 1) * size] = pre
            acts.append(gelu(pre).astype(LOW))
        if s == 0:
            for load in down_loads:
                load.wait()
        for i in range(chunks):
            z_ffn = z_ffn + nn(acts[i], down_ref[i])
        z_ffn_ref[s] = z_ffn
        normed, _ = norm_parts(z_ffn)
        result = normed * vector(vec_ref, "gain_ffn") + vector(vec_ref, "shift_ffn")
        lane = lax.broadcasted_iota(jnp.int32, norm_ref.shape, 1)
        norm_ref[...] = jnp.where(lane == s, memory_norm(result, memory_rows), norm_ref[...])
        return result

    carried = init_ref[...]
    for s in range(last):
        carried = step(s, carried)
    enter(last, carried)


def last_norm(heads, memory_rows, bias_ref, vec_ref, read, qkv, key, value, weights):
    out_w, up_ref, down_ref = weights
    attended, _, _ = memory_attention(heads, memory_rows, *qkv, key, value)
    z_attn = read + nn(attended, out_w) + vector(vec_ref, "b_out")
    normed, _ = norm_parts(z_attn)
    hidden = normed * vector(vec_ref, "gain_attn") + vector(vec_ref, "shift_attn")
    hidden_low = hidden.astype(LOW)
    z_ffn = hidden + vector(vec_ref, "b_down")
    for i in range(up_ref.shape[0]):
        pre = nt(hidden_low, up_ref[i]) + bias_ref[i]
        z_ffn = z_ffn + nn(gelu(pre).astype(LOW), down_ref[i])
    normed, _ = norm_parts(z_ffn)
    result = normed * vector(vec_ref, "gain_ffn") + vector(vec_ref, "shift_ffn")
    return memory_norm(result, memory_rows)


def chain_backward(
    layout,
    head_order,
    heads,
    memory_rows,
    reset_ref,
    place_ref,
    bias_ref,
    read_ref,
    norms_ref,
    vec_ref,
    qkv_ref,
    soft_ref,
    soft_mem_ref,
    z_attn_ref,
    pre_ref,
    z_ffn_ref,
    hidden_ref,
    *refs,
):
    segments, _, _, width = qkv_ref.shape
    part_ref, *refs = refs
    attn_from, key_from, value_from, *refs = refs
    count = len(layout.pieces())
    pieces, refs = refs[:count], refs[count:]
    (
        score_ref,
        attended_ref,
        mixed_ref,
        small_ref,
        factor_ref,
        bias_grad_ref,
        vec_grad_ref,
        init_grad_ref,
        norm_ref,
        ffn_ref,
        pre_grad_ref,
        token_part_ref,
        attn_ref,
        key_ref,
        value_ref,
        attn_arrived,
        key_arrived,
        value_arrived,
        up_ref,
        down_ref,
        arrived,
    ) = refs
    attn_loads = [
        pltpu.make_async_copy(attn_from.at[i], attn_ref.at[i], attn_arrived.at[i])
        for i in range(4)
    ]

    def token_loads(s):
        return [
            pltpu.make_async_copy(key_from.at[s], key_ref.at[s], key_arrived.at[s]),
            pltpu.make_async_copy(value_from.at[s], value_ref.at[s], value_arrived.at[s]),
        ]

    up_loads, down_loads = layout.loads(pieces, up_ref, down_ref, arrived)
    for load in attn_loads[1:3] + down_loads + up_loads + attn_loads[3:] + attn_loads[:1]:
        load.start()
    for s in (*range(segments - 2, -1, -1), segments - 1):
        for load in token_loads(s):
            load.start()
    for j in range(segments):
        token_part_ref[j] = head_groups(part_ref.at[position(j, head_order)], j)
    me = place_ref[1]
    rows = heads * PAD
    mask = head_mask(rows, width, heads)
    chunks, size, _ = up_ref.shape
    half = chunks * size // 2
    vec_grad_ref[...] = jnp.zeros_like(vec_grad_ref)
    bias_grad_ref[...] = jnp.zeros_like(bias_grad_ref)

    def add_vector(name, grad):
        i = VECTORS.index(name)
        vec_grad_ref[i : i + 1, :] += jnp.sum(grad, 0, keepdims=True)

    last = segments - 1
    for load in attn_loads[1:3]:
        load.wait()
    grad_key = token_part_ref[last ^ me, :PAD].astype(LOW)
    grad_value = token_part_ref[last ^ me, PAD:].astype(LOW)
    small_ref[last, 0] = jnp.zeros((PAD, width), LOW)
    small_ref[last, 1] = grad_key
    small_ref[last, 2] = grad_value
    add_vector("b_value", 2.0 * grad_value.astype(FULL))
    grad_read = 2.0 * (nn(grad_key, attn_ref[1]) + nn(grad_value, attn_ref[2]))
    stop = reset_ref[0, last] > 0
    init_grad_ref[...] = jnp.where(stop, grad_read, 0.0)
    grad_write = jnp.where(stop, 0.0, grad_read)

    def step(back, grad_write):
        s = segments - 2 - back
        normed, inverse = norm_parts(z_ffn_ref[s])
        add_vector("gain_ffn", grad_write * normed)
        add_vector("shift_ffn", grad_write)
        grad_sum = norm_pull(normed, inverse, grad_write * vector(vec_ref, "gain_ffn"))
        grad_low = grad_sum.astype(LOW)
        ffn_ref[s] = grad_low
        add_vector("b_down", grad_low.astype(FULL))
        grad_hidden = grad_sum

        if back == 0:
            for load in down_loads:
                load.wait()
        pre_grads = []
        for i in range(chunks):
            part = slice(i * size, (i + 1) * size)
            grad_act = nt(grad_low, down_ref[i])
            grad_pre = (grad_act * gelu_slope(pre_ref[s, :, part])).astype(LOW)
            pre_grad_ref[s, :, part] = grad_pre
            bias_grad_ref[i] += jnp.sum(grad_pre.astype(FULL), 0, keepdims=True)
            pre_grads.append(grad_pre)
        if back == 0:
            for load in up_loads:
                load.wait()
        for i in range(chunks):
            grad_hidden = grad_hidden + nn(pre_grads[i], up_ref[i])
        normed, inverse = norm_parts(z_attn_ref[s])
        add_vector("gain_attn", grad_hidden * normed)
        add_vector("shift_attn", grad_hidden)
        grad_attn = norm_pull(normed, inverse, grad_hidden * vector(vec_ref, "gain_attn"))
        add_vector("b_out", grad_attn)
        grad_mixed = grad_attn.astype(LOW)
        mixed_ref[s] = grad_mixed

        if back == 0:
            attn_loads[0].wait()
            attn_loads[3].wait()
        for load in token_loads(s):
            load.wait()
        grad_attended = nt(grad_mixed, attn_ref[3]).astype(LOW)
        attended_ref[s] = grad_attended
        queries, keys, values = qkv_ref[s, 0], qkv_ref[s, 1], qkv_ref[s, 2]
        spread = by_head(grad_attended, mask, heads)
        soft, soft_mem = soft_ref[s], soft_mem_ref[s]
        pull = nt(spread, value_ref[s])
        pull_mem = nt(spread, values)
        inner = jnp.sum(soft * pull, -1, keepdims=True) + 2.0 * jnp.sum(
            soft_mem * pull_mem, -1, keepdims=True
        )
        grad_score = (soft * (pull - inner)).astype(LOW)
        grad_score_mem = (soft_mem * (pull_mem - inner)).astype(LOW)
        score_ref[s] = grad_score
        grad_query = nn(grad_score, key_ref[s]) + 2.0 * nn(grad_score_mem, keys)
        grad_query = (SCALE * own_head(grad_query, mask, heads)).astype(LOW)
        grad_key = SCALE * tn(grad_score_mem, by_head(queries, mask, heads))
        grad_key = (token_part_ref[s ^ me, :PAD] + grad_key).astype(LOW)
        grad_value = tn(soft_mem.astype(LOW), spread)
        grad_value = (token_part_ref[s ^ me, PAD:] + grad_value).astype(LOW)
        small_ref[s, 0] = grad_query
        small_ref[s, 1] = grad_key
        small_ref[s, 2] = grad_value
        add_vector("b_query", grad_query.astype(FULL))
        add_vector("b_value", 2.0 * grad_value.astype(FULL))
        grad_read = 2.0 * (nn(grad_key, attn_ref[1]) + nn(grad_value, attn_ref[2]))
        grad_read = grad_read + nn(grad_query, attn_ref[0]) + grad_attn
        stop = (reset_ref[0, s] > 0) | (s == 0)
        init_grad_ref[...] += jnp.where(stop, grad_read, 0.0)
        return jnp.where(stop, 0.0, grad_read)

    for back in range(segments - 1):
        grad_write = step(back, grad_write)
    for load in token_loads(last):
        load.wait()
    norm = last_norm(
        heads,
        memory_rows,
        bias_ref,
        vec_ref,
        read_ref[last],
        [qkv_ref[last, i] for i in range(3)],
        key_ref[last],
        value_ref[last],
        (attn_ref[3], up_ref, down_ref),
    )
    lane = lax.broadcasted_iota(jnp.int32, norm_ref.shape, 1)
    norm_ref[...] = jnp.where(lane == last, norm, norms_ref[...])


    packed, wide = factor_ref.shape[1], (segments - 1) * PAD
    row = lax.broadcasted_iota(jnp.int32, (packed, wide), 0)
    source = lax.broadcasted_iota(jnp.int32, (packed, wide), 1)
    take = (source // PAD == row // memory_rows) & (source % PAD == row % memory_rows)
    take = jnp.where(take, 1.0, 0.0).astype(LOW)
    mine = width // 2

    def own_units(ref):
        first = ref[: segments - 1, :, :mine].reshape(wide, mine)
        second = ref[: segments - 1, :, half : half + mine].reshape(wide, mine)
        return jnp.concatenate([first, second], 1)

    acts = gelu(own_units(pre_ref)).astype(LOW)
    factor_ref[0] = nn(take, hidden_ref[: segments - 1].reshape(wide, width)).astype(LOW)
    factor_ref[1] = nn(take, ffn_ref[...].reshape(wide, width)).astype(LOW)
    factor_ref[2] = nn(take, acts).astype(LOW)
    factor_ref[3] = nn(take, own_units(pre_grad_ref)).astype(LOW)


def whole_call(
    body,
    scalars,
    operands,
    outside,
    shapes,
    flops,
    scratch=(),
    outside_shapes=(),
    limit=VMEM_LIMIT,
):
    in_vmem = pl.BlockSpec(memory_space=pltpu.VMEM)
    in_smem = pl.BlockSpec(memory_space=pltpu.SMEM)
    anywhere = pl.BlockSpec(memory_space=pl.ANY)
    size = sum(a.size * a.dtype.itemsize for a in (*operands, *outside, *shapes))
    return pl.pallas_call(
        body,
        out_shape=(*shapes, *outside_shapes),
        in_specs=[in_smem] * len(scalars) + [in_vmem] * len(operands) + [anywhere] * len(outside),
        out_specs=[in_vmem] * len(shapes) + [anywhere] * len(outside_shapes),
        scratch_shapes=scratch,
        compiler_params=pltpu.CompilerParams(vmem_limit_bytes=limit),
        cost_estimate=pl.CostEstimate(flops=flops // 1000, bytes_accessed=size // 1000, transcendentals=0),
    )(*scalars, *operands, *outside)


def unit_owner(column, order, stages, head_order, layout, index):
    head = position(partner(index, stages, "head"), head_order)
    at = head * layout.dps + position(partner(index, stages, "dp"), order)
    return column // layout.rows == at


def attention_loads(layout, place_ref, order_a, order_b, pieces, attn_ref, arrived):
    loads = []

    def copy(source, target):
        loads.append(pltpu.make_async_copy(source, target, arrived.at[len(loads)]))

    if layout.whole:
        copy(pieces[0], attn_ref)
        return loads
    here = layout.width // layout.heads
    for m in range(4):
        copy(pieces[0].at[m], attn_ref.at[m, pl.ds(0, here)])
    per = layout.dps // 4
    rows = here // per // 2
    for side, order in enumerate((order_a, order_b)):
        for index in range(layout.dps):
            flip = sum(((index >> k) & 1) * bit for k, bit in enumerate(order))
            owner = place_ref[0] ^ flip
            piece = pieces[1 + 4 * side + index // (layout.dps // 4)]
            for group in range(1, layout.heads):
                row = group * here + (owner % per) * 2 * rows + side * rows
                copy(
                    piece.at[index % (layout.dps // 4), group - 1],
                    attn_ref.at[owner // per, pl.ds(pl.multiple_of(row, 16), rows)],
                )
    return loads


def project(
    layout,
    stages,
    order_a,
    order_b,
    head_order,
    place_ref,
    token_ref,
    bias_ref,
    other_ref,
    *refs,
):
    count = 1 if layout.whole else 9
    pieces, refs = refs[:count], refs[count:]
    (
        key_ref,
        value_ref,
        x_ref,
        q_ref,
        k_ref,
        v_ref,
        vec_ref,
        bias_in_ref,
        attn_to,
        attn_ref,
        arrived,
        stored,
    ) = refs
    loads = attention_loads(layout, place_ref, order_a, order_b, pieces, attn_ref, arrived)
    for load in loads:
        load.start()
    devices, entries = bias_ref.shape
    width, rows = layout.width, layout.rows
    here = width // layout.heads
    packets = bias_ref[...].astype(FULL)

    def laid_out(first, count, period, owner):
        entry = lax.broadcasted_iota(jnp.int32, (entries, count), 0)
        column = lax.broadcasted_iota(jnp.int32, (entries, count), 1)
        pick = jnp.where(entry == first + column % period, 1.0, 0.0).astype(LOW)
        index = lax.broadcasted_iota(jnp.int32, (devices, count), 0)
        column = lax.broadcasted_iota(jnp.int32, (devices, count), 1)
        chosen = jnp.where(owner(column, index), nn(packets.astype(LOW), pick), 0.0)
        return jnp.sum(chosen, 0, keepdims=True)

    def of_head(column, index):
        head = partner(index, stages, "head")
        return (partner(index, stages, "dp") == 0) & (head == column // here)

    vec_ref[0:1, :] = laid_out(0, width, here, of_head)
    vec_ref[1:2, :] = laid_out(here, width, here, of_head)
    vec_ref[2:, :] = other_ref[...].astype(FULL)
    for half, order in enumerate((order_a, order_b)):
        owner = functools.partial(
            unit_owner, order=order, stages=stages, head_order=head_order, layout=layout
        )
        row = laid_out(
            2 * here + half * rows,
            layout.blocks * rows,
            rows,
            lambda column, index: owner(column, index=index),
        )
        per = layout.chunks // 2
        for i in range(per):
            bias_in_ref[half * per + i] = row[:, i * layout.size : (i + 1) * layout.size]

    for load in loads:
        load.wait()
    store = pltpu.make_async_copy(attn_ref, attn_to, stored)
    store.start()
    for s in range(token_ref.shape[0]):
        x = token_ref[s]
        key_ref[s] = nt(x, attn_ref[1]).astype(LOW)
        value_ref[s] = (nt(x, attn_ref[2]) + vector(vec_ref, "b_value")).astype(LOW)
    own = place_ref[1]
    x = token_ref[own]
    x_ref[...] = x
    q_ref[...] = (nt(x, attn_ref[0]) + vector(vec_ref, "b_query")).astype(LOW)
    k_ref[...] = key_ref[own]
    v_ref[...] = value_ref[own]
    store.wait()


SUMS = ("b_out", "gain_attn", "shift_attn", "b_down", "gain_ffn", "shift_ffn")


def token_layer(
    layout,
    memory_rows,
    head_dim,
    place_ref,
    x_ref,
    q_ref,
    qkv_ref,
    part_ref,
    stat_ref,
    cot_ref,
    bias_ref,
    vec_ref,
    attn_ref,
    *refs,
):
    count = len(layout.pieces())
    pieces, refs = refs[:count], refs[count:]
    (
        attended_ref,
        log_ref,
        result_ref,
        skip_ref,
        mixed_ref,
        grad_attended_ref,
        bias_sum_ref,
        sum_ref,
        *grad_refs,
        out_w_ref,
        out_arrived,
        up_ref,
        down_ref,
        arrived,
        z_attn_ref,
        hidden_ref,
        low_ref,
        total_ref,
        pre_ref,
        act_ref,
        stage_ref,
        sent,
    ) = refs
    out_load = pltpu.make_async_copy(attn_ref.at[3], out_w_ref, out_arrived)
    out_load.start()
    up_loads, down_loads = layout.loads(pieces, up_ref, down_ref, arrived)
    for load in up_loads + down_loads:
        load.start()
    chunks = layout.chunks
    pair = part_ref.shape[1]
    log_ref[...] = jnp.zeros_like(log_ref)
    for i in range(part_ref.shape[0]):
        columns = slice(i * pair, (i + 1) * pair)
        mixed, logs = with_memory(
            memory_rows,
            head_dim,
            q_ref[:, columns],
            qkv_ref[place_ref[1], 1, :, columns],
            qkv_ref[place_ref[1], 2, :, columns],
            part_ref[i],
            stat_ref[i],
        )
        attended_ref[:, columns] = mixed
        for head, log in enumerate(logs):
            log_ref[i, head : head + 1] = log
    out_load.wait()
    sum_ref[...] = jnp.zeros_like(sum_ref)

    def add_vector(name, grad):
        i = SUMS.index(name)
        sum_ref[i : i + 1, :] += jnp.sum(grad, 0, keepdims=True)

    z_attn = x_ref[...].astype(FULL) + nn(attended_ref[...], out_w_ref[...])
    z_attn = z_attn + vector(vec_ref, "b_out")
    z_attn_ref[...] = z_attn
    normed, _ = norm_parts(z_attn)
    hidden = normed * vector(vec_ref, "gain_attn") + vector(vec_ref, "shift_attn")
    hidden_ref[...] = hidden.astype(LOW)
    total_ref[...] = hidden + vector(vec_ref, "b_down")
    for load in up_loads + down_loads:
        load.wait()

    for i in range(chunks):
        pre = nt(hidden_ref[...], up_ref[i]) + bias_ref[i]
        pre_ref[i] = pre
        act = gelu(pre).astype(LOW)
        act_ref[i] = act
        total_ref[...] += nn(act, down_ref[i])
    normed, inverse = norm_parts(total_ref[...])
    result = normed * vector(vec_ref, "gain_ffn") + vector(vec_ref, "shift_ffn")
    result_ref[...] = result.astype(LOW)
    grad = cot_ref[...].astype(FULL)
    add_vector("gain_ffn", grad * normed)
    add_vector("shift_ffn", grad)
    grad = norm_pull(normed, inverse, grad * vector(vec_ref, "gain_ffn"))
    total_ref[...] = grad
    low_ref[...] = grad.astype(LOW)
    add_vector("b_down", low_ref[...].astype(FULL))

    copies = list(layout.copies())
    spans = [first for first, _ in layout.pieces()]
    stores = []
    for i in range(chunks):
        grad_pre = (nt(low_ref[...], down_ref[i]) * gelu_slope(pre_ref[i])).astype(LOW)
        bias_sum_ref[i] = jnp.sum(grad_pre.astype(FULL), 0, keepdims=True)
        total_ref[...] += nn(grad_pre, up_ref[i])
        slot = i % 2
        if i > 1:
            for store in stores[i - 2]:
                store.wait()
        stage_ref[slot, 0] = tn(grad_pre, hidden_ref[...]).astype(LOW)
        stage_ref[slot, 1] = tn(act_ref[i], low_ref[...]).astype(LOW)
        stores.append([])
        for number, entry, chunk, row, rows in copies:
            if chunk != i:
                continue
            for side in range(2):
                to_ref = grad_refs[number // (len(spans) // len(grad_refs))]
                entry_at = spans[number] - spans[number - number % (len(spans) // len(grad_refs))]
                store = pltpu.make_async_copy(
                    stage_ref.at[slot, side, pl.ds(row, rows)],
                    to_ref.at[entry_at + entry, side],
                    sent.at[i, len(stores[i])],
                )
                store.start()
                stores[i].append(store)

    grad_hidden = total_ref[...]
    normed, inverse = norm_parts(z_attn_ref[...])
    add_vector("gain_attn", grad_hidden * normed)
    add_vector("shift_attn", grad_hidden)
    grad = norm_pull(normed, inverse, grad_hidden * vector(vec_ref, "gain_attn"))
    add_vector("b_out", grad)
    skip_ref[...] = grad
    mixed_ref[...] = grad.astype(LOW)
    grad_attended_ref[...] = nt(mixed_ref[...], out_w_ref[...]).astype(LOW)
    for i in range(max(chunks - 2, 0), chunks):
        for store in stores[i]:
            store.wait()


def part_rows(keep_ref, send_ref, first, columns, grad, place_ref, order, count):
    rows = grad.shape[0] // count
    for c in range(count):
        block = grad[c * rows : (c + 1) * rows].astype(keep_ref.dtype)
        at = position(place_ref[0] ^ c, order)

        @pl.when(at < count // 2)
        def _():
            keep_ref[at, first : first + rows, columns] = block

        @pl.when(at >= count // 2)
        def _():
            send_ref[at - count // 2, first : first + rows, columns] = block


SUM_ROWS = 32


def pack_sums(
    layout, order_a, order_b, head_order, heads_here, memory_rows, place_ref, groups, rows, halves
):
    count, width = rows.shape
    dps = layout.dps
    devices = dps * groups
    here, part = width // layout.heads, width // (dps * layout.heads)
    head_dim = here // heads_here
    head_part = head_dim // dps

    def partners(index):
        head = index % groups
        dp = 0
        for k, bit in enumerate(order_a):
            dp = dp + ((index // groups >> k) & 1) * bit
        return dp, head

    shape = (devices, count, width)
    index, row, column = (lax.broadcasted_iota(jnp.int32, shape, i) for i in range(3))
    dp_flip, head_flip = partners(index)
    dp, head = place_ref[0] ^ dp_flip, place_ref[1] ^ head_flip
    plain = len(SUMS) + memory_rows
    of_device = column // part == dp * layout.heads + head
    of_head = (column // here == head_flip) & (column % head_dim // head_part == dp)
    chosen = ((row < plain) & of_device) | ((row >= plain) & of_head)
    chosen = jnp.where(chosen, jnp.broadcast_to(rows[None], shape), 0.0)
    chosen = chosen.reshape(devices * count, width).astype(LOW)
    source = lax.broadcasted_iota(jnp.int32, (width, part), 0)
    target = lax.broadcasted_iota(jnp.int32, (width, part), 1)
    plain_fold = jnp.where(source % part == target, 1.0, 0.0).astype(LOW)
    head_column = source // head_dim % heads_here * head_part + source % head_part
    head_fold = jnp.where(head_column == target, 1.0, 0.0).astype(LOW)
    row = lax.broadcasted_iota(jnp.int32, (devices, count, part), 1)
    folded = jnp.where(
        row < plain,
        nn(chosen, plain_fold).reshape(devices, count, part),
        nn(chosen, head_fold).reshape(devices, count, part),
    )
    unit_rows = []
    span = halves[0].shape[1]
    index, column = (lax.broadcasted_iota(jnp.int32, (devices, span), i) for i in range(2))
    source = lax.broadcasted_iota(jnp.int32, (span, layout.rows), 0)
    target = lax.broadcasted_iota(jnp.int32, (span, layout.rows), 1)
    fold = jnp.where(source % layout.rows == target, 1.0, 0.0).astype(LOW)
    for order, half in zip((order_a, order_b), halves):
        dp_flip, head_flip = partners(index)
        at = position(head_flip, head_order) * dps + position(dp_flip, order)
        chosen = jnp.where(column // layout.rows == at, half, 0.0)
        unit_rows.append(nn(chosen.astype(LOW), fold))
    return folded, unit_rows


def put_sums(ref, entry, first_row, first_column, packed, index, memory_rows):
    folded, unit_rows = packed
    plain = len(SUMS) + memory_rows
    part, block = folded.shape[2], unit_rows[0].shape[1]
    columns = slice(first_column, first_column + part)
    ref[entry, first_row : first_row + plain + 2, columns] = folded[index, : plain + 2].astype(LOW)
    columns = slice(first_column, first_column + block)
    for half, rows in enumerate(unit_rows):
        row = first_row + plain + 2 + half
        ref[entry, row : row + 1, columns] = rows[index : index + 1].astype(LOW)


def half_rows(ref, layout):
    per = layout.chunks // 2
    return [
        jnp.concatenate([ref[half * per + i] for i in range(per)], 1) for half in range(2)
    ]


def value_grads(
    order,
    count,
    place_ref,
    x_ref,
    mixed_ref,
    attended_ref,
    dv0_ref,
    dv1_ref,
    skip_ref,
    attn_from,
    keep_ref,
    send_ref,
    grad_x_ref,
    sum_ref,
    attn_ref,
    arrived,
):
    load = pltpu.make_async_copy(attn_from.at[2], attn_ref, arrived)
    load.start()
    x, low, high = x_ref[...], dv0_ref[...], dv1_ref[...]
    half = low.shape[1]
    share = x.shape[1] // count
    every = slice(None)
    both = jnp.concatenate([tn(x, low), tn(x, high)], 1)
    part_rows(keep_ref, send_ref, 0, every, both, place_ref, order, count)
    both = tn(mixed_ref[...], attended_ref[...])
    part_rows(keep_ref, send_ref, share, every, both, place_ref, order, count)
    sum_ref[:, :half] = jnp.sum(low.astype(FULL), 0, keepdims=True)
    sum_ref[:, half:] = jnp.sum(high.astype(FULL), 0, keepdims=True)
    load.wait()
    grad_x_ref[...] = skip_ref[...] + nn(low, attn_ref[:half]) + nn(high, attn_ref[half:])


def query_key_grads(
    layout,
    order_a,
    order_b,
    head_order,
    heads_here,
    memory_rows,
    place_ref,
    x_ref,
    dq0_ref,
    dq1_ref,
    dk0_ref,
    dk1_ref,
    part_ref,
    value_sum_ref,
    layer_sum_ref,
    bias_sum_ref,
    attn_from,
    keep_ref,
    send_ref,
    grad_x_ref,
    rows_ref,
    attn_ref,
    arrived,
):
    loads = [
        pltpu.make_async_copy(attn_from.at[i], attn_ref.at[i], arrived.at[i]) for i in range(2)
    ]
    for load in loads:
        load.start()
    count = layout.dps
    x = x_ref[...]
    half = dq0_ref.shape[1]
    share = x.shape[1] // count
    pairs = [(dq0_ref[...], dq1_ref[...]), (dk0_ref[...], dk1_ref[...])]
    for m, (low, high) in enumerate(pairs):
        both = jnp.concatenate([tn(x, low), tn(x, high)], 1)
        part_rows(keep_ref, send_ref, m * share, slice(None), both, place_ref, order_a, count)
    plain = len(SUMS) + memory_rows
    rows_ref[...] = jnp.zeros_like(rows_ref)
    rows_ref[: len(SUMS), :] = layer_sum_ref[: len(SUMS), :]
    for at, array in zip((0, half), pairs[0]):
        rows_ref[plain : plain + 1, at : at + half] = jnp.sum(array.astype(FULL), 0, keepdims=True)
    rows_ref[plain + 1 : plain + 2, :] = value_sum_ref[...]
    packed = pack_sums(
        layout,
        order_a,
        order_b,
        head_order,
        heads_here,
        memory_rows,
        place_ref,
        layout.heads,
        rows_ref[...],
        half_rows(bias_sum_ref, layout),
    )
    here = x.shape[1] // layout.heads
    for at in range(count):
        ref = keep_ref if at < count // 2 else send_ref
        entry = at % (count // 2)
        ref[entry, 2 * share :, :] = jnp.zeros((SUM_ROWS, x.shape[1]), LOW)
        for g in range(layout.heads):
            index = at * layout.heads + g
            put_sums(ref, entry, 2 * share, g * here, packed, index, memory_rows)
    total = part_ref[...]
    for m, (low, high) in enumerate(pairs):
        loads[m].wait()
        total = total + nn(low, attn_ref[m, :half]) + nn(high, attn_ref[m, half:])
    grad_x_ref[...] = total.astype(LOW)


def own_grads(
    layout,
    order_a,
    order_b,
    head_order,
    heads,
    heads_here,
    memory_rows,
    place_ref,
    score_ref,
    soft_ref,
    qkv_ref,
    attended_grad_ref,
    mixed_ref,
    attended_ref,
    small_ref,
    read_ref,
    token_ref,
    bias_grad_ref,
    vec_grad_ref,
    init_grad_ref,
    keep_ref,
    send_ref,
    rows_ref,
):
    count = layout.dps
    writes, rows, _ = score_ref.shape
    width = qkv_ref.shape[-1]
    here = width // heads * heads_here
    mine = heads_here * PAD
    mask = head_mask(rows, width, heads)[:mine]
    total = jnp.zeros((1, here), FULL)
    grads = [jnp.zeros((width, here), FULL) for _ in range(4)]
    for s in range(writes + 1):
        low = read_ref[s].astype(LOW)
        grads[1] = grads[1] + 2.0 * tn(low, small_ref[s, 1, :, :here])
        grads[2] = grads[2] + 2.0 * tn(low, small_ref[s, 2, :, :here])
        if s == writes:
            break
        grads[0] = grads[0] + tn(low, small_ref[s, 0, :, :here])
        grads[3] = grads[3] + tn(mixed_ref[s], attended_ref[s, :, :here])
        spread = by_head(qkv_ref[s, 0], mask, heads_here)[:, :here]
        pulled = by_head(attended_grad_ref[s], mask, heads_here)[:, :here]
        dk = (SCALE * tn(score_ref[s, :mine], spread)).astype(LOW)
        dv = tn(soft_ref[s, :mine].astype(LOW), pulled).astype(LOW)
        grads[1] = grads[1] + tn(token_ref[s], dk)
        grads[2] = grads[2] + tn(token_ref[s], dv)
        total = total + jnp.sum(dv.astype(FULL), 0, keepdims=True)
    both = jnp.concatenate(grads, 1)
    part_rows(keep_ref, send_ref, 0, slice(None), both, place_ref, order_a, count)
    rows_ref[...] = jnp.zeros_like(rows_ref)
    for i, name in enumerate(SUMS):
        at = VECTORS.index(name)
        rows_ref[i : i + 1, :] = vec_grad_ref[at : at + 1, :]
    for i in range(memory_rows):
        at = len(SUMS) + i
        rows_ref[at : at + 1, :] = init_grad_ref[i : i + 1, :]
    at = len(SUMS) + memory_rows
    rows_ref[at : at + 2, :] = vec_grad_ref[0:2, :]
    rows_ref[at + 1 : at + 2, :here] += total
    packed = pack_sums(
        layout,
        order_a,
        order_b,
        head_order,
        heads_here,
        memory_rows,
        place_ref,
        1,
        rows_ref[...],
        half_rows(bias_grad_ref, layout),
    )
    share = width // count
    for at in range(count):
        ref = keep_ref if at < count // 2 else send_ref
        entry = at % (count // 2)
        ref[entry, share:, :] = jnp.zeros((SUM_ROWS, width), LOW)
        put_sums(ref, entry, share, 0, packed, at, memory_rows)


def write_rows(
    heads,
    quarter,
    place_ref,
    score_ref,
    soft_ref,
    qkv_ref,
    attended_grad_ref,
    moved_ref,
    attn_from,
    grad_token_ref,
    attn_ref,
    arrived,
):
    writes, rows, _ = score_ref.shape
    loads = [
        pltpu.make_async_copy(attn_from.at[i + 1], attn_ref.at[i], arrived.at[i])
        for i in range(2)
    ]
    for load in loads:
        load.start()
    mask = head_mask(rows, qkv_ref.shape[-1], heads)
    at = pl.multiple_of(place_ref[1] * quarter, quarter)
    for load in loads:
        load.wait()
    for s in range(writes):
        spread = by_head(qkv_ref[s, 0], mask, heads)
        pulled = by_head(attended_grad_ref[s], mask, heads)
        score_here = score_ref[s, :, pl.ds(at, quarter)]
        soft_here = soft_ref[s, :, pl.ds(at, quarter)].astype(LOW)
        dk = (SCALE * tn(score_here, spread)).astype(LOW)
        dv = tn(soft_here, pulled).astype(LOW)
        extra = nn(dk, attn_ref[0]) + nn(dv, attn_ref[1])
        grad_token_ref[s] = moved_ref[s].astype(FULL) + extra
    grad_token_ref[writes] = moved_ref[writes].astype(FULL)


def finish(
    order_a,
    order_b,
    memory_rows,
    numbers,
    *refs,
):
    groups = []
    for number in numbers:
        groups.append(refs[:number])
        refs = refs[number:]
    factor_refs, *groups = groups

    def total_of(group, *at):
        total = group[0][(0, *at)].astype(FULL)
        for ref in group[1:]:
            total = total + ref[(0, *at)].astype(FULL)
        return total

    ffn_a, ffn_b, attn_terms, own_terms = groups
    (
    query_ref,
    key_ref,
    value_ref,
    b_query_ref,
    b_value_ref,
    out_ref,
    b_out_ref,
    gain_attn_ref,
    shift_attn_ref,
    up_ref,
    b_in_ref,
    down_ref,
    b_down_ref,
    gain_ffn_ref,
    shift_ffn_ref,
    init_ref,
    ) = refs
    factor = jnp.concatenate([ref[...] for ref in factor_refs], 0)
    count, _, rows, width = factor.shape
    block = width // 2 // count
    column = lax.broadcasted_iota(jnp.int32, (rows, width), 1)

    def own(j, i):
        first, second = position(j, order_a), position(j, order_b) + count
        keep = (column // block == first) | (column // block == second)
        return jnp.where(keep, factor[j, i], jnp.zeros((), LOW))

    units = []
    for side, left, right in ((0, 3, 0), (1, 2, 1)):
        chosen = jnp.concatenate([own(j, left) for j in range(count)], 0)
        others = jnp.concatenate([factor[j, right] for j in range(count)], 0)
        product = tn(chosen, others)
        halves = []
        for i in range(2):
            total = total_of((ffn_a, ffn_b)[i], side)
            for j in range(count):
                at = (i * count + j) * block
                total = total + product[at : at + block]
            halves.append(total)
        units.append(jnp.concatenate(halves, 0))
    up_ref[...] = units[0]
    down_ref[...] = units[1]
    attn, own_total = total_of(attn_terms), total_of(own_terms)
    here = attn.shape[-1] // 2
    share = own_total.shape[0] - SUM_ROWS
    totals = []
    for m in range(4):
        row, column = m % 2 * share, m // 2 * here
        from_tokens = attn[row : row + share, column : column + here]
        totals.append(from_tokens + own_total[:share, m * here : (m + 1) * here])
    query_ref[...] = totals[0]
    key_ref[...] = totals[1]
    value_ref[...] = totals[2]
    out_ref[...] = totals[3].T
    pack = attn[2 * share : 2 * share + SUM_ROWS, :here] + own_total[share:, :here]
    refs = {
        "b_out": b_out_ref,
        "gain_attn": gain_attn_ref,
        "shift_attn": shift_attn_ref,
        "b_down": b_down_ref,
        "gain_ffn": gain_ffn_ref,
        "shift_ffn": shift_ffn_ref,
    }
    part = init_ref.shape[1]
    for i, name in enumerate(SUMS):
        refs[name][...] = pack[i : i + 1, :part]
    at = len(SUMS) + memory_rows
    init_ref[...] = pack[len(SUMS) : at, :part]
    heads_here, head_part = b_query_ref.shape
    for i in range(heads_here):
        columns = slice(i * head_part, (i + 1) * head_part)
        b_query_ref[i : i + 1, :] = pack[at : at + 1, columns]
        b_value_ref[i : i + 1, :] = pack[at + 1 : at + 2, columns]
    b_in_ref[:, :block] = pack[at + 2 : at + 3, :block]
    b_in_ref[:, block:] = pack[at + 3 : at + 4, :block]


def columns_of(head, head_dim, array, factor=None):
    lane = lax.broadcasted_iota(jnp.int32, array.shape, 1) // head_dim
    if factor is not None:
        array = array * jnp.asarray(factor, array.dtype)
    return jnp.where(lane == head, array, jnp.zeros((), array.dtype))


def memory_scores(memory_rows, km, mine):
    scores = nt(km, mine)
    real_key = lax.broadcasted_iota(jnp.int32, scores.shape, 0) < memory_rows
    return jnp.where(real_key, scores, NEGATIVE)


def token_attention(head_dim, place_ref, row_ref, column_ref, q_ref, k_ref, v_ref, sum_ref, stat_ref):
    q, k, v = q_ref[...], k_ref[...], v_ref[...]
    allowed = column_ref[...] == row_ref[...]
    stat_ref[...] = jnp.zeros_like(stat_ref)
    for head in range(q.shape[1] // head_dim):
        scores = nt(k, columns_of(head, head_dim, q, SCALE))
        scores = jnp.where(allowed, scores, NEGATIVE)
        top = jnp.max(scores, 0, keepdims=True)
        raised = jnp.exp(scores - top)
        stat_ref[0, 2 * head : 2 * head + 1] = top
        stat_ref[0, 2 * head + 1 : 2 * head + 2] = jnp.sum(raised, 0, keepdims=True)
        rows = slice(head * head_dim, (head + 1) * head_dim)
        sum_ref[0, rows] = tn(v, raised.astype(LOW))[rows]


def with_memory(memory_rows, head_dim, q, km, vm, sums, stats):
    mixed, logs = [], []
    for head in range(q.shape[1] // head_dim):
        scores = memory_scores(memory_rows, km, columns_of(head, head_dim, q, SCALE))
        top_before = stats[2 * head : 2 * head + 1]
        top = jnp.maximum(jnp.max(scores, 0, keepdims=True), top_before)
        raised = jnp.exp(scores - top)
        shrink = jnp.exp(top_before - top)
        total = stats[2 * head + 1 : 2 * head + 2] * shrink
        total = total + 2.0 * jnp.sum(raised, 0, keepdims=True)
        rows = slice(head * head_dim, (head + 1) * head_dim)
        both = sums[rows] * shrink + 2.0 * tn(vm, raised.astype(LOW))[rows]
        mixed.append(both * (1.0 / total))
        logs.append(top + jnp.log(total))
    return jnp.concatenate(mixed, 0).T.astype(LOW), logs


def token_attention_back(
    memory_rows,
    head_dim,
    place_ref,
    row_ref,
    column_ref,
    q_ref,
    k_ref,
    v_ref,
    qkv_ref,
    log_ref,
    grad_ref,
    dq_ref,
    dk_ref,
    dv_ref,
    dmem_ref,
):
    q, k, v, grad = (ref[...] for ref in (q_ref, k_ref, v_ref, grad_ref))
    km, vm = qkv_ref[place_ref[1], 1], qkv_ref[place_ref[1], 2]
    allowed = column_ref[...] == row_ref[...]
    lane = lax.broadcasted_iota(jnp.int32, q.shape, 1) // head_dim
    dq, dk, dv = (jnp.zeros(q.shape, FULL) for _ in range(3))
    dkm, dvm = (jnp.zeros(km.shape, FULL) for _ in range(2))
    for head in range(q.shape[1] // head_dim):
        mine = columns_of(head, head_dim, q, SCALE)
        mine_grad = columns_of(head, head_dim, grad)
        log_total = log_ref[0, head : head + 1]
        scores = jnp.where(allowed, nt(k, mine), NEGATIVE)
        soft = jnp.exp(scores - log_total)
        soft_mem = jnp.exp(memory_scores(memory_rows, km, mine) - log_total)
        pull, pull_mem = nt(v, mine_grad), nt(vm, mine_grad)
        inner = jnp.sum(soft * pull, 0, keepdims=True) + 2.0 * jnp.sum(
            soft_mem * pull_mem, 0, keepdims=True
        )
        score = (soft * (pull - inner)).astype(LOW)
        score_mem = (soft_mem * (pull_mem - inner)).astype(LOW)
        dq = jnp.where(lane == head, tn(score, k) + 2.0 * tn(score_mem, km), dq)
        dk = dk + nn(score, mine)
        dv = dv + nn(soft.astype(LOW), mine_grad)
        dkm = dkm + nn(score_mem, mine)
        dvm = dvm + nn(soft_mem.astype(LOW), mine_grad)
    dq_ref[...] = (SCALE * dq).astype(LOW)
    dk_ref[...] = dk.astype(LOW)
    dv_ref[...] = dv.astype(LOW)
    dmem_ref[:PAD] = dkm
    dmem_ref[PAD:] = dvm


def head_pairs(body, place, doc, operands, shapes, width, flops, steps, first=0):
    seg_len = operands[0].shape[0]

    def spec(array, first):
        if len(array.shape) == 4:
            return pl.BlockSpec((*array.shape[:3], width), lambda i: (0, 0, 0, i + first))
        if len(array.shape) == 3:
            return pl.BlockSpec((1, *array.shape[1:]), lambda i: (i + first, 0, 0))
        return pl.BlockSpec((array.shape[0], width), lambda i: (0, i + first))

    return pl.pallas_call(
        body,
        grid=(steps,),
        out_shape=shapes,
        in_specs=[pl.BlockSpec(memory_space=pltpu.SMEM)]
        + [pl.BlockSpec(a.shape, lambda i: (0, 0)) for a in doc]
        + [spec(a, first) for a in operands],
        out_specs=[spec(s, 0) for s in shapes],
        compiler_params=pltpu.CompilerParams(vmem_limit_bytes=VMEM_LIMIT),
        cost_estimate=pl.CostEstimate(
            flops=flops // 1000, bytes_accessed=seg_len, transcendentals=0
        ),
    )(place, *doc, *operands)


def on_device(
    tokens,
    doc_ids,
    reset,
    mem_init,
    w_query,
    w_key,
    w_value,
    b_query,
    b_value,
    w_out,
    b_out,
    gain_attn,
    shift_attn,
    w_in,
    b_in,
    w_down,
    b_down,
    gain_ffn,
    shift_ffn,
    cotangent,
):
    chains, segments, seg_len, width = tokens.shape
    dps, groups = lax.axis_size("dp"), lax.axis_size("head")
    assert chains == 1 and segments == groups
    memory_rows = mem_init.shape[0]
    heads_here, head_dim = b_query.shape
    heads = heads_here * groups
    here = heads_here * head_dim
    units = w_in.shape[1]
    half_units = units // 2
    quarter = seg_len // groups
    dp, head = lax.axis_index("dp"), lax.axis_index("head")
    place = jnp.stack([dp, head])
    bits = bits_of(dps)
    levels = len(bits)
    order_a = bits[1:] + bits[:1]
    order_b = bits[1:][::-1] + bits[:1]
    head_order = bits_of(groups)[::-1]
    head_stages = [("head", bit) for bit in head_order]
    stages_a = head_stages + [("dp", bit) for bit in order_a]
    stages_b = head_stages + [("dp", bit) for bit in order_b]
    layout = Units(dps, groups, half_units, width)
    landing = layout.scratch()
    shape = jax.ShapeDtypeStruct
    dp_stages = [("dp", bit) for bit in bits]
    bias_groups = (head_stages[:1], dp_stages[1:], head_stages[1:] + dp_stages[:1])
    bias_stages = [stage for group in bias_groups for stage in group]
    tokens, doc_ids, cotangent = tokens[0], doc_ids[0], cotangent[0]

    shard = jnp.concatenate([w_query.T, w_key.T, w_value.T, w_out], 0)
    share = shard.shape[0] // dps
    chunk = lax.dynamic_slice_in_dim(shard, dp * share, share, 0)[None]
    biases = jnp.concatenate([b_query.reshape(-1), b_value.reshape(-1), b_in])[None]
    up = w_in.T.reshape(2, half_units, width)
    down = w_down.reshape(2, half_units, width)
    halves = [jnp.stack([up[i], down[i]])[None] for i in range(2)]
    for i, stage in enumerate(head_stages):
        chunk = gather(chunk, [stage])
        if i:
            halves = [gather(half, [head_stages[i - 1]]) for half in halves]
        biases = gather(biases, bias_groups[i])
        chunk, biases, halves = lax.optimization_barrier((chunk, biases, halves))
    halves = [gather(half, head_stages[-1:]) for half in halves]
    biases = gather(biases, bias_groups[2])
    chunk = jnp.stack([chunk[position(j, head_order)] for j in range(1, groups)])
    sides = (slice(0, share // 2), slice(share // 2, share))
    parts = []
    for rows, order in zip(sides, (order_a, order_b)):
        part = gather(chunk[None, :, rows], [("dp", bit) for bit in order[:-2]])
        parts += [part, swap(part, "dp", order[-2])]
    doc = lax.dynamic_index_in_dim(doc_ids, head, 0, False)
    doc_row, doc_column = doc[None, :], doc[:, None]
    init = jnp.pad(mem_init.astype(FULL), ((0, PAD - memory_rows), (0, 0)))
    vectors = jnp.concatenate([b_out, gain_attn, shift_attn, b_down, gain_ffn, shift_ffn])
    vectors = vectors.reshape(-1, width)
    halves, parts, biases, cotangent, doc_row, doc_column, init, vectors = (
        lax.optimization_barrier(
            (halves, parts, biases, cotangent, doc_row, doc_column, init, vectors)
        )
    )
    cotangent = lax.all_to_all(cotangent, "head", 0, 0, tiled=True).reshape(seg_len, width)
    crossed = [swap(part, "dp", bits[0]) for part in parts]
    parts = [*parts[:2], *crossed[:2], *parts[2:], *crossed[2:]]
    if layout.whole:
        chunks = []
        for i, order in ((0, order_a), (4, order_b)):
            part = jnp.concatenate(parts[i : i + 4], 0)
            native = [position(dp ^ c, order) for c in range(dps)]
            chunks.append(jnp.stack([lax.dynamic_index_in_dim(part, n, 0, False) for n in native]))
        others = jnp.concatenate(chunks, 2).transpose(1, 0, 2, 3).reshape(groups - 1, 4, here, width)
        own = shard.reshape(4, 1, here, width)
        attn_pieces = [
            jnp.concatenate([own, others.transpose(1, 0, 2, 3)], 1).reshape(4, width, width)
        ]
    else:
        attn_pieces = [shard.reshape(4, here, width), *parts]
    halves = [
        gather(half, stages[len(head_stages) : -3])
        for half, stages in zip(halves, (stages_a, stages_b))
    ]
    across = [swap(half, *st[-3]) for half, st in zip(halves, (stages_a, stages_b))]
    along = [swap(half, *st[-2]) for half, st in zip(halves, (stages_a, stages_b))]

    keys, values, x, q, k, v, vectors, bias_in, w_attn = whole_call(
        functools.partial(project, layout, bias_stages, order_a, order_b, head_order),
        (place,),
        (tokens, biases, vectors),
        attn_pieces,
        (shape(tokens.shape, LOW),) * 2
        + (shape((seg_len, width), LOW),) * 4
        + (shape((len(VECTORS), width), FULL), shape((layout.chunks, 1, layout.size), FULL)),
        6_000_000_000,
        (
            pltpu.VMEM((4, width, width), LOW),
            pltpu.SemaphoreType.DMA((4 + 2 * dps * groups,)),
            pltpu.SemaphoreType.DMA(()),
        ),
        (shape((4, width, width), LOW),),
    )

    across, along, keys, q = lax.optimization_barrier((across, along, keys, q))
    corner = [swap(side, *stages[-2]) for side, stages in zip(across, (stages_a, stages_b))]
    pair = 2 * head_dim
    partial = head_pairs(
        functools.partial(token_attention, head_dim),
        place,
        (doc_row, doc_column),
        (q, k, v),
        (shape((width // pair, pair, seg_len), FULL), shape((width // pair, 8, seg_len), FULL)),
        pair,
        8_000_000_000,
        width // pair,
    )
    corner, partial, cotangent = lax.optimization_barrier((corner, partial, cotangent))
    pieces = []
    for *near, stages in zip(halves, across, along, corner, (stages_a, stages_b)):
        pieces += near + [swap(piece, *stages[-1]) for piece in near]
    if layout.whole:
        pieces = layout.assembled([jnp.concatenate(pieces[i : i + 8], 0) for i in (0, 8)])

    ff = layout.chunks * layout.size
    writes = segments - 1
    rows_shape = lambda kind: shape((writes, PAD, width), kind)
    tokens_scratch = lambda count: (
        pltpu.VMEM((4, width, width), LOW),
        pltpu.VMEM((count, seg_len, width), LOW),
        pltpu.VMEM((count, seg_len, width), LOW),
        pltpu.SemaphoreType.DMA((4,)),
        pltpu.SemaphoreType.DMA((count,)),
        pltpu.SemaphoreType.DMA((count,)),
    )
    read, qkv, soft, soft_mem, attended_w, z_attn_w, hidden_w, pre_w, z_ffn_w, norms = whole_call(
        functools.partial(chain_forward, layout, heads, memory_rows),
        (reset,),
        (init, bias_in, vectors),
        (w_attn, keys, values, *pieces),
        (
            shape((segments, PAD, width), FULL),
            shape((segments, 3, PAD, width), LOW),
            shape((writes, heads * PAD, seg_len), FULL),
            shape((writes, heads * PAD, PAD), FULL),
            rows_shape(LOW),
            rows_shape(FULL),
            rows_shape(LOW),
            shape((writes, PAD, ff), FULL),
            rows_shape(FULL),
            shape((1, 128), FULL),
        ),
        20_000_000_000,
        tokens_scratch(writes) + landing,
    )

    if layout.whole:
        grad_shapes = (shape((layout.chunks, 2, layout.size, width), LOW),)
    else:
        grad_shapes = (shape((layout.blocks // 2, 2, half_units, width), LOW),) * 4
    sides = 2 * max(layout.size // (layout.size if layout.whole else half_units), 1)
    (
        attended,
        log_total,
        result,
        grad_attn,
        grad_mixed,
        grad_attended,
        bias_sum,
        layer_sums,
        *ffn_grads,
    ) = whole_call(
        functools.partial(token_layer, layout, memory_rows, head_dim),
        (place,),
        (x, q, qkv, *partial, cotangent, bias_in, vectors),
        (w_attn, *pieces),
        (
            shape((seg_len, width), LOW),
            shape((width // pair, 8, seg_len), FULL),
            shape((seg_len, width), LOW),
            shape((seg_len, width), FULL),
            shape((seg_len, width), LOW),
            shape((seg_len, width), LOW),
            shape((layout.chunks, 1, layout.size), FULL),
            shape((8, width), FULL),
        ),
        25_000_000_000,
        (pltpu.VMEM((width, width), LOW), pltpu.SemaphoreType.DMA(()))
        + landing
        + (
            pltpu.VMEM((seg_len, width), FULL),
            pltpu.VMEM((seg_len, width), LOW),
            pltpu.VMEM((seg_len, width), LOW),
            pltpu.VMEM((seg_len, width), FULL),
            pltpu.VMEM((layout.chunks, seg_len, layout.size), FULL),
            pltpu.VMEM((layout.chunks, seg_len, layout.size), LOW),
            pltpu.VMEM((2, 2, layout.size, width), LOW),
            pltpu.SemaphoreType.DMA((layout.chunks, sides)),
        ),
        grad_shapes,
    )
    if layout.whole:
        half_blocks = layout.blocks // 2
        ffn_grads = [
            part
            for half in layout.taken_apart(ffn_grads[0])
            for part in (half[:half_blocks], half[half_blocks:])
        ]

    back_a, back_b = stages_a[::-1], stages_b[::-1]

    def stages_of(level):
        return back_a[level], back_b[level]

    def attention_back(block, count):
        cut = width // 2
        return head_pairs(
            functools.partial(token_attention_back, memory_rows, head_dim),
            place,
            (doc_row, doc_column),
            (q, k, v, qkv, log_total, grad_attended),
            (shape((seg_len, cut), LOW),) * 3 + (shape((2 * PAD, cut), FULL),),
            pair,
            10_000_000_000,
            count,
            block * count,
        )

    blocks = width // pair // 2
    moving = [
        [keep, swap(send, *back[0])]
        for keep, send, back in zip(ffn_grads[::2], ffn_grads[1::2], (back_a, back_b))
    ]
    back_low = attention_back(0, blocks)
    back_low, moving, grad_attended = lax.optimization_barrier((back_low, moving, grad_attended))
    output = lax.all_to_all(result.reshape(groups, quarter, width), "head", 0, 0, tiled=True)
    sends = parcels(moving)
    sends, grad_attended = lax.optimization_barrier((sends, grad_attended))
    moving = posted(moving, sends, stages_of(1))
    back_high = attention_back(1, blocks)
    token_part = jnp.concatenate([back_low[3], back_high[3]], 1)
    token_part, back_high = lax.optimization_barrier((token_part, back_high))
    token_parts = gather(token_part[None], head_stages[:1])
    share = width // dps
    rows_a, rows_b, rows_own = 2 * share + SUM_ROWS, 2 * share, share + SUM_ROWS
    keep_b, send_b, grad_x, value_sum = whole_call(
        functools.partial(value_grads, order_b, dps),
        (place,),
        (x, grad_mixed, attended, back_low[2], back_high[2], grad_attn),
        (w_attn,),
        (
            *(shape((dps // 2, rows_b, width), LOW),) * 2,
            shape((seg_len, width), FULL),
            shape((1, width), FULL),
        ),
        5_000_000_000,
        (pltpu.VMEM((width, width), LOW), pltpu.SemaphoreType.DMA(())),
    )
    down_a, down_b = ([("dp", bit) for bit in order[::-1]] for order in (order_a, order_b))
    grad_x, send_b, moving, token_parts, output = lax.optimization_barrier(
        (grad_x, send_b, moving, token_parts, output)
    )
    token_parts = gather(token_parts, head_stages[1:])
    other_b = swap(send_b, *down_b[0])
    sends = parcels(moving)
    sends, grad_x = lax.optimization_barrier((sends, grad_x))
    moving = posted(moving, sends, stages_of(2))
    for level in range(3, levels):
        moving = posted(moving, parcels(moving), stages_of(level))
    sum_scratch = (pltpu.VMEM((SUM_ROWS, width), FULL),)
    keep_a, send_a, grad_x = whole_call(
        functools.partial(
            query_key_grads, layout, order_a, order_b, head_order, heads_here, memory_rows
        ),
        (place,),
        (
            x,
            back_low[0],
            back_high[0],
            back_low[1],
            back_high[1],
            grad_x,
            value_sum,
            layer_sums,
            bias_sum,
        ),
        (w_attn,),
        (
            *(shape((dps // 2, rows_a, width), LOW),) * 2,
            shape((seg_len, width), LOW),
        ),
        10_000_000_000,
        sum_scratch + (pltpu.VMEM((2, width, width), LOW), pltpu.SemaphoreType.DMA((2,))),
    )

    def advance_both(parts, level):
        return [reduce_step(p, down[level]) for p, down in zip(parts, (down_a, down_b))]

    token_parts, send_a, other_b, grad_x, moving = lax.optimization_barrier(
        (token_parts, send_a, other_b, grad_x, moving)
    )
    attn_moving = [[keep_a, swap(send_a, *down_a[0])], [keep_b, other_b]]
    sends = parcels(moving, True)
    attn_moving, sends = lax.optimization_barrier((attn_moving, sends))
    others = swap(sends[0], *back_a[levels])
    sends = parcels(attn_moving)
    sends, grad_x, token_parts = lax.optimization_barrier((sends, grad_x, token_parts))
    attn_moving = posted(attn_moving, sends, (down_a[1], down_b[1]))
    moved = lax.all_to_all(grad_x.reshape(groups, quarter, width), "head", 0, 0, tiled=True)

    packed_rows = writes * memory_rows + (-writes * memory_rows) % PAD
    score_w, grad_attended_w, grad_mixed_w, small_w, factors, bias_w, vec_w, init_w, norms = whole_call(
        functools.partial(chain_backward, layout, head_order, heads, memory_rows),
        (reset, place),
        (
            bias_in,
            read,
            norms,
            vectors,
            qkv,
            soft,
            soft_mem,
            z_attn_w,
            pre_w,
            z_ffn_w,
            hidden_w,
            token_parts,
        ),
        (w_attn, keys, values, *pieces),
        (
            shape((writes, heads * PAD, seg_len), LOW),
            shape((writes, PAD, width), LOW),
            shape((writes, PAD, width), LOW),
            shape((segments, 3, PAD, width), LOW),
            shape((4, packed_rows, width), LOW),
            shape((layout.chunks, 1, layout.size), FULL),
            shape((len(VECTORS), width), FULL),
            shape((PAD, width), FULL),
            shape((1, 128), FULL),
        ),
        20_000_000_000,
        (
            pltpu.VMEM((writes, PAD, width), LOW),
            pltpu.VMEM((writes, PAD, ff), LOW),
            pltpu.VMEM((segments, 2 * PAD, width), FULL),
        )
        + tokens_scratch(segments)
        + landing,
    )
    score_w, factors, moving, others, attn_moving, moved = lax.optimization_barrier(
        (score_w, factors, moving, others, attn_moving, moved)
    )

    moving = [terms + [others[:, i]] for i, terms in enumerate(moving)]
    sends = parcels(moving + attn_moving, True)
    sends, score_w = lax.optimization_barrier((sends, score_w))
    others = swap(sends[0], *back_a[levels + 1])
    moving = [terms + [others[:, i]] for i, terms in enumerate(moving)]
    attn_moving = posted(attn_moving, sends[1:], (down_a[2], down_b[2]))
    for level in range(3, levels):
        attn_moving = advance_both(attn_moving, level)
    factors = gather(factors[None], [("dp", order_b[0])])
    keep_own, send_own = whole_call(
        functools.partial(
            own_grads, layout, order_a, order_b, head_order, heads, heads_here, memory_rows
        ),
        (place,),
        (
            score_w,
            soft,
            qkv,
            grad_attended_w,
            grad_mixed_w,
            attended_w,
            small_w,
            read,
            tokens,
            bias_w,
            vec_w,
            init_w,
        ),
        (),
        (shape((dps // 2, rows_own, width), LOW),) * 2,
        5_000_000_000,
        sum_scratch,
    )
    keep_own, send_own, attn_moving, factors, score_w, moving = lax.optimization_barrier(
        (keep_own, send_own, attn_moving, factors, score_w, moving)
    )
    own = [keep_own, swap(send_own, *down_a[0])]
    left, right = (summed(terms)[0] for terms in attn_moving)
    right = jnp.pad(right, ((0, SUM_ROWS), (0, 0)))
    both = [
        jnp.concatenate([part[:, g * here : (g + 1) * here] for part in (left, right)], 1)
        for g in range(groups)
    ]
    attn_moving = [jnp.stack([both[partner(i, head_stages, "head")] for i in range(groups)])]
    attn_send = summed(attn_moving, LOW, groups // 2)
    own_send = summed(own, LOW, own[-1].shape[0] // 2)
    attn_send, own_send, score_w = lax.optimization_barrier((attn_send, own_send, score_w))
    attn_moving = attn_moving + [swap(attn_send, "head", head_order[-1])]
    own = own + [swap(own_send, *down_a[1])]
    factors = gather(factors, [("dp", order_b[1])])
    for level in range(2, levels - 1):
        own = reduce_step(own, down_a[level])
    attn_send = summed(attn_moving, LOW, attn_moving[-1].shape[0] // 2)
    own_send = summed(own, LOW, own[-1].shape[0] // 2)
    attn_send, own_send, score_w = lax.optimization_barrier((attn_send, own_send, score_w))
    attn_moving = attn_moving + [swap(attn_send, "head", head_order[0])]
    own = own + [swap(own_send, *down_a[levels - 1])]
    factors = gather(factors, stages_b[len(head_stages) + 2 : -1])
    factors = [factors, swap(factors, *stages_b[-1])]
    (grad_tokens,) = whole_call(
        functools.partial(write_rows, heads, quarter),
        (place,),
        (score_w, soft, qkv, grad_attended_w, moved),
        (w_attn,),
        (shape((segments, quarter, width), FULL),),
        5_000_000_000,
        (pltpu.VMEM((2, width, width), LOW), pltpu.SemaphoreType.DMA((2,))),
    )
    grad_tokens, own, factors, attn_moving = lax.optimization_barrier(
        (grad_tokens, own, factors, attn_moving)
    )
    own, factors, attn_moving, moving = lax.optimization_barrier(
        (own, factors, attn_moving, moving)
    )
    part = width // dps // groups
    row = shape((1, part), FULL)
    groups_in = [factors, *moving, attn_moving, own]
    first_entry = lambda array: pl.BlockSpec(
        (1, *array.shape[1:]), lambda i: (0,) * len(array.shape)
    )
    whole = lambda array: pl.BlockSpec(array.shape, lambda i: (0,) * len(array.shape))
    shapes = (
        *(shape((share, here), FULL),) * 3,
        *(shape((heads_here, head_dim // dps), FULL),) * 2,
        shape((here, share), FULL),
        *(row,) * 3,
        shape((units, width), FULL),
        shape((1, units), FULL),
        shape((units, width), FULL),
        *(row,) * 3,
        shape((memory_rows, part), FULL),
    )
    outs = pl.pallas_call(
        functools.partial(
            finish,
            order_in(order_a, order_b),
            order_in(order_b, order_b),
            memory_rows,
            [len(group) for group in groups_in],
        ),
        grid=(1,),
        out_shape=shapes,
        in_specs=[whole(a) for a in factors]
        + [first_entry(a) for group in groups_in[1:] for a in group],
        out_specs=[whole(a) for a in shapes],
        compiler_params=pltpu.CompilerParams(vmem_limit_bytes=VMEM_LIMIT),
        cost_estimate=pl.CostEstimate(flops=1000, bytes_accessed=1000, transcendentals=0),
    )(*(a for group in groups_in for a in group))
    flat = (6, 7, 8, 10, 12, 13, 14)
    outs = [out.reshape(-1) if i in flat else out for i, out in enumerate(outs)]
    outs[9] = outs[9].T
    return (output[None], norms[:, :segments], grad_tokens[None], *outs)


def solution(mesh):
    in_specs = (
        P("dp", None, None, None),
        P("dp", None, None),
        P("dp", None),
        P(),
        P(None, "head"),
        P(None, "head"),
        P(None, "head"),
        P("head", None),
        P("head", None),
        P("head", None),
        P(),
        P(),
        P(),
        P(None, ("dp", "head")),
        P(("dp", "head")),
        P(("dp", "head"), None),
        P(),
        P(),
        P(),
        P("dp", None, "head", None),
    )
    out_specs = (
        P("dp", None, "head", None),
        P("dp", None),
        P("dp", None, "head", None),
        P("dp", "head"),
        P("dp", "head"),
        P("dp", "head"),
        P("head", "dp"),
        P("head", "dp"),
        P("head", "dp"),
        P(("dp", "head")),
        P(("dp", "head")),
        P(("dp", "head")),
        P(None, ("dp", "head")),
        P(("dp", "head")),
        P(("dp", "head"), None),
        P(("dp", "head")),
        P(("dp", "head")),
        P(("dp", "head")),
        P(None, ("dp", "head")),
    )
    return jax.shard_map(
        on_device, mesh=mesh, in_specs=in_specs, out_specs=out_specs, check_vma=False
    )
```

```python
import functools

import jax
import jax.numpy as jnp
from jax import lax
from jax.experimental import pallas as pl
from jax.experimental.pallas import tpu as pltpu
from jax.sharding import PartitionSpec as P

EPSILON = 1e-06
SCALE = 0.125
NEGATIVE = -1e30
ROOT_HALF = 0.7071067811865476
DENSITY = 0.3989422804014327
LOW = jnp.bfloat16
FULL = jnp.float32
PAD = 16
VECTORS = ("b_query", "b_value", "b_out", "gain_attn", "shift_attn", "b_down", "gain_ffn", "shift_ffn")
VMEM_LIMIT = 60 * 1024 * 1024


def nn(left, right):
    return lax.dot_general(left, right, (((1,), (0,)), ((), ())), preferred_element_type=FULL)


def nt(left, right):
    return lax.dot_general(left, right, (((1,), (1,)), ((), ())), preferred_element_type=FULL)


def tn(left, right):
    return lax.dot_general(left, right, (((0,), (0,)), ((), ())), preferred_element_type=FULL)


def norm_parts(rows):
    centred = rows - jnp.mean(rows, -1, keepdims=True)
    inverse = lax.rsqrt(jnp.mean(centred * centred, -1, keepdims=True) + EPSILON)
    return centred * inverse, inverse


def norm_pull(normed, inverse, grad):
    along = jnp.mean(grad * normed, -1, keepdims=True)
    return inverse * (grad - jnp.mean(grad, -1, keepdims=True) - normed * along)


def gelu(v):
    return 0.5 * v * (1.0 + lax.erf(v * ROOT_HALF))


def gelu_slope(v):
    return 0.5 * (1.0 + lax.erf(v * ROOT_HALF)) + v * (DENSITY * jnp.exp(-0.5 * v * v))


def swap(array, axis, bit):
    return lax.ppermute(array, axis, [(i, i ^ bit) for i in range(lax.axis_size(axis))])


def bits_of(count):
    return [1 << i for i in range(count.bit_length() - 1)]


def gather(array, stages):
    for axis, bit in stages:
        array = jnp.concatenate([array, swap(array, axis, bit)], 0)
    return array


def summed(terms, kind=LOW, first=0):
    size = terms[-1].shape[0] - first
    total = terms[0][first : first + size].astype(FULL)
    for term in terms[1:]:
        total = total + term[first : first + size].astype(FULL)
    return total.astype(kind)


def add_up(count, together, *refs):
    out_refs = list(refs[sum(count) :])
    pair_ref = None
    if together:
        pair_ref = out_refs[0]
        out_refs = [None, None] + out_refs[1:]
    at = 0
    for number_of, (number, out_ref) in enumerate(zip(count, out_refs)):
        total = refs[at][...].astype(FULL)
        for ref in refs[at + 1 : at + number]:
            total = total + ref[...].astype(FULL)
        total = total.astype(refs[at].dtype)
        at += number
        if pair_ref is not None and number_of < 2:
            pair_ref[:, number_of] = total
        else:
            out_ref[...] = total


def parcels(groups, together=False):
    halves = [terms[-1].shape[0] // 2 for terms in groups]
    steps = min(min(halves), 2)
    in_specs, operands, out_specs, shapes = [], [], [], []

    def spec(half, rest, first):
        index = lambda i: (first + i,) + (0,) * len(rest)
        return pl.BlockSpec((half // steps, *rest), index)

    for half, terms in zip(halves, groups):
        rest = terms[0].shape[1:]
        in_specs += [spec(half, rest, steps)] * len(terms)
        operands += terms
        if together and len(operands) < len(groups[0]) + len(groups[1]) + 1:
            if len(shapes):
                continue
            rest = (2, *rest)
        out_specs.append(spec(half, rest, 0))
        shapes.append(jax.ShapeDtypeStruct((half, *rest), terms[0].dtype))
    return pl.pallas_call(
        functools.partial(add_up, [len(terms) for terms in groups], together),
        grid=(steps,),
        out_shape=shapes,
        in_specs=in_specs,
        out_specs=out_specs,
        compiler_params=pltpu.CompilerParams(vmem_limit_bytes=VMEM_LIMIT),
        cost_estimate=pl.CostEstimate(flops=1000, bytes_accessed=1000, transcendentals=0),
    )(*operands)


def posted(groups, sends, stages):
    return [
        terms + [swap(send, *stage)] for terms, send, stage in zip(groups, sends, stages)
    ]


def reduce_step(terms, stage):
    half = terms[-1].shape[0] // 2
    return terms + [swap(summed(terms, terms[0].dtype, half), *stage)]


def partner(index, stages, axis):
    place = 0
    for k, (name, bit) in enumerate(stages):
        if name == axis:
            place = place + ((index >> k) & 1) * bit
    return place


def position(partner_bits, order):
    place = 0
    for k, bit in enumerate(order):
        place = place + ((partner_bits // bit) % 2) * (1 << k)
    return place


def order_in(order, index_order):
    return [1 << index_order.index(bit) for bit in order]


def head_mask(rows, width, heads):
    group = lax.broadcasted_iota(jnp.int32, (rows, width), 0) // PAD
    column = lax.broadcasted_iota(jnp.int32, (rows, width), 1) // (width // heads)
    return group == column


def by_head(rows, mask, heads):
    return jnp.where(mask, jnp.concatenate([rows] * heads, 0), jnp.zeros((), rows.dtype))


def own_head(rows, mask, heads):
    kept = jnp.where(mask, rows, 0.0)
    total = kept[:PAD]
    for i in range(1, heads):
        total = total + kept[i * PAD : (i + 1) * PAD]
    return total


def vector(vec_ref, name):
    i = VECTORS.index(name)
    return vec_ref[i : i + 1, :]


class Units:
    def __init__(self, dps, heads, rows, width):
        self.dps, self.heads, self.rows, self.width = dps, heads, rows, width
        self.blocks = dps * heads
        self.chunks = max(2 * self.blocks * rows // width, 4)
        self.size = 2 * self.blocks * rows // self.chunks
        self.whole = rows % 16 != 0

    def at(self, index):
        return (index % self.heads) * self.dps + index // self.heads

    def pieces(self):
        if self.whole:
            return [(0, self.chunks)]
        part = self.blocks // 8
        return [(half * self.blocks + p * part, part) for half in range(2) for p in range(8)]

    def copies(self):
        for number, (first, count) in enumerate(self.pieces()):
            for entry in range(count):
                if self.whole:
                    yield number, entry, entry, 0, self.size
                    continue
                half, index = divmod(first + entry, self.blocks)
                row = (half * self.blocks + self.at(index)) * self.rows
                yield number, entry, row // self.size, row % self.size, self.rows

    def scratch(self):
        buffer = pltpu.VMEM((self.chunks, self.size, self.width), LOW)
        count = sum(2 for _ in self.copies())
        return (buffer, buffer, pltpu.SemaphoreType.DMA((count,)))

    def loads(self, pieces, up_ref, down_ref, arrived):
        made = []
        for number, entry, chunk, row, rows in self.copies():
            for side, to_ref in enumerate((up_ref, down_ref)):
                made.append(
                    pltpu.make_async_copy(
                        pieces[number].at[entry, side],
                        to_ref.at[chunk, pl.ds(row, rows)],
                        arrived.at[len(made)],
                    )
                )
        return made[::2], made[1::2]

    def assembled(self, halves):
        rows = []
        for array in halves:
            array = array.reshape(self.dps, self.heads, 2, self.rows, self.width)
            rows.append(array.transpose(1, 0, 3, 2, 4).reshape(-1, 2, self.width))
        rows = jnp.concatenate(rows, 0).reshape(self.chunks, self.size, 2, self.width)
        return [rows.transpose(0, 2, 1, 3)]

    def taken_apart(self, piece):
        rows = piece.transpose(0, 2, 1, 3).reshape(2, self.heads, self.dps, self.rows, 2, -1)
        rows = rows.transpose(0, 2, 1, 4, 3, 5)
        return [half.reshape(self.blocks, 2, self.rows, self.width) for half in rows]


def head_groups(ref, flip):
    value = ref[...]
    half = value.shape[1] // 2
    low, high = value[:, :half], value[:, half:]
    if flip & 2:
        low, high = high, low
    if flip & 1:
        low, high = pltpu.roll(low, half // 2, 1), pltpu.roll(high, half // 2, 1)
    return jnp.concatenate([low, high], 1)


def memory_queries(read, attn_ref, vec_ref):
    low = read.astype(LOW)
    queries = (nt(low, attn_ref[0]) + vector(vec_ref, "b_query")).astype(LOW)
    keys = nt(low, attn_ref[1]).astype(LOW)
    values = (nt(low, attn_ref[2]) + vector(vec_ref, "b_value")).astype(LOW)
    return queries, keys, values


def memory_attention(heads, memory_rows, queries, keys, values, key_low, value_low):
    rows, width = heads * PAD, queries.shape[1]
    mask = head_mask(rows, width, heads)
    real_key = lax.broadcasted_iota(jnp.int32, (rows, PAD), 1) < memory_rows
    spread = by_head(queries, mask, heads)
    scores = nt(spread, key_low) * SCALE
    scores_mem = jnp.where(real_key, nt(spread, keys) * SCALE, NEGATIVE)
    top = jnp.maximum(jnp.max(scores, -1, keepdims=True), jnp.max(scores_mem, -1, keepdims=True))
    raised = jnp.exp(scores - top)
    raised_mem = jnp.exp(scores_mem - top)
    total = jnp.sum(raised, -1, keepdims=True) + 2.0 * jnp.sum(raised_mem, -1, keepdims=True)
    soft = raised / total
    soft_mem = raised_mem / total
    mixed = nn(soft.astype(LOW), value_low) + 2.0 * nn(soft_mem.astype(LOW), values)
    return own_head(mixed, mask, heads).astype(LOW), soft, soft_mem


def memory_norm(result, memory_rows):
    real_row = lax.broadcasted_iota(jnp.int32, result.shape, 0) < memory_rows
    square = jnp.sum(jnp.where(real_row, result * result, 0.0), axis=(0, 1), keepdims=True)
    return jnp.sqrt(square / (memory_rows * result.shape[1]))


def chain_forward(
    layout,
    heads,
    memory_rows,
    reset_ref,
    init_ref,
    bias_ref,
    vec_ref,
    attn_from,
    key_from,
    value_from,
    *refs,
):
    count = len(layout.pieces())
    pieces, refs = refs[:count], refs[count:]
    (
        read_ref,
        qkv_ref,
        soft_ref,
        soft_mem_ref,
        attended_ref,
        z_attn_ref,
        hidden_ref,
        pre_ref,
        z_ffn_ref,
        norm_ref,
        attn_ref,
        key_ref,
        value_ref,
        attn_arrived,
        key_arrived,
        value_arrived,
        up_ref,
        down_ref,
        arrived,
    ) = refs
    last = key_ref.shape[0]
    attn_loads = [
        pltpu.make_async_copy(attn_from.at[i], attn_ref.at[i], attn_arrived.at[i])
        for i in range(4)
    ]

    def token_loads(s):
        return [
            pltpu.make_async_copy(key_from.at[s], key_ref.at[s], key_arrived.at[s]),
            pltpu.make_async_copy(value_from.at[s], value_ref.at[s], value_arrived.at[s]),
        ]

    up_loads, down_loads = layout.loads(pieces, up_ref, down_ref, arrived)
    for load in attn_loads[:3] + token_loads(0) + attn_loads[3:] + up_loads + down_loads:
        load.start()
    for s in range(1, last):
        for load in token_loads(s):
            load.start()
    chunks, size, _ = up_ref.shape
    norm_ref[...] = jnp.zeros_like(norm_ref)
    for load in attn_loads[:3]:
        load.wait()

    def enter(s, carried):
        fresh = (reset_ref[0, s] > 0) | (s == 0)
        read = jnp.where(fresh, init_ref[...], carried)
        read_ref[s] = read
        queries, keys, values = memory_queries(read, attn_ref, vec_ref)
        qkv_ref[s, 0] = queries
        qkv_ref[s, 1] = keys
        qkv_ref[s, 2] = values
        return read, queries, keys, values

    def step(s, carried):
        read, queries, keys, values = enter(s, carried)
        for load in token_loads(s):
            load.wait()
        attended, soft, soft_mem = memory_attention(
            heads, memory_rows, queries, keys, values, key_ref[s], value_ref[s]
        )
        soft_ref[s] = soft
        soft_mem_ref[s] = soft_mem
        attended_ref[s] = attended

        if s == 0:
            attn_loads[3].wait()
        z_attn = read + nn(attended, attn_ref[3]) + vector(vec_ref, "b_out")
        z_attn_ref[s] = z_attn
        normed, _ = norm_parts(z_attn)
        hidden = normed * vector(vec_ref, "gain_attn") + vector(vec_ref, "shift_attn")
        hidden_low = hidden.astype(LOW)
        hidden_ref[s] = hidden_low
        z_ffn = hidden + vector(vec_ref, "b_down")

        if s == 0:
            for load in up_loads:
                load.wait()
        acts = []
        for i in range(chunks):
            pre = nt(hidden_low, up_ref[i]) + bias_ref[i]
            pre_ref[s, :, i * size : (i + 1) * size] = pre
            acts.append(gelu(pre).astype(LOW))
        if s == 0:
            for load in down_loads:
                load.wait()
        for i in range(chunks):
            z_ffn = z_ffn + nn(acts[i], down_ref[i])
        z_ffn_ref[s] = z_ffn
        normed, _ = norm_parts(z_ffn)
        result = normed * vector(vec_ref, "gain_ffn") + vector(vec_ref, "shift_ffn")
        lane = lax.broadcasted_iota(jnp.int32, norm_ref.shape, 1)
        norm_ref[...] = jnp.where(lane == s, memory_norm(result, memory_rows), norm_ref[...])
        return result

    carried = init_ref[...]
    for s in range(last):
        carried = step(s, carried)
    enter(last, carried)


def last_norm(heads, memory_rows, bias_ref, vec_ref, read, qkv, key, value, weights):
    out_w, up_ref, down_ref = weights
    attended, _, _ = memory_attention(heads, memory_rows, *qkv, key, value)
    z_attn = read + nn(attended, out_w) + vector(vec_ref, "b_out")
    normed, _ = norm_parts(z_attn)
    hidden = normed * vector(vec_ref, "gain_attn") + vector(vec_ref, "shift_attn")
    hidden_low = hidden.astype(LOW)
    z_ffn = hidden + vector(vec_ref, "b_down")
    for i in range(up_ref.shape[0]):
        pre = nt(hidden_low, up_ref[i]) + bias_ref[i]
        z_ffn = z_ffn + nn(gelu(pre).astype(LOW), down_ref[i])
    normed, _ = norm_parts(z_ffn)
    result = normed * vector(vec_ref, "gain_ffn") + vector(vec_ref, "shift_ffn")
    return memory_norm(result, memory_rows)


def chain_backward(
    layout,
    head_order,
    heads,
    memory_rows,
    reset_ref,
    place_ref,
    bias_ref,
    read_ref,
    norms_ref,
    vec_ref,
    qkv_ref,
    soft_ref,
    soft_mem_ref,
    z_attn_ref,
    pre_ref,
    z_ffn_ref,
    hidden_ref,
    *refs,
):
    segments, _, _, width = qkv_ref.shape
    part_ref, *refs = refs
    attn_from, key_from, value_from, *refs = refs
    count = len(layout.pieces())
    pieces, refs = refs[:count], refs[count:]
    (
        score_ref,
        attended_ref,
        mixed_ref,
        small_ref,
        factor_ref,
        bias_grad_ref,
        vec_grad_ref,
        init_grad_ref,
        norm_ref,
        ffn_ref,
        pre_grad_ref,
        token_part_ref,
        attn_ref,
        key_ref,
        value_ref,
        attn_arrived,
        key_arrived,
        value_arrived,
        up_ref,
        down_ref,
        arrived,
    ) = refs
    attn_loads = [
        pltpu.make_async_copy(attn_from.at[i], attn_ref.at[i], attn_arrived.at[i])
        for i in range(4)
    ]

    def token_loads(s):
        return [
            pltpu.make_async_copy(key_from.at[s], key_ref.at[s], key_arrived.at[s]),
            pltpu.make_async_copy(value_from.at[s], value_ref.at[s], value_arrived.at[s]),
        ]

    up_loads, down_loads = layout.loads(pieces, up_ref, down_ref, arrived)
    for load in attn_loads[1:3] + down_loads + up_loads + attn_loads[3:] + attn_loads[:1]:
        load.start()
    for s in (*range(segments - 2, -1, -1), segments - 1):
        for load in token_loads(s):
            load.start()
    for j in range(segments):
        token_part_ref[j] = head_groups(part_ref.at[position(j, head_order)], j)
    me = place_ref[1]
    rows = heads * PAD
    mask = head_mask(rows, width, heads)
    chunks, size, _ = up_ref.shape
    half = chunks * size // 2
    vec_grad_ref[...] = jnp.zeros_like(vec_grad_ref)
    bias_grad_ref[...] = jnp.zeros_like(bias_grad_ref)

    def add_vector(name, grad):
        i = VECTORS.index(name)
        vec_grad_ref[i : i + 1, :] += jnp.sum(grad, 0, keepdims=True)

    last = segments - 1
    for load in attn_loads[1:3]:
        load.wait()
    grad_key = token_part_ref[last ^ me, :PAD].astype(LOW)
    grad_value = token_part_ref[last ^ me, PAD:].astype(LOW)
    small_ref[last, 0] = jnp.zeros((PAD, width), LOW)
    small_ref[last, 1] = grad_key
    small_ref[last, 2] = grad_value
    add_vector("b_value", 2.0 * grad_value.astype(FULL))
    grad_read = 2.0 * (nn(grad_key, attn_ref[1]) + nn(grad_value, attn_ref[2]))
    stop = reset_ref[0, last] > 0
    init_grad_ref[...] = jnp.where(stop, grad_read, 0.0)
    grad_write = jnp.where(stop, 0.0, grad_read)

    def step(back, grad_write):
        s = segments - 2 - back
        normed, inverse = norm_parts(z_ffn_ref[s])
        add_vector("gain_ffn", grad_write * normed)
        add_vector("shift_ffn", grad_write)
        grad_sum = norm_pull(normed, inverse, grad_write * vector(vec_ref, "gain_ffn"))
        grad_low = grad_sum.astype(LOW)
        ffn_ref[s] = grad_low
        add_vector("b_down", grad_low.astype(FULL))
        grad_hidden = grad_sum

        if back == 0:
            for load in down_loads:
                load.wait()
        pre_grads = []
        for i in range(chunks):
            part = slice(i * size, (i + 1) * size)
            grad_act = nt(grad_low, down_ref[i])
            grad_pre = (grad_act * gelu_slope(pre_ref[s, :, part])).astype(LOW)
            pre_grad_ref[s, :, part] = grad_pre
            bias_grad_ref[i] += jnp.sum(grad_pre.astype(FULL), 0, keepdims=True)
            pre_grads.append(grad_pre)
        if back == 0:
            for load in up_loads:
                load.wait()
        for i in range(chunks):
            grad_hidden = grad_hidden + nn(pre_grads[i], up_ref[i])
        normed, inverse = norm_parts(z_attn_ref[s])
        add_vector("gain_attn", grad_hidden * normed)
        add_vector("shift_attn", grad_hidden)
        grad_attn = norm_pull(normed, inverse, grad_hidden * vector(vec_ref, "gain_attn"))
        add_vector("b_out", grad_attn)
        grad_mixed = grad_attn.astype(LOW)
        mixed_ref[s] = grad_mixed

        if back == 0:
            attn_loads[0].wait()
            attn_loads[3].wait()
        for load in token_loads(s):
            load.wait()
        grad_attended = nt(grad_mixed, attn_ref[3]).astype(LOW)
        attended_ref[s] = grad_attended
        queries, keys, values = qkv_ref[s, 0], qkv_ref[s, 1], qkv_ref[s, 2]
        spread = by_head(grad_attended, mask, heads)
        soft, soft_mem = soft_ref[s], soft_mem_ref[s]
        pull = nt(spread, value_ref[s])
        pull_mem = nt(spread, values)
        inner = jnp.sum(soft * pull, -1, keepdims=True) + 2.0 * jnp.sum(
            soft_mem * pull_mem, -1, keepdims=True
        )
        grad_score = (soft * (pull - inner)).astype(LOW)
        grad_score_mem = (soft_mem * (pull_mem - inner)).astype(LOW)
        score_ref[s] = grad_score
        grad_query = nn(grad_score, key_ref[s]) + 2.0 * nn(grad_score_mem, keys)
        grad_query = (SCALE * own_head(grad_query, mask, heads)).astype(LOW)
        grad_key = SCALE * tn(grad_score_mem, by_head(queries, mask, heads))
        grad_key = (token_part_ref[s ^ me, :PAD] + grad_key).astype(LOW)
        grad_value = tn(soft_mem.astype(LOW), spread)
        grad_value = (token_part_ref[s ^ me, PAD:] + grad_value).astype(LOW)
        small_ref[s, 0] = grad_query
        small_ref[s, 1] = grad_key
        small_ref[s, 2] = grad_value
        add_vector("b_query", grad_query.astype(FULL))
        add_vector("b_value", 2.0 * grad_value.astype(FULL))
        grad_read = 2.0 * (nn(grad_key, attn_ref[1]) + nn(grad_value, attn_ref[2]))
        grad_read = grad_read + nn(grad_query, attn_ref[0]) + grad_attn
        stop = (reset_ref[0, s] > 0) | (s == 0)
        init_grad_ref[...] += jnp.where(stop, grad_read, 0.0)
        return jnp.where(stop, 0.0, grad_read)

    for back in range(segments - 1):
        grad_write = step(back, grad_write)
    for load in token_loads(last):
        load.wait()
    norm = last_norm(
        heads,
        memory_rows,
        bias_ref,
        vec_ref,
        read_ref[last],
        [qkv_ref[last, i] for i in range(3)],
        key_ref[last],
        value_ref[last],
        (attn_ref[3], up_ref, down_ref),
    )
    lane = lax.broadcasted_iota(jnp.int32, norm_ref.shape, 1)
    norm_ref[...] = jnp.where(lane == last, norm, norms_ref[...])


    packed, wide = factor_ref.shape[1], (segments - 1) * PAD
    row = lax.broadcasted_iota(jnp.int32, (packed, wide), 0)
    source = lax.broadcasted_iota(jnp.int32, (packed, wide), 1)
    take = (source // PAD == row // memory_rows) & (source % PAD == row % memory_rows)
    take = jnp.where(take, 1.0, 0.0).astype(LOW)
    mine = width // 2

    def own_units(ref):
        first = ref[: segments - 1, :, :mine].reshape(wide, mine)
        second = ref[: segments - 1, :, half : half + mine].reshape(wide, mine)
        return jnp.concatenate([first, second], 1)

    acts = gelu(own_units(pre_ref)).astype(LOW)
    factor_ref[0] = nn(take, hidden_ref[: segments - 1].reshape(wide, width)).astype(LOW)
    factor_ref[1] = nn(take, ffn_ref[...].reshape(wide, width)).astype(LOW)
    factor_ref[2] = nn(take, acts).astype(LOW)
    factor_ref[3] = nn(take, own_units(pre_grad_ref)).astype(LOW)


def whole_call(
    body,
    scalars,
    operands,
    outside,
    shapes,
    flops,
    scratch=(),
    outside_shapes=(),
    limit=VMEM_LIMIT,
):
    in_vmem = pl.BlockSpec(memory_space=pltpu.VMEM)
    in_smem = pl.BlockSpec(memory_space=pltpu.SMEM)
    anywhere = pl.BlockSpec(memory_space=pl.ANY)
    size = sum(a.size * a.dtype.itemsize for a in (*operands, *outside, *shapes))
    return pl.pallas_call(
        body,
        out_shape=(*shapes, *outside_shapes),
        in_specs=[in_smem] * len(scalars) + [in_vmem] * len(operands) + [anywhere] * len(outside),
        out_specs=[in_vmem] * len(shapes) + [anywhere] * len(outside_shapes),
        scratch_shapes=scratch,
        compiler_params=pltpu.CompilerParams(vmem_limit_bytes=limit),
        cost_estimate=pl.CostEstimate(flops=flops // 1000, bytes_accessed=size // 1000, transcendentals=0),
    )(*scalars, *operands, *outside)


def unit_owner(column, order, stages, head_order, layout, index):
    head = position(partner(index, stages, "head"), head_order)
    at = head * layout.dps + position(partner(index, stages, "dp"), order)
    return column // layout.rows == at


def attention_loads(layout, place_ref, order_a, order_b, pieces, attn_ref, arrived):
    loads = []

    def copy(source, target):
        loads.append(pltpu.make_async_copy(source, target, arrived.at[len(loads)]))

    if layout.whole:
        copy(pieces[0], attn_ref)
        return loads
    here = layout.width // layout.heads
    for m in range(4):
        copy(pieces[0].at[m], attn_ref.at[m, pl.ds(0, here)])
    per = layout.dps // 4
    rows = here // per // 2
    for side, order in enumerate((order_a, order_b)):
        for index in range(layout.dps):
            flip = sum(((index >> k) & 1) * bit for k, bit in enumerate(order))
            owner = place_ref[0] ^ flip
            piece = pieces[1 + 4 * side + index // (layout.dps // 4)]
            for group in range(1, layout.heads):
                row = group * here + (owner % per) * 2 * rows + side * rows
                copy(
                    piece.at[index % (layout.dps // 4), group - 1],
                    attn_ref.at[owner // per, pl.ds(pl.multiple_of(row, 16), rows)],
                )
    return loads


def project(
    layout,
    stages,
    order_a,
    order_b,
    head_order,
    place_ref,
    token_ref,
    bias_ref,
    other_ref,
    *refs,
):
    count = 1 if layout.whole else 9
    pieces, refs = refs[:count], refs[count:]
    (
        key_ref,
        value_ref,
        x_ref,
        q_ref,
        k_ref,
        v_ref,
        vec_ref,
        bias_in_ref,
        attn_to,
        attn_ref,
        arrived,
        stored,
    ) = refs
    loads = attention_loads(layout, place_ref, order_a, order_b, pieces, attn_ref, arrived)
    for load in loads:
        load.start()
    devices, entries = bias_ref.shape
    width, rows = layout.width, layout.rows
    here = width // layout.heads
    packets = bias_ref[...].astype(FULL)

    def laid_out(first, count, period, owner):
        entry = lax.broadcasted_iota(jnp.int32, (entries, count), 0)
        column = lax.broadcasted_iota(jnp.int32, (entries, count), 1)
        pick = jnp.where(entry == first + column % period, 1.0, 0.0).astype(LOW)
        index = lax.broadcasted_iota(jnp.int32, (devices, count), 0)
        column = lax.broadcasted_iota(jnp.int32, (devices, count), 1)
        chosen = jnp.where(owner(column, index), nn(packets.astype(LOW), pick), 0.0)
        return jnp.sum(chosen, 0, keepdims=True)

    def of_head(column, index):
        head = partner(index, stages, "head")
        return (partner(index, stages, "dp") == 0) & (head == column // here)

    vec_ref[0:1, :] = laid_out(0, width, here, of_head)
    vec_ref[1:2, :] = laid_out(here, width, here, of_head)
    vec_ref[2:, :] = other_ref[...].astype(FULL)
    for half, order in enumerate((order_a, order_b)):
        owner = functools.partial(
            unit_owner, order=order, stages=stages, head_order=head_order, layout=layout
        )
        row = laid_out(
            2 * here + half * rows,
            layout.blocks * rows,
            rows,
            lambda column, index: owner(column, index=index),
        )
        per = layout.chunks // 2
        for i in range(per):
            bias_in_ref[half * per + i] = row[:, i * layout.size : (i + 1) * layout.size]

    for load in loads:
        load.wait()
    store = pltpu.make_async_copy(attn_ref, attn_to, stored)
    store.start()
    for s in range(token_ref.shape[0]):
        x = token_ref[s]
        key_ref[s] = nt(x, attn_ref[1]).astype(LOW)
        value_ref[s] = (nt(x, attn_ref[2]) + vector(vec_ref, "b_value")).astype(LOW)
    own = place_ref[1]
    x = token_ref[own]
    x_ref[...] = x
    q_ref[...] = (nt(x, attn_ref[0]) + vector(vec_ref, "b_query")).astype(LOW)
    k_ref[...] = key_ref[own]
    v_ref[...] = value_ref[own]
    store.wait()


SUMS = ("b_out", "gain_attn", "shift_attn", "b_down", "gain_ffn", "shift_ffn")


def token_layer(
    layout,
    memory_rows,
    head_dim,
    place_ref,
    x_ref,
    q_ref,
    qkv_ref,
    part_ref,
    stat_ref,
    cot_ref,
    bias_ref,
    vec_ref,
    attn_ref,
    *refs,
):
    count = len(layout.pieces())
    pieces, refs = refs[:count], refs[count:]
    (
        attended_ref,
        log_ref,
        result_ref,
        skip_ref,
        mixed_ref,
        grad_attended_ref,
        bias_sum_ref,
        sum_ref,
        *grad_refs,
        out_w_ref,
        out_arrived,
        up_ref,
        down_ref,
        arrived,
        z_attn_ref,
        hidden_ref,
        low_ref,
        total_ref,
        pre_ref,
        act_ref,
        stage_ref,
        sent,
    ) = refs
    out_load = pltpu.make_async_copy(attn_ref.at[3], out_w_ref, out_arrived)
    out_load.start()
    up_loads, down_loads = layout.loads(pieces, up_ref, down_ref, arrived)
    for load in up_loads + down_loads:
        load.start()
    chunks = layout.chunks
    pair = part_ref.shape[1]
    log_ref[...] = jnp.zeros_like(log_ref)
    for i in range(part_ref.shape[0]):
        columns = slice(i * pair, (i + 1) * pair)
        mixed, logs = with_memory(
            memory_rows,
            head_dim,
            q_ref[:, columns],
            qkv_ref[place_ref[1], 1, :, columns],
            qkv_ref[place_ref[1], 2, :, columns],
            part_ref[i],
            stat_ref[i],
        )
        attended_ref[:, columns] = mixed
        for head, log in enumerate(logs):
            log_ref[i, head : head + 1] = log
    out_load.wait()
    sum_ref[...] = jnp.zeros_like(sum_ref)

    def add_vector(name, grad):
        i = SUMS.index(name)
        sum_ref[i : i + 1, :] += jnp.sum(grad, 0, keepdims=True)

    z_attn = x_ref[...].astype(FULL) + nn(attended_ref[...], out_w_ref[...])
    z_attn = z_attn + vector(vec_ref, "b_out")
    z_attn_ref[...] = z_attn
    normed, _ = norm_parts(z_attn)
    hidden = normed * vector(vec_ref, "gain_attn") + vector(vec_ref, "shift_attn")
    hidden_ref[...] = hidden.astype(LOW)
    total_ref[...] = hidden + vector(vec_ref, "b_down")
    for load in up_loads + down_loads:
        load.wait()

    for i in range(chunks):
        pre = nt(hidden_ref[...], up_ref[i]) + bias_ref[i]
        pre_ref[i] = pre
        act = gelu(pre).astype(LOW)
        act_ref[i] = act
        total_ref[...] += nn(act, down_ref[i])
    normed, inverse = norm_parts(total_ref[...])
    result = normed * vector(vec_ref, "gain_ffn") + vector(vec_ref, "shift_ffn")
    result_ref[...] = result.astype(LOW)
    grad = cot_ref[...].astype(FULL)
    add_vector("gain_ffn", grad * normed)
    add_vector("shift_ffn", grad)
    grad = norm_pull(normed, inverse, grad * vector(vec_ref, "gain_ffn"))
    total_ref[...] = grad
    low_ref[...] = grad.astype(LOW)
    add_vector("b_down", low_ref[...].astype(FULL))

    copies = list(layout.copies())
    spans = [first for first, _ in layout.pieces()]
    stores = []
    for i in range(chunks):
        grad_pre = (nt(low_ref[...], down_ref[i]) * gelu_slope(pre_ref[i])).astype(LOW)
        bias_sum_ref[i] = jnp.sum(grad_pre.astype(FULL), 0, keepdims=True)
        total_ref[...] += nn(grad_pre, up_ref[i])
        slot = i % 2
        if i > 1:
            for store in stores[i - 2]:
                store.wait()
        stage_ref[slot, 0] = tn(grad_pre, hidden_ref[...]).astype(LOW)
        stage_ref[slot, 1] = tn(act_ref[i], low_ref[...]).astype(LOW)
        stores.append([])
        for number, entry, chunk, row, rows in copies:
            if chunk != i:
                continue
            for side in range(2):
                to_ref = grad_refs[number // (len(spans) // len(grad_refs))]
                entry_at = spans[number] - spans[number - number % (len(spans) // len(grad_refs))]
                store = pltpu.make_async_copy(
                    stage_ref.at[slot, side, pl.ds(row, rows)],
                    to_ref.at[entry_at + entry, side],
                    sent.at[i, len(stores[i])],
                )
                store.start()
                stores[i].append(store)

    grad_hidden = total_ref[...]
    normed, inverse = norm_parts(z_attn_ref[...])
    add_vector("gain_attn", grad_hidden * normed)
    add_vector("shift_attn", grad_hidden)
    grad = norm_pull(normed, inverse, grad_hidden * vector(vec_ref, "gain_attn"))
    add_vector("b_out", grad)
    skip_ref[...] = grad
    mixed_ref[...] = grad.astype(LOW)
    grad_attended_ref[...] = nt(mixed_ref[...], out_w_ref[...]).astype(LOW)
    for i in range(max(chunks - 2, 0), chunks):
        for store in stores[i]:
            store.wait()


def part_rows(keep_ref, send_ref, first, columns, grad, place_ref, order, count):
    rows = grad.shape[0] // count
    for c in range(count):
        block = grad[c * rows : (c + 1) * rows].astype(keep_ref.dtype)
        at = position(place_ref[0] ^ c, order)

        @pl.when(at < count // 2)
        def _():
            keep_ref[at, first : first + rows, columns] = block

        @pl.when(at >= count // 2)
        def _():
            send_ref[at - count // 2, first : first + rows, columns] = block


SUM_ROWS = 32


def pack_sums(
    layout, order_a, order_b, head_order, heads_here, memory_rows, place_ref, groups, rows, halves
):
    count, width = rows.shape
    dps = layout.dps
    devices = dps * groups
    here, part = width // layout.heads, width // (dps * layout.heads)
    head_dim = here // heads_here
    head_part = head_dim // dps

    def partners(index):
        head = index % groups
        dp = 0
        for k, bit in enumerate(order_a):
            dp = dp + ((index // groups >> k) & 1) * bit
        return dp, head

    shape = (devices, count, width)
    index, row, column = (lax.broadcasted_iota(jnp.int32, shape, i) for i in range(3))
    dp_flip, head_flip = partners(index)
    dp, head = place_ref[0] ^ dp_flip, place_ref[1] ^ head_flip
    plain = len(SUMS) + memory_rows
    of_device = column // part == dp * layout.heads + head
    of_head = (column // here == head_flip) & (column % head_dim // head_part == dp)
    chosen = ((row < plain) & of_device) | ((row >= plain) & of_head)
    chosen = jnp.where(chosen, jnp.broadcast_to(rows[None], shape), 0.0)
    chosen = chosen.reshape(devices * count, width).astype(LOW)
    source = lax.broadcasted_iota(jnp.int32, (width, part), 0)
    target = lax.broadcasted_iota(jnp.int32, (width, part), 1)
    plain_fold = jnp.where(source % part == target, 1.0, 0.0).astype(LOW)
    head_column = source // head_dim % heads_here * head_part + source % head_part
    head_fold = jnp.where(head_column == target, 1.0, 0.0).astype(LOW)
    row = lax.broadcasted_iota(jnp.int32, (devices, count, part), 1)
    folded = jnp.where(
        row < plain,
        nn(chosen, plain_fold).reshape(devices, count, part),
        nn(chosen, head_fold).reshape(devices, count, part),
    )
    unit_rows = []
    span = halves[0].shape[1]
    index, column = (lax.broadcasted_iota(jnp.int32, (devices, span), i) for i in range(2))
    source = lax.broadcasted_iota(jnp.int32, (span, layout.rows), 0)
    target = lax.broadcasted_iota(jnp.int32, (span, layout.rows), 1)
    fold = jnp.where(source % layout.rows == target, 1.0, 0.0).astype(LOW)
    for order, half in zip((order_a, order_b), halves):
        dp_flip, head_flip = partners(index)
        at = position(head_flip, head_order) * dps + position(dp_flip, order)
        chosen = jnp.where(column // layout.rows == at, half, 0.0)
        unit_rows.append(nn(chosen.astype(LOW), fold))
    return folded, unit_rows


def put_sums(ref, entry, first_row, first_column, packed, index, memory_rows):
    folded, unit_rows = packed
    plain = len(SUMS) + memory_rows
    part, block = folded.shape[2], unit_rows[0].shape[1]
    columns = slice(first_column, first_column + part)
    ref[entry, first_row : first_row + plain + 2, columns] = folded[index, : plain + 2].astype(LOW)
    columns = slice(first_column, first_column + block)
    for half, rows in enumerate(unit_rows):
        row = first_row + plain + 2 + half
        ref[entry, row : row + 1, columns] = rows[index : index + 1].astype(LOW)


def half_rows(ref, layout):
    per = layout.chunks // 2
    return [
        jnp.concatenate([ref[half * per + i] for i in range(per)], 1) for half in range(2)
    ]


def value_grads(
    order,
    count,
    place_ref,
    x_ref,
    mixed_ref,
    attended_ref,
    dv0_ref,
    dv1_ref,
    skip_ref,
    attn_from,
    keep_ref,
    send_ref,
    grad_x_ref,
    sum_ref,
    attn_ref,
    arrived,
):
    load = pltpu.make_async_copy(attn_from.at[2], attn_ref, arrived)
    load.start()
    x, low, high = x_ref[...], dv0_ref[...], dv1_ref[...]
    half = low.shape[1]
    share = x.shape[1] // count
    every = slice(None)
    both = jnp.concatenate([tn(x, low), tn(x, high)], 1)
    part_rows(keep_ref, send_ref, 0, every, both, place_ref, order, count)
    both = tn(mixed_ref[...], attended_ref[...])
    part_rows(keep_ref, send_ref, share, every, both, place_ref, order, count)
    sum_ref[:, :half] = jnp.sum(low.astype(FULL), 0, keepdims=True)
    sum_ref[:, half:] = jnp.sum(high.astype(FULL), 0, keepdims=True)
    load.wait()
    grad_x_ref[...] = skip_ref[...] + nn(low, attn_ref[:half]) + nn(high, attn_ref[half:])


def query_key_grads(
    layout,
    order_a,
    order_b,
    head_order,
    heads_here,
    memory_rows,
    place_ref,
    x_ref,
    dq0_ref,
    dq1_ref,
    dk0_ref,
    dk1_ref,
    part_ref,
    value_sum_ref,
    layer_sum_ref,
    bias_sum_ref,
    attn_from,
    keep_ref,
    send_ref,
    grad_x_ref,
    rows_ref,
    attn_ref,
    arrived,
):
    loads = [
        pltpu.make_async_copy(attn_from.at[i], attn_ref.at[i], arrived.at[i]) for i in range(2)
    ]
    for load in loads:
        load.start()
    count = layout.dps
    x = x_ref[...]
    half = dq0_ref.shape[1]
    share = x.shape[1] // count
    pairs = [(dq0_ref[...], dq1_ref[...]), (dk0_ref[...], dk1_ref[...])]
    for m, (low, high) in enumerate(pairs):
        both = jnp.concatenate([tn(x, low), tn(x, high)], 1)
        part_rows(keep_ref, send_ref, m * share, slice(None), both, place_ref, order_a, count)
    plain = len(SUMS) + memory_rows
    rows_ref[...] = jnp.zeros_like(rows_ref)
    rows_ref[: len(SUMS), :] = layer_sum_ref[: len(SUMS), :]
    for at, array in zip((0, half), pairs[0]):
        rows_ref[plain : plain + 1, at : at + half] = jnp.sum(array.astype(FULL), 0, keepdims=True)
    rows_ref[plain + 1 : plain + 2, :] = value_sum_ref[...]
    packed = pack_sums(
        layout,
        order_a,
        order_b,
        head_order,
        heads_here,
        memory_rows,
        place_ref,
        layout.heads,
        rows_ref[...],
        half_rows(bias_sum_ref, layout),
    )
    here = x.shape[1] // layout.heads
    for at in range(count):
        ref = keep_ref if at < count // 2 else send_ref
        entry = at % (count // 2)
        ref[entry, 2 * share :, :] = jnp.zeros((SUM_ROWS, x.shape[1]), LOW)
        for g in range(layout.heads):
            index = at * layout.heads + g
            put_sums(ref, entry, 2 * share, g * here, packed, index, memory_rows)
    total = part_ref[...]
    for m, (low, high) in enumerate(pairs):
        loads[m].wait()
        total = total + nn(low, attn_ref[m, :half]) + nn(high, attn_ref[m, half:])
    grad_x_ref[...] = total.astype(LOW)


def own_grads(
    layout,
    order_a,
    order_b,
    head_order,
    heads,
    heads_here,
    memory_rows,
    place_ref,
    score_ref,
    soft_ref,
    qkv_ref,
    attended_grad_ref,
    mixed_ref,
    attended_ref,
    small_ref,
    read_ref,
    token_ref,
    bias_grad_ref,
    vec_grad_ref,
    init_grad_ref,
    keep_ref,
    send_ref,
    rows_ref,
):
    count = layout.dps
    writes, rows, _ = score_ref.shape
    width = qkv_ref.shape[-1]
    here = width // heads * heads_here
    mine = heads_here * PAD
    mask = head_mask(rows, width, heads)[:mine]
    total = jnp.zeros((1, here), FULL)
    grads = [jnp.zeros((width, here), FULL) for _ in range(4)]
    for s in range(writes + 1):
        low = read_ref[s].astype(LOW)
        grads[1] = grads[1] + 2.0 * tn(low, small_ref[s, 1, :, :here])
        grads[2] = grads[2] + 2.0 * tn(low, small_ref[s, 2, :, :here])
        if s == writes:
            break
        grads[0] = grads[0] + tn(low, small_ref[s, 0, :, :here])
        grads[3] = grads[3] + tn(mixed_ref[s], attended_ref[s, :, :here])
        spread = by_head(qkv_ref[s, 0], mask, heads_here)[:, :here]
        pulled = by_head(attended_grad_ref[s], mask, heads_here)[:, :here]
        dk = (SCALE * tn(score_ref[s, :mine], spread)).astype(LOW)
        dv = tn(soft_ref[s, :mine].astype(LOW), pulled).astype(LOW)
        grads[1] = grads[1] + tn(token_ref[s], dk)
        grads[2] = grads[2] + tn(token_ref[s], dv)
        total = total + jnp.sum(dv.astype(FULL), 0, keepdims=True)
    both = jnp.concatenate(grads, 1)
    part_rows(keep_ref, send_ref, 0, slice(None), both, place_ref, order_a, count)
    rows_ref[...] = jnp.zeros_like(rows_ref)
    for i, name in enumerate(SUMS):
        at = VECTORS.index(name)
        rows_ref[i : i + 1, :] = vec_grad_ref[at : at + 1, :]
    for i in range(memory_rows):
        at = len(SUMS) + i
        rows_ref[at : at + 1, :] = init_grad_ref[i : i + 1, :]
    at = len(SUMS) + memory_rows
    rows_ref[at : at + 2, :] = vec_grad_ref[0:2, :]
    rows_ref[at + 1 : at + 2, :here] += total
    packed = pack_sums(
        layout,
        order_a,
        order_b,
        head_order,
        heads_here,
        memory_rows,
        place_ref,
        1,
        rows_ref[...],
        half_rows(bias_grad_ref, layout),
    )
    share = width // count
    for at in range(count):
        ref = keep_ref if at < count // 2 else send_ref
        entry = at % (count // 2)
        ref[entry, share:, :] = jnp.zeros((SUM_ROWS, width), LOW)
        put_sums(ref, entry, share, 0, packed, at, memory_rows)


def write_rows(
    heads,
    quarter,
    place_ref,
    score_ref,
    soft_ref,
    qkv_ref,
    attended_grad_ref,
    moved_ref,
    attn_from,
    grad_token_ref,
    attn_ref,
    arrived,
):
    writes, rows, _ = score_ref.shape
    loads = [
        pltpu.make_async_copy(attn_from.at[i + 1], attn_ref.at[i], arrived.at[i])
        for i in range(2)
    ]
    for load in loads:
        load.start()
    mask = head_mask(rows, qkv_ref.shape[-1], heads)
    at = pl.multiple_of(place_ref[1] * quarter, quarter)
    for load in loads:
        load.wait()
    for s in range(writes):
        spread = by_head(qkv_ref[s, 0], mask, heads)
        pulled = by_head(attended_grad_ref[s], mask, heads)
        score_here = score_ref[s, :, pl.ds(at, quarter)]
        soft_here = soft_ref[s, :, pl.ds(at, quarter)].astype(LOW)
        dk = (SCALE * tn(score_here, spread)).astype(LOW)
        dv = tn(soft_here, pulled).astype(LOW)
        extra = nn(dk, attn_ref[0]) + nn(dv, attn_ref[1])
        grad_token_ref[s] = moved_ref[s].astype(FULL) + extra
    grad_token_ref[writes] = moved_ref[writes].astype(FULL)


def finish(
    order_a,
    order_b,
    memory_rows,
    numbers,
    *refs,
):
    groups = []
    for number in numbers:
        groups.append(refs[:number])
        refs = refs[number:]
    factor_refs, *groups = groups

    def total_of(group, *at):
        total = group[0][(0, *at)].astype(FULL)
        for ref in group[1:]:
            total = total + ref[(0, *at)].astype(FULL)
        return total

    ffn_a, ffn_b, attn_terms, own_terms = groups
    (
    query_ref,
    key_ref,
    value_ref,
    b_query_ref,
    b_value_ref,
    out_ref,
    b_out_ref,
    gain_attn_ref,
    shift_attn_ref,
    up_ref,
    b_in_ref,
    down_ref,
    b_down_ref,
    gain_ffn_ref,
    shift_ffn_ref,
    init_ref,
    ) = refs
    factor = jnp.concatenate([ref[...] for ref in factor_refs], 0)
    count, _, rows, width = factor.shape
    block = width // 2 // count
    column = lax.broadcasted_iota(jnp.int32, (rows, width), 1)

    def own(j, i):
        first, second = position(j, order_a), position(j, order_b) + count
        keep = (column // block == first) | (column // block == second)
        return jnp.where(keep, factor[j, i], jnp.zeros((), LOW))

    units = []
    for side, left, right in ((0, 3, 0), (1, 2, 1)):
        chosen = jnp.concatenate([own(j, left) for j in range(count)], 0)
        others = jnp.concatenate([factor[j, right] for j in range(count)], 0)
        product = tn(chosen, others)
        halves = []
        for i in range(2):
            total = total_of((ffn_a, ffn_b)[i], side)
            for j in range(count):
                at = (i * count + j) * block
                total = total + product[at : at + block]
            halves.append(total)
        units.append(jnp.concatenate(halves, 0))
    up_ref[...] = units[0]
    down_ref[...] = units[1]
    attn, own_total = total_of(attn_terms), total_of(own_terms)
    here = attn.shape[-1] // 2
    share = own_total.shape[0] - SUM_ROWS
    totals = []
    for m in range(4):
        row, column = m % 2 * share, m // 2 * here
        from_tokens = attn[row : row + share, column : column + here]
        totals.append(from_tokens + own_total[:share, m * here : (m + 1) * here])
    query_ref[...] = totals[0]
    key_ref[...] = totals[1]
    value_ref[...] = totals[2]
    out_ref[...] = totals[3].T
    pack = attn[2 * share : 2 * share + SUM_ROWS, :here] + own_total[share:, :here]
    refs = {
        "b_out": b_out_ref,
        "gain_attn": gain_attn_ref,
        "shift_attn": shift_attn_ref,
        "b_down": b_down_ref,
        "gain_ffn": gain_ffn_ref,
        "shift_ffn": shift_ffn_ref,
    }
    part = init_ref.shape[1]
    for i, name in enumerate(SUMS):
        refs[name][...] = pack[i : i + 1, :part]
    at = len(SUMS) + memory_rows
    init_ref[...] = pack[len(SUMS) : at, :part]
    heads_here, head_part = b_query_ref.shape
    for i in range(heads_here):
        columns = slice(i * head_part, (i + 1) * head_part)
        b_query_ref[i : i + 1, :] = pack[at : at + 1, columns]
        b_value_ref[i : i + 1, :] = pack[at + 1 : at + 2, columns]
    b_in_ref[:, :block] = pack[at + 2 : at + 3, :block]
    b_in_ref[:, block:] = pack[at + 3 : at + 4, :block]


def columns_of(head, head_dim, array, factor=None):
    lane = lax.broadcasted_iota(jnp.int32, array.shape, 1) // head_dim
    if factor is not None:
        array = array * jnp.asarray(factor, array.dtype)
    return jnp.where(lane == head, array, jnp.zeros((), array.dtype))


def memory_scores(memory_rows, km, mine):
    scores = nt(km, mine)
    real_key = lax.broadcasted_iota(jnp.int32, scores.shape, 0) < memory_rows
    return jnp.where(real_key, scores, NEGATIVE)


def token_attention(head_dim, place_ref, row_ref, column_ref, q_ref, k_ref, v_ref, sum_ref, stat_ref):
    q, k, v = q_ref[...], k_ref[...], v_ref[...]
    allowed = column_ref[...] == row_ref[...]
    stat_ref[...] = jnp.zeros_like(stat_ref)
    for head in range(q.shape[1] // head_dim):
        scores = nt(k, columns_of(head, head_dim, q, SCALE))
        scores = jnp.where(allowed, scores, NEGATIVE)
        top = jnp.max(scores, 0, keepdims=True)
        raised = jnp.exp(scores - top)
        stat_ref[0, 2 * head : 2 * head + 1] = top
        stat_ref[0, 2 * head + 1 : 2 * head + 2] = jnp.sum(raised, 0, keepdims=True)
        rows = slice(head * head_dim, (head + 1) * head_dim)
        sum_ref[0, rows] = tn(v, raised.astype(LOW))[rows]


def with_memory(memory_rows, head_dim, q, km, vm, sums, stats):
    mixed, logs = [], []
    for head in range(q.shape[1] // head_dim):
        scores = memory_scores(memory_rows, km, columns_of(head, head_dim, q, SCALE))
        top_before = stats[2 * head : 2 * head + 1]
        top = jnp.maximum(jnp.max(scores, 0, keepdims=True), top_before)
        raised = jnp.exp(scores - top)
        shrink = jnp.exp(top_before - top)
        total = stats[2 * head + 1 : 2 * head + 2] * shrink
        total = total + 2.0 * jnp.sum(raised, 0, keepdims=True)
        rows = slice(head * head_dim, (head + 1) * head_dim)
        both = sums[rows] * shrink + 2.0 * tn(vm, raised.astype(LOW))[rows]
        mixed.append(both * (1.0 / total))
        logs.append(top + jnp.log(total))
    return jnp.concatenate(mixed, 0).T.astype(LOW), logs


def token_attention_back(
    memory_rows,
    head_dim,
    place_ref,
    row_ref,
    column_ref,
    q_ref,
    k_ref,
    v_ref,
    qkv_ref,
    log_ref,
    grad_ref,
    dq_ref,
    dk_ref,
    dv_ref,
    dmem_ref,
):
    q, k, v, grad = (ref[...] for ref in (q_ref, k_ref, v_ref, grad_ref))
    km, vm = qkv_ref[place_ref[1], 1], qkv_ref[place_ref[1], 2]
    allowed = column_ref[...] == row_ref[...]
    lane = lax.broadcasted_iota(jnp.int32, q.shape, 1) // head_dim
    dq, dk, dv = (jnp.zeros(q.shape, FULL) for _ in range(3))
    dkm, dvm = (jnp.zeros(km.shape, FULL) for _ in range(2))
    for head in range(q.shape[1] // head_dim):
        mine = columns_of(head, head_dim, q, SCALE)
        mine_grad = columns_of(head, head_dim, grad)
        log_total = log_ref[0, head : head + 1]
        scores = jnp.where(allowed, nt(k, mine), NEGATIVE)
        soft = jnp.exp(scores - log_total)
        soft_mem = jnp.exp(memory_scores(memory_rows, km, mine) - log_total)
        pull, pull_mem = nt(v, mine_grad), nt(vm, mine_grad)
        inner = jnp.sum(soft * pull, 0, keepdims=True) + 2.0 * jnp.sum(
            soft_mem * pull_mem, 0, keepdims=True
        )
        score = (soft * (pull - inner)).astype(LOW)
        score_mem = (soft_mem * (pull_mem - inner)).astype(LOW)
        dq = jnp.where(lane == head, tn(score, k) + 2.0 * tn(score_mem, km), dq)
        dk = dk + nn(score, mine)
        dv = dv + nn(soft.astype(LOW), mine_grad)
        dkm = dkm + nn(score_mem, mine)
        dvm = dvm + nn(soft_mem.astype(LOW), mine_grad)
    dq_ref[...] = (SCALE * dq).astype(LOW)
    dk_ref[...] = dk.astype(LOW)
    dv_ref[...] = dv.astype(LOW)
    dmem_ref[:PAD] = dkm
    dmem_ref[PAD:] = dvm


def head_pairs(body, place, doc, operands, shapes, width, flops, steps, first=0):
    seg_len = operands[0].shape[0]

    def spec(array, first):
        if len(array.shape) == 4:
            return pl.BlockSpec((*array.shape[:3], width), lambda i: (0, 0, 0, i + first))
        if len(array.shape) == 3:
            return pl.BlockSpec((1, *array.shape[1:]), lambda i: (i + first, 0, 0))
        return pl.BlockSpec((array.shape[0], width), lambda i: (0, i + first))

    return pl.pallas_call(
        body,
        grid=(steps,),
        out_shape=shapes,
        in_specs=[pl.BlockSpec(memory_space=pltpu.SMEM)]
        + [pl.BlockSpec(a.shape, lambda i: (0, 0)) for a in doc]
        + [spec(a, first) for a in operands],
        out_specs=[spec(s, 0) for s in shapes],
        compiler_params=pltpu.CompilerParams(vmem_limit_bytes=VMEM_LIMIT),
        cost_estimate=pl.CostEstimate(
            flops=flops // 1000, bytes_accessed=seg_len, transcendentals=0
        ),
    )(place, *doc, *operands)


def on_device(
    tokens,
    doc_ids,
    reset,
    mem_init,
    w_query,
    w_key,
    w_value,
    b_query,
    b_value,
    w_out,
    b_out,
    gain_attn,
    shift_attn,
    w_in,
    b_in,
    w_down,
    b_down,
    gain_ffn,
    shift_ffn,
    cotangent,
):
    chains, segments, seg_len, width = tokens.shape
    dps, groups = lax.axis_size("dp"), lax.axis_size("head")
    assert chains == 1 and segments == groups
    memory_rows = mem_init.shape[0]
    heads_here, head_dim = b_query.shape
    heads = heads_here * groups
    here = heads_here * head_dim
    units = w_in.shape[1]
    half_units = units // 2
    quarter = seg_len // groups
    dp, head = lax.axis_index("dp"), lax.axis_index("head")
    place = jnp.stack([dp, head])
    bits = bits_of(dps)
    levels = len(bits)
    order_a = bits[1:] + bits[:1]
    order_b = bits[1:][::-1] + bits[:1]
    head_order = bits_of(groups)[::-1]
    head_stages = [("head", bit) for bit in head_order]
    stages_a = head_stages + [("dp", bit) for bit in order_a]
    stages_b = head_stages + [("dp", bit) for bit in order_b]
    layout = Units(dps, groups, half_units, width)
    landing = layout.scratch()
    shape = jax.ShapeDtypeStruct
    dp_stages = [("dp", bit) for bit in bits]
    bias_groups = (head_stages[:1], dp_stages[1:], head_stages[1:] + dp_stages[:1])
    bias_stages = [stage for group in bias_groups for stage in group]
    tokens, doc_ids, cotangent = tokens[0], doc_ids[0], cotangent[0]

    shard = jnp.concatenate([w_query.T, w_key.T, w_value.T, w_out], 0)
    share = shard.shape[0] // dps
    chunk = lax.dynamic_slice_in_dim(shard, dp * share, share, 0)[None]
    biases = jnp.concatenate([b_query.reshape(-1), b_value.reshape(-1), b_in])[None]
    up = w_in.T.reshape(2, half_units, width)
    down = w_down.reshape(2, half_units, width)
    halves = [jnp.stack([up[i], down[i]])[None] for i in range(2)]
    for i, stage in enumerate(head_stages):
        chunk = gather(chunk, [stage])
        if i:
            halves = [gather(half, [head_stages[i - 1]]) for half in halves]
        biases = gather(biases, bias_groups[i])
        chunk, biases, halves = lax.optimization_barrier((chunk, biases, halves))
    halves = [gather(half, head_stages[-1:]) for half in halves]
    biases = gather(biases, bias_groups[2])
    chunk = jnp.stack([chunk[position(j, head_order)] for j in range(1, groups)])
    sides = (slice(0, share // 2), slice(share // 2, share))
    parts = []
    for rows, order in zip(sides, (order_a, order_b)):
        part = gather(chunk[None, :, rows], [("dp", bit) for bit in order[:-2]])
        parts += [part, swap(part, "dp", order[-2])]
    doc = lax.dynamic_index_in_dim(doc_ids, head, 0, False)
    doc_row, doc_column = doc[None, :], doc[:, None]
    init = jnp.pad(mem_init.astype(FULL), ((0, PAD - memory_rows), (0, 0)))
    vectors = jnp.concatenate([b_out, gain_attn, shift_attn, b_down, gain_ffn, shift_ffn])
    vectors = vectors.reshape(-1, width)
    halves, parts, biases, cotangent, doc_row, doc_column, init, vectors = (
        lax.optimization_barrier(
            (halves, parts, biases, cotangent, doc_row, doc_column, init, vectors)
        )
    )
    cotangent = lax.all_to_all(cotangent, "head", 0, 0, tiled=True).reshape(seg_len, width)
    crossed = [swap(part, "dp", bits[0]) for part in parts]
    parts = [*parts[:2], *crossed[:2], *parts[2:], *crossed[2:]]
    if layout.whole:
        chunks = []
        for i, order in ((0, order_a), (4, order_b)):
            part = jnp.concatenate(parts[i : i + 4], 0)
            native = [position(dp ^ c, order) for c in range(dps)]
            chunks.append(jnp.stack([lax.dynamic_index_in_dim(part, n, 0, False) for n in native]))
        others = jnp.concatenate(chunks, 2).transpose(1, 0, 2, 3).reshape(groups - 1, 4, here, width)
        own = shard.reshape(4, 1, here, width)
        attn_pieces = [
            jnp.concatenate([own, others.transpose(1, 0, 2, 3)], 1).reshape(4, width, width)
        ]
    else:
        attn_pieces = [shard.reshape(4, here, width), *parts]
    halves = [
        gather(half, stages[len(head_stages) : -3])
        for half, stages in zip(halves, (stages_a, stages_b))
    ]
    across = [swap(half, *st[-3]) for half, st in zip(halves, (stages_a, stages_b))]
    along = [swap(half, *st[-2]) for half, st in zip(halves, (stages_a, stages_b))]

    keys, values, x, q, k, v, vectors, bias_in, w_attn = whole_call(
        functools.partial(project, layout, bias_stages, order_a, order_b, head_order),
        (place,),
        (tokens, biases, vectors),
        attn_pieces,
        (shape(tokens.shape, LOW),) * 2
        + (shape((seg_len, width), LOW),) * 4
        + (shape((len(VECTORS), width), FULL), shape((layout.chunks, 1, layout.size), FULL)),
        6_000_000_000,
        (
            pltpu.VMEM((4, width, width), LOW),
            pltpu.SemaphoreType.DMA((4 + 2 * dps * groups,)),
            pltpu.SemaphoreType.DMA(()),
        ),
        (shape((4, width, width), LOW),),
    )

    across, along, keys, q = lax.optimization_barrier((across, along, keys, q))
    corner = [swap(side, *stages[-2]) for side, stages in zip(across, (stages_a, stages_b))]
    pair = 2 * head_dim
    partial = head_pairs(
        functools.partial(token_attention, head_dim),
        place,
        (doc_row, doc_column),
        (q, k, v),
        (shape((width // pair, pair, seg_len), FULL), shape((width // pair, 8, seg_len), FULL)),
        pair,
        8_000_000_000,
        width // pair,
    )
    corner, partial, cotangent = lax.optimization_barrier((corner, partial, cotangent))
    pieces = []
    for *near, stages in zip(halves, across, along, corner, (stages_a, stages_b)):
        pieces += near + [swap(piece, *stages[-1]) for piece in near]
    if layout.whole:
        pieces = layout.assembled([jnp.concatenate(pieces[i : i + 8], 0) for i in (0, 8)])

    ff = layout.chunks * layout.size
    writes = segments - 1
    rows_shape = lambda kind: shape((writes, PAD, width), kind)
    tokens_scratch = lambda count: (
        pltpu.VMEM((4, width, width), LOW),
        pltpu.VMEM((count, seg_len, width), LOW),
        pltpu.VMEM((count, seg_len, width), LOW),
        pltpu.SemaphoreType.DMA((4,)),
        pltpu.SemaphoreType.DMA((count,)),
        pltpu.SemaphoreType.DMA((count,)),
    )
    read, qkv, soft, soft_mem, attended_w, z_attn_w, hidden_w, pre_w, z_ffn_w, norms = whole_call(
        functools.partial(chain_forward, layout, heads, memory_rows),
        (reset,),
        (init, bias_in, vectors),
        (w_attn, keys, values, *pieces),
        (
            shape((segments, PAD, width), FULL),
            shape((segments, 3, PAD, width), LOW),
            shape((writes, heads * PAD, seg_len), FULL),
            shape((writes, heads * PAD, PAD), FULL),
            rows_shape(LOW),
            rows_shape(FULL),
            rows_shape(LOW),
            shape((writes, PAD, ff), FULL),
            rows_shape(FULL),
            shape((1, 128), FULL),
        ),
        20_000_000_000,
        tokens_scratch(writes) + landing,
    )

    if layout.whole:
        grad_shapes = (shape((layout.chunks, 2, layout.size, width), LOW),)
    else:
        grad_shapes = (shape((layout.blocks // 2, 2, half_units, width), LOW),) * 4
    sides = 2 * max(layout.size // (layout.size if layout.whole else half_units), 1)
    (
        attended,
        log_total,
        result,
        grad_attn,
        grad_mixed,
        grad_attended,
        bias_sum,
        layer_sums,
        *ffn_grads,
    ) = whole_call(
        functools.partial(token_layer, layout, memory_rows, head_dim),
        (place,),
        (x, q, qkv, *partial, cotangent, bias_in, vectors),
        (w_attn, *pieces),
        (
            shape((seg_len, width), LOW),
            shape((width // pair, 8, seg_len), FULL),
            shape((seg_len, width), LOW),
            shape((seg_len, width), FULL),
            shape((seg_len, width), LOW),
            shape((seg_len, width), LOW),
            shape((layout.chunks, 1, layout.size), FULL),
            shape((8, width), FULL),
        ),
        25_000_000_000,
        (pltpu.VMEM((width, width), LOW), pltpu.SemaphoreType.DMA(()))
        + landing
        + (
            pltpu.VMEM((seg_len, width), FULL),
            pltpu.VMEM((seg_len, width), LOW),
            pltpu.VMEM((seg_len, width), LOW),
            pltpu.VMEM((seg_len, width), FULL),
            pltpu.VMEM((layout.chunks, seg_len, layout.size), FULL),
            pltpu.VMEM((layout.chunks, seg_len, layout.size), LOW),
            pltpu.VMEM((2, 2, layout.size, width), LOW),
            pltpu.SemaphoreType.DMA((layout.chunks, sides)),
        ),
        grad_shapes,
    )
    if layout.whole:
        half_blocks = layout.blocks // 2
        ffn_grads = [
            part
            for half in layout.taken_apart(ffn_grads[0])
            for part in (half[:half_blocks], half[half_blocks:])
        ]

    back_a, back_b = stages_a[::-1], stages_b[::-1]

    def stages_of(level):
        return back_a[level], back_b[level]

    def attention_back(block, count):
        cut = width // 2
        return head_pairs(
            functools.partial(token_attention_back, memory_rows, head_dim),
            place,
            (doc_row, doc_column),
            (q, k, v, qkv, log_total, grad_attended),
            (shape((seg_len, cut), LOW),) * 3 + (shape((2 * PAD, cut), FULL),),
            pair,
            10_000_000_000,
            count,
            block * count,
        )

    blocks = width // pair // 2
    moving = [
        [keep, swap(send, *back[0])]
        for keep, send, back in zip(ffn_grads[::2], ffn_grads[1::2], (back_a, back_b))
    ]
    back_low = attention_back(0, blocks)
    back_low, moving, grad_attended = lax.optimization_barrier((back_low, moving, grad_attended))
    output = lax.all_to_all(result.reshape(groups, quarter, width), "head", 0, 0, tiled=True)
    sends = parcels(moving)
    sends, grad_attended = lax.optimization_barrier((sends, grad_attended))
    moving = posted(moving, sends, stages_of(1))
    back_high = attention_back(1, blocks)
    token_part = jnp.concatenate([back_low[3], back_high[3]], 1)
    token_part, back_high = lax.optimization_barrier((token_part, back_high))
    token_parts = gather(token_part[None], head_stages[:1])
    share = width // dps
    rows_a, rows_b, rows_own = 2 * share + SUM_ROWS, 2 * share, share + SUM_ROWS
    keep_b, send_b, grad_x, value_sum = whole_call(
        functools.partial(value_grads, order_b, dps),
        (place,),
        (x, grad_mixed, attended, back_low[2], back_high[2], grad_attn),
        (w_attn,),
        (
            *(shape((dps // 2, rows_b, width), LOW),) * 2,
            shape((seg_len, width), FULL),
            shape((1, width), FULL),
        ),
        5_000_000_000,
        (pltpu.VMEM((width, width), LOW), pltpu.SemaphoreType.DMA(())),
    )
    down_a, down_b = ([("dp", bit) for bit in order[::-1]] for order in (order_a, order_b))
    grad_x, send_b, moving, token_parts, output = lax.optimization_barrier(
        (grad_x, send_b, moving, token_parts, output)
    )
    token_parts = gather(token_parts, head_stages[1:])
    other_b = swap(send_b, *down_b[0])
    sends = parcels(moving)
    sends, grad_x = lax.optimization_barrier((sends, grad_x))
    moving = posted(moving, sends, stages_of(2))
    for level in range(3, levels):
        moving = posted(moving, parcels(moving), stages_of(level))
    sum_scratch = (pltpu.VMEM((SUM_ROWS, width), FULL),)
    keep_a, send_a, grad_x = whole_call(
        functools.partial(
            query_key_grads, layout, order_a, order_b, head_order, heads_here, memory_rows
        ),
        (place,),
        (
            x,
            back_low[0],
            back_high[0],
            back_low[1],
            back_high[1],
            grad_x,
            value_sum,
            layer_sums,
            bias_sum,
        ),
        (w_attn,),
        (
            *(shape((dps // 2, rows_a, width), LOW),) * 2,
            shape((seg_len, width), LOW),
        ),
        10_000_000_000,
        sum_scratch + (pltpu.VMEM((2, width, width), LOW), pltpu.SemaphoreType.DMA((2,))),
    )

    def advance_both(parts, level):
        return [reduce_step(p, down[level]) for p, down in zip(parts, (down_a, down_b))]

    token_parts, send_a, other_b, grad_x, moving = lax.optimization_barrier(
        (token_parts, send_a, other_b, grad_x, moving)
    )
    attn_moving = [[keep_a, swap(send_a, *down_a[0])], [keep_b, other_b]]
    sends = parcels(moving, True)
    attn_moving, sends = lax.optimization_barrier((attn_moving, sends))
    others = swap(sends[0], *back_a[levels])
    sends = parcels(attn_moving)
    sends, grad_x, token_parts = lax.optimization_barrier((sends, grad_x, token_parts))
    attn_moving = posted(attn_moving, sends, (down_a[1], down_b[1]))
    moved = lax.all_to_all(grad_x.reshape(groups, quarter, width), "head", 0, 0, tiled=True)

    packed_rows = writes * memory_rows + (-writes * memory_rows) % PAD
    score_w, grad_attended_w, grad_mixed_w, small_w, factors, bias_w, vec_w, init_w, norms = whole_call(
        functools.partial(chain_backward, layout, head_order, heads, memory_rows),
        (reset, place),
        (
            bias_in,
            read,
            norms,
            vectors,
            qkv,
            soft,
            soft_mem,
            z_attn_w,
            pre_w,
            z_ffn_w,
            hidden_w,
            token_parts,
        ),
        (w_attn, keys, values, *pieces),
        (
            shape((writes, heads * PAD, seg_len), LOW),
            shape((writes, PAD, width), LOW),
            shape((writes, PAD, width), LOW),
            shape((segments, 3, PAD, width), LOW),
            shape((4, packed_rows, width), LOW),
            shape((layout.chunks, 1, layout.size), FULL),
            shape((len(VECTORS), width), FULL),
            shape((PAD, width), FULL),
            shape((1, 128), FULL),
        ),
        20_000_000_000,
        (
            pltpu.VMEM((writes, PAD, width), LOW),
            pltpu.VMEM((writes, PAD, ff), LOW),
            pltpu.VMEM((segments, 2 * PAD, width), FULL),
        )
        + tokens_scratch(segments)
        + landing,
    )
    score_w, factors, moving, others, attn_moving, moved = lax.optimization_barrier(
        (score_w, factors, moving, others, attn_moving, moved)
    )

    moving = [terms + [others[:, i]] for i, terms in enumerate(moving)]
    sends = parcels(moving + attn_moving, True)
    sends, score_w = lax.optimization_barrier((sends, score_w))
    others = swap(sends[0], *back_a[levels + 1])
    moving = [terms + [others[:, i]] for i, terms in enumerate(moving)]
    attn_moving = posted(attn_moving, sends[1:], (down_a[2], down_b[2]))
    for level in range(3, levels):
        attn_moving = advance_both(attn_moving, level)
    factors = gather(factors[None], [("dp", order_b[0])])
    keep_own, send_own = whole_call(
        functools.partial(
            own_grads, layout, order_a, order_b, head_order, heads, heads_here, memory_rows
        ),
        (place,),
        (
            score_w,
            soft,
            qkv,
            grad_attended_w,
            grad_mixed_w,
            attended_w,
            small_w,
            read,
            tokens,
            bias_w,
            vec_w,
            init_w,
        ),
        (),
        (shape((dps // 2, rows_own, width), LOW),) * 2,
        5_000_000_000,
        sum_scratch,
    )
    keep_own, send_own, attn_moving, factors, score_w, moving = lax.optimization_barrier(
        (keep_own, send_own, attn_moving, factors, score_w, moving)
    )
    own = [keep_own, swap(send_own, *down_a[0])]
    left, right = (summed(terms)[0] for terms in attn_moving)
    right = jnp.pad(right, ((0, SUM_ROWS), (0, 0)))
    both = [
        jnp.concatenate([part[:, g * here : (g + 1) * here] for part in (left, right)], 1)
        for g in range(groups)
    ]
    attn_moving = [jnp.stack([both[partner(i, head_stages, "head")] for i in range(groups)])]
    attn_send = summed(attn_moving, LOW, groups // 2)
    own_send = summed(own, LOW, own[-1].shape[0] // 2)
    attn_send, own_send, score_w = lax.optimization_barrier((attn_send, own_send, score_w))
    attn_moving = attn_moving + [swap(attn_send, "head", head_order[-1])]
    own = own + [swap(own_send, *down_a[1])]
    factors = gather(factors, [("dp", order_b[1])])
    for level in range(2, levels - 1):
        own = reduce_step(own, down_a[level])
    attn_send = summed(attn_moving, LOW, attn_moving[-1].shape[0] // 2)
    own_send = summed(own, LOW, own[-1].shape[0] // 2)
    attn_send, own_send, score_w = lax.optimization_barrier((attn_send, own_send, score_w))
    attn_moving = attn_moving + [swap(attn_send, "head", head_order[0])]
    own = own + [swap(own_send, *down_a[levels - 1])]
    factors = gather(factors, stages_b[len(head_stages) + 2 : -1])
    factors = [factors, swap(factors, *stages_b[-1])]
    (grad_tokens,) = whole_call(
        functools.partial(write_rows, heads, quarter),
        (place,),
        (score_w, soft, qkv, grad_attended_w, moved),
        (w_attn,),
        (shape((segments, quarter, width), FULL),),
        5_000_000_000,
        (pltpu.VMEM((2, width, width), LOW), pltpu.SemaphoreType.DMA((2,))),
    )
    grad_tokens, own, factors, attn_moving = lax.optimization_barrier(
        (grad_tokens, own, factors, attn_moving)
    )
    own, factors, attn_moving, moving = lax.optimization_barrier(
        (own, factors, attn_moving, moving)
    )
    part = width // dps // groups
    row = shape((1, part), FULL)
    groups_in = [factors, *moving, attn_moving, own]
    first_entry = lambda array: pl.BlockSpec(
        (1, *array.shape[1:]), lambda i: (0,) * len(array.shape)
    )
    whole = lambda array: pl.BlockSpec(array.shape, lambda i: (0,) * len(array.shape))
    shapes = (
        *(shape((share, here), FULL),) * 3,
        *(shape((heads_here, head_dim // dps), FULL),) * 2,
        shape((here, share), FULL),
        *(row,) * 3,
        shape((units, width), FULL),
        shape((1, units), FULL),
        shape((units, width), FULL),
        *(row,) * 3,
        shape((memory_rows, part), FULL),
    )
    outs = pl.pallas_call(
        functools.partial(
            finish,
            order_in(order_a, order_b),
            order_in(order_b, order_b),
            memory_rows,
            [len(group) for group in groups_in],
        ),
        grid=(1,),
        out_shape=shapes,
        in_specs=[whole(a) for a in factors]
        + [first_entry(a) for group in groups_in[1:] for a in group],
        out_specs=[whole(a) for a in shapes],
        compiler_params=pltpu.CompilerParams(vmem_limit_bytes=VMEM_LIMIT),
        cost_estimate=pl.CostEstimate(flops=1000, bytes_accessed=1000, transcendentals=0),
    )(*(a for group in groups_in for a in group))
    flat = (6, 7, 8, 10, 12, 13, 14)
    outs = [out.reshape(-1) if i in flat else out for i, out in enumerate(outs)]
    outs[9] = outs[9].T
    return (output[None], norms[:, :segments], grad_tokens[None], *outs)


def solution(mesh):
    in_specs = (
        P("dp", None, None, None),
        P("dp", None, None),
        P("dp", None),
        P(),
        P(None, "head"),
        P(None, "head"),
        P(None, "head"),
        P("head", None),
        P("head", None),
        P("head", None),
        P(),
        P(),
        P(),
        P(None, ("dp", "head")),
        P(("dp", "head")),
        P(("dp", "head"), None),
        P(),
        P(),
        P(),
        P("dp", None, "head", None),
    )
    out_specs = (
        P("dp", None, "head", None),
        P("dp", None),
        P("dp", None, "head", None),
        P("dp", "head"),
        P("dp", "head"),
        P("dp", "head"),
        P("head", "dp"),
        P("head", "dp"),
        P("head", "dp"),
        P(("dp", "head")),
        P(("dp", "head")),
        P(("dp", "head")),
        P(None, ("dp", "head")),
        P(("dp", "head")),
        P(("dp", "head"), None),
        P(("dp", "head")),
        P(("dp", "head")),
        P(("dp", "head")),
        P(None, ("dp", "head")),
    )
    return jax.shard_map(
        on_device, mesh=mesh, in_specs=in_specs, out_specs=out_specs, check_vma=False
    )
```

```python
import functools

import jax
import jax.numpy as jnp
from jax import lax
from jax.experimental import pallas as pl
from jax.experimental.pallas import tpu as pltpu
from jax.sharding import PartitionSpec as P

EPSILON = 1e-06
SCALE = 0.125
NEGATIVE = -1e30
ROOT_HALF = 0.7071067811865476
DENSITY = 0.3989422804014327
LOW = jnp.bfloat16
FULL = jnp.float32
PAD = 16
VECTORS = ("b_query", "b_value", "b_out", "gain_attn", "shift_attn", "b_down", "gain_ffn", "shift_ffn")
VMEM_LIMIT = 60 * 1024 * 1024


def nn(left, right):
    return lax.dot_general(left, right, (((1,), (0,)), ((), ())), preferred_element_type=FULL)


def nt(left, right):
    return lax.dot_general(left, right, (((1,), (1,)), ((), ())), preferred_element_type=FULL)


def tn(left, right):
    return lax.dot_general(left, right, (((0,), (0,)), ((), ())), preferred_element_type=FULL)


def norm_parts(rows):
    centred = rows - jnp.mean(rows, -1, keepdims=True)
    inverse = lax.rsqrt(jnp.mean(centred * centred, -1, keepdims=True) + EPSILON)
    return centred * inverse, inverse


def norm_pull(normed, inverse, grad):
    along = jnp.mean(grad * normed, -1, keepdims=True)
    return inverse * (grad - jnp.mean(grad, -1, keepdims=True) - normed * along)


def gelu(v):
    return 0.5 * v * (1.0 + lax.erf(v * ROOT_HALF))


def gelu_slope(v):
    return 0.5 * (1.0 + lax.erf(v * ROOT_HALF)) + v * (DENSITY * jnp.exp(-0.5 * v * v))


def swap(array, axis, bit):
    return lax.ppermute(array, axis, [(i, i ^ bit) for i in range(lax.axis_size(axis))])


def bits_of(count):
    return [1 << i for i in range(count.bit_length() - 1)]


def gather(array, stages):
    for axis, bit in stages:
        array = jnp.concatenate([array, swap(array, axis, bit)], 0)
    return array


def summed(terms, kind=LOW, first=0):
    size = terms[-1].shape[0] - first
    total = terms[0][first : first + size].astype(FULL)
    for term in terms[1:]:
        total = total + term[first : first + size].astype(FULL)
    return total.astype(kind)


def add_up(count, together, *refs):
    out_refs = list(refs[sum(count) :])
    pair_ref = None
    if together:
        pair_ref = out_refs[0]
        out_refs = [None, None] + out_refs[1:]
    at = 0
    for number_of, (number, out_ref) in enumerate(zip(count, out_refs)):
        total = refs[at][...].astype(FULL)
        for ref in refs[at + 1 : at + number]:
            total = total + ref[...].astype(FULL)
        total = total.astype(refs[at].dtype)
        at += number
        if pair_ref is not None and number_of < 2:
            pair_ref[:, number_of] = total
        else:
            out_ref[...] = total


def parcels(groups, together=False):
    halves = [terms[-1].shape[0] // 2 for terms in groups]
    steps = min(min(halves), 2)
    in_specs, operands, out_specs, shapes = [], [], [], []

    def spec(half, rest, first):
        index = lambda i: (first + i,) + (0,) * len(rest)
        return pl.BlockSpec((half // steps, *rest), index)

    for half, terms in zip(halves, groups):
        rest = terms[0].shape[1:]
        in_specs += [spec(half, rest, steps)] * len(terms)
        operands += terms
        if together and len(operands) < len(groups[0]) + len(groups[1]) + 1:
            if len(shapes):
                continue
            rest = (2, *rest)
        out_specs.append(spec(half, rest, 0))
        shapes.append(jax.ShapeDtypeStruct((half, *rest), terms[0].dtype))
    return pl.pallas_call(
        functools.partial(add_up, [len(terms) for terms in groups], together),
        grid=(steps,),
        out_shape=shapes,
        in_specs=in_specs,
        out_specs=out_specs,
        compiler_params=pltpu.CompilerParams(vmem_limit_bytes=VMEM_LIMIT),
        cost_estimate=pl.CostEstimate(flops=1000, bytes_accessed=1000, transcendentals=0),
    )(*operands)


def posted(groups, sends, stages):
    return [
        terms + [swap(send, *stage)] for terms, send, stage in zip(groups, sends, stages)
    ]


def reduce_step(terms, stage):
    half = terms[-1].shape[0] // 2
    return terms + [swap(summed(terms, terms[0].dtype, half), *stage)]


def partner(index, stages, axis):
    place = 0
    for k, (name, bit) in enumerate(stages):
        if name == axis:
            place = place + ((index >> k) & 1) * bit
    return place


def position(partner_bits, order):
    place = 0
    for k, bit in enumerate(order):
        place = place + ((partner_bits // bit) % 2) * (1 << k)
    return place


def order_in(order, index_order):
    return [1 << index_order.index(bit) for bit in order]


def head_mask(rows, width, heads):
    group = lax.broadcasted_iota(jnp.int32, (rows, width), 0) // PAD
    column = lax.broadcasted_iota(jnp.int32, (rows, width), 1) // (width // heads)
    return group == column


def by_head(rows, mask, heads):
    return jnp.where(mask, jnp.concatenate([rows] * heads, 0), jnp.zeros((), rows.dtype))


def own_head(rows, mask, heads):
    kept = jnp.where(mask, rows, 0.0)
    total = kept[:PAD]
    for i in range(1, heads):
        total = total + kept[i * PAD : (i + 1) * PAD]
    return total


def vector(vec_ref, name):
    i = VECTORS.index(name)
    return vec_ref[i : i + 1, :]


class Units:
    def __init__(self, dps, heads, rows, width):
        self.dps, self.heads, self.rows, self.width = dps, heads, rows, width
        self.blocks = dps * heads
        self.chunks = max(2 * self.blocks * rows // width, 4)
        self.size = 2 * self.blocks * rows // self.chunks
        self.whole = rows % 16 != 0

    def at(self, index):
        return (index % self.heads) * self.dps + index // self.heads

    def pieces(self):
        if self.whole:
            return [(0, self.chunks)]
        part = self.blocks // 8
        return [(half * self.blocks + p * part, part) for half in range(2) for p in range(8)]

    def copies(self):
        for number, (first, count) in enumerate(self.pieces()):
            for entry in range(count):
                if self.whole:
                    yield number, entry, entry, 0, self.size
                    continue
                half, index = divmod(first + entry, self.blocks)
                row = (half * self.blocks + self.at(index)) * self.rows
                yield number, entry, row // self.size, row % self.size, self.rows

    def scratch(self):
        buffer = pltpu.VMEM((self.chunks, self.size, self.width), LOW)
        count = sum(2 for _ in self.copies())
        return (buffer, buffer, pltpu.SemaphoreType.DMA((count,)))

    def loads(self, pieces, up_ref, down_ref, arrived):
        made = []
        for number, entry, chunk, row, rows in self.copies():
            for side, to_ref in enumerate((up_ref, down_ref)):
                made.append(
                    pltpu.make_async_copy(
                        pieces[number].at[entry, side],
                        to_ref.at[chunk, pl.ds(row, rows)],
                        arrived.at[len(made)],
                    )
                )
        return made[::2], made[1::2]

    def assembled(self, halves):
        rows = []
        for array in halves:
            array = array.reshape(self.dps, self.heads, 2, self.rows, self.width)
            rows.append(array.transpose(1, 0, 3, 2, 4).reshape(-1, 2, self.width))
        rows = jnp.concatenate(rows, 0).reshape(self.chunks, self.size, 2, self.width)
        return [rows.transpose(0, 2, 1, 3)]

    def taken_apart(self, piece):
        rows = piece.transpose(0, 2, 1, 3).reshape(2, self.heads, self.dps, self.rows, 2, -1)
        rows = rows.transpose(0, 2, 1, 4, 3, 5)
        return [half.reshape(self.blocks, 2, self.rows, self.width) for half in rows]


def head_groups(ref, flip):
    value = ref[...]
    half = value.shape[1] // 2
    low, high = value[:, :half], value[:, half:]
    if flip & 2:
        low, high = high, low
    if flip & 1:
        low, high = pltpu.roll(low, half // 2, 1), pltpu.roll(high, half // 2, 1)
    return jnp.concatenate([low, high], 1)


def memory_queries(read, attn_ref, vec_ref):
    low = read.astype(LOW)
    queries = (nt(low, attn_ref[0]) + vector(vec_ref, "b_query")).astype(LOW)
    keys = nt(low, attn_ref[1]).astype(LOW)
    values = (nt(low, attn_ref[2]) + vector(vec_ref, "b_value")).astype(LOW)
    return queries, keys, values


def memory_attention(heads, memory_rows, queries, keys, values, key_low, value_low):
    rows, width = heads * PAD, queries.shape[1]
    mask = head_mask(rows, width, heads)
    real_key = lax.broadcasted_iota(jnp.int32, (rows, PAD), 1) < memory_rows
    spread = by_head(queries, mask, heads)
    scores = nt(spread, key_low) * SCALE
    scores_mem = jnp.where(real_key, nt(spread, keys) * SCALE, NEGATIVE)
    top = jnp.maximum(jnp.max(scores, -1, keepdims=True), jnp.max(scores_mem, -1, keepdims=True))
    raised = jnp.exp(scores - top)
    raised_mem = jnp.exp(scores_mem - top)
    total = jnp.sum(raised, -1, keepdims=True) + 2.0 * jnp.sum(raised_mem, -1, keepdims=True)
    soft = raised / total
    soft_mem = raised_mem / total
    mixed = nn(soft.astype(LOW), value_low) + 2.0 * nn(soft_mem.astype(LOW), values)
    return own_head(mixed, mask, heads).astype(LOW), soft, soft_mem


def memory_norm(result, memory_rows):
    real_row = lax.broadcasted_iota(jnp.int32, result.shape, 0) < memory_rows
    square = jnp.sum(jnp.where(real_row, result * result, 0.0), axis=(0, 1), keepdims=True)
    return jnp.sqrt(square / (memory_rows * result.shape[1]))


def chain_forward(
    layout,
    heads,
    memory_rows,
    reset_ref,
    init_ref,
    bias_ref,
    vec_ref,
    attn_from,
    key_from,
    value_from,
    *refs,
):
    count = len(layout.pieces())
    pieces, refs = refs[:count], refs[count:]
    (
        read_ref,
        qkv_ref,
        soft_ref,
        soft_mem_ref,
        attended_ref,
        z_attn_ref,
        hidden_ref,
        pre_ref,
        z_ffn_ref,
        norm_ref,
        attn_ref,
        key_ref,
        value_ref,
        attn_arrived,
        key_arrived,
        value_arrived,
        up_ref,
        down_ref,
        arrived,
    ) = refs
    last = key_ref.shape[0]
    attn_loads = [
        pltpu.make_async_copy(attn_from.at[i], attn_ref.at[i], attn_arrived.at[i])
        for i in range(4)
    ]

    def token_loads(s):
        return [
            pltpu.make_async_copy(key_from.at[s], key_ref.at[s], key_arrived.at[s]),
            pltpu.make_async_copy(value_from.at[s], value_ref.at[s], value_arrived.at[s]),
        ]

    up_loads, down_loads = layout.loads(pieces, up_ref, down_ref, arrived)
    for load in attn_loads[:3] + token_loads(0) + attn_loads[3:] + up_loads + down_loads:
        load.start()
    for s in range(1, last):
        for load in token_loads(s):
            load.start()
    chunks, size, _ = up_ref.shape
    norm_ref[...] = jnp.zeros_like(norm_ref)
    for load in attn_loads[:3]:
        load.wait()

    def enter(s, carried):
        fresh = (reset_ref[0, s] > 0) | (s == 0)
        read = jnp.where(fresh, init_ref[...], carried)
        read_ref[s] = read
        queries, keys, values = memory_queries(read, attn_ref, vec_ref)
        qkv_ref[s, 0] = queries
        qkv_ref[s, 1] = keys
        qkv_ref[s, 2] = values
        return read, queries, keys, values

    def step(s, carried):
        read, queries, keys, values = enter(s, carried)
        for load in token_loads(s):
            load.wait()
        attended, soft, soft_mem = memory_attention(
            heads, memory_rows, queries, keys, values, key_ref[s], value_ref[s]
        )
        soft_ref[s] = soft
        soft_mem_ref[s] = soft_mem
        attended_ref[s] = attended

        if s == 0:
            attn_loads[3].wait()
        z_attn = read + nn(attended, attn_ref[3]) + vector(vec_ref, "b_out")
        z_attn_ref[s] = z_attn
        normed, _ = norm_parts(z_attn)
        hidden = normed * vector(vec_ref, "gain_attn") + vector(vec_ref, "shift_attn")
        hidden_low = hidden.astype(LOW)
        hidden_ref[s] = hidden_low
        z_ffn = hidden + vector(vec_ref, "b_down")

        if s == 0:
            for load in up_loads:
                load.wait()
        acts = []
        for i in range(chunks):
            pre = nt(hidden_low, up_ref[i]) + bias_ref[i]
            pre_ref[s, :, i * size : (i + 1) * size] = pre
            acts.append(gelu(pre).astype(LOW))
        if s == 0:
            for load in down_loads:
                load.wait()
        for i in range(chunks):
            z_ffn = z_ffn + nn(acts[i], down_ref[i])
        z_ffn_ref[s] = z_ffn
        normed, _ = norm_parts(z_ffn)
        result = normed * vector(vec_ref, "gain_ffn") + vector(vec_ref, "shift_ffn")
        lane = lax.broadcasted_iota(jnp.int32, norm_ref.shape, 1)
        norm_ref[...] = jnp.where(lane == s, memory_norm(result, memory_rows), norm_ref[...])
        return result

    carried = init_ref[...]
    for s in range(last):
        carried = step(s, carried)
    enter(last, carried)


def last_norm(heads, memory_rows, bias_ref, vec_ref, read, qkv, key, value, weights):
    out_w, up_ref, down_ref = weights
    attended, _, _ = memory_attention(heads, memory_rows, *qkv, key, value)
    z_attn = read + nn(attended, out_w) + vector(vec_ref, "b_out")
    normed, _ = norm_parts(z_attn)
    hidden = normed * vector(vec_ref, "gain_attn") + vector(vec_ref, "shift_attn")
    hidden_low = hidden.astype(LOW)
    z_ffn = hidden + vector(vec_ref, "b_down")
    for i in range(up_ref.shape[0]):
        pre = nt(hidden_low, up_ref[i]) + bias_ref[i]
        z_ffn = z_ffn + nn(gelu(pre).astype(LOW), down_ref[i])
    normed, _ = norm_parts(z_ffn)
    result = normed * vector(vec_ref, "gain_ffn") + vector(vec_ref, "shift_ffn")
    return memory_norm(result, memory_rows)


def chain_backward(
    layout,
    head_order,
    heads,
    memory_rows,
    reset_ref,
    place_ref,
    bias_ref,
    read_ref,
    norms_ref,
    vec_ref,
    qkv_ref,
    soft_ref,
    soft_mem_ref,
    z_attn_ref,
    pre_ref,
    z_ffn_ref,
    hidden_ref,
    *refs,
):
    segments, _, _, width = qkv_ref.shape
    part_ref, *refs = refs
    attn_from, key_from, value_from, *refs = refs
    count = len(layout.pieces())
    pieces, refs = refs[:count], refs[count:]
    (
        score_ref,
        attended_ref,
        mixed_ref,
        small_ref,
        factor_ref,
        bias_grad_ref,
        vec_grad_ref,
        init_grad_ref,
        norm_ref,
        ffn_ref,
        pre_grad_ref,
        token_part_ref,
        attn_ref,
        key_ref,
        value_ref,
        attn_arrived,
        key_arrived,
        value_arrived,
        up_ref,
        down_ref,
        arrived,
    ) = refs
    attn_loads = [
        pltpu.make_async_copy(attn_from.at[i], attn_ref.at[i], attn_arrived.at[i])
        for i in range(4)
    ]

    def token_loads(s):
        return [
            pltpu.make_async_copy(key_from.at[s], key_ref.at[s], key_arrived.at[s]),
            pltpu.make_async_copy(value_from.at[s], value_ref.at[s], value_arrived.at[s]),
        ]

    up_loads, down_loads = layout.loads(pieces, up_ref, down_ref, arrived)
    for load in attn_loads[1:3] + down_loads + up_loads + attn_loads[3:] + attn_loads[:1]:
        load.start()
    for s in (*range(segments - 2, -1, -1), segments - 1):
        for load in token_loads(s):
            load.start()
    for j in range(segments):
        token_part_ref[j] = head_groups(part_ref.at[position(j, head_order)], j)
    me = place_ref[1]
    rows = heads * PAD
    mask = head_mask(rows, width, heads)
    chunks, size, _ = up_ref.shape
    half = chunks * size // 2
    vec_grad_ref[...] = jnp.zeros_like(vec_grad_ref)
    bias_grad_ref[...] = jnp.zeros_like(bias_grad_ref)

    def add_vector(name, grad):
        i = VECTORS.index(name)
        vec_grad_ref[i : i + 1, :] += jnp.sum(grad, 0, keepdims=True)

    last = segments - 1
    for load in attn_loads[1:3]:
        load.wait()
    grad_key = token_part_ref[last ^ me, :PAD].astype(LOW)
    grad_value = token_part_ref[last ^ me, PAD:].astype(LOW)
    small_ref[last, 0] = jnp.zeros((PAD, width), LOW)
    small_ref[last, 1] = grad_key
    small_ref[last, 2] = grad_value
    add_vector("b_value", 2.0 * grad_value.astype(FULL))
    grad_read = 2.0 * (nn(grad_key, attn_ref[1]) + nn(grad_value, attn_ref[2]))
    stop = reset_ref[0, last] > 0
    init_grad_ref[...] = jnp.where(stop, grad_read, 0.0)
    grad_write = jnp.where(stop, 0.0, grad_read)

    def step(back, grad_write):
        s = segments - 2 - back
        normed, inverse = norm_parts(z_ffn_ref[s])
        add_vector("gain_ffn", grad_write * normed)
        add_vector("shift_ffn", grad_write)
        grad_sum = norm_pull(normed, inverse, grad_write * vector(vec_ref, "gain_ffn"))
        grad_low = grad_sum.astype(LOW)
        ffn_ref[s] = grad_low
        add_vector("b_down", grad_low.astype(FULL))
        grad_hidden = grad_sum

        if back == 0:
            for load in down_loads:
                load.wait()
        pre_grads = []
        for i in range(chunks):
            part = slice(i * size, (i + 1) * size)
            grad_act = nt(grad_low, down_ref[i])
            grad_pre = (grad_act * gelu_slope(pre_ref[s, :, part])).astype(LOW)
            pre_grad_ref[s, :, part] = grad_pre
            bias_grad_ref[i] += jnp.sum(grad_pre.astype(FULL), 0, keepdims=True)
            pre_grads.append(grad_pre)
        if back == 0:
            for load in up_loads:
                load.wait()
        for i in range(chunks):
            grad_hidden = grad_hidden + nn(pre_grads[i], up_ref[i])
        normed, inverse = norm_parts(z_attn_ref[s])
        add_vector("gain_attn", grad_hidden * normed)
        add_vector("shift_attn", grad_hidden)
        grad_attn = norm_pull(normed, inverse, grad_hidden * vector(vec_ref, "gain_attn"))
        add_vector("b_out", grad_attn)
        grad_mixed = grad_attn.astype(LOW)
        mixed_ref[s] = grad_mixed

        if back == 0:
            attn_loads[0].wait()
            attn_loads[3].wait()
        for load in token_loads(s):
            load.wait()
        grad_attended = nt(grad_mixed, attn_ref[3]).astype(LOW)
        attended_ref[s] = grad_attended
        queries, keys, values = qkv_ref[s, 0], qkv_ref[s, 1], qkv_ref[s, 2]
        spread = by_head(grad_attended, mask, heads)
        soft, soft_mem = soft_ref[s], soft_mem_ref[s]
        pull = nt(spread, value_ref[s])
        pull_mem = nt(spread, values)
        inner = jnp.sum(soft * pull, -1, keepdims=True) + 2.0 * jnp.sum(
            soft_mem * pull_mem, -1, keepdims=True
        )
        grad_score = (soft * (pull - inner)).astype(LOW)
        grad_score_mem = (soft_mem * (pull_mem - inner)).astype(LOW)
        score_ref[s] = grad_score
        grad_query = nn(grad_score, key_ref[s]) + 2.0 * nn(grad_score_mem, keys)
        grad_query = (SCALE * own_head(grad_query, mask, heads)).astype(LOW)
        grad_key = SCALE * tn(grad_score_mem, by_head(queries, mask, heads))
        grad_key = (token_part_ref[s ^ me, :PAD] + grad_key).astype(LOW)
        grad_value = tn(soft_mem.astype(LOW), spread)
        grad_value = (token_part_ref[s ^ me, PAD:] + grad_value).astype(LOW)
        small_ref[s, 0] = grad_query
        small_ref[s, 1] = grad_key
        small_ref[s, 2] = grad_value
        add_vector("b_query", grad_query.astype(FULL))
        add_vector("b_value", 2.0 * grad_value.astype(FULL))
        grad_read = 2.0 * (nn(grad_key, attn_ref[1]) + nn(grad_value, attn_ref[2]))
        grad_read = grad_read + nn(grad_query, attn_ref[0]) + grad_attn
        stop = (reset_ref[0, s] > 0) | (s == 0)
        init_grad_ref[...] += jnp.where(stop, grad_read, 0.0)
        return jnp.where(stop, 0.0, grad_read)

    for back in range(segments - 1):
        grad_write = step(back, grad_write)
    for load in token_loads(last):
        load.wait()
    norm = last_norm(
        heads,
        memory_rows,
        bias_ref,
        vec_ref,
        read_ref[last],
        [qkv_ref[last, i] for i in range(3)],
        key_ref[last],
        value_ref[last],
        (attn_ref[3], up_ref, down_ref),
    )
    lane = lax.broadcasted_iota(jnp.int32, norm_ref.shape, 1)
    norm_ref[...] = jnp.where(lane == last, norm, norms_ref[...])


    packed, wide = factor_ref.shape[1], (segments - 1) * PAD
    row = lax.broadcasted_iota(jnp.int32, (packed, wide), 0)
    source = lax.broadcasted_iota(jnp.int32, (packed, wide), 1)
    take = (source // PAD == row // memory_rows) & (source % PAD == row % memory_rows)
    take = jnp.where(take, 1.0, 0.0).astype(LOW)
    mine = width // 2

    def own_units(ref):
        first = ref[: segments - 1, :, :mine].reshape(wide, mine)
        second = ref[: segments - 1, :, half : half + mine].reshape(wide, mine)
        return jnp.concatenate([first, second], 1)

    acts = gelu(own_units(pre_ref)).astype(LOW)
    factor_ref[0] = nn(take, hidden_ref[: segments - 1].reshape(wide, width)).astype(LOW)
    factor_ref[1] = nn(take, ffn_ref[...].reshape(wide, width)).astype(LOW)
    factor_ref[2] = nn(take, acts).astype(LOW)
    factor_ref[3] = nn(take, own_units(pre_grad_ref)).astype(LOW)


def whole_call(
    body,
    scalars,
    operands,
    outside,
    shapes,
    flops,
    scratch=(),
    outside_shapes=(),
    limit=VMEM_LIMIT,
):
    in_vmem = pl.BlockSpec(memory_space=pltpu.VMEM)
    in_smem = pl.BlockSpec(memory_space=pltpu.SMEM)
    anywhere = pl.BlockSpec(memory_space=pl.ANY)
    size = sum(a.size * a.dtype.itemsize for a in (*operands, *outside, *shapes))
    return pl.pallas_call(
        body,
        out_shape=(*shapes, *outside_shapes),
        in_specs=[in_smem] * len(scalars) + [in_vmem] * len(operands) + [anywhere] * len(outside),
        out_specs=[in_vmem] * len(shapes) + [anywhere] * len(outside_shapes),
        scratch_shapes=scratch,
        compiler_params=pltpu.CompilerParams(vmem_limit_bytes=limit),
        cost_estimate=pl.CostEstimate(flops=flops // 1000, bytes_accessed=size // 1000, transcendentals=0),
    )(*scalars, *operands, *outside)


def unit_owner(column, order, stages, head_order, layout, index):
    head = position(partner(index, stages, "head"), head_order)
    at = head * layout.dps + position(partner(index, stages, "dp"), order)
    return column // layout.rows == at


def attention_loads(layout, place_ref, order_a, order_b, pieces, attn_ref, arrived):
    loads = []

    def copy(source, target):
        loads.append(pltpu.make_async_copy(source, target, arrived.at[len(loads)]))

    if layout.whole:
        copy(pieces[0], attn_ref)
        return loads
    here = layout.width // layout.heads
    for m in range(4):
        copy(pieces[0].at[m], attn_ref.at[m, pl.ds(0, here)])
    per = layout.dps // 4
    rows = here // per // 2
    for side, order in enumerate((order_a, order_b)):
        for index in range(layout.dps):
            flip = sum(((index >> k) & 1) * bit for k, bit in enumerate(order))
            owner = place_ref[0] ^ flip
            piece = pieces[1 + 4 * side + index // (layout.dps // 4)]
            for group in range(1, layout.heads):
                row = group * here + (owner % per) * 2 * rows + side * rows
                copy(
                    piece.at[index % (layout.dps // 4), group - 1],
                    attn_ref.at[owner // per, pl.ds(pl.multiple_of(row, 16), rows)],
                )
    return loads


def project(
    layout,
    stages,
    order_a,
    order_b,
    head_order,
    place_ref,
    token_ref,
    bias_ref,
    other_ref,
    *refs,
):
    count = 1 if layout.whole else 9
    pieces, refs = refs[:count], refs[count:]
    (
        key_ref,
        value_ref,
        x_ref,
        q_ref,
        k_ref,
        v_ref,
        vec_ref,
        bias_in_ref,
        attn_to,
        attn_ref,
        arrived,
        stored,
    ) = refs
    loads = attention_loads(layout, place_ref, order_a, order_b, pieces, attn_ref, arrived)
    for load in loads:
        load.start()
    devices, entries = bias_ref.shape
    width, rows = layout.width, layout.rows
    here = width // layout.heads
    packets = bias_ref[...].astype(FULL)

    def laid_out(first, count, period, owner):
        entry = lax.broadcasted_iota(jnp.int32, (entries, count), 0)
        column = lax.broadcasted_iota(jnp.int32, (entries, count), 1)
        pick = jnp.where(entry == first + column % period, 1.0, 0.0).astype(LOW)
        index = lax.broadcasted_iota(jnp.int32, (devices, count), 0)
        column = lax.broadcasted_iota(jnp.int32, (devices, count), 1)
        chosen = jnp.where(owner(column, index), nn(packets.astype(LOW), pick), 0.0)
        return jnp.sum(chosen, 0, keepdims=True)

    def of_head(column, index):
        head = partner(index, stages, "head")
        return (partner(index, stages, "dp") == 0) & (head == column // here)

    vec_ref[0:1, :] = laid_out(0, width, here, of_head)
    vec_ref[1:2, :] = laid_out(here, width, here, of_head)
    vec_ref[2:, :] = other_ref[...].astype(FULL)
    for half, order in enumerate((order_a, order_b)):
        owner = functools.partial(
            unit_owner, order=order, stages=stages, head_order=head_order, layout=layout
        )
        row = laid_out(
            2 * here + half * rows,
            layout.blocks * rows,
            rows,
            lambda column, index: owner(column, index=index),
        )
        per = layout.chunks // 2
        for i in range(per):
            bias_in_ref[half * per + i] = row[:, i * layout.size : (i + 1) * layout.size]

    for load in loads:
        load.wait()
    store = pltpu.make_async_copy(attn_ref, attn_to, stored)
    store.start()
    for s in range(token_ref.shape[0]):
        x = token_ref[s]
        key_ref[s] = nt(x, attn_ref[1]).astype(LOW)
        value_ref[s] = (nt(x, attn_ref[2]) + vector(vec_ref, "b_value")).astype(LOW)
    own = place_ref[1]
    x = token_ref[own]
    x_ref[...] = x
    q_ref[...] = (nt(x, attn_ref[0]) + vector(vec_ref, "b_query")).astype(LOW)
    k_ref[...] = key_ref[own]
    v_ref[...] = value_ref[own]
    store.wait()


SUMS = ("b_out", "gain_attn", "shift_attn", "b_down", "gain_ffn", "shift_ffn")


def token_layer(
    layout,
    memory_rows,
    head_dim,
    place_ref,
    x_ref,
    q_ref,
    qkv_ref,
    part_ref,
    stat_ref,
    cot_ref,
    bias_ref,
    vec_ref,
    attn_ref,
    *refs,
):
    count = len(layout.pieces())
    pieces, refs = refs[:count], refs[count:]
    (
        attended_ref,
        log_ref,
        result_ref,
        skip_ref,
        mixed_ref,
        grad_attended_ref,
        bias_sum_ref,
        sum_ref,
        *grad_refs,
        out_w_ref,
        out_arrived,
        up_ref,
        down_ref,
        arrived,
        z_attn_ref,
        hidden_ref,
        low_ref,
        total_ref,
        pre_ref,
        act_ref,
        stage_ref,
        sent,
    ) = refs
    out_load = pltpu.make_async_copy(attn_ref.at[3], out_w_ref, out_arrived)
    out_load.start()
    up_loads, down_loads = layout.loads(pieces, up_ref, down_ref, arrived)
    for load in up_loads + down_loads:
        load.start()
    chunks = layout.chunks
    pair = part_ref.shape[1]
    log_ref[...] = jnp.zeros_like(log_ref)
    for i in range(part_ref.shape[0]):
        columns = slice(i * pair, (i + 1) * pair)
        mixed, logs = with_memory(
            memory_rows,
            head_dim,
            q_ref[:, columns],
            qkv_ref[place_ref[1], 1, :, columns],
            qkv_ref[place_ref[1], 2, :, columns],
            part_ref[i],
            stat_ref[i],
        )
        attended_ref[:, columns] = mixed
        for head, log in enumerate(logs):
            log_ref[i, head : head + 1] = log
    out_load.wait()
    sum_ref[...] = jnp.zeros_like(sum_ref)

    def add_vector(name, grad):
        i = SUMS.index(name)
        sum_ref[i : i + 1, :] += jnp.sum(grad, 0, keepdims=True)

    z_attn = x_ref[...].astype(FULL) + nn(attended_ref[...], out_w_ref[...])
    z_attn = z_attn + vector(vec_ref, "b_out")
    z_attn_ref[...] = z_attn
    normed, _ = norm_parts(z_attn)
    hidden = normed * vector(vec_ref, "gain_attn") + vector(vec_ref, "shift_attn")
    hidden_ref[...] = hidden.astype(LOW)
    total_ref[...] = hidden + vector(vec_ref, "b_down")
    for load in up_loads + down_loads:
        load.wait()

    for i in range(chunks):
        pre = nt(hidden_ref[...], up_ref[i]) + bias_ref[i]
        pre_ref[i] = pre
        act = gelu(pre).astype(LOW)
        act_ref[i] = act
        total_ref[...] += nn(act, down_ref[i])
    normed, inverse = norm_parts(total_ref[...])
    result = normed * vector(vec_ref, "gain_ffn") + vector(vec_ref, "shift_ffn")
    result_ref[...] = result.astype(LOW)
    grad = cot_ref[...].astype(FULL)
    add_vector("gain_ffn", grad * normed)
    add_vector("shift_ffn", grad)
    grad = norm_pull(normed, inverse, grad * vector(vec_ref, "gain_ffn"))
    total_ref[...] = grad
    low_ref[...] = grad.astype(LOW)
    add_vector("b_down", low_ref[...].astype(FULL))

    copies = list(layout.copies())
    spans = [first for first, _ in layout.pieces()]
    stores = []
    for i in range(chunks):
        grad_pre = (nt(low_ref[...], down_ref[i]) * gelu_slope(pre_ref[i])).astype(LOW)
        bias_sum_ref[i] = jnp.sum(grad_pre.astype(FULL), 0, keepdims=True)
        total_ref[...] += nn(grad_pre, up_ref[i])
        slot = i % 2
        if i > 1:
            for store in stores[i - 2]:
                store.wait()
        stage_ref[slot, 0] = tn(grad_pre, hidden_ref[...]).astype(LOW)
        stage_ref[slot, 1] = tn(act_ref[i], low_ref[...]).astype(LOW)
        stores.append([])
        for number, entry, chunk, row, rows in copies:
            if chunk != i:
                continue
            for side in range(2):
                to_ref = grad_refs[number // (len(spans) // len(grad_refs))]
                entry_at = spans[number] - spans[number - number % (len(spans) // len(grad_refs))]
                store = pltpu.make_async_copy(
                    stage_ref.at[slot, side, pl.ds(row, rows)],
                    to_ref.at[entry_at + entry, side],
                    sent.at[i, len(stores[i])],
                )
                store.start()
                stores[i].append(store)

    grad_hidden = total_ref[...]
    normed, inverse = norm_parts(z_attn_ref[...])
    add_vector("gain_attn", grad_hidden * normed)
    add_vector("shift_attn", grad_hidden)
    grad = norm_pull(normed, inverse, grad_hidden * vector(vec_ref, "gain_attn"))
    add_vector("b_out", grad)
    skip_ref[...] = grad
    mixed_ref[...] = grad.astype(LOW)
    grad_attended_ref[...] = nt(mixed_ref[...], out_w_ref[...]).astype(LOW)
    for i in range(max(chunks - 2, 0), chunks):
        for store in stores[i]:
            store.wait()


def part_rows(keep_ref, send_ref, first, columns, grad, place_ref, order, count):
    rows = grad.shape[0] // count
    for c in range(count):
        block = grad[c * rows : (c + 1) * rows].astype(keep_ref.dtype)
        at = position(place_ref[0] ^ c, order)

        @pl.when(at < count // 2)
        def _():
            keep_ref[at, first : first + rows, columns] = block

        @pl.when(at >= count // 2)
        def _():
            send_ref[at - count // 2, first : first + rows, columns] = block


SUM_ROWS = 32


def pack_sums(
    layout, order_a, order_b, head_order, heads_here, memory_rows, place_ref, groups, rows, halves
):
    count, width = rows.shape
    dps = layout.dps
    devices = dps * groups
    here, part = width // layout.heads, width // (dps * layout.heads)
    head_dim = here // heads_here
    head_part = head_dim // dps

    def partners(index):
        head = index % groups
        dp = 0
        for k, bit in enumerate(order_a):
            dp = dp + ((index // groups >> k) & 1) * bit
        return dp, head

    shape = (devices, count, width)
    index, row, column = (lax.broadcasted_iota(jnp.int32, shape, i) for i in range(3))
    dp_flip, head_flip = partners(index)
    dp, head = place_ref[0] ^ dp_flip, place_ref[1] ^ head_flip
    plain = len(SUMS) + memory_rows
    of_device = column // part == dp * layout.heads + head
    of_head = (column // here == head_flip) & (column % head_dim // head_part == dp)
    chosen = ((row < plain) & of_device) | ((row >= plain) & of_head)
    chosen = jnp.where(chosen, jnp.broadcast_to(rows[None], shape), 0.0)
    chosen = chosen.reshape(devices * count, width).astype(LOW)
    source = lax.broadcasted_iota(jnp.int32, (width, part), 0)
    target = lax.broadcasted_iota(jnp.int32, (width, part), 1)
    plain_fold = jnp.where(source % part == target, 1.0, 0.0).astype(LOW)
    head_column = source // head_dim % heads_here * head_part + source % head_part
    head_fold = jnp.where(head_column == target, 1.0, 0.0).astype(LOW)
    row = lax.broadcasted_iota(jnp.int32, (devices, count, part), 1)
    folded = jnp.where(
        row < plain,
        nn(chosen, plain_fold).reshape(devices, count, part),
        nn(chosen, head_fold).reshape(devices, count, part),
    )
    unit_rows = []
    span = halves[0].shape[1]
    index, column = (lax.broadcasted_iota(jnp.int32, (devices, span), i) for i in range(2))
    source = lax.broadcasted_iota(jnp.int32, (span, layout.rows), 0)
    target = lax.broadcasted_iota(jnp.int32, (span, layout.rows), 1)
    fold = jnp.where(source % layout.rows == target, 1.0, 0.0).astype(LOW)
    for order, half in zip((order_a, order_b), halves):
        dp_flip, head_flip = partners(index)
        at = position(head_flip, head_order) * dps + position(dp_flip, order)
        chosen = jnp.where(column // layout.rows == at, half, 0.0)
        unit_rows.append(nn(chosen.astype(LOW), fold))
    return folded, unit_rows


def put_sums(ref, entry, first_row, first_column, packed, index, memory_rows):
    folded, unit_rows = packed
    plain = len(SUMS) + memory_rows
    part, block = folded.shape[2], unit_rows[0].shape[1]
    columns = slice(first_column, first_column + part)
    ref[entry, first_row : first_row + plain + 2, columns] = folded[index, : plain + 2].astype(LOW)
    columns = slice(first_column, first_column + block)
    for half, rows in enumerate(unit_rows):
        row = first_row + plain + 2 + half
        ref[entry, row : row + 1, columns] = rows[index : index + 1].astype(LOW)


def half_rows(ref, layout):
    per = layout.chunks // 2
    return [
        jnp.concatenate([ref[half * per + i] for i in range(per)], 1) for half in range(2)
    ]


def value_grads(
    order,
    count,
    place_ref,
    x_ref,
    mixed_ref,
    attended_ref,
    dv0_ref,
    dv1_ref,
    skip_ref,
    attn_from,
    keep_ref,
    send_ref,
    grad_x_ref,
    sum_ref,
    attn_ref,
    arrived,
):
    load = pltpu.make_async_copy(attn_from.at[2], attn_ref, arrived)
    load.start()
    x, low, high = x_ref[...], dv0_ref[...], dv1_ref[...]
    half = low.shape[1]
    share = x.shape[1] // count
    every = slice(None)
    both = jnp.concatenate([tn(x, low), tn(x, high)], 1)
    part_rows(keep_ref, send_ref, 0, every, both, place_ref, order, count)
    both = tn(mixed_ref[...], attended_ref[...])
    part_rows(keep_ref, send_ref, share, every, both, place_ref, order, count)
    sum_ref[:, :half] = jnp.sum(low.astype(FULL), 0, keepdims=True)
    sum_ref[:, half:] = jnp.sum(high.astype(FULL), 0, keepdims=True)
    load.wait()
    grad_x_ref[...] = skip_ref[...] + nn(low, attn_ref[:half]) + nn(high, attn_ref[half:])


def query_key_grads(
    layout,
    order_a,
    order_b,
    head_order,
    heads_here,
    memory_rows,
    place_ref,
    x_ref,
    dq0_ref,
    dq1_ref,
    dk0_ref,
    dk1_ref,
    part_ref,
    value_sum_ref,
    layer_sum_ref,
    bias_sum_ref,
    attn_from,
    keep_ref,
    send_ref,
    grad_x_ref,
    rows_ref,
    attn_ref,
    arrived,
):
    loads = [
        pltpu.make_async_copy(attn_from.at[i], attn_ref.at[i], arrived.at[i]) for i in range(2)
    ]
    for load in loads:
        load.start()
    count = layout.dps
    x = x_ref[...]
    half = dq0_ref.shape[1]
    share = x.shape[1] // count
    pairs = [(dq0_ref[...], dq1_ref[...]), (dk0_ref[...], dk1_ref[...])]
    for m, (low, high) in enumerate(pairs):
        both = jnp.concatenate([tn(x, low), tn(x, high)], 1)
        part_rows(keep_ref, send_ref, m * share, slice(None), both, place_ref, order_a, count)
    plain = len(SUMS) + memory_rows
    rows_ref[...] = jnp.zeros_like(rows_ref)
    rows_ref[: len(SUMS), :] = layer_sum_ref[: len(SUMS), :]
    for at, array in zip((0, half), pairs[0]):
        rows_ref[plain : plain + 1, at : at + half] = jnp.sum(array.astype(FULL), 0, keepdims=True)
    rows_ref[plain + 1 : plain + 2, :] = value_sum_ref[...]
    packed = pack_sums(
        layout,
        order_a,
        order_b,
        head_order,
        heads_here,
        memory_rows,
        place_ref,
        layout.heads,
        rows_ref[...],
        half_rows(bias_sum_ref, layout),
    )
    here = x.shape[1] // layout.heads
    for at in range(count):
        ref = keep_ref if at < count // 2 else send_ref
        entry = at % (count // 2)
        ref[entry, 2 * share :, :] = jnp.zeros((SUM_ROWS, x.shape[1]), LOW)
        for g in range(layout.heads):
            index = at * layout.heads + g
            put_sums(ref, entry, 2 * share, g * here, packed, index, memory_rows)
    total = part_ref[...]
    for m, (low, high) in enumerate(pairs):
        loads[m].wait()
        total = total + nn(low, attn_ref[m, :half]) + nn(high, attn_ref[m, half:])
    grad_x_ref[...] = total.astype(LOW)


def own_grads(
    layout,
    order_a,
    order_b,
    head_order,
    heads,
    heads_here,
    memory_rows,
    place_ref,
    score_ref,
    soft_ref,
    qkv_ref,
    attended_grad_ref,
    mixed_ref,
    attended_ref,
    small_ref,
    read_ref,
    token_ref,
    bias_grad_ref,
    vec_grad_ref,
    init_grad_ref,
    keep_ref,
    send_ref,
    rows_ref,
):
    count = layout.dps
    writes, rows, _ = score_ref.shape
    width = qkv_ref.shape[-1]
    here = width // heads * heads_here
    mine = heads_here * PAD
    mask = head_mask(rows, width, heads)[:mine]
    total = jnp.zeros((1, here), FULL)
    grads = [jnp.zeros((width, here), FULL) for _ in range(4)]
    for s in range(writes + 1):
        low = read_ref[s].astype(LOW)
        grads[1] = grads[1] + 2.0 * tn(low, small_ref[s, 1, :, :here])
        grads[2] = grads[2] + 2.0 * tn(low, small_ref[s, 2, :, :here])
        if s == writes:
            break
        grads[0] = grads[0] + tn(low, small_ref[s, 0, :, :here])
        grads[3] = grads[3] + tn(mixed_ref[s], attended_ref[s, :, :here])
        spread = by_head(qkv_ref[s, 0], mask, heads_here)[:, :here]
        pulled = by_head(attended_grad_ref[s], mask, heads_here)[:, :here]
        dk = (SCALE * tn(score_ref[s, :mine], spread)).astype(LOW)
        dv = tn(soft_ref[s, :mine].astype(LOW), pulled).astype(LOW)
        grads[1] = grads[1] + tn(token_ref[s], dk)
        grads[2] = grads[2] + tn(token_ref[s], dv)
        total = total + jnp.sum(dv.astype(FULL), 0, keepdims=True)
    both = jnp.concatenate(grads, 1)
    part_rows(keep_ref, send_ref, 0, slice(None), both, place_ref, order_a, count)
    rows_ref[...] = jnp.zeros_like(rows_ref)
    for i, name in enumerate(SUMS):
        at = VECTORS.index(name)
        rows_ref[i : i + 1, :] = vec_grad_ref[at : at + 1, :]
    for i in range(memory_rows):
        at = len(SUMS) + i
        rows_ref[at : at + 1, :] = init_grad_ref[i : i + 1, :]
    at = len(SUMS) + memory_rows
    rows_ref[at : at + 2, :] = vec_grad_ref[0:2, :]
    rows_ref[at + 1 : at + 2, :here] += total
    packed = pack_sums(
        layout,
        order_a,
        order_b,
        head_order,
        heads_here,
        memory_rows,
        place_ref,
        1,
        rows_ref[...],
        half_rows(bias_grad_ref, layout),
    )
    share = width // count
    for at in range(count):
        ref = keep_ref if at < count // 2 else send_ref
        entry = at % (count // 2)
        ref[entry, share:, :] = jnp.zeros((SUM_ROWS, width), LOW)
        put_sums(ref, entry, share, 0, packed, at, memory_rows)


def write_rows(
    heads,
    quarter,
    place_ref,
    score_ref,
    soft_ref,
    qkv_ref,
    attended_grad_ref,
    moved_ref,
    attn_from,
    grad_token_ref,
    attn_ref,
    arrived,
):
    writes, rows, _ = score_ref.shape
    loads = [
        pltpu.make_async_copy(attn_from.at[i + 1], attn_ref.at[i], arrived.at[i])
        for i in range(2)
    ]
    for load in loads:
        load.start()
    mask = head_mask(rows, qkv_ref.shape[-1], heads)
    at = pl.multiple_of(place_ref[1] * quarter, quarter)
    for load in loads:
        load.wait()
    for s in range(writes):
        spread = by_head(qkv_ref[s, 0], mask, heads)
        pulled = by_head(attended_grad_ref[s], mask, heads)
        score_here = score_ref[s, :, pl.ds(at, quarter)]
        soft_here = soft_ref[s, :, pl.ds(at, quarter)].astype(LOW)
        dk = (SCALE * tn(score_here, spread)).astype(LOW)
        dv = tn(soft_here, pulled).astype(LOW)
        extra = nn(dk, attn_ref[0]) + nn(dv, attn_ref[1])
        grad_token_ref[s] = moved_ref[s].astype(FULL) + extra
    grad_token_ref[writes] = moved_ref[writes].astype(FULL)


def by_group(stages, numbers, *refs):
    keep_ref, send_ref = refs[-2:]
    sums, at = [], 0
    for number in numbers:
        total = refs[at][0].astype(FULL)
        for ref in refs[at + 1 : at + number]:
            total = total + ref[0].astype(FULL)
        sums.append(total.astype(LOW))
        at += number
    left, right = sums
    here = keep_ref.shape[2] // 2
    half = keep_ref.shape[0]
    keep_ref[...] = jnp.zeros_like(keep_ref)
    send_ref[...] = jnp.zeros_like(send_ref)
    for i in range(2 * half):
        g = partner(i, stages, "head")
        columns = slice(g * here, (g + 1) * here)
        ref = keep_ref if i < half else send_ref
        ref[i % half, :, :here] = left[:, columns]
        ref[i % half, : right.shape[0], here:] = right[:, columns]


def finish(
    order_a,
    order_b,
    memory_rows,
    numbers,
    *refs,
):
    groups = []
    for number in numbers:
        groups.append(refs[:number])
        refs = refs[number:]
    factor_refs, *groups = groups

    def total_of(group, *at):
        total = group[0][(0, *at)].astype(FULL)
        for ref in group[1:]:
            total = total + ref[(0, *at)].astype(FULL)
        return total

    ffn_a, ffn_b, attn_terms, own_terms = groups
    (
    query_ref,
    key_ref,
    value_ref,
    b_query_ref,
    b_value_ref,
    out_ref,
    b_out_ref,
    gain_attn_ref,
    shift_attn_ref,
    up_ref,
    b_in_ref,
    down_ref,
    b_down_ref,
    gain_ffn_ref,
    shift_ffn_ref,
    init_ref,
    ) = refs
    factor = jnp.concatenate([ref[...] for ref in factor_refs], 0)
    count, _, rows, width = factor.shape
    block = width // 2 // count
    column = lax.broadcasted_iota(jnp.int32, (rows, width), 1)

    def own(j, i):
        first, second = position(j, order_a), position(j, order_b) + count
        keep = (column // block == first) | (column // block == second)
        return jnp.where(keep, factor[j, i], jnp.zeros((), LOW))

    units = []
    for side, left, right in ((0, 3, 0), (1, 2, 1)):
        chosen = jnp.concatenate([own(j, left) for j in range(count)], 0)
        others = jnp.concatenate([factor[j, right] for j in range(count)], 0)
        product = tn(chosen, others)
        halves = []
        for i in range(2):
            total = total_of((ffn_a, ffn_b)[i], side)
            for j in range(count):
                at = (i * count + j) * block
                total = total + product[at : at + block]
            halves.append(total)
        units.append(jnp.concatenate(halves, 0))
    up_ref[...] = units[0]
    down_ref[...] = units[1]
    attn, own_total = total_of(attn_terms), total_of(own_terms)
    here = attn.shape[-1] // 2
    share = own_total.shape[0] - SUM_ROWS
    totals = []
    for m in range(4):
        row, column = m % 2 * share, m // 2 * here
        from_tokens = attn[row : row + share, column : column + here]
        totals.append(from_tokens + own_total[:share, m * here : (m + 1) * here])
    query_ref[...] = totals[0]
    key_ref[...] = totals[1]
    value_ref[...] = totals[2]
    out_ref[...] = totals[3].T
    pack = attn[2 * share : 2 * share + SUM_ROWS, :here] + own_total[share:, :here]
    refs = {
        "b_out": b_out_ref,
        "gain_attn": gain_attn_ref,
        "shift_attn": shift_attn_ref,
        "b_down": b_down_ref,
        "gain_ffn": gain_ffn_ref,
        "shift_ffn": shift_ffn_ref,
    }
    part = init_ref.shape[1]
    for i, name in enumerate(SUMS):
        refs[name][...] = pack[i : i + 1, :part]
    at = len(SUMS) + memory_rows
    init_ref[...] = pack[len(SUMS) : at, :part]
    heads_here, head_part = b_query_ref.shape
    for i in range(heads_here):
        columns = slice(i * head_part, (i + 1) * head_part)
        b_query_ref[i : i + 1, :] = pack[at : at + 1, columns]
        b_value_ref[i : i + 1, :] = pack[at + 1 : at + 2, columns]
    b_in_ref[:, :block] = pack[at + 2 : at + 3, :block]
    b_in_ref[:, block:] = pack[at + 3 : at + 4, :block]


def columns_of(head, head_dim, array, factor=None):
    lane = lax.broadcasted_iota(jnp.int32, array.shape, 1) // head_dim
    if factor is not None:
        array = array * jnp.asarray(factor, array.dtype)
    return jnp.where(lane == head, array, jnp.zeros((), array.dtype))


def memory_scores(memory_rows, km, mine):
    scores = nt(km, mine)
    real_key = lax.broadcasted_iota(jnp.int32, scores.shape, 0) < memory_rows
    return jnp.where(real_key, scores, NEGATIVE)


def token_attention(head_dim, place_ref, row_ref, column_ref, q_ref, k_ref, v_ref, sum_ref, stat_ref):
    q, k, v = q_ref[...], k_ref[...], v_ref[...]
    allowed = column_ref[...] == row_ref[...]
    stat_ref[...] = jnp.zeros_like(stat_ref)
    for head in range(q.shape[1] // head_dim):
        scores = nt(k, columns_of(head, head_dim, q, SCALE))
        scores = jnp.where(allowed, scores, NEGATIVE)
        top = jnp.max(scores, 0, keepdims=True)
        raised = jnp.exp(scores - top)
        stat_ref[0, 2 * head : 2 * head + 1] = top
        stat_ref[0, 2 * head + 1 : 2 * head + 2] = jnp.sum(raised, 0, keepdims=True)
        rows = slice(head * head_dim, (head + 1) * head_dim)
        sum_ref[0, rows] = tn(v, raised.astype(LOW))[rows]


def with_memory(memory_rows, head_dim, q, km, vm, sums, stats):
    mixed, logs = [], []
    for head in range(q.shape[1] // head_dim):
        scores = memory_scores(memory_rows, km, columns_of(head, head_dim, q, SCALE))
        top_before = stats[2 * head : 2 * head + 1]
        top = jnp.maximum(jnp.max(scores, 0, keepdims=True), top_before)
        raised = jnp.exp(scores - top)
        shrink = jnp.exp(top_before - top)
        total = stats[2 * head + 1 : 2 * head + 2] * shrink
        total = total + 2.0 * jnp.sum(raised, 0, keepdims=True)
        rows = slice(head * head_dim, (head + 1) * head_dim)
        both = sums[rows] * shrink + 2.0 * tn(vm, raised.astype(LOW))[rows]
        mixed.append(both * (1.0 / total))
        logs.append(top + jnp.log(total))
    return jnp.concatenate(mixed, 0).T.astype(LOW), logs


def token_attention_back(
    memory_rows,
    head_dim,
    place_ref,
    row_ref,
    column_ref,
    q_ref,
    k_ref,
    v_ref,
    qkv_ref,
    log_ref,
    grad_ref,
    dq_ref,
    dk_ref,
    dv_ref,
    dmem_ref,
):
    q, k, v, grad = (ref[...] for ref in (q_ref, k_ref, v_ref, grad_ref))
    km, vm = qkv_ref[place_ref[1], 1], qkv_ref[place_ref[1], 2]
    allowed = column_ref[...] == row_ref[...]
    lane = lax.broadcasted_iota(jnp.int32, q.shape, 1) // head_dim
    dq, dk, dv = (jnp.zeros(q.shape, FULL) for _ in range(3))
    dkm, dvm = (jnp.zeros(km.shape, FULL) for _ in range(2))
    for head in range(q.shape[1] // head_dim):
        mine = columns_of(head, head_dim, q, SCALE)
        mine_grad = columns_of(head, head_dim, grad)
        log_total = log_ref[0, head : head + 1]
        scores = jnp.where(allowed, nt(k, mine), NEGATIVE)
        soft = jnp.exp(scores - log_total)
        soft_mem = jnp.exp(memory_scores(memory_rows, km, mine) - log_total)
        pull, pull_mem = nt(v, mine_grad), nt(vm, mine_grad)
        inner = jnp.sum(soft * pull, 0, keepdims=True) + 2.0 * jnp.sum(
            soft_mem * pull_mem, 0, keepdims=True
        )
        score = (soft * (pull - inner)).astype(LOW)
        score_mem = (soft_mem * (pull_mem - inner)).astype(LOW)
        dq = jnp.where(lane == head, tn(score, k) + 2.0 * tn(score_mem, km), dq)
        dk = dk + nn(score, mine)
        dv = dv + nn(soft.astype(LOW), mine_grad)
        dkm = dkm + nn(score_mem, mine)
        dvm = dvm + nn(soft_mem.astype(LOW), mine_grad)
    dq_ref[...] = (SCALE * dq).astype(LOW)
    dk_ref[...] = dk.astype(LOW)
    dv_ref[...] = dv.astype(LOW)
    dmem_ref[:PAD] = dkm
    dmem_ref[PAD:] = dvm


def head_pairs(body, place, doc, operands, shapes, width, flops, steps, first=0):
    seg_len = operands[0].shape[0]

    def spec(array, first):
        if len(array.shape) == 4:
            return pl.BlockSpec((*array.shape[:3], width), lambda i: (0, 0, 0, i + first))
        if len(array.shape) == 3:
            return pl.BlockSpec((1, *array.shape[1:]), lambda i: (i + first, 0, 0))
        return pl.BlockSpec((array.shape[0], width), lambda i: (0, i + first))

    return pl.pallas_call(
        body,
        grid=(steps,),
        out_shape=shapes,
        in_specs=[pl.BlockSpec(memory_space=pltpu.SMEM)]
        + [pl.BlockSpec(a.shape, lambda i: (0, 0)) for a in doc]
        + [spec(a, first) for a in operands],
        out_specs=[spec(s, 0) for s in shapes],
        compiler_params=pltpu.CompilerParams(vmem_limit_bytes=VMEM_LIMIT),
        cost_estimate=pl.CostEstimate(
            flops=flops // 1000, bytes_accessed=seg_len, transcendentals=0
        ),
    )(place, *doc, *operands)


def on_device(
    tokens,
    doc_ids,
    reset,
    mem_init,
    w_query,
    w_key,
    w_value,
    b_query,
    b_value,
    w_out,
    b_out,
    gain_attn,
    shift_attn,
    w_in,
    b_in,
    w_down,
    b_down,
    gain_ffn,
    shift_ffn,
    cotangent,
):
    chains, segments, seg_len, width = tokens.shape
    dps, groups = lax.axis_size("dp"), lax.axis_size("head")
    assert chains == 1 and segments == groups
    memory_rows = mem_init.shape[0]
    heads_here, head_dim = b_query.shape
    heads = heads_here * groups
    here = heads_here * head_dim
    units = w_in.shape[1]
    half_units = units // 2
    quarter = seg_len // groups
    dp, head = lax.axis_index("dp"), lax.axis_index("head")
    place = jnp.stack([dp, head])
    bits = bits_of(dps)
    levels = len(bits)
    order_a = bits[1:] + bits[:1]
    order_b = bits[1:][::-1] + bits[:1]
    head_order = bits_of(groups)[::-1]
    head_stages = [("head", bit) for bit in head_order]
    stages_a = head_stages + [("dp", bit) for bit in order_a]
    stages_b = head_stages + [("dp", bit) for bit in order_b]
    layout = Units(dps, groups, half_units, width)
    landing = layout.scratch()
    shape = jax.ShapeDtypeStruct
    dp_stages = [("dp", bit) for bit in bits]
    bias_groups = (head_stages[:1], dp_stages[1:], head_stages[1:] + dp_stages[:1])
    bias_stages = [stage for group in bias_groups for stage in group]
    tokens, doc_ids, cotangent = tokens[0], doc_ids[0], cotangent[0]

    shard = jnp.concatenate([w_query.T, w_key.T, w_value.T, w_out], 0)
    share = shard.shape[0] // dps
    chunk = lax.dynamic_slice_in_dim(shard, dp * share, share, 0)[None]
    biases = jnp.concatenate([b_query.reshape(-1), b_value.reshape(-1), b_in])[None]
    up = w_in.T.reshape(2, half_units, width)
    down = w_down.reshape(2, half_units, width)
    halves = [jnp.stack([up[i], down[i]])[None] for i in range(2)]
    for i, stage in enumerate(head_stages):
        chunk = gather(chunk, [stage])
        if i:
            halves = [gather(half, [head_stages[i - 1]]) for half in halves]
        biases = gather(biases, bias_groups[i])
        chunk, biases, halves = lax.optimization_barrier((chunk, biases, halves))
    halves = [gather(half, head_stages[-1:]) for half in halves]
    biases = gather(biases, bias_groups[2])
    chunk = jnp.stack([chunk[position(j, head_order)] for j in range(1, groups)])
    sides = (slice(0, share // 2), slice(share // 2, share))
    parts = []
    for rows, order in zip(sides, (order_a, order_b)):
        part = gather(chunk[None, :, rows], [("dp", bit) for bit in order[:-2]])
        parts += [part, swap(part, "dp", order[-2])]
    doc = lax.dynamic_index_in_dim(doc_ids, head, 0, False)
    doc_row, doc_column = doc[None, :], doc[:, None]
    init = jnp.pad(mem_init.astype(FULL), ((0, PAD - memory_rows), (0, 0)))
    vectors = jnp.concatenate([b_out, gain_attn, shift_attn, b_down, gain_ffn, shift_ffn])
    vectors = vectors.reshape(-1, width)
    halves, parts, biases, cotangent, doc_row, doc_column, init, vectors = (
        lax.optimization_barrier(
            (halves, parts, biases, cotangent, doc_row, doc_column, init, vectors)
        )
    )
    cotangent = lax.all_to_all(cotangent, "head", 0, 0, tiled=True).reshape(seg_len, width)
    crossed = [swap(part, "dp", bits[0]) for part in parts]
    parts = [*parts[:2], *crossed[:2], *parts[2:], *crossed[2:]]
    if layout.whole:
        chunks = []
        for i, order in ((0, order_a), (4, order_b)):
            part = jnp.concatenate(parts[i : i + 4], 0)
            native = [position(dp ^ c, order) for c in range(dps)]
            chunks.append(jnp.stack([lax.dynamic_index_in_dim(part, n, 0, False) for n in native]))
        others = jnp.concatenate(chunks, 2).transpose(1, 0, 2, 3).reshape(groups - 1, 4, here, width)
        own = shard.reshape(4, 1, here, width)
        attn_pieces = [
            jnp.concatenate([own, others.transpose(1, 0, 2, 3)], 1).reshape(4, width, width)
        ]
    else:
        attn_pieces = [shard.reshape(4, here, width), *parts]
    halves = [
        gather(half, stages[len(head_stages) : -3])
        for half, stages in zip(halves, (stages_a, stages_b))
    ]
    across = [swap(half, *st[-3]) for half, st in zip(halves, (stages_a, stages_b))]
    along = [swap(half, *st[-2]) for half, st in zip(halves, (stages_a, stages_b))]

    keys, values, x, q, k, v, vectors, bias_in, w_attn = whole_call(
        functools.partial(project, layout, bias_stages, order_a, order_b, head_order),
        (place,),
        (tokens, biases, vectors),
        attn_pieces,
        (shape(tokens.shape, LOW),) * 2
        + (shape((seg_len, width), LOW),) * 4
        + (shape((len(VECTORS), width), FULL), shape((layout.chunks, 1, layout.size), FULL)),
        6_000_000_000,
        (
            pltpu.VMEM((4, width, width), LOW),
            pltpu.SemaphoreType.DMA((4 + 2 * dps * groups,)),
            pltpu.SemaphoreType.DMA(()),
        ),
        (shape((4, width, width), LOW),),
    )

    across, along, keys, q = lax.optimization_barrier((across, along, keys, q))
    corner = [swap(side, *stages[-2]) for side, stages in zip(across, (stages_a, stages_b))]
    pair = 2 * head_dim
    partial = head_pairs(
        functools.partial(token_attention, head_dim),
        place,
        (doc_row, doc_column),
        (q, k, v),
        (shape((width // pair, pair, seg_len), FULL), shape((width // pair, 8, seg_len), FULL)),
        pair,
        8_000_000_000,
        width // pair,
    )
    corner, partial, cotangent = lax.optimization_barrier((corner, partial, cotangent))
    pieces = []
    for *near, stages in zip(halves, across, along, corner, (stages_a, stages_b)):
        pieces += near + [swap(piece, *stages[-1]) for piece in near]
    if layout.whole:
        pieces = layout.assembled([jnp.concatenate(pieces[i : i + 8], 0) for i in (0, 8)])

    ff = layout.chunks * layout.size
    writes = segments - 1
    rows_shape = lambda kind: shape((writes, PAD, width), kind)
    tokens_scratch = lambda count: (
        pltpu.VMEM((4, width, width), LOW),
        pltpu.VMEM((count, seg_len, width), LOW),
        pltpu.VMEM((count, seg_len, width), LOW),
        pltpu.SemaphoreType.DMA((4,)),
        pltpu.SemaphoreType.DMA((count,)),
        pltpu.SemaphoreType.DMA((count,)),
    )
    read, qkv, soft, soft_mem, attended_w, z_attn_w, hidden_w, pre_w, z_ffn_w, norms = whole_call(
        functools.partial(chain_forward, layout, heads, memory_rows),
        (reset,),
        (init, bias_in, vectors),
        (w_attn, keys, values, *pieces),
        (
            shape((segments, PAD, width), FULL),
            shape((segments, 3, PAD, width), LOW),
            shape((writes, heads * PAD, seg_len), FULL),
            shape((writes, heads * PAD, PAD), FULL),
            rows_shape(LOW),
            rows_shape(FULL),
            rows_shape(LOW),
            shape((writes, PAD, ff), FULL),
            rows_shape(FULL),
            shape((1, 128), FULL),
        ),
        20_000_000_000,
        tokens_scratch(writes) + landing,
    )

    if layout.whole:
        grad_shapes = (shape((layout.chunks, 2, layout.size, width), LOW),)
    else:
        grad_shapes = (shape((layout.blocks // 2, 2, half_units, width), LOW),) * 4
    sides = 2 * max(layout.size // (layout.size if layout.whole else half_units), 1)
    (
        attended,
        log_total,
        result,
        grad_attn,
        grad_mixed,
        grad_attended,
        bias_sum,
        layer_sums,
        *ffn_grads,
    ) = whole_call(
        functools.partial(token_layer, layout, memory_rows, head_dim),
        (place,),
        (x, q, qkv, *partial, cotangent, bias_in, vectors),
        (w_attn, *pieces),
        (
            shape((seg_len, width), LOW),
            shape((width // pair, 8, seg_len), FULL),
            shape((seg_len, width), LOW),
            shape((seg_len, width), FULL),
            shape((seg_len, width), LOW),
            shape((seg_len, width), LOW),
            shape((layout.chunks, 1, layout.size), FULL),
            shape((8, width), FULL),
        ),
        25_000_000_000,
        (pltpu.VMEM((width, width), LOW), pltpu.SemaphoreType.DMA(()))
        + landing
        + (
            pltpu.VMEM((seg_len, width), FULL),
            pltpu.VMEM((seg_len, width), LOW),
            pltpu.VMEM((seg_len, width), LOW),
            pltpu.VMEM((seg_len, width), FULL),
            pltpu.VMEM((layout.chunks, seg_len, layout.size), FULL),
            pltpu.VMEM((layout.chunks, seg_len, layout.size), LOW),
            pltpu.VMEM((2, 2, layout.size, width), LOW),
            pltpu.SemaphoreType.DMA((layout.chunks, sides)),
        ),
        grad_shapes,
    )
    if layout.whole:
        half_blocks = layout.blocks // 2
        ffn_grads = [
            part
            for half in layout.taken_apart(ffn_grads[0])
            for part in (half[:half_blocks], half[half_blocks:])
        ]

    back_a, back_b = stages_a[::-1], stages_b[::-1]

    def stages_of(level):
        return back_a[level], back_b[level]

    def attention_back(block, count):
        cut = width // 2
        return head_pairs(
            functools.partial(token_attention_back, memory_rows, head_dim),
            place,
            (doc_row, doc_column),
            (q, k, v, qkv, log_total, grad_attended),
            (shape((seg_len, cut), LOW),) * 3 + (shape((2 * PAD, cut), FULL),),
            pair,
            10_000_000_000,
            count,
            block * count,
        )

    blocks = width // pair // 2
    moving = [
        [keep, swap(send, *back[0])]
        for keep, send, back in zip(ffn_grads[::2], ffn_grads[1::2], (back_a, back_b))
    ]
    back_low = attention_back(0, blocks)
    back_low, moving, grad_attended = lax.optimization_barrier((back_low, moving, grad_attended))
    output = lax.all_to_all(result.reshape(groups, quarter, width), "head", 0, 0, tiled=True)
    sends = parcels(moving)
    sends, grad_attended = lax.optimization_barrier((sends, grad_attended))
    moving = posted(moving, sends, stages_of(1))
    back_high = attention_back(1, blocks)
    token_part = jnp.concatenate([back_low[3], back_high[3]], 1)
    token_part, back_high = lax.optimization_barrier((token_part, back_high))
    token_parts = gather(token_part[None], head_stages[:1])
    share = width // dps
    rows_a, rows_b, rows_own = 2 * share + SUM_ROWS, 2 * share, share + SUM_ROWS
    keep_b, send_b, grad_x, value_sum = whole_call(
        functools.partial(value_grads, order_b, dps),
        (place,),
        (x, grad_mixed, attended, back_low[2], back_high[2], grad_attn),
        (w_attn,),
        (
            *(shape((dps // 2, rows_b, width), LOW),) * 2,
            shape((seg_len, width), FULL),
            shape((1, width), FULL),
        ),
        5_000_000_000,
        (pltpu.VMEM((width, width), LOW), pltpu.SemaphoreType.DMA(())),
    )
    down_a, down_b = ([("dp", bit) for bit in order[::-1]] for order in (order_a, order_b))
    grad_x, send_b, moving, token_parts, output = lax.optimization_barrier(
        (grad_x, send_b, moving, token_parts, output)
    )
    token_parts = gather(token_parts, head_stages[1:])
    other_b = swap(send_b, *down_b[0])
    sends = parcels(moving)
    sends, grad_x = lax.optimization_barrier((sends, grad_x))
    moving = posted(moving, sends, stages_of(2))
    for level in range(3, levels):
        moving = posted(moving, parcels(moving), stages_of(level))
    sum_scratch = (pltpu.VMEM((SUM_ROWS, width), FULL),)
    keep_a, send_a, grad_x = whole_call(
        functools.partial(
            query_key_grads, layout, order_a, order_b, head_order, heads_here, memory_rows
        ),
        (place,),
        (
            x,
            back_low[0],
            back_high[0],
            back_low[1],
            back_high[1],
            grad_x,
            value_sum,
            layer_sums,
            bias_sum,
        ),
        (w_attn,),
        (
            *(shape((dps // 2, rows_a, width), LOW),) * 2,
            shape((seg_len, width), LOW),
        ),
        10_000_000_000,
        sum_scratch + (pltpu.VMEM((2, width, width), LOW), pltpu.SemaphoreType.DMA((2,))),
    )

    def advance_both(parts, level):
        return [reduce_step(p, down[level]) for p, down in zip(parts, (down_a, down_b))]

    token_parts, send_a, other_b, grad_x, moving = lax.optimization_barrier(
        (token_parts, send_a, other_b, grad_x, moving)
    )
    attn_moving = [[keep_a, swap(send_a, *down_a[0])], [keep_b, other_b]]
    sends = parcels(moving, True)
    attn_moving, sends = lax.optimization_barrier((attn_moving, sends))
    others = swap(sends[0], *back_a[levels])
    sends = parcels(attn_moving)
    sends, grad_x, token_parts = lax.optimization_barrier((sends, grad_x, token_parts))
    attn_moving = posted(attn_moving, sends, (down_a[1], down_b[1]))
    moved = lax.all_to_all(grad_x.reshape(groups, quarter, width), "head", 0, 0, tiled=True)

    packed_rows = writes * memory_rows + (-writes * memory_rows) % PAD
    score_w, grad_attended_w, grad_mixed_w, small_w, factors, bias_w, vec_w, init_w, norms = whole_call(
        functools.partial(chain_backward, layout, head_order, heads, memory_rows),
        (reset, place),
        (
            bias_in,
            read,
            norms,
            vectors,
            qkv,
            soft,
            soft_mem,
            z_attn_w,
            pre_w,
            z_ffn_w,
            hidden_w,
            token_parts,
        ),
        (w_attn, keys, values, *pieces),
        (
            shape((writes, heads * PAD, seg_len), LOW),
            shape((writes, PAD, width), LOW),
            shape((writes, PAD, width), LOW),
            shape((segments, 3, PAD, width), LOW),
            shape((4, packed_rows, width), LOW),
            shape((layout.chunks, 1, layout.size), FULL),
            shape((len(VECTORS), width), FULL),
            shape((PAD, width), FULL),
            shape((1, 128), FULL),
        ),
        20_000_000_000,
        (
            pltpu.VMEM((writes, PAD, width), LOW),
            pltpu.VMEM((writes, PAD, ff), LOW),
            pltpu.VMEM((segments, 2 * PAD, width), FULL),
        )
        + tokens_scratch(segments)
        + landing,
    )
    score_w, factors, moving, others, attn_moving, moved = lax.optimization_barrier(
        (score_w, factors, moving, others, attn_moving, moved)
    )

    moving = [terms + [others[:, i]] for i, terms in enumerate(moving)]
    sends = parcels(moving + attn_moving, True)
    sends, score_w = lax.optimization_barrier((sends, score_w))
    others = swap(sends[0], *back_a[levels + 1])
    moving = [terms + [others[:, i]] for i, terms in enumerate(moving)]
    attn_moving = posted(attn_moving, sends[1:], (down_a[2], down_b[2]))
    for level in range(3, levels):
        attn_moving = advance_both(attn_moving, level)
    factors = gather(factors[None], [("dp", order_b[0])])
    keep_own, send_own = whole_call(
        functools.partial(
            own_grads, layout, order_a, order_b, head_order, heads, heads_here, memory_rows
        ),
        (place,),
        (
            score_w,
            soft,
            qkv,
            grad_attended_w,
            grad_mixed_w,
            attended_w,
            small_w,
            read,
            tokens,
            bias_w,
            vec_w,
            init_w,
        ),
        (),
        (shape((dps // 2, rows_own, width), LOW),) * 2,
        5_000_000_000,
        sum_scratch,
    )
    keep_own, send_own, attn_moving, factors, score_w, moving = lax.optimization_barrier(
        (keep_own, send_own, attn_moving, factors, score_w, moving)
    )
    own = [keep_own, swap(send_own, *down_a[0])]
    first_entry = lambda array: pl.BlockSpec(
        (1, *array.shape[1:]), lambda i: (0,) * len(array.shape)
    )
    half_group = shape((groups // 2, rows_a, 2 * here), LOW)
    terms = [t for group in attn_moving for t in group]
    attn_keep, attn_send = pl.pallas_call(
        functools.partial(by_group, head_stages, [len(group) for group in attn_moving]),
        grid=(1,),
        out_shape=(half_group, half_group),
        in_specs=[first_entry(t) for t in terms],
        out_specs=[pl.BlockSpec(half_group.shape, lambda i: (0, 0, 0))] * 2,
        compiler_params=pltpu.CompilerParams(vmem_limit_bytes=VMEM_LIMIT),
        cost_estimate=pl.CostEstimate(flops=1000, bytes_accessed=1000, transcendentals=0),
    )(*terms)
    attn_moving = [attn_keep]
    own_send = summed(own, LOW, own[-1].shape[0] // 2)
    attn_send, own_send, score_w = lax.optimization_barrier((attn_send, own_send, score_w))
    attn_moving = attn_moving + [swap(attn_send, "head", head_order[-1])]
    own = own + [swap(own_send, *down_a[1])]
    factors = gather(factors, [("dp", order_b[1])])
    for level in range(2, levels - 1):
        own = reduce_step(own, down_a[level])
    attn_send = summed(attn_moving, LOW, attn_moving[-1].shape[0] // 2)
    own_send = summed(own, LOW, own[-1].shape[0] // 2)
    attn_send, own_send, score_w = lax.optimization_barrier((attn_send, own_send, score_w))
    attn_moving = attn_moving + [swap(attn_send, "head", head_order[0])]
    own = own + [swap(own_send, *down_a[levels - 1])]
    factors = gather(factors, stages_b[len(head_stages) + 2 : -1])
    factors = [factors, swap(factors, *stages_b[-1])]
    (grad_tokens,) = whole_call(
        functools.partial(write_rows, heads, quarter),
        (place,),
        (score_w, soft, qkv, grad_attended_w, moved),
        (w_attn,),
        (shape((segments, quarter, width), FULL),),
        5_000_000_000,
        (pltpu.VMEM((2, width, width), LOW), pltpu.SemaphoreType.DMA((2,))),
    )
    grad_tokens, own, factors, attn_moving = lax.optimization_barrier(
        (grad_tokens, own, factors, attn_moving)
    )
    own, factors, attn_moving, moving = lax.optimization_barrier(
        (own, factors, attn_moving, moving)
    )
    part = width // dps // groups
    row = shape((1, part), FULL)
    groups_in = [factors, *moving, attn_moving, own]
    whole = lambda array: pl.BlockSpec(array.shape, lambda i: (0,) * len(array.shape))
    shapes = (
        *(shape((share, here), FULL),) * 3,
        *(shape((heads_here, head_dim // dps), FULL),) * 2,
        shape((here, share), FULL),
        *(row,) * 3,
        shape((units, width), FULL),
        shape((1, units), FULL),
        shape((units, width), FULL),
        *(row,) * 3,
        shape((memory_rows, part), FULL),
    )
    outs = pl.pallas_call(
        functools.partial(
            finish,
            order_in(order_a, order_b),
            order_in(order_b, order_b),
            memory_rows,
            [len(group) for group in groups_in],
        ),
        grid=(1,),
        out_shape=shapes,
        in_specs=[whole(a) for a in factors]
        + [first_entry(a) for group in groups_in[1:] for a in group],
        out_specs=[whole(a) for a in shapes],
        compiler_params=pltpu.CompilerParams(vmem_limit_bytes=VMEM_LIMIT),
        cost_estimate=pl.CostEstimate(flops=1000, bytes_accessed=1000, transcendentals=0),
    )(*(a for group in groups_in for a in group))
    flat = (6, 7, 8, 10, 12, 13, 14)
    outs = [out.reshape(-1) if i in flat else out for i, out in enumerate(outs)]
    outs[9] = outs[9].T
    return (output[None], norms[:, :segments], grad_tokens[None], *outs)


def solution(mesh):
    in_specs = (
        P("dp", None, None, None),
        P("dp", None, None),
        P("dp", None),
        P(),
        P(None, "head"),
        P(None, "head"),
        P(None, "head"),
        P("head", None),
        P("head", None),
        P("head", None),
        P(),
        P(),
        P(),
        P(None, ("dp", "head")),
        P(("dp", "head")),
        P(("dp", "head"), None),
        P(),
        P(),
        P(),
        P("dp", None, "head", None),
    )
    out_specs = (
        P("dp", None, "head", None),
        P("dp", None),
        P("dp", None, "head", None),
        P("dp", "head"),
        P("dp", "head"),
        P("dp", "head"),
        P("head", "dp"),
        P("head", "dp"),
        P("head", "dp"),
        P(("dp", "head")),
        P(("dp", "head")),
        P(("dp", "head")),
        P(None, ("dp", "head")),
        P(("dp", "head")),
        P(("dp", "head"), None),
        P(("dp", "head")),
        P(("dp", "head")),
        P(("dp", "head")),
        P(None, ("dp", "head")),
    )
    return jax.shard_map(
        on_device, mesh=mesh, in_specs=in_specs, out_specs=out_specs, check_vma=False
    )
```
